32 devices in a mesh: blk: 16 (over z, x, core), dp: 2 (over y).
Axes of the slice: x: 2, y: 2, z: 4, core: 2. Of those that a mesh axis runs over, the one named last changes fastest.
Arguments:
- hidden_in: bfloat16 [4, 4096, 512], P('dp', 'blk'), may hold values from -6 to 6
- item_lengths: int32 [4, 64], P('dp'), may hold values from 0 to 4096, as said below
- live_mask: int32 [4, 4096], P('dp', 'blk'), may hold values 0 or 1
- cotangent: bfloat16 [4, 4096, 512], P('dp', 'blk'), may hold values from -6 to 6
- query_weight: bfloat16 [512, 384], replicated, may hold values from -0.125 to 0.125
- key_weight: bfloat16 [512, 384], replicated, may hold values from -0.125 to 0.125
- value_weight: bfloat16 [512, 384], replicated, may hold values from -0.25 to 0.25
- output_weight: bfloat16 [384, 512], replicated, may hold values from -1.25 to 1.25
- bucket_bias_table: float32 [32, 6], replicated, may hold values from -4 to 4
- norm_attention: float32 [512], replicated, may hold values from 0.5 to 1.5
- norm_feed: float32 [512], replicated, may hold values from 0.5 to 1.5
- gate_weight: bfloat16 [512, 1024], replicated, may hold values from -0.25 to 0.25
- up_weight: bfloat16 [512, 1024], replicated, may hold values from -0.25 to 0.25
- down_weight: bfloat16 [1024, 512], replicated, may hold values from -0.1875 to 0.1875
Outputs:
- output: bfloat16 [4, 4096, 512], P('dp', 'blk')
- input_gradient: bfloat16 [4, 4096, 512], P('dp', 'blk')
- query_weight_gradient: float32 [512, 384], replicated
- key_weight_gradient: float32 [512, 384], replicated
- value_weight_gradient: float32 [512, 384], replicated
- output_weight_gradient: float32 [384, 512], replicated
- bias_table_gradient: float32 [32, 6], replicated
- norm_attention_gradient: float32 [512], replicated
- norm_feed_gradient: float32 [512], replicated
- gate_weight_grad_sum: float32 [512, 1024], replicated
- up_weight_gradient: float32 [512, 1024], replicated
- down_weight_gradient: float32 [1024, 512], replicated
The draws below stay inside these ranges and needn't reach their ends.
Inputs may be any that keep to these rules, and one draw needn't show every extreme that they name: `item_lengths`: row s lists the lengths of the items of stream s in order from the stream's first position, and sums to 4096; items may be empty. The first item of every row holds more than 3840 positions; one row, drawn from the seed, is a single item of 4096 positions followed by empty items.
All inputs are finite; a program needn't handle non-finite values. No bound on the sum of `live_mask` on one device may be relied on, other than what follows from the above.
Results may differ from the reference program's by a relative error of at most 0.03.
Values may be sent and summed in bfloat16 or wider, within the bound.
No kernel may reach another device: no remote copies, remote signals or barrier semaphores. Data moves between devices by JAX's collectives and lax.ppermute only.
A program may use at most 128 MiB of HBM per device.

```python
import math
import jax
import jax.numpy as jnp
from jax import lax

D = 512
HEADS = 6
HD = 64
FF = 1024
BUCKETS = 32
MAXDIST = 128
BLOCK = 256
STREAMS = 2
ITEMS = 64
INNER = 384
LEN = 4096
NSTREAMS = 4
N_DP = 2


def draw_item_lengths(key, part):
    key = jax.random.fold_in(key, 11)
    tail_key, cut_key, pick_key = jax.random.split(key, 3)
    stream_count = STREAMS * N_DP
    tails = jax.random.randint(tail_key, (stream_count,), 0, BLOCK).astype(jnp.int32)
    chosen = jax.random.randint(pick_key, (), 0, stream_count)
    tails = jnp.where(jnp.arange(stream_count, dtype=jnp.int32) == chosen, 0, tails).astype(jnp.int32)
    raw_cuts = jax.random.randint(cut_key, (stream_count, ITEMS - 2), 0, LEN).astype(jnp.int32)
    cut_points = jnp.sort(raw_cuts % (tails[:, None] + 1), axis=1)
    bounds = jnp.concatenate([jnp.zeros((stream_count, 1), jnp.int32), cut_points, tails[:, None]], axis=1)
    pieces = bounds[:, 1:] - bounds[:, :-1]
    first_item = (LEN - tails)[:, None]
    return jnp.concatenate([first_item, pieces], axis=1).astype(jnp.int32)


def with_ends(array, key, least, largest):
    extent = array.shape
    index_at = [jax.random.randint(jax.random.fold_in(key, axis), (), 0, extent[axis]) for axis in range(len(extent))]
    array = array.at[tuple(index_at)].set(least)
    longest = extent.index(max(extent))
    index_at[longest] = (index_at[longest] + 1) % extent[longest]
    return array.at[tuple(index_at)].set(largest)


def block_scale(rng, dims, cuts, low, top_value):
    gain = 1.0
    for dim, parts in cuts:
        heights = jax.random.uniform(jax.random.fold_in(jax.random.fold_in(rng, 6), dim), (parts,), jnp.float32, low / len(cuts), top_value / len(cuts))
        gain = gain * jnp.repeat(jnp.exp(heights), dims[dim] // parts).reshape((-1,) + (1,) * (len(dims) - 1 - dim))
    return gain


def centred(stream_key, shape, spread, most, cuts=(), kind=jnp.bfloat16):
    values = spread * jax.random.normal(stream_key, shape, jnp.float32)
    if cuts:
        values = values * block_scale(stream_key, shape, cuts, -0.22, 0.18)
    return jnp.clip(values, -most, most).astype(kind)


def setup_inputs(seed: int = 0) -> dict:
    streams_of = jax.random.split(jax.random.key(seed), 15)
    return {
        "hidden_in": centred(streams_of[0], (NSTREAMS, LEN, D), 1.0, 6.0, ((0, 2), (1, 16))),
        "item_lengths": draw_item_lengths(jax.random.fold_in(streams_of[14], 71), 0),
        "live_mask": with_ends((jax.random.randint(streams_of[2], (NSTREAMS, LEN), 0, 8) < 7).astype(jnp.int32), jax.random.fold_in(streams_of[2], 1), 0, 1),
        "cotangent": centred(streams_of[3], (NSTREAMS, LEN, D), 1.0, 6.0, ((0, 2), (1, 16))),
        "query_weight": centred(streams_of[4], (D, INNER), (4 * D) ** -0.5, 0.125),
        "key_weight": centred(streams_of[5], (D, INNER), (4 * D) ** -0.5, 0.125),
        "value_weight": centred(streams_of[6], (D, INNER), D ** -0.5, 0.25),
        "output_weight": centred(streams_of[7], (INNER, D), (INNER // 16) ** -0.5, 1.25),
        "bucket_bias_table": centred(streams_of[8], (BUCKETS, HEADS), 1.0, 4.0, (), jnp.float32),
        "norm_attention": jnp.clip(1.0 + 0.1 * jax.random.normal(streams_of[9], (D,), jnp.float32), 0.5, 1.5),
        "norm_feed": jnp.clip(1.0 + 0.1 * jax.random.normal(streams_of[10], (D,), jnp.float32), 0.5, 1.5),
        "gate_weight": centred(streams_of[11], (D, FF), D ** -0.5, 0.25),
        "up_weight": centred(streams_of[12], (D, FF), D ** -0.5, 0.25),
        "down_weight": centred(streams_of[13], (FF, D), FF ** -0.5, 0.1875),
    }


EPSILON = 1e-06
NEG_FILL = -1e+30
HIGHEST_PRECISION = lax.Precision.HIGHEST

@jax.custom_vjp
def low(v):
    return lax.optimization_barrier(v.astype(jnp.bfloat16)).astype(jnp.float32)

@jax.custom_vjp
def low_back(v):
    return v

def low_keep(v):
    return (low(v), None)

def low_pass(kept, grad):
    return (grad,)

def back_keep(v):
    return (v, None)

def back_low(kept, grad):
    return (low(grad),)
low.defvjp(low_keep, low_pass)
low_back.defvjp(back_keep, back_low)

def bucket_edges():
    half_count = BUCKETS // 2
    exact_count = half_count // 2
    log_levels = half_count - exact_count
    thresholds = []
    for level_index in range(1, log_levels):
        candidate = exact_count
        while candidate ** log_levels * exact_count ** level_index < MAXDIST ** level_index * exact_count ** log_levels:
            candidate = candidate + 1
        thresholds.append(candidate)
    return (half_count, exact_count, thresholds)

def relative_bucket_index(offsets):
    half_count, exact_count, thresholds = bucket_edges()
    distance = jnp.abs(offsets)
    beyond = jnp.zeros_like(offsets)
    for threshold in thresholds:
        beyond = beyond + (distance >= threshold).astype(jnp.int32)
    upper_half = jnp.where(offsets > 0, half_count, 0).astype(jnp.int32)
    return upper_half + jnp.where(distance < exact_count, distance, exact_count + beyond)

def rms_apply(values, gain_vector):
    inverse = lax.rsqrt(lax.optimization_barrier(jnp.mean(values * values, axis=-1, keepdims=True)) + EPSILON)
    return values * inverse * gain_vector

def gated_unit(gate_value, up_value):
    return jax.nn.gelu(gate_value, approximate=True) * up_value

def stream_attention(queries, keys, values, segments, live_flags, bucket_bias_table):
    key_positions_flat = jnp.arange(LEN, dtype=jnp.int32)
    query_block = math.gcd(LEN, 512)

    def one_block(block_start):
        block_queries = lax.dynamic_slice_in_dim(queries, block_start, query_block, 0)
        segment_query = lax.dynamic_slice_in_dim(segments, block_start, query_block, 0)
        query_places = block_start + jnp.arange(query_block, dtype=jnp.int32)
        buckets = relative_bucket_index(key_positions_flat[None, :] - query_places[:, None])
        relative_bias = jnp.transpose(bucket_bias_table[buckets], (2, 0, 1))
        scores = jnp.einsum('qhe,khe->hqk', block_queries, keys, precision=HIGHEST_PRECISION) + relative_bias
        scores = low_back(scores)
        attend_allowed = (segment_query[:, None] == segments[None, :]) & ((live_flags[None, :] > 0) | (query_places[:, None] == key_positions_flat[None, :]))
        masked = jnp.where(attend_allowed[None], scores, NEG_FILL)
        row_max = lax.optimization_barrier(jnp.max(masked, axis=-1, keepdims=True))
        exp_scores = jnp.where(attend_allowed[None], jnp.exp(masked - row_max), 0.0)
        probs_low = low(exp_scores / lax.optimization_barrier(jnp.sum(exp_scores, axis=-1, keepdims=True)))
        return jnp.einsum('hqk,khe->qhe', probs_low, values, precision=HIGHEST_PRECISION)
    starts = jnp.arange(LEN // query_block, dtype=jnp.int32) * query_block
    blocks_out = lax.map(jax.checkpoint(one_block), starts)
    return blocks_out.reshape(LEN, HEADS, HD)

def reference(hidden_in, item_lengths, live_mask, cotangent, query_weight, key_weight, value_weight, output_weight, bucket_bias_table, norm_attention, norm_feed, gate_weight, up_weight, down_weight):
    item_ends = jnp.cumsum(item_lengths, axis=1)
    places = jnp.arange(LEN, dtype=jnp.int32)
    segments = lax.optimization_barrier(jnp.sum((places[None, :, None] >= item_ends[:, None, :]).astype(jnp.int32), axis=2))

    def dot_high(left, right):
        return jnp.dot(left, right, precision=HIGHEST_PRECISION, preferred_element_type=jnp.float32)

    def forward(flat_in, query_matrix, key_matrix, value_matrix, output_matrix, table_values, gain_attention, gain_feed, gate_matrix, up_matrix, down_matrix):
        attn_in = low(rms_apply(flat_in, gain_attention))

        def project(matrix):
            return low_back(low(dot_high(attn_in, matrix))).reshape(NSTREAMS, LEN, HEADS, HD)
        queries = project(query_matrix)
        keys = project(key_matrix)
        values = project(value_matrix)

        def one_stream(stream_parts):
            return stream_attention(stream_parts[0], stream_parts[1], stream_parts[2], stream_parts[3], stream_parts[4], table_values)
        context = lax.map(one_stream, (queries, keys, values, segments, live_mask))
        context = low_back(low(context.reshape(NSTREAMS * LEN, HEADS * HD)))
        attention_out = low_back(dot_high(context, output_matrix))
        residual = flat_in + attention_out
        feed_in = low(rms_apply(residual, gain_feed))
        gate_value = low_back(dot_high(feed_in, gate_matrix))
        up_value = low_back(dot_high(feed_in, up_matrix))
        hidden_act = low(gated_unit(gate_value, up_value))
        return residual + dot_high(hidden_act, down_matrix)
    float_args = (hidden_in.reshape(NSTREAMS * LEN, D).astype(jnp.float32), query_weight.astype(jnp.float32), key_weight.astype(jnp.float32), value_weight.astype(jnp.float32), output_weight.astype(jnp.float32), bucket_bias_table.astype(jnp.float32), norm_attention.astype(jnp.float32), norm_feed.astype(jnp.float32), gate_weight.astype(jnp.float32), up_weight.astype(jnp.float32), down_weight.astype(jnp.float32))
    output, pullback = jax.vjp(forward, *float_args)
    grads = pullback(cotangent.reshape(NSTREAMS * LEN, D).astype(jnp.float32))
    return (output.reshape(NSTREAMS, LEN, D).astype(jnp.bfloat16), grads[0].reshape(NSTREAMS, LEN, D).astype(jnp.bfloat16), grads[1], grads[2], grads[3], grads[4], grads[5], grads[6], grads[7], grads[8], grads[9], grads[10])
```

```python
import functools

import jax
import jax.numpy as jnp
from jax import lax
from jax.experimental import pallas as pl
from jax.experimental.pallas import tpu as pltpu
from jax.sharding import PartitionSpec as P

HEADS = 6
HD = 64
PAIRS = HEADS // 2
BUCKETS = 32
MAXDIST = 128
EPSILON = 1e-06
BIG = 1e30
TILE = 128
LOW = jnp.bfloat16
WIDE = jnp.float32
VMEM_LIMIT = 56 * 1024 * 1024


def bucket_edges():
    half_count = BUCKETS // 2
    exact_count = half_count // 2
    log_levels = half_count - exact_count
    thresholds = []
    for level_index in range(1, log_levels):
        candidate = exact_count
        while (
            candidate**log_levels * exact_count**level_index
            < MAXDIST**level_index * exact_count**log_levels
        ):
            candidate = candidate + 1
        thresholds.append(candidate)
    return (half_count, exact_count, thresholds)


def relative_bucket_index(offsets):
    half_count, exact_count, thresholds = bucket_edges()
    distance = jnp.abs(offsets)
    beyond = jnp.zeros_like(offsets)
    for threshold in thresholds:
        beyond = beyond + (distance >= threshold).astype(jnp.int32)
    upper_half = jnp.where(offsets > 0, half_count, 0).astype(jnp.int32)
    return upper_half + jnp.where(distance < exact_count, distance, exact_count + beyond)


FAR_BEFORE = BUCKETS // 2 - 1
FAR_AFTER = BUCKETS - 1
NEAR = 3 * TILE
TURN = 4 * TILE


def rms_apply(values, gain_vector):
    inverse = lax.rsqrt(jnp.mean(values * values, axis=-1, keepdims=True) + EPSILON)
    return values * inverse * gain_vector


def gated_unit(gate_value, up_value):
    return jax.nn.gelu(gate_value, approximate=True) * up_value


def dot_nt(left, right):
    return lax.dot_general(
        left, right, (((1,), (1,)), ((), ())), preferred_element_type=WIDE
    )


def dot_nn(left, right):
    return jnp.dot(left, right, preferred_element_type=WIDE)


def pair_columns(pair):
    return pl.ds(pl.multiple_of(pair * 2 * HD, 2 * HD), 2 * HD)


def lane_ids():
    return lax.broadcasted_iota(jnp.int32, (1, 2 * HD), 1)


def half_of(array, head_in_pair):
    keep = (lane_ids() // HD) == head_in_pair
    return jnp.where(keep, array, jnp.zeros_like(array))


def column(array, index):
    picked = jnp.where(lane_ids() == index, array, 0.0)
    return jnp.sum(picked, axis=1, keepdims=True)


def build_strip(strip_ref, near_ref, vec_ref, far_ref, before_base, after_base, chunk):
    edge = chunk - TILE
    for head in range(HEADS):
        row = jnp.broadcast_to(vec_ref[head : head + 1, :], (TILE, TURN))
        near = pltpu.roll(row, 0, 1, stride=1, stride_axis=0)[:, :NEAR]
        near_ref[head] = near
        if strip_ref is not None:
            width = strip_ref.shape[2]
            strip_ref[head, :, : edge - TILE] = jnp.full(
                (TILE, edge - TILE), far_ref[before_base + head], WIDE
            )
            strip_ref[head, :, edge - TILE : edge + 2 * TILE] = near
            rest = width - edge - 2 * TILE
            strip_ref[head, :, edge + 2 * TILE :] = jnp.full(
                (TILE, rest), far_ref[after_base + head], WIDE
            )


def tile_place(tile, core):
    per_block = 2
    return (tile // per_block) * 2 * per_block + core * per_block + tile % per_block


def strip_slice(strip_ref, head, tile, core, chunk):
    start = (chunk - TILE) - tile_place(tile, core) * TILE
    return strip_ref[head, :, pl.ds(pl.multiple_of(start, TILE), chunk)]


def project(a_ref, w_ref, qkv_ref, chunk):
    for part in range(3):
        cols = slice(part * HEADS * HD, (part + 1) * HEADS * HD)
        qkv_ref[:, cols] = dot_nn(a_ref[:chunk, :], w_ref[:, cols]).astype(LOW)


def live_row(a_ref, chunk):
    rows = a_ref[chunk : chunk + 16, :].astype(WIDE)
    return jnp.concatenate([rows[0:1, :], rows[1:2, :]], axis=1)


def forward_own_kernel(
    sc_ref, far_ref, a_ref, w_ref, vec_ref, qinfo_ref, kinfo_ref,
    qkv_ref, mask_ref, qm_ref, acc_ref, ml_ref,
    strip_ref, near_ref, gen_ref,
):
    core, first_end, quad = sc_ref[3], sc_ref[4], sc_ref[2]
    chunk = qkv_ref.shape[0]
    mine = acc_ref.shape[0]
    block = mine // 2
    inner = HEADS * HD
    project(a_ref, w_ref, qkv_ref, chunk)
    build_strip(strip_ref, near_ref, vec_ref, far_ref, 0, 8, chunk)
    live = live_row(a_ref, chunk)
    places = quad * chunk + lax.broadcasted_iota(jnp.int32, (1, chunk), 1)
    seen = (live > 0.5) & (places < first_end)
    mask_ref[0] = jnp.broadcast_to(jnp.where(seen, 0.0, -BIG), (8, chunk))
    visible = (qinfo_ref[:, 0:1] == kinfo_ref[0:1, :]) & (
        (live > 0.5) | (qinfo_ref[:, 1:2] == kinfo_ref[1:2, :])
    )
    gen_ref[...] = jnp.where(visible, 0.0, -BIG)
    for part in range(2):
        start = pl.multiple_of(core * block + part * 2 * block, block)
        q_rows = qkv_ref[pl.ds(start, block), 2 * inner :]
        for head in range(HEADS):
            pair = q_rows[:, (head // 2) * 2 * HD : (head // 2 + 1) * 2 * HD]
            qm_ref[head, part * block : (part + 1) * block, :] = half_of(pair, head % 2)
    ml_ref[...] = jnp.zeros_like(ml_ref)
    lane = lane_ids()

    def one_pair(pair, carry):
        cols = pair_columns(pair)
        k_pair = qkv_ref[:, cols]
        v_pair = qkv_ref[:, pl.ds(pl.multiple_of(inner + pair * 2 * HD, 2 * HD), 2 * HD)]
        v_ext = [jnp.where(lane // HD == hh, v_pair, jnp.ones_like(v_pair)) for hh in range(2)]
        for tile in range(mine // TILE):
            rows = slice(tile * TILE, (tile + 1) * TILE)
            ml = ml_ref[rows, :]
            sums = []
            for hh in range(2):
                head = pair * 2 + hh
                s = dot_nt(qm_ref[head, rows, :], k_pair)
                s = s + strip_slice(strip_ref, head, tile, core, chunk) + gen_ref[rows, :]
                top = jnp.max(s, axis=1, keepdims=True)
                p = jnp.exp(s - top).astype(LOW)
                pv = dot_nn(p, v_ext[hh])
                total = pv[:, HD * (1 - hh) : HD * (1 - hh) + 1]
                ml = jnp.where(lane == head, top, ml)
                ml = jnp.where(lane == head + 8, total, ml)
                sums.append(pv)
            ml_ref[rows, :] = ml
            acc_ref[rows, cols] = jnp.where(lane < HD, sums[0], sums[1])
        return carry

    lax.fori_loop(0, PAIRS, one_pair, 0)


def forward_kernel(
    sc_ref, far_ref, a_ref, w_ref, vec_ref, qinfo_ref, qm_ref, acc_in, ml_in, qkv_in, mask_in,
    qkv_ref, mask_ref, acc_ref, ml_ref,
    near_ref,
):
    valid, place, quad, core, first_end = (sc_ref[i] for i in range(5))
    chunk = qkv_ref.shape[0]
    mine = acc_ref.shape[0]
    inner = HEADS * HD
    acc_ref[...] = acc_in[...]
    ml_ref[...] = ml_in[...]
    lane = lane_ids()

    @pl.when(valid > 0)
    def _():
        project(a_ref, w_ref, qkv_ref, chunk)
        build_strip(None, near_ref, vec_ref, far_ref, 0, 8, chunk)
        live = live_row(a_ref, chunk)
        places = place * chunk + lax.broadcasted_iota(jnp.int32, (1, chunk), 1)
        seen = (live > 0.5) & (places < first_end)
        mask = jnp.where(seen, 0.0, -BIG)
        mask_ref[0] = jnp.broadcast_to(mask, (8, chunk))
        far_base = jnp.where(place > quad, 8, 0)
        fix_low = jnp.where((place == quad - 1) & (core == 0), 1.0, 0.0)
        fix_high = jnp.where((place == quad + 1) & (core == 1), 1.0, 0.0)
        rows_each = 2 * TILE

        def one_pair(pair, carry):
            cols = pair_columns(pair)
            k_pair = qkv_ref[:, cols]
            v_pair = qkv_ref[:, pl.ds(pl.multiple_of(inner + pair * 2 * HD, 2 * HD), 2 * HD)]
            v_ext = [
                jnp.where(lane // HD == hh, v_pair, jnp.ones_like(v_pair)) for hh in range(2)
            ]
            for step in range(mine // rows_each):
                rows = slice(step * rows_each, (step + 1) * rows_each)
                ml = ml_ref[rows, :]
                pen = qinfo_ref[rows, 2:3]
                sums = []
                for hh in range(2):
                    head = pair * 2 + hh
                    far = far_ref[far_base + head]
                    s = dot_nt(qm_ref[head, rows, :], k_pair) + (mask + far)
                    if step == 0:
                        fix = fix_low * (near_ref[head, :, :TILE] - far)
                        upper = jnp.concatenate(
                            [s[:TILE, : chunk - TILE], s[:TILE, chunk - TILE :] + fix], axis=1
                        )
                        s = jnp.concatenate([upper, s[TILE:]], axis=0)
                    if step == mine // rows_each - 1:
                        fix = fix_high * (near_ref[head, :, 2 * TILE :] - far)
                        lower = jnp.concatenate([s[TILE:, :TILE] + fix, s[TILE:, TILE:]], axis=1)
                        s = jnp.concatenate([s[:TILE], lower], axis=0)
                    old = column(ml, head)
                    top = jnp.maximum(old, jnp.max(s, axis=1, keepdims=True) - pen)
                    p = jnp.exp(s - (top + pen)).astype(LOW)
                    pv = dot_nn(p, v_ext[hh])
                    keep = jnp.exp(old - top)
                    total = column(ml, head + 8) * keep + pv[:, HD * (1 - hh) : HD * (1 - hh) + 1]
                    ml = jnp.where(lane == head, top, ml)
                    ml = jnp.where(lane == head + 8, total, ml)
                    sums.append((keep, pv))
                ml_ref[rows, :] = ml
                scale = jnp.where(lane < HD, sums[0][0], sums[1][0])
                added = jnp.where(lane < HD, sums[0][1], sums[1][1])
                acc_ref[rows, cols] = acc_ref[rows, cols] * scale + added
            return carry

        lax.fori_loop(0, PAIRS, one_pair, 0)


def queries_kernel(
    sc_ref, far_ref, qkv_ref, mask_ref, vec_ref, qm_ref, dom_ref, ld_ref, qinfo_ref, kinfo_ref, gen_in,
    dq_ref, diag_ref, sums_ref,
    strip_ref, near_ref, dq6_ref, grad_near_ref,
):
    quad, core = sc_ref[2], sc_ref[3]
    place = pl.program_id(0)
    chunk = qkv_ref.shape[0]
    mine = dq_ref.shape[0]
    inner = HEADS * HD
    lane = lane_ids()

    @pl.when(place == 0)
    def _():
        build_strip(strip_ref, near_ref, vec_ref, far_ref, 0, 8, chunk)
        dq6_ref[...] = jnp.zeros_like(dq6_ref)
        grad_near_ref[...] = jnp.zeros_like(grad_near_ref)

    block_of_key = lax.broadcasted_iota(jnp.int32, (chunk, 2 * HD), 0) // TILE
    gap = place - quad
    spread = jnp.where(jnp.abs(gap) <= 1, 1, 0)
    first_lane = jnp.where(spread == 1, 16 + 8 * gap, jnp.where(gap < 0, 0, 1))
    lane_of_key = first_lane + spread * block_of_key

    def operands(pair):
        cols = pair_columns(pair)
        k_pair = qkv_ref[:, cols]
        v_pair = qkv_ref[:, pl.ds(pl.multiple_of(inner + pair * 2 * HD, 2 * HD), 2 * HD)]
        k_ext = []
        for hh in range(2):
            other = lane - HD * (1 - hh)
            marks = jnp.where(other == lane_of_key, 1.0, 0.0).astype(LOW)
            k_ext.append(jnp.where(lane // HD == hh, k_pair, marks))
        return k_pair, v_pair, k_ext

    @pl.when(place == quad)
    def _():
        def one_pair(pair, carry):
            k_pair, v_pair, k_ext = operands(pair)
            for tile in range(mine // TILE):
                rows = slice(tile * TILE, (tile + 1) * TILE)
                ld = ld_ref[rows, :]
                for hh in range(2):
                    head = pair * 2 + hh
                    s = dot_nt(qm_ref[head, rows, :], k_pair)
                    s = s + strip_slice(strip_ref, head, tile, core, chunk) + gen_in[rows, :]
                    p = jnp.exp(s - column(ld, head))
                    dp = dot_nt(dom_ref[head, rows, :], v_pair)
                    ds = (p * (dp - column(ld, head + 8))).astype(LOW)
                    dq6_ref[head, rows, :] += dot_nn(ds, k_ext[hh])
                    where = tile_place(tile, core)
                    ds_wide = ds.astype(WIDE)
                    for step in range(chunk // TILE):
                        shift = step - where
                        part = ds_wide[:, step * TILE : (step + 1) * TILE]

                        @pl.when((shift >= -1) & (shift <= 1))
                        def _():
                            at = pl.ds(pl.multiple_of((shift + 1) * TILE, TILE), TILE)
                            grad_near_ref[head, :, at] += part

            return carry

        lax.fori_loop(0, PAIRS, one_pair, 0)

    @pl.when(place != quad)
    def _():
        far_base = jnp.where(place > quad, 8, 0)
        fix_low = jnp.where((place == quad - 1) & (core == 0), 1.0, 0.0)
        fix_high = jnp.where((place == quad + 1) & (core == 1), 1.0, 0.0)
        rows_each = 2 * TILE
        mask = mask_ref[0, 0:1, :]

        def one_pair(pair, carry):
            k_pair, v_pair, k_ext = operands(pair)
            for step in range(mine // rows_each):
                rows = slice(step * rows_each, (step + 1) * rows_each)
                ld = ld_ref[rows, :]
                pen = qinfo_ref[rows, 2:3]
                for hh in range(2):
                    head = pair * 2 + hh
                    far = far_ref[far_base + head]
                    s = dot_nt(qm_ref[head, rows, :], k_pair) + (mask + far)
                    if step == 0:
                        fix = fix_low * (near_ref[head, :, :TILE] - far)
                        upper = jnp.concatenate(
                            [s[:TILE, : chunk - TILE], s[:TILE, chunk - TILE :] + fix], axis=1
                        )
                        s = jnp.concatenate([upper, s[TILE:]], axis=0)
                    if step == mine // rows_each - 1:
                        fix = fix_high * (near_ref[head, :, 2 * TILE :] - far)
                        lower = jnp.concatenate([s[TILE:, :TILE] + fix, s[TILE:, TILE:]], axis=1)
                        s = jnp.concatenate([s[:TILE], lower], axis=0)
                    p = jnp.exp(s - (column(ld, head) + pen))
                    dp = dot_nt(dom_ref[head, rows, :], v_pair)
                    ds = (p * (dp - column(ld, head + 8))).astype(LOW)
                    dq6_ref[head, rows, :] += dot_nn(ds, k_ext[hh])
                    if step == 0:
                        grad_near_ref[head, :, :TILE] += fix_low * ds[
                            :TILE, chunk - TILE :
                        ].astype(WIDE)
                    if step == mine // rows_each - 1:
                        grad_near_ref[head, :, 2 * TILE :] += fix_high * ds[TILE:, :TILE].astype(
                            WIDE
                        )
            return carry

        lax.fori_loop(0, PAIRS, one_pair, 0)

    @pl.when(place == pl.num_programs(0) - 1)
    def _():
        flip = (
            lax.broadcasted_iota(jnp.int32, (TILE, TILE), 0)
            + lax.broadcasted_iota(jnp.int32, (TILE, TILE), 1)
            == TILE - 1
        ).astype(WIDE)
        diag_ref[...] = jnp.zeros_like(diag_ref)
        sums_ref[...] = jnp.zeros_like(sums_ref)
        for head in range(HEADS):
            turned = jnp.dot(
                flip, grad_near_ref[head], precision=lax.Precision.HIGHEST,
                preferred_element_type=WIDE,
            )
            wide = jnp.concatenate([turned, jnp.zeros((TILE, TURN - NEAR), WIDE)], axis=1)
            skewed = pltpu.roll(wide, 0, 1, stride=1, stride_axis=0)
            diag_ref[head : head + 1, :] = jnp.sum(skewed, axis=0, keepdims=True)
            for tile in range(mine // TILE):
                rows = slice(tile * TILE, (tile + 1) * TILE)
                sums_ref[head, tile : tile + 1, :] = jnp.sum(
                    dq6_ref[head, rows, :], axis=0, keepdims=True
                )
        for pair in range(PAIRS):
            dq_ref[:, pair * 2 * HD : (pair + 1) * 2 * HD] = jnp.where(
                lane < HD, dq6_ref[2 * pair], dq6_ref[2 * pair + 1]
            ).astype(LOW)


def keys_kernel(
    own, sc_ref, far_ref, pieces_ref, dox_ref, q_ref, kv0_ref, kv1_ref, vec_ref, kinfo_ref, rowinfo_ref, dkv_in,
    dkv_ref,
    strip_ref, near_ref, gen_ref,
):
    valid, place, quad, core = (sc_ref[i] for i in range(4))
    chunk = q_ref.shape[0]
    mine = dkv_ref.shape[0]
    block = mine // 2
    inner = HEADS * HD
    lane = lane_ids()
    if own:
        build_strip(strip_ref, near_ref, vec_ref, far_ref, 8, 0, chunk)
        visible = (kinfo_ref[:, 0:1] == rowinfo_ref[0:1, :]) & (
            (kinfo_ref[:, 3:4] > 0.5) | (kinfo_ref[:, 1:2] == rowinfo_ref[1:2, :])
        )
        gen_ref[...] = jnp.where(visible, 0.0, -BIG)
    else:
        dkv_ref[...] = dkv_in[...]

    @pl.when(valid > 0)
    def _():
        if not own:
            build_strip(None, near_ref, vec_ref, far_ref, 8, 0, chunk)
        far_base = jnp.where(place > quad, 0, 8)
        fix_low = jnp.where((place == quad - 1) & (core == 0), 1.0, 0.0)
        fix_high = jnp.where((place == quad + 1) & (core == 1), 1.0, 0.0)
        ext = dox_ref[:, inner:]
        rows_each = TILE if own else 2 * TILE

        def one_pair(pair, carry):
            cols = pair_columns(pair)
            vcols = pl.ds(pl.multiple_of(inner + pair * 2 * HD, 2 * HD), 2 * HD)
            q_pair = q_ref[:, cols]
            do_pair = dox_ref[:, cols]
            q_ext = jnp.concatenate([q_pair, ext], axis=1)
            do_ext = jnp.concatenate([do_pair, ext], axis=1)
            for step in range(mine // rows_each):
                start = step * rows_each
                rows = slice(start, start + rows_each)
                half_ref = kv0_ref if start < block else kv1_ref
                inside = slice(start % block, start % block + rows_each)
                k_rows = half_ref[inside, cols]
                v_rows = half_ref[inside, vcols]
                grads = []
                for hh in range(2):
                    head = pair * 2 + hh
                    marks = jnp.where(
                        (lane == head) | (lane == head + 6) | (lane == head + 12), 1.0, 0.0
                    )
                    if own:
                        marks = jnp.broadcast_to(marks, (rows_each, 2 * HD))
                    else:
                        for number, at in enumerate((36, 38, 39)):
                            marks = jnp.where(
                                lane == at, pieces_ref[number * 16 + far_base + head], marks
                            )
                        marks = jnp.where(lane == 37, 1.0, marks)
                        marks = jnp.where(lane == 40, kinfo_ref[rows, 2:3], marks)
                    s = dot_nt(
                        jnp.concatenate([half_of(k_rows, hh), marks.astype(LOW)], axis=1), q_ext
                    )
                    if own:
                        s = s + strip_slice(strip_ref, head, step, core, chunk) + gen_ref[rows, :]
                    else:
                        far = far_ref[far_base + head]
                        if step == 0:
                            fix = fix_low * (near_ref[head, :, :TILE] - far)
                            upper = jnp.concatenate(
                                [s[:TILE, : chunk - TILE], s[:TILE, chunk - TILE :] + fix], axis=1
                            )
                            s = jnp.concatenate([upper, s[TILE:]], axis=0)
                        if step == mine // rows_each - 1:
                            fix = fix_high * (near_ref[head, :, 2 * TILE :] - far)
                            lower = jnp.concatenate(
                                [s[TILE:, :TILE] + fix, s[TILE:, TILE:]], axis=1
                            )
                            s = jnp.concatenate([s[:TILE], lower], axis=0)
                    p = jnp.exp(s)
                    grad_v = dot_nn(p.astype(LOW), do_pair)
                    delta_marks = jnp.where(
                        (lane == head + 18) | (lane == head + 24) | (lane == head + 30), 1.0, 0.0
                    )
                    delta_marks = jnp.broadcast_to(delta_marks, (rows_each, 2 * HD)).astype(LOW)
                    dp = dot_nt(
                        jnp.concatenate([half_of(v_rows, hh), delta_marks], axis=1), do_ext
                    )
                    ds = (p * dp).astype(LOW)
                    grads.append((dot_nn(ds, q_pair), grad_v))
                grad_k = jnp.where(lane < HD, grads[0][0], grads[1][0])
                grad_v = jnp.where(lane < HD, grads[0][1], grads[1][1])
                if own:
                    dkv_ref[rows, cols] = grad_k
                    dkv_ref[rows, vcols] = grad_v
                else:
                    dkv_ref[rows, cols] += grad_k
                    dkv_ref[rows, vcols] += grad_v
            return carry

        lax.fori_loop(0, PAIRS, one_pair, 0)


def group_sum(value, plan):
    for axis, size, index, pairs in plan:
        part = value.shape[0] // size
        total = lax.dynamic_slice_in_dim(value, index * part, part, 0).astype(WIDE)
        for shift in range(1, size):
            target = (index + shift) % size
            sent = lax.dynamic_slice_in_dim(value, target * part, part, 0)
            total = total + lax.ppermute(sent, axis, pairs(shift)).astype(WIDE)
        value = total.astype(LOW)
    for axis, size, index, pairs in reversed(plan):
        gathered = [value]
        for shift in range(1, size):
            gathered.append(lax.ppermute(value, axis, pairs(shift)))
        if size == 2:
            low = jnp.where(index == 0, gathered[0], gathered[1])
            high = jnp.where(index == 0, gathered[1], gathered[0])
            value = jnp.concatenate([low, high], axis=0)
        else:
            whole = jnp.zeros((size,) + value.shape, value.dtype)
            for shift, part in enumerate(gathered):
                whole = lax.dynamic_update_slice_in_dim(
                    whole, part[None], (index - shift) % size, 0
                )
            value = whole.reshape((-1,) + value.shape[1:])
    return value.astype(WIDE)


def padded_rows(arrays, multiple):
    stacked = jnp.concatenate([a.astype(LOW) for a in arrays], axis=0)
    short = -stacked.shape[0] % multiple
    return jnp.pad(stacked, ((0, short), (0, 0)))


def body(
    hidden_in,
    item_lengths,
    live_mask,
    cotangent,
    query_weight,
    key_weight,
    value_weight,
    output_weight,
    bucket_bias_table,
    norm_attention,
    norm_feed,
    gate_weight,
    up_weight,
    down_weight,
):
    streams, block, width = hidden_in.shape
    inner = query_weight.shape[1]
    blocks = lax.axis_size("blk")
    parts = lax.axis_size("dp")
    quads = blocks // 4
    here = lax.axis_index("blk")
    core, side, quad = here % 2, (here // 2) % 2, here // 4
    mine, chunk = 2 * block, 4 * block

    across = [(k, k ^ 2) for k in range(blocks)]
    between = [(k, k ^ 1) for k in range(blocks)]
    onward = []
    for k in range(blocks):
        if k % 2 == 0:
            onward.append((k, k + 4 if k + 4 < blocks else k + 1))
        else:
            onward.append((k, k - 4 if k >= 4 else k - 1))

    def to_streams(both):
        kept = lax.dynamic_index_in_dim(both, side, 0, False)
        sent = lax.dynamic_index_in_dim(both, 1 - side, 0, False)
        got = lax.ppermute(sent, "blk", across)
        return jnp.where(side == 0, kept, got), jnp.where(side == 0, got, kept)

    def from_streams(rows):
        split = rows.reshape(2, block, rows.shape[1])
        kept = lax.dynamic_index_in_dim(split, side, 0, False)
        sent = lax.dynamic_index_in_dim(split, 1 - side, 0, False)
        got = lax.ppermute(sent, "blk", across)
        return jnp.stack([jnp.where(side == 0, kept, got), jnp.where(side == 0, got, kept)])

    def with_other_core(rows):
        got = lax.ppermute(rows, "blk", between)
        return jnp.where(core == 0, rows, got), jnp.where(core == 0, got, rows)

    live_rows = jnp.pad(live_mask.astype(LOW)[:, None, :], ((0, 0), (0, 15), (0, width - block)))
    first, second = to_streams(jnp.concatenate([hidden_in, live_rows], axis=1))
    x_low = jnp.concatenate([first[:block], second[:block]], axis=0)
    live_own = jnp.concatenate([first[block, :block], second[block, :block]])
    x = x_low.astype(WIDE)
    attn_in = rms_apply(x, norm_attention).astype(LOW)
    packed = jnp.concatenate([attn_in, jnp.pad(live_own[None, :], ((0, 15), (0, 0)))], axis=0)
    even, odd = with_other_core(packed)
    live_even, live_odd = even[mine], odd[mine]
    live_chunk = jnp.concatenate(
        [live_even[:block], live_odd[:block], live_even[block:], live_odd[block:]]
    )
    own_chunk = jnp.concatenate(
        [
            even[:block],
            odd[:block],
            even[block:mine],
            odd[block:mine],
            jnp.pad(live_chunk.reshape(2, 2 * block), ((0, 14), (0, 0))),
        ],
        axis=0,
    )

    item_ends = jnp.cumsum(item_lengths, axis=1)
    ends = lax.dynamic_index_in_dim(item_ends, side, 0, False)
    places = quad * chunk + jnp.arange(chunk, dtype=jnp.int32)
    segments = jnp.sum((places[:, None] >= ends[None, :]).astype(jnp.int32), axis=1)

    def own_part(vector):
        quarter = vector.reshape(2, 2, block)
        return lax.dynamic_index_in_dim(quarter, core, 1, False).reshape(mine)

    own_segments, own_places = own_part(segments), own_part(places)
    pen = jnp.where(own_segments > 0, BIG, 0.0)
    key_off = jnp.where((live_own > 0.5) & (own_segments == 0), 0.0, -BIG)
    qinfo = jnp.stack(
        [own_segments.astype(WIDE), own_places.astype(WIDE), pen, live_own.astype(WIDE)], axis=1
    )
    qinfo = jnp.pad(qinfo, ((0, 0), (0, 4)))
    kinfo = jnp.stack(
        [own_segments.astype(WIDE), own_places.astype(WIDE), key_off, live_own.astype(WIDE)], axis=1
    )
    kinfo = jnp.pad(kinfo, ((0, 0), (0, 4)))
    rowinfo = jnp.stack(
        [segments.astype(WIDE), places.astype(WIDE), live_chunk.astype(WIDE)], axis=0
    )
    rowinfo = jnp.pad(rowinfo, ((0, 5), (0, 0)))

    turns = jnp.arange(TURN, dtype=jnp.int32)
    offsets = jnp.where(turns < NEAR, turns, turns - TURN) - TILE

    def bias_of(offset):
        chosen = relative_bucket_index(offset)[:, None] == jnp.arange(BUCKETS, dtype=jnp.int32)
        return jnp.einsum(
            "bh,ob->ho", bucket_bias_table, chosen.astype(WIDE), precision=lax.Precision.HIGHEST
        )

    vec = jnp.pad(bias_of(offsets), ((0, 2), (0, 0)))
    vec_back = jnp.pad(bias_of(-offsets), ((0, 2), (0, 0)))
    far = jnp.zeros((16,), WIDE)
    far = far.at[:HEADS].set(bucket_bias_table[FAR_BEFORE])
    far = far.at[8 : 8 + HEADS].set(bucket_bias_table[FAR_AFTER])

    def in_pieces(values):
        high = lax.reduce_precision(values, 8, 7)
        mid = lax.reduce_precision(values - high, 8, 7)
        low = lax.reduce_precision(values - high - mid, 8, 7)
        return high, mid, low

    pieces = jnp.concatenate(in_pieces(far))
    w_all = jnp.concatenate([key_weight, value_weight, query_weight], axis=1)

    def scalars(valid, place):
        zero = jnp.zeros((), jnp.int32)
        out = jnp.where(valid, place, quads)
        return jnp.stack(
            [valid.astype(jnp.int32), place, quad, core, ends[0], out, zero, zero]
        ).astype(jnp.int32)

    own_scalars = scalars(jnp.bool_(True), quad)
    smem = pl.BlockSpec(memory_space=pltpu.SMEM)
    vmem = pl.BlockSpec(memory_space=pltpu.VMEM)
    anywhere = pl.BlockSpec(memory_space=pl.ANY)
    params = pltpu.CompilerParams(vmem_limit_bytes=VMEM_LIMIT)
    shape = jax.ShapeDtypeStruct
    qkv_shape = shape(((quads + 1) * chunk, 3 * inner), LOW)
    mask_shape = shape((quads + 1, 8, chunk), WIDE)
    strip_shape = pltpu.VMEM((HEADS, TILE, 2 * chunk - TILE), WIDE)
    near_shape = pltpu.VMEM((HEADS, TILE, NEAR), WIDE)
    gen_shape = pltpu.VMEM((mine, chunk), WIDE)
    pair_shape = shape((HEADS, mine, 2 * HD), LOW)

    def at_out(columns):
        return pl.BlockSpec((chunk, columns), lambda i, sc: (sc[5], 0))

    mask_out = pl.BlockSpec((1, 8, chunk), lambda i, sc: (sc[5], 0, 0))

    def cost(products, exps):
        pairs = mine * chunk * HEADS
        return pl.CostEstimate(
            flops=2 * 4 * HD * products * pairs, bytes_accessed=8 << 20, transcendentals=exps * pairs
        )

    qkv, masks, qm, acc, ml = pl.pallas_call(
        forward_own_kernel,
        grid_spec=pltpu.PrefetchScalarGridSpec(
            num_scalar_prefetch=1,
            grid=(1,),
            in_specs=[smem] + [vmem] * 5,
            out_specs=(at_out(3 * inner), mask_out, vmem, vmem, vmem),
            scratch_shapes=[strip_shape, near_shape, gen_shape],
        ),
        out_shape=(
            qkv_shape, mask_shape, pair_shape, shape((mine, inner), WIDE), shape((mine, 2 * HD), WIDE),
        ),
        compiler_params=params,
        cost_estimate=cost(2, 1),
        name="attend_own",
    )(own_scalars, far, own_chunk, w_all, vec, qinfo, rowinfo)

    def forward_step(state, a_chunk, valid, place):
        qkv, masks, acc, ml = state
        return pl.pallas_call(
            forward_kernel,
            grid_spec=pltpu.PrefetchScalarGridSpec(
                num_scalar_prefetch=1,
                grid=(1,),
                in_specs=[smem] + [vmem] * 7 + [anywhere, anywhere],
                out_specs=(at_out(3 * inner), mask_out, vmem, vmem),
                scratch_shapes=[near_shape],
            ),
            out_shape=(
                qkv_shape, mask_shape, shape((mine, inner), WIDE), shape((mine, 2 * HD), WIDE),
            ),
            input_output_aliases={9: 0, 10: 1, 7: 2, 8: 3},
            compiler_params=params,
            cost_estimate=cost(2, 1),
            name="attend_other",
        )(scalars(valid, place), far, a_chunk, w_all, vec, qinfo, qm, acc, ml, qkv, masks)

    def arrivals(chunk_array):
        held = chunk_array
        for step in range(1, quads):
            held = lax.ppermute(held, "blk", onward)
            other = lax.ppermute(held, "blk", between)
            below, above = quad - step, quad + step
            direct = jnp.where(core == 0, below, above)
            swapped = jnp.where(core == 0, above, below)
            for array, place in ((held, direct), (other, swapped)):
                yield array, (place >= 0) & (place < quads), place

    state = (qkv, masks, acc, ml)
    for a_chunk, valid, place in arrivals(own_chunk):
        state = forward_step(state, a_chunk, valid, place)
    qkv, masks, acc, ml = state

    row_total = ml[:, 8 : 8 + HEADS]
    log_total = ml[:, :HEADS] + jnp.log(row_total)
    context_wide = acc / jnp.repeat(row_total, HD, axis=1)
    context = context_wide.astype(LOW)

    cot_first, cot_second = to_streams(cotangent)
    flat_cot = jnp.concatenate([cot_first, cot_second], axis=0)
    residual = x + dot_nn(context, output_weight)
    feed_in = rms_apply(residual, norm_feed).astype(LOW)
    gate_value = dot_nn(feed_in, gate_weight)
    up_value = dot_nn(feed_in, up_weight)
    hidden_act = gated_unit(gate_value, up_value).astype(LOW)
    output = (residual + dot_nn(hidden_act, down_weight)).astype(LOW)
    grad_hidden = dot_nt(flat_cot, down_weight)
    unused_unit, unit_pull = jax.vjp(gated_unit, gate_value, up_value)
    grad_gate_wide, grad_up_wide = unit_pull(grad_hidden)
    grad_gate_low, grad_up_low = grad_gate_wide.astype(LOW), grad_up_wide.astype(LOW)
    grad_feed_in = dot_nt(grad_gate_low, gate_weight) + dot_nt(grad_up_low, up_weight)
    unused_norm, norm_pull = jax.vjp(rms_apply, residual, norm_feed)
    grad_residual_norm, grad_norm_feed = norm_pull(grad_feed_in)
    grad_residual = flat_cot.astype(WIDE) + grad_residual_norm
    grad_branch = grad_residual.astype(LOW)
    grad_context = dot_nt(grad_branch, output_weight).astype(LOW)
    row_delta = jnp.sum(
        (grad_context.astype(WIDE) * context_wide).reshape(mine, HEADS, HD), axis=2
    )

    ones = jnp.ones((mine, 1), WIDE)
    ext = jnp.concatenate(
        [*in_pieces(-log_total), *in_pieces(-row_delta), ones, -pen[:, None], ones, ones, ones],
        axis=1,
    )
    ext = jnp.pad(ext, ((0, 0), (0, 2 * HD - ext.shape[1]))).astype(LOW)
    do_ext = jnp.concatenate([grad_context, ext], axis=1)
    do_even, do_odd = with_other_core(do_ext)
    do_chunk = jnp.concatenate(
        [do_even[:block], do_odd[:block], do_even[block:], do_odd[block:]], axis=0
    )

    def tn(left, right):
        return lax.dot_general(left, right, (((0,), (0,)), ((), ())), preferred_element_type=WIDE)

    def group(axis, size, index, pair_of):
        return (axis, size, index, pair_of)

    plan = [
        group("blk", 2, core, lambda s: between),
        group("blk", 2, side, lambda s: across),
        group("dp", parts, lax.axis_index("dp"), lambda s: [(k, (k + s) % parts) for k in range(parts)]),
        group(
            "blk", quads, quad,
            lambda s: [(k, (k + 4 * s) % blocks) for k in range(blocks)],
        ),
    ]

    grad_gate = tn(feed_in, grad_gate_low)
    grad_up = tn(feed_in, grad_up_low)
    grad_down = tn(hidden_act, flat_cot)
    grad_output_weight = tn(context, grad_branch)
    feed_rows = padded_rows(
        [
            grad_gate[:, :width], grad_gate[:, width:], grad_up[:, :width], grad_up[:, width:],
            grad_down, grad_output_weight, grad_norm_feed[None, :],
        ],
        512,
    )
    feed_sum = group_sum(feed_rows, plan)

    ld = jnp.zeros((mine, 2 * HD), WIDE)
    ld = ld.at[:, :HEADS].set(log_total).at[:, 8 : 8 + HEADS].set(row_delta)
    lane_half = (jnp.arange(2 * HD) // HD)[None, :]
    dom = jnp.stack(
        [
            jnp.where(
                lane_half == head % 2,
                grad_context[:, (head // 2) * 2 * HD : (head // 2 + 1) * 2 * HD],
                jnp.zeros((), LOW),
            )
            for head in range(HEADS)
        ]
    )
    visible = (own_segments[:, None] == segments[None, :]) & (
        (live_chunk[None, :] > 0.5) | (own_places[:, None] == places[None, :])
    )
    gen = jnp.where(visible, 0.0, -BIG)
    grad_queries, diag, sums = pl.pallas_call(
        queries_kernel,
        grid_spec=pltpu.PrefetchScalarGridSpec(
            num_scalar_prefetch=1,
            grid=(quads,),
            in_specs=[
                smem,
                pl.BlockSpec((chunk, 2 * inner), lambda i, sc: (i, 0)),
                pl.BlockSpec((1, 8, chunk), lambda i, sc: (i, 0, 0)),
            ]
            + [vmem] * 7,
            out_specs=(vmem, vmem, vmem),
            scratch_shapes=[
                strip_shape, near_shape, pltpu.VMEM((HEADS, mine, 2 * HD), WIDE),
                pltpu.VMEM((HEADS, TILE, NEAR), WIDE),
            ],
        ),
        out_shape=(shape((mine, inner), LOW), shape((8, TURN), WIDE), shape((HEADS, 8, 2 * HD), WIDE)),
        compiler_params=params,
        cost_estimate=cost(3 * 4, 4),
        name="grad_queries",
    )(own_scalars, far, qkv, masks, vec, qm, dom, ld, qinfo, rowinfo, gen)

    steps = jnp.arange(TURN, dtype=jnp.int32) - (TILE - 1) - TILE
    chosen = relative_bucket_index(steps)[:, None] == jnp.arange(BUCKETS, dtype=jnp.int32)[None, :]
    table_grad = jnp.einsum(
        "ho,ob->bh", diag[:HEADS], chosen.astype(WIDE), precision=lax.Precision.HIGHEST
    )
    tiles = jnp.arange(mine // TILE, dtype=jnp.int32)
    where = (tiles // 2) * 4 + core * 2 + tiles % 2
    lanes = jnp.arange(HD, dtype=jnp.int32)
    relative = (lanes - 16)[None, :] - where[:, None]
    inside = (lanes >= 8) & (lanes < 32)
    before = (lanes == 0)[None, :] | (inside[None, :] & (relative < -1))
    after = (lanes == 1)[None, :] | (inside[None, :] & (relative > 1))
    block_sums = jnp.stack(
        [sums[head, : mine // TILE, HD * (1 - head % 2) : HD * (2 - head % 2)] for head in range(HEADS)]
    )
    table_grad = table_grad.at[FAR_BEFORE].add(
        jnp.sum(jnp.where(before[None], block_sums, 0.0), axis=(1, 2))
    )
    table_grad = table_grad.at[FAR_AFTER].add(
        jnp.sum(jnp.where(after[None], block_sums, 0.0), axis=(1, 2))
    )

    def keys_step(own, dkv, do_array, valid, place):
        sc = scalars(valid, place)
        sc = sc.at[6].set(jnp.clip(place, 0, quads - 1))
        return pl.pallas_call(
            functools.partial(keys_kernel, own),
            grid_spec=pltpu.PrefetchScalarGridSpec(
                num_scalar_prefetch=1,
                grid=(1,),
                in_specs=[
                    smem,
                    smem,
                    vmem,
                    pl.BlockSpec((chunk, inner), lambda i, sc: (sc[6], 2)),
                    pl.BlockSpec((block, 2 * inner), lambda i, sc: (4 * sc[2] + sc[3], 0)),
                    pl.BlockSpec((block, 2 * inner), lambda i, sc: (4 * sc[2] + sc[3] + 2, 0)),
                    vmem,
                    vmem,
                    vmem,
                    vmem,
                ],
                out_specs=vmem,
                scratch_shapes=[strip_shape, near_shape, gen_shape],
            ),
            out_shape=shape((mine, 2 * inner), WIDE),
            input_output_aliases={10: 0},
            compiler_params=params,
            cost_estimate=cost(4, 1),
            name="grad_keys_own" if own else "grad_keys_other",
        )(sc, far, pieces, do_array, qkv, qkv, qkv, vec_back, kinfo, rowinfo, dkv)

    dkv = jnp.zeros((mine, 2 * inner), WIDE)
    dkv = keys_step(True, dkv, do_chunk, jnp.bool_(True), quad)
    for do_array, valid, place in arrivals(do_chunk):
        dkv = keys_step(False, dkv, do_array, valid, place)
    grad_keys = dkv[:, :inner].astype(LOW)
    grad_values = dkv[:, inner:].astype(LOW)

    grad_attn_in = dot_nt(grad_queries, query_weight)
    grad_attn_in = grad_attn_in + dot_nt(grad_keys, key_weight)
    grad_attn_in = grad_attn_in + dot_nt(grad_values, value_weight)
    unused_first, first_pull = jax.vjp(rms_apply, x, norm_attention)
    grad_flat, grad_norm_attention = first_pull(grad_attn_in)
    input_gradient = (grad_residual + grad_flat).astype(LOW)

    small = jnp.concatenate(
        [
            grad_norm_attention,
            jnp.zeros((2 * inner - width,), WIDE),
            table_grad.reshape(-1),
            jnp.zeros((inner - table_grad.size,), WIDE),
        ]
    ).reshape(3, inner)
    attention_rows = padded_rows(
        [
            tn(attn_in, grad_queries), tn(attn_in, grad_keys), tn(attn_in, grad_values), small,
        ],
        256,
    )
    attention_sum = group_sum(attention_rows, plan)

    hidden = gate_weight.shape[1]
    base = 4 * width
    return (
        from_streams(output),
        from_streams(input_gradient),
        attention_sum[:width],
        attention_sum[width : 2 * width],
        attention_sum[2 * width : 3 * width],
        feed_sum[base + hidden : base + hidden + inner],
        attention_sum[3 * width + 2].reshape(-1)[: BUCKETS * HEADS].reshape(BUCKETS, HEADS),
        attention_sum[3 * width : 3 * width + 2].reshape(-1)[:width],
        feed_sum[base + hidden + inner],
        jnp.concatenate([feed_sum[:width], feed_sum[width : 2 * width]], axis=1),
        jnp.concatenate([feed_sum[2 * width : 3 * width], feed_sum[3 * width : base]], axis=1),
        feed_sum[base : base + hidden],
    )


def solution(mesh):
    return jax.shard_map(
        body,
        mesh=mesh,
        in_specs=(
            P("dp", "blk", None),
            P("dp", None),
            P("dp", "blk"),
            P("dp", "blk", None),
            P(),
            P(),
            P(),
            P(),
            P(),
            P(),
            P(),
            P(),
            P(),
            P(),
        ),
        out_specs=(
            P("dp", "blk", None),
            P("dp", "blk", None),
            P(),
            P(),
            P(),
            P(),
            P(),
            P(),
            P(),
            P(),
            P(),
            P(),
        ),
        check_vma=False,
    )
```

```python
import functools

import jax
import jax.numpy as jnp
import numpy as np
from jax import lax
from jax.experimental import pallas as pl
from jax.experimental.pallas import tpu as pltpu
from jax.sharding import PartitionSpec as P

HEADS = 6
HD = 64
WIDTH2 = 2 * HD
PAIRS = HEADS // 2
INNER = HEADS * HD
BUCKETS = 32
MAXDIST = 128
EPSILON = 1e-06
BIG = 1e30
TILE = 128
NEAR = 3 * TILE
TURN = 4 * TILE
FAR_BEFORE = BUCKETS // 2 - 1
FAR_AFTER = BUCKETS - 1
LOW = jnp.bfloat16
WIDE = jnp.float32
GELU_A = 0.7978845608028654
GELU_B = 0.044715

QUAD, CORE, SIDE, PLACE, SOURCE, FIRST_END = range(6)
MASK, BEFORE, AFTER, PEN, STAT, LIVE, SEG = 0, 1, 2, 7, 8, 11, 12
ONE_A, OFF, ONE_B, ONE_C, ONE_D = 36, 37, 38, 39, 40


def bucket_edges():
    half_count = BUCKETS // 2
    exact_count = half_count // 2
    log_levels = half_count - exact_count
    thresholds = []
    for level_index in range(1, log_levels):
        candidate = exact_count
        while (
            candidate**log_levels * exact_count**level_index
            < MAXDIST**level_index * exact_count**log_levels
        ):
            candidate = candidate + 1
        thresholds.append(candidate)
    return (half_count, exact_count, thresholds)


def dot_nt(left, right):
    return lax.dot_general(
        left, right, (((1,), (1,)), ((), ())), preferred_element_type=WIDE
    )


def dot_nn(left, right):
    return jnp.dot(left, right, preferred_element_type=WIDE)


def dot_tn(left, right):
    return lax.dot_general(
        left, right, (((0,), (0,)), ((), ())), preferred_element_type=WIDE
    )


def rows_of(count, width):
    return lax.broadcasted_iota(jnp.int32, (count, width), 0)


def lanes_of(count, width):
    return lax.broadcasted_iota(jnp.int32, (count, width), 1)


def lane_half(array, half, other):
    return jnp.where(lanes_of(1, WIDTH2) // HD == half, array, other)


def row_half(array, half, other):
    return jnp.where(rows_of(WIDTH2, 1) // HD == half, array, other)


def pair_slice(pair, base=0):
    return slice(base + pair * WIDTH2, base + (pair + 1) * WIDTH2)


def tile_place(tile, core):
    return (tile // 2) * 4 + core * 2 + tile % 2


def rms_scale(values):
    return lax.rsqrt(jnp.mean(values * values, axis=-1, keepdims=True) + EPSILON)


def three_pieces(values):
    high = values.astype(LOW).astype(WIDE)
    mid = (values - high).astype(LOW).astype(WIDE)
    low = (values - high - mid).astype(LOW).astype(WIDE)
    return high, mid, low


def pipelined(items, first, second, depth):
    ahead = []
    for item in items:
        ahead.append((item, first(item)))
        if len(ahead) > depth:
            second(*ahead.pop(0))
    for waiting in ahead:
        second(*waiting)


def far_bias(table_ref, after, head):
    return table_ref[FAR_AFTER if after else FAR_BEFORE, head]


def build_near(near_ref, vec_ref, back, heads):
    for index, head in enumerate(heads):
        row = vec_ref[head : head + 1, back * TURN : (back + 1) * TURN]
        row = jnp.broadcast_to(row, (NEAR, TURN))
        near_ref[index] = pltpu.roll(row, 0, 1, stride=1, stride_axis=0)[:, :TILE]


def build_strip(strip_ref, near_ref, table_ref, back, chunk, heads):
    edge = chunk - TILE
    rest = strip_ref.shape[1] - edge - 2 * TILE
    for index, head in enumerate(heads):
        far_before = far_bias(table_ref, back, head)
        far_after = far_bias(table_ref, not back, head)
        strip_ref[index, : edge - TILE, :] = jnp.full((edge - TILE, TILE), far_before, WIDE)
        strip_ref[index, edge - TILE : edge + 2 * TILE, :] = near_ref[index]
        strip_ref[index, edge + 2 * TILE :, :] = jnp.full((rest, TILE), far_after, WIDE)


def strip_rows(strip_ref, index, first_tile, tiles, core, chunk):
    parts = []
    for tile in range(first_tile, first_tile + tiles):
        start = (chunk - TILE) - tile_place(tile, core) * TILE
        parts.append(strip_ref[index, pl.ds(pl.multiple_of(start, TILE), chunk), :])
    return jnp.concatenate(parts, axis=1)


def near_fixes(near_ref, table_ref, flags, index, head, back):
    low, high = flags
    return (
        low * (near_ref[index, :TILE, :] - far_bias(table_ref, back, head)),
        high * (near_ref[index, 2 * TILE :, :] - far_bias(table_ref, not back, head)),
    )


def fix_near(scores, step, steps, fixes):
    low, high = fixes
    chunk, width = scores.shape
    if step == 0:
        last = jnp.concatenate(
            [scores[chunk - TILE :, :TILE] + low, scores[chunk - TILE :, TILE:]], axis=1
        )
        scores = jnp.concatenate([scores[: chunk - TILE], last], axis=0)
    if step == steps - 1:
        first = jnp.concatenate(
            [scores[:TILE, : width - TILE], scores[:TILE, width - TILE :] + high], axis=1
        )
        scores = jnp.concatenate([first, scores[TILE:]], axis=0)
    return scores


def near_flags(place, quad, core):
    low = jnp.where((place == quad - 1) & (core == 0), 1.0, 0.0)
    high = jnp.where((place == quad + 1) & (core == 1), 1.0, 0.0)
    return low, high


def natural_row(even, odd):
    block = even.shape[1] // 2
    return jnp.concatenate(
        [even[:, :block], odd[:, :block], even[:, block:], odd[:, block:]], axis=1
    )


def key_columns(rows, lanes):
    places = rows[0].shape[1]
    stack = jnp.zeros((16, places), WIDE)
    spread = jnp.zeros((16, WIDTH2), WIDE)
    number, lane = rows_of(16, 1), lanes_of(16, WIDTH2)
    for index, row in enumerate(rows):
        stack = jnp.where(number == index, row, stack)
    for index, at, scale in lanes:
        spread = jnp.where((number == index) & (lane == at), scale, spread)
    return dot_tn(stack.astype(LOW), spread.astype(LOW))


def visible_mask(gen_ref, segment_column, segment_row, live, core, keys_down):
    chunk, mine = gen_ref.shape
    down = rows_of(chunk, 1)
    for tile in range(mine // TILE):
        lanes = slice(tile * TILE, (tile + 1) * TILE)
        across = tile_place(tile, core) * TILE + lanes_of(1, TILE)
        alive = live if keys_down else live[:, lanes]
        visible = (segment_column == segment_row[:, lanes]) & ((alive > 0.5) | (down == across))
        gen_ref[:, lanes] = jnp.where(visible, 0.0, -BIG)


def project(a, weight_refs, qkv_ref):
    for part, w_ref in enumerate(weight_refs):
        cols = slice(part * INNER, (part + 1) * INNER)
        qkv_ref[:, cols] = dot_nn(a, w_ref[...]).astype(LOW)


def halves_copies(source, swapped, core, rows_ref, live_ref, sems):
    first_core = 1 - core if swapped else core
    block = rows_ref.shape[0] // 4
    half = source.shape[0] // 2
    copies = []
    for index in range(2):
        owner = first_core if index == 0 else 1 - first_core
        for part in range(2):
            at = pl.multiple_of(part * 2 * block + owner * block, block)
            copies.append((source.at[pl.ds(index * half + part * block, block), :], rows_ref.at[pl.ds(at, block), :]))
        if live_ref is not None:
            copies.append((source.at[pl.ds(index * half + 2 * block, 16), :], live_ref.at[owner]))
    return [
        pltpu.make_async_copy(start, end, sems.at[index]) for index, (start, end) in enumerate(copies)
    ]


def start_fetch(sc_ref, step, sources, rows_ref, live_ref, sems):
    core = sc_ref[0, CORE]
    for index, source in enumerate(sources):

        @pl.when(sc_ref[step, SOURCE] == index)
        def _():
            for copy in halves_copies(source, index % 2 == 1, core, rows_ref, live_ref, sems):
                copy.start()


def wait_fetch(sc_ref, sources, rows_ref, live_ref, sems):
    for copy in halves_copies(sources[0], False, sc_ref[0, CORE], rows_ref, live_ref, sems):
        copy.wait()


def norm_kernel(
    sc_ref, lengths_ref, hidden_ref, live_ref, got_ref, gain_ref, table_ref, onehot_ref,
    packed_ref, x_ref, rowk_ref, rowq_ref, vec_ref,
):
    side, core, quad = sc_ref[0, SIDE], sc_ref[0, CORE], sc_ref[0, QUAD]
    block = hidden_ref.shape[1]
    mine, chunk = 2 * block, 4 * block
    kept, got = hidden_ref[side], got_ref[:block, :]
    live_kept = live_ref[pl.ds(side, 1), :].astype(WIDE)
    live_got = got_ref[block : block + 16, :block].astype(WIDE)[0:1, :]
    for part in range(2):
        rows = jnp.where(side == part, kept, got)
        x_ref[part * block : (part + 1) * block, :] = rows
        wide = rows.astype(WIDE)
        normed = wide * rms_scale(wide) * gain_ref[...]
        packed_ref[part * block : (part + 1) * block, :] = normed.astype(LOW)
    live = jnp.concatenate(
        [jnp.where(side == 0, live_kept, live_got), jnp.where(side == 0, live_got, live_kept)],
        axis=1,
    )
    packed_ref[mine:, :] = jnp.broadcast_to(live, (16, mine)).astype(LOW)

    places = quad * chunk + lanes_of(1, chunk)

    def one_item(item, carry):
        end, segment = carry
        end = end + lengths_ref[side, item]
        return end, segment + jnp.where(places >= end, 1.0, 0.0)

    zero = jnp.zeros((1, chunk), WIDE)
    end, segment = lax.fori_loop(0, lengths_ref.shape[1], one_item, (jnp.int32(0), zero))
    rowk_ref[...] = jnp.broadcast_to(segment, (8, chunk))
    own = jnp.concatenate(
        [
            rowk_ref[0:1, pl.ds(pl.multiple_of(part * mine + core * block, block), block)]
            for part in range(2)
        ],
        axis=1,
    )
    number = rows_of(8, 1)
    rowq = jnp.where(number == 0, own, 0.0)
    rowq = jnp.where(number == 2, jnp.where(own > 0.5, BIG, 0.0), rowq)
    rowq = jnp.where(number == 3, live, rowq)
    off = jnp.where((live > 0.5) & (own < 0.5), 0.0, -BIG)
    rowq_ref[...] = jnp.where(number == 4, off, rowq)
    found = lax.dot_general(
        table_ref[...], onehot_ref[...], (((0,), (0,)), ((), ())),
        precision=lax.Precision.HIGHEST, preferred_element_type=WIDE,
    )
    vec_ref[...] = jnp.concatenate([found, jnp.zeros((8 - HEADS, found.shape[1]), WIDE)], axis=0)


def forward_items(mine):
    steps = mine // (2 * TILE)
    return [(pair, step, hh) for pair in range(PAIRS) for step in range(steps) for hh in range(2)]


def forward_operands(qkv_ref, ext):
    made = {}

    def operands(pair):
        if pair not in made:
            k_ext = jnp.concatenate([qkv_ref[:, pair_slice(pair)], ext], axis=1)
            v_turned = qkv_ref[:, pair_slice(pair, INNER)].T
            made[pair] = (
                k_ext, [row_half(v_turned, hh, jnp.ones_like(v_turned)) for hh in range(2)]
            )
        return made[pair]

    return operands


def step_lanes(step):
    return slice(step * 2 * TILE, (step + 1) * 2 * TILE)


def head_rows(head):
    return slice(head * HD, (head + 1) * HD)


def forward_own_kernel(
    sc_ref, table_ref, source_ref, wk_ref, wv_ref, wq_ref, vec_ref, rowq_ref, rowk_ref,
    qkv_ref, ext_ref, qx_ref, acc_ref, ml_ref,
    a_ref, live_ref, strip_ref, near_ref, gen_ref, sems,
):
    core = sc_ref[0, CORE]
    chunk = qkv_ref.shape[0]
    mine = acc_ref.shape[1]
    block = mine // 2
    start_fetch(sc_ref, 0, [source_ref], a_ref, live_ref, sems)
    build_near(near_ref, vec_ref, 0, range(HEADS))
    build_strip(strip_ref, near_ref, table_ref, False, chunk, range(HEADS))
    number = rows_of(WIDTH2, 1)
    for head in range(HEADS):
        rows = jnp.where(number == MASK, 1.0, 0.0)
        for which, after in ((BEFORE, False), (AFTER, True)):
            far = jnp.full((1, mine), far_bias(table_ref, after, head), WIDE)
            for piece, value in enumerate(three_pieces(far)):
                rows = jnp.where(number == which + 2 * piece, value, rows)
        rows = jnp.where(number == PEN, -rowq_ref[2:3, :], rows)
        qx_ref[head, WIDTH2:, :] = rows.astype(LOW)
    wait_fetch(sc_ref, [source_ref], a_ref, live_ref, sems)
    project(a_ref[...], (wk_ref, wv_ref, wq_ref), qkv_ref)
    live = natural_row(live_ref[0].astype(WIDE)[0:1, :], live_ref[1].astype(WIDE)[0:1, :])
    columns = key_columns(
        [jnp.ones_like(live), live, rowk_ref[0:1, :]],
        [(0, STAT, 1.0), (0, STAT + 1, 1.0), (0, STAT + 2, 1.0), (1, LIVE, 1.0), (2, SEG, 1.0)],
    )
    ext_ref[...] = columns.astype(LOW)
    visible_mask(
        gen_ref, columns[:, SEG : SEG + 1], rowq_ref[0:1, :], columns[:, LIVE : LIVE + 1], core, True
    )
    for part in range(2):
        at = pl.ds(pl.multiple_of(part * mine + core * block, block), block)
        lanes = slice(part * block, (part + 1) * block)
        for pair in range(PAIRS):
            turned = qkv_ref[at, pair_slice(pair, 2 * INNER)].T
            for hh in range(2):
                qx_ref[2 * pair + hh, :WIDTH2, lanes] = row_half(
                    turned, hh, jnp.zeros_like(turned)
                )
    ml_ref[...] = jnp.zeros_like(ml_ref)
    operands = forward_operands(qkv_ref, ext_ref[...])

    def first(item):
        pair, step, hh = item
        s = dot_nn(operands(pair)[0], qx_ref[2 * pair + hh, :, step_lanes(step)])
        s = s + strip_rows(strip_ref, 2 * pair + hh, 2 * step, 2, core, chunk)
        return s + gen_ref[:, step_lanes(step)]

    def second(item, s):
        pair, step, hh = item
        head, lanes = 2 * pair + hh, step_lanes(step)
        top = jnp.max(s, axis=0, keepdims=True)
        p = jnp.exp(s - top).astype(LOW)
        pv = dot_nn(operands(pair)[1][hh], p)
        ml_ref[head : head + 1, lanes] = top
        ml_ref[8 + head : 9 + head, lanes] = pv[HD * (1 - hh) : HD * (1 - hh) + 1, :]
        acc_ref[head_rows(head), lanes] = pv[hh * HD : (hh + 1) * HD, :]

    pipelined(forward_items(mine), first, second, 2)


def forward_kernel(
    step_number, sources, sc_ref, table_ref, wk_ref, wv_ref, wq_ref, vec_ref, qx_ref, acc_in, ml_in,
    qkv_in, ext_in, *rest,
):
    source_refs, rest = rest[:sources], rest[sources:]
    qkv_ref, ext_ref, acc_ref, ml_ref, a_ref, live_ref, near_ref, sems = rest
    quad, core, place = (sc_ref[step_number, i] for i in (QUAD, CORE, PLACE))
    chunk = qkv_ref.shape[0]
    mine = acc_ref.shape[1]
    start_fetch(sc_ref, step_number, source_refs, a_ref, live_ref, sems)
    build_near(near_ref, vec_ref, 0, range(HEADS))
    wait_fetch(sc_ref, source_refs, a_ref, live_ref, sems)
    project(a_ref[...], (wk_ref, wv_ref, wq_ref), qkv_ref)
    live = natural_row(live_ref[0].astype(WIDE)[0:1, :], live_ref[1].astype(WIDE)[0:1, :])
    places = place * chunk + lanes_of(1, chunk)
    seen = (live > 0.5) & (places < sc_ref[step_number, FIRST_END])
    is_before = jnp.where(place < quad, 1.0, 0.0)
    is_after = 1.0 - is_before
    marks = [(0, MASK, 1.0), (1, PEN, 1.0)]
    marks += [(1, STAT + n, 1.0) for n in range(3)]
    marks += [(1, BEFORE + 2 * n, is_before) for n in range(3)]
    marks += [(1, AFTER + 2 * n, is_after) for n in range(3)]
    ext = key_columns([jnp.where(seen, 0.0, -BIG), jnp.ones_like(live)], marks).astype(LOW)
    ext_ref[...] = ext
    flags = near_flags(place, quad, core)
    steps = mine // (2 * TILE)
    operands = forward_operands(qkv_ref, ext)

    def first(item):
        pair, step, hh = item
        head = 2 * pair + hh
        s = dot_nn(operands(pair)[0], qx_ref[head, :, step_lanes(step)])
        return fix_near(s, step, steps, near_fixes(near_ref, table_ref, flags, head, head, False))

    def second(item, s):
        pair, step, hh = item
        head, lanes = 2 * pair + hh, step_lanes(step)
        old = ml_in[head : head + 1, lanes]
        top = jnp.maximum(old, jnp.max(s, axis=0, keepdims=True))
        keep = jnp.exp(old - top)
        p = jnp.exp(s - top).astype(LOW)
        pv = dot_nn(operands(pair)[1][hh], p)
        ml_ref[head : head + 1, lanes] = top
        total = ml_in[8 + head : 9 + head, lanes] * keep
        ml_ref[8 + head : 9 + head, lanes] = total + pv[HD * (1 - hh) : HD * (1 - hh) + 1, :]
        rows = head_rows(head)
        acc_ref[rows, lanes] = acc_in[rows, lanes] * keep + pv[hh * HD : (hh + 1) * HD, :]

    pipelined(forward_items(mine), first, second, 2)


def middle_kernel(
    sc_ref, acc_ref, ml_ref, x_ref, cot_in, cot_got, rowq_ref, wo_ref, gate_ref, up_ref, down_ref, gain_ref,
    do_ref, dot_ref, stat_ref, keep_ref, send_ref, grad_res_ref, act_ref, feed_ref, gg_ref, gu_ref,
    ctx_ref, branch_ref, gain_grad_ref, cot_ref,
):
    side = sc_ref[0, SIDE]
    mine = x_ref.shape[0]
    block = mine // 2
    gain = gain_ref[...]
    context = []
    for head in range(HEADS):
        context.append(acc_ref[head_rows(head), :] / ml_ref[8 + head : 9 + head, :])
    for pair in range(PAIRS):
        both = jnp.concatenate(context[2 * pair : 2 * pair + 2], axis=0).astype(LOW)
        ctx_ref[:, pair_slice(pair)] = both.T
    gain_grad = jnp.zeros_like(gain)
    cot_kept = cot_in[side]
    for part in range(2):
        rows = slice(part * block, (part + 1) * block)
        cot_ref[rows, :] = jnp.where(side == part, cot_kept, cot_got[...])

    def first(part):
        rows = slice(part * block, (part + 1) * block)
        residual = x_ref[rows, :].astype(WIDE) + dot_nn(ctx_ref[rows, :], wo_ref[...])
        scale = rms_scale(residual)
        z = residual * scale
        feed = (z * gain).astype(LOW)
        feed_ref[rows, :] = feed
        v = dot_nn(feed, gate_ref[...])
        up = dot_nn(feed, up_ref[...])
        return residual, scale, z, v, up, dot_nt(cot_ref[rows, :], down_ref[...])

    def second(part, made):
        nonlocal gain_grad
        residual, scale, z, v, up, grad_hidden = made
        rows = slice(part * block, (part + 1) * block)
        square = v * v
        t = jnp.tanh(GELU_A * v * (1.0 + GELU_B * square))
        half = 0.5 * (1.0 + t)
        g = v * half
        slope = half + 0.5 * v * (1.0 - t * t) * (GELU_A * (1.0 + 3.0 * GELU_B * square))
        act = (g * up).astype(LOW)
        act_ref[rows, :] = act
        grad_gate = (grad_hidden * up * slope).astype(LOW)
        grad_up = (grad_hidden * g).astype(LOW)
        gg_ref[rows, :] = grad_gate
        gu_ref[rows, :] = grad_up
        grad_feed = dot_nt(grad_gate, gate_ref[...]) + dot_nt(grad_up, up_ref[...])
        u = grad_feed * gain
        gain_grad = gain_grad + jnp.sum(grad_feed * z, axis=0, keepdims=True)
        cot = cot_ref[rows, :].astype(WIDE)
        grad_res = cot + scale * (u - z * jnp.mean(u * z, axis=-1, keepdims=True))
        grad_res_ref[rows, :] = grad_res
        branch = grad_res.astype(LOW)
        branch_ref[rows, :] = branch
        do_ref[rows, :INNER] = dot_nt(branch, wo_ref[...]).astype(LOW)
        output = (residual + dot_nn(act, down_ref[...])).astype(LOW)

        @pl.when(side == part)
        def _():
            keep_ref[...] = output

        @pl.when(side != part)
        def _():
            send_ref[...] = output

    pipelined(range(2), first, second, 1)
    gain_grad_ref[...] = jnp.broadcast_to(gain_grad, gain_grad_ref.shape)
    number = rows_of(WIDTH2, 1)
    stat = jnp.where((number == ONE_A) | ((number >= ONE_B) & (number <= ONE_D)), 1.0, 0.0)
    stat = jnp.where(number == OFF, -rowq_ref[2:3, :], stat)
    for pair in range(PAIRS):
        turned = do_ref[:, pair_slice(pair)].T
        dot_ref[pair_slice(pair), :] = turned
        for hh in range(2):
            head = 2 * pair + hh
            grads = turned[hh * HD : (hh + 1) * HD, :].astype(WIDE)
            delta = jnp.sum(grads * context[head], axis=0, keepdims=True)
            lse = ml_ref[head : head + 1, :] + jnp.log(ml_ref[8 + head : 9 + head, :])
            for base, value in ((0, lse), (3 * HEADS, delta)):
                for index, piece in enumerate(three_pieces(-value)):
                    stat = jnp.where(number == base + HEADS * index + head, piece, stat)
    stat_low = stat.astype(LOW)
    stat_ref[...] = stat_low
    do_ref[:, INNER:] = stat_low.T


def put_half(core, keep_ref, send_ref, row, value):
    rows = keep_ref.shape[0]
    half, start = row // rows, row % rows

    @pl.when(core == half)
    def _():
        keep_ref[start : start + value.shape[0], : value.shape[1]] = value

    @pl.when(core != half)
    def _():
        send_ref[start : start + value.shape[0], : value.shape[1]] = value


def put_rows(core, keep_ref, send_ref, row, value):
    rows = keep_ref.shape[0]
    value = value.astype(LOW)
    first = min(value.shape[0], rows - row % rows)
    put_half(core, keep_ref, send_ref, row, value[:first])
    if first < value.shape[0]:
        put_half(core, keep_ref, send_ref, row + first, value[first:])


def feed_grads_kernel(
    sc_ref, act_ref, feed_ref, gg_ref, gu_ref, ctx_ref, branch_ref, cot_ref, gain_grad_ref,
    keep_ref, send_ref,
):
    core = sc_ref[0, CORE]
    put = functools.partial(put_rows, core, keep_ref, send_ref)
    width = keep_ref.shape[1]
    hidden = act_ref.shape[1]
    feed = feed_ref[...].T
    row = 0
    for grads in (gg_ref, gu_ref):
        for start in range(0, hidden, width):
            put(row, dot_nn(feed, grads[:, start : start + width]))
            row += width
    act = act_ref[...].T
    put(row, dot_nn(act, cot_ref[...]))
    row += hidden
    put(row, dot_nn(ctx_ref[...].T, branch_ref[...]))
    row += INNER
    rest = 2 * keep_ref.shape[0] - row
    put(row, jnp.where(rows_of(rest, 1) == 0, gain_grad_ref[0:1, :], 0.0))


def queries_kernel(
    pair, sc_ref, table_ref, k_ref, v_ref, ext_ref, vec_ref, rowq_ref, qx_in, dot_in, stat_ref, onehot_ref,
    dq_ref, table_grad_ref,
    strip_ref, near_ref, gen_ref, qx_ref, dx_ref, dq2_ref, grad_near_ref, ds_ref,
):
    quad, core = sc_ref[0, QUAD], sc_ref[0, CORE]
    place = pl.program_id(0)
    chunk = k_ref.shape[0]
    mine = dq_ref.shape[1]
    steps = mine // (2 * TILE)
    number = rows_of(WIDTH2, 1)
    heads = (2 * pair, 2 * pair + 1)

    @pl.when(place == 0)
    def _():
        build_near(near_ref, vec_ref, 0, heads)
        dq2_ref[...] = jnp.zeros_like(dq2_ref)
        grad_near_ref[...] = jnp.zeros_like(grad_near_ref)
        turned = dot_in[...]
        for hh, head in enumerate(heads):
            dx_ref[hh, :WIDTH2, :] = row_half(turned, hh, jnp.zeros_like(turned))
            lse_rows = qx_in[hh, WIDTH2:, :].astype(WIDE)
            delta_rows = jnp.zeros((WIDTH2, 1), WIDE)
            for index in range(3):
                at = HEADS * index + head
                lse_piece = stat_ref[at : at + 1, :].astype(WIDE)
                at = at + 3 * HEADS
                delta_piece = stat_ref[at : at + 1, :].astype(WIDE)
                lse_rows = jnp.where(number == STAT + index, lse_piece, lse_rows)
                delta_rows = jnp.where(number == STAT + index, delta_piece, delta_rows)
            qx_ref[hh, :WIDTH2, :] = qx_in[hh, :WIDTH2, :]
            qx_ref[hh, WIDTH2:, :] = lse_rows.astype(LOW)
            dx_ref[hh, WIDTH2:, :] = delta_rows.astype(LOW)

    gap = place - quad
    spread = jnp.where(jnp.abs(gap) <= 1, 1, 0)
    first_mark = jnp.where(spread == 1, 16 + 8 * gap, jnp.where(gap < 0, 0, 1))
    mark_of_key = first_mark + spread * (rows_of(chunk, 1) // TILE)
    items = [(step, hh) for step in range(steps) for hh in range(2)]

    def run(score, after):
        ext = ext_ref[...]
        k_pair = k_ref[...]
        k_ext = jnp.concatenate([k_pair, ext], axis=1)
        v_ext = jnp.concatenate([v_ref[...], ext], axis=1)
        k_turned = []
        for hh in range(2):
            lane = lanes_of(1, WIDTH2) - HD * (1 - hh)
            marks = jnp.where(lane == mark_of_key, 1.0, 0.0).astype(LOW)
            k_turned.append(lane_half(k_pair, hh, marks).T)

        def first(item):
            step, hh = item
            lanes = step_lanes(step)
            s = score(dot_nn(k_ext, qx_ref[hh, :, lanes]), step, hh)
            return s, dot_nn(v_ext, dx_ref[hh, :, lanes])

        def second(item, made):
            step, hh = item
            s, dp = made
            ds = (jnp.exp(s) * dp).astype(LOW)
            dq2_ref[hh, :, step_lanes(step)] += dot_nn(k_turned[hh], ds)
            after(ds, step, hh)

        pipelined(items, first, second, 1)

    @pl.when(place == quad)
    def _():
        build_strip(strip_ref, near_ref, table_ref, False, chunk, heads)
        wide = ext_ref[...].astype(WIDE)
        visible_mask(
            gen_ref, wide[:, SEG : SEG + 1], rowq_ref[0:1, :], wide[:, LIVE : LIVE + 1], core, True
        )
        ds_ref[:, :TILE, :] = jnp.zeros((2, TILE, mine), LOW)
        ds_ref[:, chunk + TILE :, :] = jnp.zeros((2, TILE, mine), LOW)

        def score(s, step, hh):
            s = s + strip_rows(strip_ref, hh, 2 * step, 2, core, chunk)
            return s + gen_ref[:, step_lanes(step)]

        def after(ds, step, hh):
            ds_ref[hh, TILE : chunk + TILE, step_lanes(step)] = ds

        run(score, after)
        for hh in range(2):
            total = jnp.zeros((NEAR, TILE), WIDE)
            for tile in range(mine // TILE):
                rows = pl.ds(pl.multiple_of(tile_place(tile, core) * TILE, TILE), NEAR)
                lanes = slice(tile * TILE, (tile + 1) * TILE)
                total = total + ds_ref[hh, rows, lanes].astype(WIDE)
            grad_near_ref[hh] += total

    @pl.when(place != quad)
    def _():
        low, high = near_flags(place, quad, core)
        fixes = [
            near_fixes(near_ref, table_ref, (low, high), hh, heads[hh], False) for hh in range(2)
        ]

        def score(s, step, hh):
            return fix_near(s, step, steps, fixes[hh])

        def after(ds, step, hh):
            if step == 0:
                grad_near_ref[hh, :TILE, :] += low * ds[chunk - TILE :, :TILE].astype(WIDE)
            if step == steps - 1:
                grad_near_ref[hh, 2 * TILE :, :] += high * ds[:TILE, TILE:].astype(WIDE)

        run(score, after)

    @pl.when(place == pl.num_programs(0) - 1)
    def _():
        flip = (rows_of(TILE, TILE) + lanes_of(TILE, TILE) == TILE - 1).astype(WIDE)
        exact = functools.partial(
            jnp.dot, precision=lax.Precision.HIGHEST, preferred_element_type=WIDE
        )
        mark = rows_of(HD, 1)
        lane = lanes_of(1, WIDTH2)
        head_row = rows_of(8, 1)
        table = jnp.zeros((8, WIDTH2), WIDE)
        for part in range(3):
            sums = jnp.zeros((8, 2 * TILE), WIDE)
            for hh, head in enumerate(heads):
                turned = exact(flip, grad_near_ref[hh, part * TILE : (part + 1) * TILE, :])
                padded = jnp.concatenate([turned, jnp.zeros((TILE, TILE), WIDE)], axis=1)
                skewed = pltpu.roll(padded, 0, 1, stride=1, stride_axis=0)
                total = jnp.sum(skewed, axis=0, keepdims=True)
                sums = jnp.where(head_row == head, total, sums)
            table = table + exact(sums, onehot_ref[part * 2 * TILE : (part + 1) * 2 * TILE, :])
        where = jnp.concatenate(
            [jnp.broadcast_to(tile_place(tile, core), (1, TILE)) for tile in range(mine // TILE)],
            axis=1,
        )
        relative = (mark - 16) - where
        inside = (mark >= 8) & (mark < 32)
        is_before = (mark == 0) | (inside & (relative < -1))
        is_after = (mark == 1) | (inside & (relative > 1))
        for hh, head in enumerate(heads):
            found = dq2_ref[hh, HD * (1 - hh) : HD * (2 - hh), :]
            for chosen, bucket in ((is_before, FAR_BEFORE), (is_after, FAR_AFTER)):
                total = jnp.sum(jnp.where(chosen, found, 0.0))
                table = table + jnp.where((head_row == head) & (lane == bucket), total, 0.0)
        table_grad_ref[...] = table
        dq_ref[...] = jnp.concatenate([dq2_ref[0, :HD, :], dq2_ref[1, HD:, :]], axis=0).astype(LOW)


def keys_kernel(group, counts, sc_ref, table_ref, q_ref, kv0_ref, kv1_ref, vec_ref, rowq_ref, ext_ref, *rest):
    has_in = group[0] > 0
    dkv_in, rest = (rest[0], rest[1:]) if has_in else (None, rest)
    total = sum(counts)
    flat, rest = rest[:total], rest[total:]
    dkv_ref, do_refs, acc_ref, side_ref, strip_ref, near_ref, gen_ref, sems = rest
    sources, taken = [], 0
    for count in counts:
        sources.append(flat[taken : taken + count])
        taken += count
    index = pl.program_id(0)
    quad, core = sc_ref[0, QUAD], sc_ref[0, CORE]
    place = sc_ref[group[0] + index, PLACE]
    chunk = q_ref.shape[0]
    mine = acc_ref.shape[1]
    steps = mine // (2 * TILE)
    number = rows_of(WIDTH2, 1)
    slot = index % 2

    def start(which):
        start_fetch(
            sc_ref, group[which], sources[which], do_refs.at[which % 2], None, sems.at[which % 2]
        )

    @pl.when(index == 0)
    def _():
        start(0)
        build_near(near_ref, vec_ref, 1, range(HEADS))
        for pair in range(PAIRS):
            for part in range(2):
                turned = jnp.concatenate(
                    [half[:, pair_slice(pair, part * INNER)].T for half in (kv0_ref, kv1_ref)],
                    axis=1,
                )
                for hh in range(2):
                    head = 2 * pair + hh
                    first = part * 3 * HEADS + head
                    rows = jnp.where(
                        (number == first) | (number == first + HEADS) | (number == first + 2 * HEADS),
                        1.0, 0.0,
                    )
                    side_ref[part, head, :WIDTH2, :] = row_half(turned, hh, jnp.zeros_like(turned))
                    side_ref[part, head, WIDTH2:, :] = jnp.broadcast_to(rows, (WIDTH2, mine)).astype(
                        LOW
                    )
        if has_in:
            acc_ref[...] = dkv_in[...]
        else:
            build_strip(strip_ref, near_ref, table_ref, True, chunk, range(HEADS))
            visible_mask(
                gen_ref, ext_ref[...].astype(WIDE)[:, SEG : SEG + 1], rowq_ref[0:1, :],
                rowq_ref[3:4, :], core, False,
            )

    for which in range(len(group)):

        @pl.when(index == which)
        def _():
            wait_fetch(sc_ref, sources[which], do_refs.at[which % 2], None, sems.at[which % 2])
            if which + 1 < len(group):
                start(which + 1)

    def run(score, add):
        ext = do_refs[slot, :, INNER:]
        items = forward_items(mine)
        made = {}

        def operands(pair):
            if pair not in made:
                q_pair = q_ref[:, pair_slice(pair)]
                do_pair = do_refs[slot, :, pair_slice(pair)]
                made[pair] = (
                    jnp.concatenate([q_pair, ext], axis=1),
                    jnp.concatenate([do_pair, ext], axis=1),
                    q_pair.T,
                    do_pair.T,
                )
            return made[pair]

        def first(item):
            pair, step, hh = item
            head, lanes = 2 * pair + hh, step_lanes(step)
            q_ext, do_ext = operands(pair)[:2]
            s = score(dot_nn(q_ext, side_ref[0, head, :, lanes]), step, head)
            return s, dot_nn(do_ext, side_ref[1, head, :, lanes])

        def second(item, found):
            pair, step, hh = item
            head, lanes = 2 * pair + hh, step_lanes(step)
            s, dp = found
            p = jnp.exp(s)
            ds = (p * dp).astype(LOW)
            mine_rows = slice(hh * HD, (hh + 1) * HD)
            for part, product in (
                (0, dot_nn(operands(pair)[2], ds)),
                (1, dot_nn(operands(pair)[3], p.astype(LOW))),
            ):
                rows = slice(part * INNER + head * HD, part * INNER + (head + 1) * HD)
                value = product[mine_rows, :]
                acc_ref[rows, lanes] = acc_ref[rows, lanes] + value if add else value

        pipelined(items, first, second, 1)

    def score_own(s, step, head):
        s = s + strip_rows(strip_ref, head, 2 * step, 2, core, chunk)
        return s + gen_ref[:, step_lanes(step)]

    def other():
        flags = near_flags(place, quad, core)
        is_before = place < quad
        for head in range(HEADS):
            far = jnp.where(
                is_before, far_bias(table_ref, True, head), far_bias(table_ref, False, head)
            )
            rows = jnp.where(
                (number == head) | (number == head + HEADS) | (number == head + 2 * HEADS), 1.0, 0.0
            )
            wide = jnp.full((1, mine), far, WIDE)
            for at, piece in zip((ONE_A, ONE_B, ONE_C), three_pieces(wide)):
                rows = jnp.where(number == at, piece, rows)
            rows = jnp.where(number == OFF, 1.0, rows)
            rows = jnp.where(number == ONE_D, rowq_ref[4:5, :], rows)
            side_ref[0, head, WIDTH2:, :] = rows.astype(LOW)

        def score(s, step, head):
            return fix_near(
                s, step, steps, near_fixes(near_ref, table_ref, flags, head, head, True)
            )

        run(score, True)

    if has_in:
        other()
    elif len(group) == 1:
        run(score_own, False)
    else:

        @pl.when(index == 0)
        def _():
            run(score_own, False)

        @pl.when(index > 0)
        def _():
            other()

    @pl.when(index == pl.num_programs(0) - 1)
    def _():
        dkv_ref[...] = acc_ref[...].astype(dkv_ref.dtype)


def last_kernel(
    sc_ref, *refs
):
    (dq0_ref, dq1_ref, dq2_ref, dkv_ref, packed_ref, x_ref, grad_res_ref, wq_ref, wk_ref, wv_ref, gain_ref,
     table0_ref, table1_ref, table2_ref, keep_out, send_out, keep_ref, send_ref) = refs
    side, core = sc_ref[0, SIDE], sc_ref[0, CORE]
    mine = x_ref.shape[0]
    block = mine // 2
    put = functools.partial(put_rows, core, keep_ref, send_ref)
    queries = jnp.concatenate([dq0_ref[...], dq1_ref[...], dq2_ref[...]], axis=0)
    grads = [queries, dkv_ref[:INNER, :].astype(LOW), dkv_ref[INNER:, :].astype(LOW)]
    turned = packed_ref[:mine, :].T
    width = turned.shape[0]
    for part in range(3):
        put(part * width, dot_nt(turned, grads[part]))
    gain = gain_ref[...]
    gain_grad = jnp.zeros_like(gain)
    for part in range(2):
        rows = slice(part * block, (part + 1) * block)
        grad_in = jnp.zeros((block, width), WIDE)
        for grad, w_ref in zip(grads, (wq_ref, wk_ref, wv_ref)):
            grad_in = grad_in + dot_nt(grad[:, rows].T, w_ref[...])
        x = x_ref[rows, :].astype(WIDE)
        scale = rms_scale(x)
        z = x * scale
        u = grad_in * gain
        gain_grad = gain_grad + jnp.sum(grad_in * z, axis=0, keepdims=True)
        result = grad_res_ref[rows, :] + scale * (u - z * jnp.mean(u * z, axis=-1, keepdims=True))
        result = result.astype(LOW)

        @pl.when(side == part)
        def _():
            keep_out[...] = result

        @pl.when(side != part)
        def _():
            send_out[...] = result

    rest = 2 * keep_ref.shape[0] - 3 * width
    number = rows_of(rest, 1)
    small = jnp.where(number == 0, gain_grad[:, :INNER], 0.0)
    tail = jnp.concatenate(
        [gain_grad[:, INNER:], jnp.zeros((1, 2 * INNER - width), WIDE)], axis=1
    )
    small = jnp.where(number == 1, tail, small)
    table = table0_ref[...] + table1_ref[...] + table2_ref[...]
    table = jnp.concatenate([table, jnp.zeros((8, INNER - WIDTH2), WIDE)], axis=1)
    for head in range(HEADS):
        small = jnp.where(number == 2 + head, table[head : head + 1, :], small)
    put(3 * width, small)


def tie_kernel(sc_ref, in_ref, out_ref):
    pass


def add_kernel(sc_ref, order_ref, *refs):
    outs = refs[-order_ref.shape[0] :]
    ins = refs[: len(refs) - len(outs)]
    for index, out_ref in enumerate(outs):
        which = order_ref[index]
        total = ins[0][which].astype(WIDE)
        for in_ref in ins[1:]:
            total = total + in_ref[which].astype(WIDE)
        out_ref[...] = total.astype(LOW)


def place_kernel(sc_ref, owner_ref, *refs):
    out_ref = refs[-1]
    for index, part_ref in enumerate(refs[:-1]):
        out_ref[owner_ref[index]] = part_ref[...]


def whole_rows(core, kept_ref, got_ref, first, count):
    half = kept_ref.shape[0]
    parts = []
    for number in range(2):
        low, high = max(first, number * half), min(first + count, (number + 1) * half)
        if low < high:
            rows = slice(low - number * half, high - number * half)
            part = jnp.where(core == number, kept_ref[rows, :], got_ref[rows, :])
            parts.append(part.astype(WIDE))
    return parts[0] if len(parts) == 1 else jnp.concatenate(parts, axis=0)


def unpack_feed_kernel(sc_ref, kept_ref, got_ref, out_ref, gate_ref, up_ref, down_ref, gain_ref):
    take = functools.partial(whole_rows, sc_ref[0, CORE], kept_ref, got_ref)
    width, hidden = gate_ref.shape
    row = 0
    for grads in (gate_ref, up_ref):
        for start in range(0, hidden, width):
            grads[:, start : start + width] = take(row, width)
            row += width
    down_ref[...] = take(row, hidden)
    row += hidden
    out_ref[...] = take(row, INNER)
    row += INNER
    gain_ref[...] = take(row, 16)[0:1, :]


def unpack_last_kernel(sc_ref, kept_ref, got_ref, query_ref, key_ref, value_ref, table_ref, gain_ref):
    take = functools.partial(whole_rows, sc_ref[0, CORE], kept_ref, got_ref)
    width = gain_ref.shape[1]
    for part, grads in enumerate((query_ref, key_ref, value_ref)):
        grads[...] = take(part * width, width)
    small = take(3 * width, 16)
    gain_ref[...] = jnp.concatenate([small[0:1, :], small[1:2, : width - INNER]], axis=1)
    table_ref[...] = small[2 : 2 + HEADS, :BUCKETS]


def staged_sum(kept, sent, between, plan, add, place):
    came = [kept, lax.ppermute(sent, "blk", between)]
    after = yield sent
    for axes, size, index, peer, pairs in plan:
        order = jnp.stack([index] + [peer(index, shift) for shift in range(1, size)])
        own, *sends = add(order.astype(jnp.int32), came, after)
        came = [own] + [
            lax.ppermute(part, axes, pairs(shift)) for shift, part in enumerate(sends, 1)
        ]
        after = yield own
    (value,) = add(jnp.zeros((1,), jnp.int32), came, after)
    for axes, size, index, peer, pairs in reversed(plan):
        came = [lax.ppermute(value, axes, pairs(shift)) for shift in range(1, size)]
        after = yield value
        owners = jnp.stack([index] + [peer(index, -shift) for shift in range(1, size)])
        value = place(owners.astype(jnp.int32), [value] + came, after)
    got = lax.ppermute(value, "blk", between)
    after = yield value
    yield (value, got)


def finish(stages):
    for now in iter(lambda: stages.send(()), None):
        if isinstance(now, tuple):
            return now


def nearest_order(quads):
    return [
        sorted(range(quads), key=lambda k: (abs(k - place), k)) for place in range(quads)
    ]


def onehot_tables():
    thresholds = bucket_edges()

    def bucket(offset):
        half_count, exact_count, edges = thresholds
        distance = abs(offset)
        beyond = sum(distance >= edge for edge in edges)
        return (half_count if offset > 0 else 0) + (
            distance if distance < exact_count else exact_count + beyond
        )

    rows = np.zeros((BUCKETS, 2 * TURN), np.float32)
    for turn in range(TURN):
        back = turn if turn < TILE else turn - TURN
        rows[bucket(-TILE - back), turn] = 1.0
        rows[bucket(TILE + back), TURN + turn] = 1.0
    diagonals = np.zeros((6 * TILE, WIDTH2), np.float32)
    for part in range(3):
        for at in range(2 * TILE - 1):
            diagonals[part * 2 * TILE + at, bucket(TILE * part - 1 - at)] = 1.0
    return rows, diagonals


def body(
    hidden_in,
    item_lengths,
    live_mask,
    cotangent,
    query_weight,
    key_weight,
    value_weight,
    output_weight,
    bucket_bias_table,
    norm_attention,
    norm_feed,
    gate_weight,
    up_weight,
    down_weight,
):
    streams, block, width = hidden_in.shape
    hidden = gate_weight.shape[1]
    blocks = lax.axis_size("blk")
    parts = lax.axis_size("dp")
    quads = blocks // 4
    here = lax.axis_index("blk")
    replica = lax.axis_index("dp")
    core, side, quad = here % 2, (here // 2) % 2, here // 4
    mine, chunk = 2 * block, 4 * block

    across = [(k, k ^ 2) for k in range(blocks)]
    between = [(k, k ^ 1) for k in range(blocks)]
    onward = []
    for k in range(blocks):
        if k % 2 == 0:
            onward.append((k, k + 4 if k + 4 < blocks else k + 1))
        else:
            onward.append((k, k - 4 if k >= 4 else k - 1))

    order = nearest_order(quads)
    distances = [
        sorted({abs(order[place][step] - place) for place in range(quads)}) for step in range(quads)
    ]
    spots = jnp.asarray(np.array(order, np.int32).T)
    nearest = jnp.asarray(np.array([found[0] for found in distances], np.int32))[:, None]
    is_here = jnp.arange(quads, dtype=jnp.int32)[None, :] == quad
    place = jnp.sum(jnp.where(is_here, spots, 0), axis=1, keepdims=True)
    swapped = ((place > quad) != (core == 1)) & (place != quad)
    source = 2 * (jnp.abs(place - quad) - nearest) + swapped.astype(jnp.int32)
    first_end = jnp.where(side == 0, item_lengths[0, 0], item_lengths[1, 0])
    col = jnp.arange(8, dtype=jnp.int32)[None, :]
    sc = jnp.where(col == QUAD, quad, 0)
    sc = jnp.where(col == CORE, core, sc)
    sc = jnp.where(col == SIDE, side, sc)
    sc = jnp.where(col == PLACE, place, sc)
    sc = jnp.where(col == SOURCE, source, sc)
    sc = jnp.where(col == FIRST_END, first_end, sc).astype(jnp.int32)

    turned_onehot, diagonal_onehot = (jnp.asarray(t) for t in onehot_tables())

    smem = pl.BlockSpec(memory_space=pltpu.SMEM)
    vmem = pl.BlockSpec(memory_space=pltpu.VMEM)
    anywhere = pl.BlockSpec(memory_space=pl.ANY)
    shape = jax.ShapeDtypeStruct
    strip_rows_count = 2 * chunk - TILE
    near_shape = pltpu.VMEM((HEADS, NEAR, TILE), WIDE)
    strip_shape = pltpu.VMEM((HEADS, strip_rows_count, TILE), WIDE)
    gen_shape = pltpu.VMEM((chunk, mine), WIDE)
    dma = pltpu.SemaphoreType.DMA
    pairs_in_chunk = mine * chunk * HEADS

    def call(kernel, name, in_specs, out_specs, out_shape, scratch, operands, grid=(1,), aliases=None, us=5.0, after=(), limit=24):
        count = 1 + len(operands)

        def without_ties(*refs):
            kernel(*refs[:count], *refs[count + len(after) :])

        return pl.pallas_call(
            without_ties if after else kernel,
            grid_spec=pltpu.PrefetchScalarGridSpec(
                num_scalar_prefetch=1,
                grid=grid,
                in_specs=list(in_specs) + [anywhere] * len(after),
                out_specs=out_specs,
                scratch_shapes=scratch,
            ),
            out_shape=out_shape,
            input_output_aliases=aliases or {},
            compiler_params=pltpu.CompilerParams(vmem_limit_bytes=limit * 1024 * 1024),
            cost_estimate=pl.CostEstimate(
                flops=int(us * 4e9), bytes_accessed=4 << 20, transcendentals=0
            ),
            name=name,
        )(sc, *operands, *after)

    def far_away(array):
        return pltpu.with_memory_space_constraint(array, pltpu.HBM)

    def tied(array, after):
        return call(
            tie_kernel, "tie", [anywhere], anywhere, shape(array.shape, array.dtype), [], (array,),
            aliases={1: 0}, us=0.3, after=after, limit=16,
        )

    def pick(both, index):
        return lax.dynamic_index_in_dim(both, index, 0, False)

    live_rows = jnp.pad(live_mask.astype(LOW)[:, None, :], ((0, 0), (0, 15), (0, width - block)))
    payload = jnp.concatenate([pick(hidden_in, 1 - side), pick(live_rows, 1 - side)], axis=0)
    got = lax.ppermute(payload, "blk", across)
    packed, x_low, rowk, rowq, vec = call(
        norm_kernel, "norm_rows", [smem] + [vmem] * 6, (vmem,) * 5,
        (
            shape((mine + 16, width), LOW), pltpu.HBM((mine, width), LOW), shape((8, chunk), WIDE),
            shape((8, mine), WIDE), shape((8, 2 * TURN), WIDE),
        ), [],
        (item_lengths, hidden_in, live_mask, got, norm_attention[None, :], bucket_bias_table, turned_onehot),
        us=2.0, limit=56,
    )
    own_chunk = jnp.concatenate([packed, lax.ppermute(packed, "blk", between)], axis=0)
    cot_got = lax.ppermute(pick(cotangent, 1 - side), "blk", across)

    qkv_shape = pltpu.HBM((quads * chunk, 3 * INNER), LOW)
    ext_shape = pltpu.HBM((quads * chunk, WIDTH2), LOW)
    state_shapes = (shape((INNER, mine), WIDE), shape((16, mine), WIDE))

    def chunk_out(step, columns):
        return pl.BlockSpec((chunk, columns), lambda i, sc: (sc[step, PLACE], 0))

    chunk_scratch = [pltpu.VMEM((chunk, width), LOW), pltpu.VMEM((2, 16, width), LOW)]
    held = lax.ppermute(own_chunk, "blk", onward)
    qkv, ext, qx, acc, ml = call(
        forward_own_kernel, "attend_own", [smem, anywhere] + [vmem] * 6,
        (chunk_out(0, 3 * INNER), chunk_out(0, WIDTH2), vmem, vmem, vmem),
        (qkv_shape, ext_shape, shape((HEADS, 2 * WIDTH2, mine), LOW)) + state_shapes,
        chunk_scratch + [strip_shape, near_shape, gen_shape, dma((6,))],
        (bucket_bias_table, own_chunk, key_weight, value_weight, query_weight, vec, rowq, rowk),
        us=12.0,
    )

    came = []
    for step in range(1, quads):
        held, acc = lax.optimization_barrier((held, acc))
        came.append((held, lax.ppermute(held, "blk", between)))
        if step + 1 < quads:
            held = lax.ppermute(held, "blk", onward)
        arrays = [array for distance in distances[step] for array in came[distance - 1]]
        qkv, ext, acc, ml = call(
            functools.partial(forward_kernel, step, len(arrays)), "attend_other",
            [smem] + [vmem] * 7 + [anywhere] * (2 + len(arrays)),
            (chunk_out(step, 3 * INNER), chunk_out(step, WIDTH2), vmem, vmem),
            (qkv_shape, ext_shape) + state_shapes,
            chunk_scratch + [near_shape, dma((6,))],
            (bucket_bias_table, key_weight, value_weight, query_weight, vec, qx, acc, ml, qkv, ext, *arrays),
            aliases={7: 2, 8: 3, 9: 0, 10: 1}, us=10.0,
        )

    (do_mine, do_turned, stat, out_kept, out_sent, grad_res, act, feed, grad_gate, grad_up,
     context, branch, gain_grad, cot) = call(
        middle_kernel, "feed_both_ways", [vmem] * 11, (vmem,) * 14,
        (
            shape((mine, INNER + WIDTH2), LOW), pltpu.HBM((INNER, mine), LOW), pltpu.HBM((WIDTH2, mine), LOW),
            shape((block, width), LOW), shape((block, width), LOW), pltpu.HBM((mine, width), WIDE),
            shape((mine, hidden), LOW), shape((mine, width), LOW), shape((mine, hidden), LOW),
            shape((mine, hidden), LOW), shape((mine, INNER), LOW), shape((mine, width), LOW),
            shape((8, width), WIDE), shape((mine, width), LOW),
        ), [],
        (
            acc, ml, x_low, cotangent, cot_got, rowq, output_weight, gate_weight, up_weight, down_weight,
            norm_feed[None, :],
        ),
        us=12.0,
    )
    do_other = lax.ppermute(do_mine, "blk", between)
    do_chunk = jnp.concatenate([do_mine, do_other], axis=0)
    do_came = [(do_chunk,)]
    held = lax.ppermute(do_chunk, "blk", onward)

    def joined(kept, got):
        return jnp.where(side == 0, jnp.stack([kept, got]), jnp.stack([got, kept]))

    def over_blocks(shift):
        return [(k, (k + 4 * shift) % blocks) for k in range(blocks)]

    if parts == 2:

        def over_square(shift):
            pairs = []
            for k in range(blocks):
                for r in range(parts):
                    k2, r2 = k ^ (2 * (shift >> 1)), r ^ (shift & 1)
                    pairs.append((k * parts + r, k2 * parts + r2))
            return pairs

        plan = [(("blk", "dp"), 4, side * 2 + replica, lambda i, s: i ^ abs(s), over_square)]
    else:
        plan = [
            ("blk", 2, side, lambda i, s: i ^ 1, lambda s: across),
            (
                "dp", parts, replica, lambda i, s: (i + s) % parts,
                lambda s: [(k, (k + s) % parts) for k in range(parts)],
            ),
        ]
    plan.append(("blk", quads, quad, lambda i, s: (i + s) % quads, over_blocks))
    pieces_in_all = 8 * 2 * 2 * parts * quads

    def padded(rows):
        return -(-rows // pieces_in_all) * pieces_in_all

    feed_rows = padded(3 * hidden + INNER + 8) // 2
    feed_kept, feed_sent = call(
        feed_grads_kernel, "feed_weight_grads", [vmem] * 8, (vmem, vmem),
        (shape((feed_rows, width), LOW),) * 2, [],
        (act, feed, grad_gate, grad_up, context, branch, cot, gain_grad), us=7.0, after=(do_chunk,),
    )
    def add_parts(order, arrays, after):
        size = order.shape[0]
        split = [a.reshape((size, a.shape[0] // size, a.shape[1])) for a in arrays]
        return call(
            add_kernel, "add_parts", [smem] + [vmem] * len(split), (vmem,) * size,
            (shape(split[0].shape[1:], LOW),) * size, [], (order, *split), us=2.0, after=after, limit=16,
        )

    def place_parts(owners, arrays, after):
        one = arrays[0].shape
        whole = call(
            place_kernel, "place_parts", [smem] + [vmem] * len(arrays), vmem,
            shape((len(arrays),) + one, LOW), [], (owners, *arrays), us=1.0, after=after, limit=16,
        )
        return whole.reshape((-1,) + one[1:])

    feed_stages = staged_sum(feed_kept, feed_sent, between, plan, add_parts, place_parts)
    next(feed_stages)
    ties = [do_chunk, feed_stages.send((do_chunk,))]
    out_got = lax.ppermute(out_sent, "blk", across)

    qkv, ext = far_away(qkv), far_away(ext)
    pair_strip = pltpu.VMEM((2, strip_rows_count, TILE), WIDE)
    grad_queries, table_grads = [], []
    for pair in range(PAIRS):

        def pair_columns(base, pair=pair):
            return pl.BlockSpec((chunk, WIDTH2), lambda i, sc: (i, base + pair))

        dq, table_grad = call(
            functools.partial(queries_kernel, pair), "grad_queries",
            [
                smem, pair_columns(0), pair_columns(PAIRS),
                pl.BlockSpec((chunk, WIDTH2), lambda i, sc: (i, 0)), vmem, vmem,
                pl.BlockSpec((2, 2 * WIDTH2, mine), lambda i, sc, pair=pair: (pair, 0, 0)),
                pl.BlockSpec((WIDTH2, mine), lambda i, sc, pair=pair: (pair, 0)), vmem, vmem,
            ],
            (vmem, vmem),
            (shape((WIDTH2, mine), LOW), shape((8, WIDTH2), WIDE)),
            [
                pair_strip, pltpu.VMEM((2, NEAR, TILE), WIDE), gen_shape,
                pltpu.VMEM((2, 2 * WIDTH2, mine), LOW), pltpu.VMEM((2, 2 * WIDTH2, mine), LOW),
                pltpu.VMEM((2, WIDTH2, mine), WIDE), pltpu.VMEM((2, NEAR, TILE), WIDE),
                pltpu.VMEM((2, chunk + 2 * TILE, mine), LOW),
            ],
            (bucket_bias_table, qkv, qkv, ext, vec, rowq, qx, do_turned, stat, diagonal_onehot),
            grid=(quads,), us=9.0, after=ties, limit=20,
        )
        grad_queries.append(dq)
        table_grads.append(table_grad)
        ties = [dq]
        if pair == 1:
            ties.append(out_got)
        if len(do_came) < quads:
            held = tied(held, (dq,))
            ties.append(held)
            do_came.append((held, lax.ppermute(held, "blk", between)))
            if len(do_came) < quads:
                held = lax.ppermute(held, "blk", onward)
        if pair > 0:
            for _ in range(len(plan) - 1 if pair == 1 else 1):
                tie = feed_stages.send((dq,))
            ties.append(tie)
    while len(do_came) < quads:
        do_came.append((held, lax.ppermute(held, "blk", between)))
        if len(do_came) < quads:
            held = lax.ppermute(held, "blk", onward)

    def own_blocks(n):
        return pl.BlockSpec(
            (block, 2 * INNER), lambda i, sc: (4 * sc[0, QUAD] + sc[0, CORE] + 2 * n, 0)
        )

    dkv = None
    for group in (range(quads - 2), range(quads - 2, quads - 1), range(quads - 1, quads)):
        arrays, counts = [], []
        for step in group:
            found = [array for distance in distances[step] for array in do_came[distance]]
            arrays += found
            counts.append(len(found))
        last = group[-1] == quads - 1
        first = group[0]
        dkv = call(
            functools.partial(keys_kernel, tuple(group), tuple(counts)), "grad_keys",
            [
                smem, pl.BlockSpec((chunk, INNER), lambda i, sc, first=first: (sc[first + i, PLACE], 2)),
                own_blocks(0), own_blocks(1), vmem, vmem, chunk_out(0, WIDTH2),
            ] + ([vmem] if first else []) + [anywhere] * len(arrays),
            vmem, shape((2 * INNER, mine), LOW if last else WIDE),
            [
                pltpu.VMEM((2, chunk, INNER + WIDTH2), LOW), pltpu.VMEM((2 * INNER, mine), WIDE),
                pltpu.VMEM((2, HEADS, 2 * WIDTH2, mine), LOW),
                strip_shape if not first else pltpu.VMEM((8, TILE), WIDE), near_shape,
                gen_shape if not first else pltpu.VMEM((8, TILE), WIDE), dma((2, 4)),
            ],
            (bucket_bias_table, qkv, qkv, qkv, vec, rowq, ext) + ((dkv,) if first else ()) + tuple(arrays),
            grid=(len(group),), us=8.0 * len(group), after=ties, limit=28,
        )
        ties = []
        if not first or last:
            for _ in range(1 if last else len(plan) - 1):
                ties = [feed_stages.send((dkv,))]

    last_rows = padded(3 * width + 8) // 2
    in_kept, in_sent, last_kept, last_sent = call(
        last_kernel, "attention_weight_grads", [vmem] * 14, (vmem,) * 4,
        (
            shape((block, width), LOW), shape((block, width), LOW),
            shape((last_rows, INNER), LOW), shape((last_rows, INNER), LOW),
        ), [],
        (
            *grad_queries, dkv, packed, x_low, grad_res, query_weight, key_weight, value_weight,
            norm_attention[None, :], *table_grads,
        ),
        us=6.0, after=ties,
    )
    last_stages = staged_sum(last_kept, last_sent, between, plan, add_parts, place_parts)
    next(last_stages)
    in_got = lax.ppermute(in_sent, "blk", across)
    feed_kept, feed_got = feed_stages.send(())
    last_stages.send(())
    grad_out, grad_gate, grad_up, grad_down, grad_norm_feed = call(
        unpack_feed_kernel, "unpack_feed", [vmem] * 2, (vmem,) * 5,
        (
            shape((INNER, width), WIDE), shape((width, hidden), WIDE), shape((width, hidden), WIDE),
            shape((hidden, width), WIDE), shape((1, width), WIDE),
        ), [],
        (feed_kept, feed_got), us=5.0,
    )
    last_stages.send((grad_norm_feed,))
    last_stages.send((in_got,))
    last_kept, last_got = finish(last_stages)
    grad_query, grad_key, grad_value, grad_table, grad_norm_attention = call(
        unpack_last_kernel, "unpack_attention", [vmem] * 2, (vmem,) * 5,
        (shape((width, INNER), WIDE),) * 3 + (shape((HEADS, BUCKETS), WIDE), shape((1, width), WIDE)), [],
        (last_kept, last_got), us=2.0,
    )
    return (
        joined(out_kept, out_got),
        joined(in_kept, in_got),
        grad_query,
        grad_key,
        grad_value,
        grad_out,
        grad_table.T,
        grad_norm_attention[0],
        grad_norm_feed[0],
        grad_gate,
        grad_up,
        grad_down,
    )


def solution(mesh):
    return jax.shard_map(
        body,
        mesh=mesh,
        in_specs=(
            P("dp", "blk", None),
            P("dp", None),
            P("dp", "blk"),
            P("dp", "blk", None),
            P(),
            P(),
            P(),
            P(),
            P(),
            P(),
            P(),
            P(),
            P(),
            P(),
        ),
        out_specs=(
            P("dp", "blk", None),
            P("dp", "blk", None),
            P(),
            P(),
            P(),
            P(),
            P(),
            P(),
            P(),
            P(),
            P(),
            P(),
        ),
        check_vma=False,
    )
```

```python
import functools

import jax
import jax.numpy as jnp
import numpy as np
from jax import lax
from jax.experimental import pallas as pl
from jax.experimental.pallas import tpu as pltpu
from jax.sharding import PartitionSpec as P

HEADS = 6
HD = 64
WIDTH2 = 2 * HD
PAIRS = HEADS // 2
INNER = HEADS * HD
BUCKETS = 32
MAXDIST = 128
EPSILON = 1e-06
BIG = 1e30
TILE = 128
NEAR = 3 * TILE
TURN = 4 * TILE
FAR_BEFORE = BUCKETS // 2 - 1
FAR_AFTER = BUCKETS - 1
LOW = jnp.bfloat16
WIDE = jnp.float32
GELU_A = 0.7978845608028654
GELU_B = 0.044715

QUAD, CORE, SIDE, PLACE, SOURCE, FIRST_END, CHUNK, UP, DOWN = range(9)
MASK, BEFORE, AFTER, PEN, STAT, LIVE, SEG = 0, 1, 2, 7, 8, 11, 12
ONE_A, OFF, ONE_B, ONE_C, ONE_D = 36, 37, 38, 39, 40


def bucket_edges():
    half_count = BUCKETS // 2
    exact_count = half_count // 2
    log_levels = half_count - exact_count
    thresholds = []
    for level_index in range(1, log_levels):
        candidate = exact_count
        while (
            candidate**log_levels * exact_count**level_index
            < MAXDIST**level_index * exact_count**log_levels
        ):
            candidate = candidate + 1
        thresholds.append(candidate)
    return (half_count, exact_count, thresholds)


def dot_nt(left, right):
    return lax.dot_general(
        left, right, (((1,), (1,)), ((), ())), preferred_element_type=WIDE
    )


def dot_nn(left, right):
    return jnp.dot(left, right, preferred_element_type=WIDE)


def dot_tn(left, right):
    return lax.dot_general(
        left, right, (((0,), (0,)), ((), ())), preferred_element_type=WIDE
    )


def rows_of(count, width):
    return lax.broadcasted_iota(jnp.int32, (count, width), 0)


def lanes_of(count, width):
    return lax.broadcasted_iota(jnp.int32, (count, width), 1)


def lane_half(array, half, other):
    return jnp.where(lanes_of(1, WIDTH2) // HD == half, array, other)


def row_half(array, half, other):
    return jnp.where(rows_of(WIDTH2, 1) // HD == half, array, other)


def pair_slice(pair, base=0):
    return slice(base + pair * WIDTH2, base + (pair + 1) * WIDTH2)


def tile_place(tile, core):
    return (tile // 2) * 4 + core * 2 + tile % 2


def rms_scale(values):
    return lax.rsqrt(jnp.mean(values * values, axis=-1, keepdims=True) + EPSILON)


def three_pieces(values):
    high = values.astype(LOW).astype(WIDE)
    mid = (values - high).astype(LOW).astype(WIDE)
    low = (values - high - mid).astype(LOW).astype(WIDE)
    return high, mid, low


def pipelined(items, first, second, depth):
    ahead = []
    for item in items:
        ahead.append((item, first(item)))
        if len(ahead) > depth:
            second(*ahead.pop(0))
    for waiting in ahead:
        second(*waiting)


def far_bias(table_ref, after, head):
    return table_ref[FAR_AFTER if after else FAR_BEFORE, head]


def build_near(near_ref, vec_ref, back, heads):
    for index, head in enumerate(heads):
        row = vec_ref[head : head + 1, back * TURN : (back + 1) * TURN]
        row = jnp.broadcast_to(row, (NEAR, TURN))
        near_ref[index] = pltpu.roll(row, 0, 1, stride=1, stride_axis=0)[:, :TILE]


def build_strip(strip_ref, near_ref, table_ref, back, chunk, heads):
    edge = chunk - TILE
    rest = strip_ref.shape[1] - edge - 2 * TILE
    for index, head in enumerate(heads):
        far_before = far_bias(table_ref, back, head)
        far_after = far_bias(table_ref, not back, head)
        strip_ref[index, : edge - TILE, :] = jnp.full((edge - TILE, TILE), far_before, WIDE)
        strip_ref[index, edge - TILE : edge + 2 * TILE, :] = near_ref[index]
        strip_ref[index, edge + 2 * TILE :, :] = jnp.full((rest, TILE), far_after, WIDE)


def strip_rows(strip_ref, index, first_tile, tiles, core, chunk):
    parts = []
    for tile in range(first_tile, first_tile + tiles):
        start = (chunk - TILE) - tile_place(tile, core) * TILE
        parts.append(strip_ref[index, pl.ds(pl.multiple_of(start, TILE), chunk), :])
    return jnp.concatenate(parts, axis=1)


def near_fixes(near_ref, table_ref, flags, index, head, back):
    low, high = flags
    return (
        low * (near_ref[index, :TILE, :] - far_bias(table_ref, back, head)),
        high * (near_ref[index, 2 * TILE :, :] - far_bias(table_ref, not back, head)),
    )


def fix_near(scores, step, steps, fixes):
    low, high = fixes
    chunk, width = scores.shape
    if step == 0:
        last = jnp.concatenate(
            [scores[chunk - TILE :, :TILE] + low, scores[chunk - TILE :, TILE:]], axis=1
        )
        scores = jnp.concatenate([scores[: chunk - TILE], last], axis=0)
    if step == steps - 1:
        first = jnp.concatenate(
            [scores[:TILE, : width - TILE], scores[:TILE, width - TILE :] + high], axis=1
        )
        scores = jnp.concatenate([first, scores[TILE:]], axis=0)
    return scores


def near_flags(place, quad, core):
    low = jnp.where((place == quad - 1) & (core == 0), 1.0, 0.0)
    high = jnp.where((place == quad + 1) & (core == 1), 1.0, 0.0)
    return low, high


def natural_row(even, odd):
    block = even.shape[1] // 2
    return jnp.concatenate(
        [even[:, :block], odd[:, :block], even[:, block:], odd[:, block:]], axis=1
    )


def key_columns(rows, lanes):
    places = rows[0].shape[1]
    stack = jnp.zeros((16, places), WIDE)
    spread = jnp.zeros((16, WIDTH2), WIDE)
    number, lane = rows_of(16, 1), lanes_of(16, WIDTH2)
    for index, row in enumerate(rows):
        stack = jnp.where(number == index, row, stack)
    for index, at, scale in lanes:
        spread = jnp.where((number == index) & (lane == at), scale, spread)
    return dot_tn(stack.astype(LOW), spread.astype(LOW))


def visible_mask(gen_ref, segment_column, segment_row, live, core, keys_down):
    chunk, mine = gen_ref.shape
    down = rows_of(chunk, 1)
    for tile in range(mine // TILE):
        lanes = slice(tile * TILE, (tile + 1) * TILE)
        across = tile_place(tile, core) * TILE + lanes_of(1, TILE)
        alive = live if keys_down else live[:, lanes]
        visible = (segment_column == segment_row[:, lanes]) & ((alive > 0.5) | (down == across))
        gen_ref[:, lanes] = jnp.where(visible, 0.0, -BIG)


def project(a, weight_refs, qkv_ref):
    for part, w_ref in enumerate(weight_refs):
        cols = slice(part * INNER, (part + 1) * INNER)
        qkv_ref[:, cols] = dot_nn(a, w_ref[...]).astype(LOW)


def halves_copies(source, swapped, core, rows_ref, live_ref, sems):
    first_core = 1 - core if swapped else core
    block = rows_ref.shape[0] // 4
    half = source.shape[0] // 2
    copies = []
    for index in range(2):
        owner = first_core if index == 0 else 1 - first_core
        for part in range(2):
            at = pl.multiple_of(part * 2 * block + owner * block, block)
            copies.append((source.at[pl.ds(index * half + part * block, block), :], rows_ref.at[pl.ds(at, block), :]))
        if live_ref is not None:
            copies.append((source.at[pl.ds(index * half + 2 * block, 16), :], live_ref.at[owner]))
    return [
        pltpu.make_async_copy(start, end, sems.at[index]) for index, (start, end) in enumerate(copies)
    ]


def start_fetch(sc_ref, step, sources, rows_ref, live_ref, sems):
    core = sc_ref[0, CORE]
    for index, source in enumerate(sources):

        @pl.when(sc_ref[step, SOURCE] == index)
        def _():
            for copy in halves_copies(source, index % 2 == 1, core, rows_ref, live_ref, sems):
                copy.start()


def wait_fetch(sc_ref, sources, rows_ref, live_ref, sems):
    for copy in halves_copies(sources[0], False, sc_ref[0, CORE], rows_ref, live_ref, sems):
        copy.wait()


def norm_kernel(
    sc_ref, lengths_ref, hidden_ref, live_ref, got_ref, gain_ref, table_ref, onehot_ref,
    packed_ref, x_ref, rowk_ref, rowq_ref, vec_ref,
):
    side, core, quad = sc_ref[0, SIDE], sc_ref[0, CORE], sc_ref[0, QUAD]
    block = hidden_ref.shape[1]
    mine, chunk = 2 * block, 4 * block
    kept, got = hidden_ref[side], got_ref[:block, :]
    live_kept = live_ref[pl.ds(side, 1), :].astype(WIDE)
    live_got = got_ref[block : block + 16, :block].astype(WIDE)[0:1, :]
    for part in range(2):
        rows = jnp.where(side == part, kept, got)
        x_ref[part * block : (part + 1) * block, :] = rows
        wide = rows.astype(WIDE)
        normed = wide * rms_scale(wide) * gain_ref[...]
        packed_ref[part * block : (part + 1) * block, :] = normed.astype(LOW)
    live = jnp.concatenate(
        [jnp.where(side == 0, live_kept, live_got), jnp.where(side == 0, live_got, live_kept)],
        axis=1,
    )
    packed_ref[mine:, :] = jnp.broadcast_to(live, (16, mine)).astype(LOW)

    places = quad * chunk + lanes_of(1, chunk)

    def one_item(item, carry):
        end, segment = carry
        end = end + lengths_ref[side, item]
        return end, segment + jnp.where(places >= end, 1.0, 0.0)

    zero = jnp.zeros((1, chunk), WIDE)
    end, segment = lax.fori_loop(0, lengths_ref.shape[1], one_item, (jnp.int32(0), zero))
    rowk_ref[...] = jnp.broadcast_to(segment, (8, chunk))
    own = jnp.concatenate(
        [
            rowk_ref[0:1, pl.ds(pl.multiple_of(part * mine + core * block, block), block)]
            for part in range(2)
        ],
        axis=1,
    )
    number = rows_of(8, 1)
    rowq = jnp.where(number == 0, own, 0.0)
    rowq = jnp.where(number == 2, jnp.where(own > 0.5, BIG, 0.0), rowq)
    rowq = jnp.where(number == 3, live, rowq)
    off = jnp.where((live > 0.5) & (own < 0.5), 0.0, -BIG)
    rowq_ref[...] = jnp.where(number == 4, off, rowq)
    found = lax.dot_general(
        table_ref[...], onehot_ref[...], (((0,), (0,)), ((), ())),
        precision=lax.Precision.HIGHEST, preferred_element_type=WIDE,
    )
    vec_ref[...] = jnp.concatenate([found, jnp.zeros((8 - HEADS, found.shape[1]), WIDE)], axis=0)


def forward_items(mine):
    steps = mine // (2 * TILE)
    return [(pair, step, hh) for pair in range(PAIRS) for step in range(steps) for hh in range(2)]


def forward_operands(qkv_ref, ext):
    made = {}

    def operands(pair):
        if pair not in made:
            k_ext = jnp.concatenate([qkv_ref[:, pair_slice(pair)], ext], axis=1)
            v_turned = qkv_ref[:, pair_slice(pair, INNER)].T
            made[pair] = (
                k_ext, [row_half(v_turned, hh, jnp.ones_like(v_turned)) for hh in range(2)]
            )
        return made[pair]

    return operands


def step_lanes(step):
    return slice(step * 2 * TILE, (step + 1) * 2 * TILE)


def head_rows(head):
    return slice(head * HD, (head + 1) * HD)


def forward_own_kernel(
    sc_ref, table_ref, source_ref, wk_ref, wv_ref, wq_ref, vec_ref, rowq_ref, rowk_ref,
    qkv_ref, ext_ref, a_ref, qx_ref, acc_ref, ml_ref,
    live_ref, strip_ref, near_ref, gen_ref, sems,
):
    core = sc_ref[0, CORE]
    chunk = qkv_ref.shape[0]
    mine = acc_ref.shape[1]
    block = mine // 2
    start_fetch(sc_ref, 0, [source_ref], a_ref, live_ref, sems)
    build_near(near_ref, vec_ref, 0, range(HEADS))
    build_strip(strip_ref, near_ref, table_ref, False, chunk, range(HEADS))
    number = rows_of(WIDTH2, 1)
    for head in range(HEADS):
        rows = jnp.where(number == MASK, 1.0, 0.0)
        for which, after in ((BEFORE, False), (AFTER, True)):
            far = jnp.full((1, mine), far_bias(table_ref, after, head), WIDE)
            for piece, value in enumerate(three_pieces(far)):
                rows = jnp.where(number == which + 2 * piece, value, rows)
        rows = jnp.where(number == PEN, -rowq_ref[2:3, :], rows)
        qx_ref[head, WIDTH2:, :] = rows.astype(LOW)
    wait_fetch(sc_ref, [source_ref], a_ref, live_ref, sems)
    project(a_ref[...], (wk_ref, wv_ref, wq_ref), qkv_ref)
    live = natural_row(live_ref[0].astype(WIDE)[0:1, :], live_ref[1].astype(WIDE)[0:1, :])
    columns = key_columns(
        [jnp.ones_like(live), live, rowk_ref[0:1, :]],
        [(0, STAT, 1.0), (0, STAT + 1, 1.0), (0, STAT + 2, 1.0), (1, LIVE, 1.0), (2, SEG, 1.0)],
    )
    ext_ref[...] = columns.astype(LOW)
    visible_mask(
        gen_ref, columns[:, SEG : SEG + 1], rowq_ref[0:1, :], columns[:, LIVE : LIVE + 1], core, True
    )
    for part in range(2):
        at = pl.ds(pl.multiple_of(part * mine + core * block, block), block)
        lanes = slice(part * block, (part + 1) * block)
        for pair in range(PAIRS):
            turned = qkv_ref[at, pair_slice(pair, 2 * INNER)].T
            for hh in range(2):
                qx_ref[2 * pair + hh, :WIDTH2, lanes] = row_half(
                    turned, hh, jnp.zeros_like(turned)
                )
    ml_ref[...] = jnp.zeros_like(ml_ref)
    operands = forward_operands(qkv_ref, ext_ref[...])

    def first(item):
        pair, step, hh = item
        s = dot_nn(operands(pair)[0], qx_ref[2 * pair + hh, :, step_lanes(step)])
        s = s + strip_rows(strip_ref, 2 * pair + hh, 2 * step, 2, core, chunk)
        return s + gen_ref[:, step_lanes(step)]

    def second(item, s):
        pair, step, hh = item
        head, lanes = 2 * pair + hh, step_lanes(step)
        top = jnp.max(s, axis=0, keepdims=True)
        p = jnp.exp(s - top).astype(LOW)
        pv = dot_nn(operands(pair)[1][hh], p)
        ml_ref[head : head + 1, lanes] = top
        ml_ref[8 + head : 9 + head, lanes] = pv[HD * (1 - hh) : HD * (1 - hh) + 1, :]
        acc_ref[head_rows(head), lanes] = pv[hh * HD : (hh + 1) * HD, :]

    pipelined(forward_items(mine), first, second, 2)


def forward_kernel(
    step_number, sources, sc_ref, table_ref, wk_ref, wv_ref, wq_ref, vec_ref, qx_ref, acc_in, ml_in,
    qkv_in, ext_in, a_in, *rest,
):
    source_refs, rest = rest[:sources], rest[sources:]
    qkv_ref, ext_ref, a_ref, acc_ref, ml_ref, live_ref, near_ref, sems = rest
    quad, core, place = (sc_ref[step_number, i] for i in (QUAD, CORE, PLACE))
    chunk = qkv_ref.shape[0]
    mine = acc_ref.shape[1]
    start_fetch(sc_ref, step_number, source_refs, a_ref, live_ref, sems)
    build_near(near_ref, vec_ref, 0, range(HEADS))
    wait_fetch(sc_ref, source_refs, a_ref, live_ref, sems)
    project(a_ref[...], (wk_ref, wv_ref, wq_ref), qkv_ref)
    live = natural_row(live_ref[0].astype(WIDE)[0:1, :], live_ref[1].astype(WIDE)[0:1, :])
    places = place * chunk + lanes_of(1, chunk)
    seen = (live > 0.5) & (places < sc_ref[step_number, FIRST_END])
    is_before = jnp.where(place < quad, 1.0, 0.0)
    is_after = 1.0 - is_before
    marks = [(0, MASK, 1.0), (1, PEN, 1.0)]
    marks += [(1, STAT + n, 1.0) for n in range(3)]
    marks += [(1, BEFORE + 2 * n, is_before) for n in range(3)]
    marks += [(1, AFTER + 2 * n, is_after) for n in range(3)]
    ext = key_columns([jnp.where(seen, 0.0, -BIG), jnp.ones_like(live)], marks).astype(LOW)
    ext_ref[...] = ext
    flags = near_flags(place, quad, core)
    steps = mine // (2 * TILE)
    operands = forward_operands(qkv_ref, ext)

    def first(item):
        pair, step, hh = item
        head = 2 * pair + hh
        s = dot_nn(operands(pair)[0], qx_ref[head, :, step_lanes(step)])
        return fix_near(s, step, steps, near_fixes(near_ref, table_ref, flags, head, head, False))

    def second(item, s):
        pair, step, hh = item
        head, lanes = 2 * pair + hh, step_lanes(step)
        old = ml_in[head : head + 1, lanes]
        top = jnp.maximum(old, jnp.max(s, axis=0, keepdims=True))
        keep = jnp.exp(old - top)
        p = jnp.exp(s - top).astype(LOW)
        pv = dot_nn(operands(pair)[1][hh], p)
        ml_ref[head : head + 1, lanes] = top
        total = ml_in[8 + head : 9 + head, lanes] * keep
        ml_ref[8 + head : 9 + head, lanes] = total + pv[HD * (1 - hh) : HD * (1 - hh) + 1, :]
        rows = head_rows(head)
        acc_ref[rows, lanes] = acc_in[rows, lanes] * keep + pv[hh * HD : (hh + 1) * HD, :]

    pipelined(forward_items(mine), first, second, 2)


def middle_kernel(
    sc_ref, acc_ref, ml_ref, x_ref, cot_in, cot_got, rowq_ref, wo_ref, gate_ref, up_ref, down_ref, gain_ref,
    do_ref, keep_ref, send_ref, grad_res_ref, act_ref, feed_ref, gg_ref, gu_ref,
    ctx_ref, branch_ref, gain_grad_ref, cot_ref,
):
    side = sc_ref[0, SIDE]
    mine = x_ref.shape[0]
    block = mine // 2
    gain = gain_ref[...]
    context = []
    for head in range(HEADS):
        context.append(acc_ref[head_rows(head), :] / ml_ref[8 + head : 9 + head, :])
    for pair in range(PAIRS):
        both = jnp.concatenate(context[2 * pair : 2 * pair + 2], axis=0).astype(LOW)
        ctx_ref[:, pair_slice(pair)] = both.T
    gain_grad = jnp.zeros_like(gain)
    cot_kept = cot_in[side]
    for part in range(2):
        rows = slice(part * block, (part + 1) * block)
        cot_ref[rows, :] = jnp.where(side == part, cot_kept, cot_got[...])

    def first(part):
        rows = slice(part * block, (part + 1) * block)
        residual = x_ref[rows, :].astype(WIDE) + dot_nn(ctx_ref[rows, :], wo_ref[...])
        scale = rms_scale(residual)
        z = residual * scale
        feed = (z * gain).astype(LOW)
        feed_ref[rows, :] = feed
        v = dot_nn(feed, gate_ref[...])
        up = dot_nn(feed, up_ref[...])
        return residual, scale, z, v, up, dot_nt(cot_ref[rows, :], down_ref[...])

    def second(part, made):
        nonlocal gain_grad
        residual, scale, z, v, up, grad_hidden = made
        rows = slice(part * block, (part + 1) * block)
        square = v * v
        t = jnp.tanh(GELU_A * v * (1.0 + GELU_B * square))
        half = 0.5 * (1.0 + t)
        g = v * half
        slope = half + 0.5 * v * (1.0 - t * t) * (GELU_A * (1.0 + 3.0 * GELU_B * square))
        act = (g * up).astype(LOW)
        act_ref[rows, :] = act
        grad_gate = (grad_hidden * up * slope).astype(LOW)
        grad_up = (grad_hidden * g).astype(LOW)
        gg_ref[rows, :] = grad_gate
        gu_ref[rows, :] = grad_up
        grad_feed = dot_nt(grad_gate, gate_ref[...]) + dot_nt(grad_up, up_ref[...])
        u = grad_feed * gain
        gain_grad = gain_grad + jnp.sum(grad_feed * z, axis=0, keepdims=True)
        cot = cot_ref[rows, :].astype(WIDE)
        grad_res = cot + scale * (u - z * jnp.mean(u * z, axis=-1, keepdims=True))
        grad_res_ref[rows, :] = grad_res
        branch = grad_res.astype(LOW)
        branch_ref[rows, :] = branch
        do_ref[rows, :INNER] = dot_nt(branch, wo_ref[...]).astype(LOW)
        output = (residual + dot_nn(act, down_ref[...])).astype(LOW)

        @pl.when(side == part)
        def _():
            keep_ref[...] = output

        @pl.when(side != part)
        def _():
            send_ref[...] = output

    pipelined(range(2), first, second, 1)
    gain_grad_ref[...] = jnp.broadcast_to(gain_grad, gain_grad_ref.shape)
    number = rows_of(WIDTH2, 1)
    stat = jnp.where((number == ONE_A) | ((number >= ONE_B) & (number <= ONE_D)), 1.0, 0.0)
    stat = jnp.where(number == OFF, -rowq_ref[2:3, :], stat)
    for pair in range(PAIRS):
        turned = do_ref[:, pair_slice(pair)].T
        for hh in range(2):
            head = 2 * pair + hh
            grads = turned[hh * HD : (hh + 1) * HD, :].astype(WIDE)
            delta = jnp.sum(grads * context[head], axis=0, keepdims=True)
            lse = ml_ref[head : head + 1, :] + jnp.log(ml_ref[8 + head : 9 + head, :])
            for base, value in ((0, lse), (3 * HEADS, delta)):
                for index, piece in enumerate(three_pieces(-value)):
                    stat = jnp.where(number == base + HEADS * index + head, piece, stat)
    do_ref[:, INNER:] = stat.astype(LOW).T


def put_half(core, keep_ref, send_ref, row, value):
    rows = keep_ref.shape[0]
    half, start = row // rows, row % rows

    @pl.when(core == half)
    def _():
        keep_ref[start : start + value.shape[0], : value.shape[1]] = value

    @pl.when(core != half)
    def _():
        send_ref[start : start + value.shape[0], : value.shape[1]] = value


def put_rows(core, keep_ref, send_ref, row, value):
    rows = keep_ref.shape[0]
    value = value.astype(LOW)
    first = min(value.shape[0], rows - row % rows)
    put_half(core, keep_ref, send_ref, row, value[:first])
    if first < value.shape[0]:
        put_half(core, keep_ref, send_ref, row + first, value[first:])


def feed_grads_kernel(
    sc_ref, act_ref, feed_ref, gg_ref, gu_ref, ctx_ref, branch_ref, cot_ref, gain_grad_ref,
    keep_ref, send_ref,
):
    core = sc_ref[0, CORE]
    put = functools.partial(put_rows, core, keep_ref, send_ref)
    width = keep_ref.shape[1]
    hidden = act_ref.shape[1]
    feed = feed_ref[...].T
    row = 0
    for grads in (gg_ref, gu_ref):
        for start in range(0, hidden, width):
            put(row, dot_nn(feed, grads[:, start : start + width]))
            row += width
    act = act_ref[...].T
    put(row, dot_nn(act, cot_ref[...]))
    row += hidden
    put(row, dot_nn(ctx_ref[...].T, branch_ref[...]))
    row += INNER
    rest = 2 * keep_ref.shape[0] - row
    put(row, jnp.where(rows_of(rest, 1) == 0, gain_grad_ref[0:1, :], 0.0))


def chunk_kernel(slot, own, sc_ref, table_ref, source_ref, q_ref, kv0_ref, kv1_ref, a0_ref, a1_ref, e0_ref, e1_ref,
                 wk_ref, wv_ref, vec_ref, *rest):
    if slot > 0:
        (dq_in, w_in, near_in, marks_in), rest = rest[:4], rest[4:]
    if own:
        (extq_ref, rowq_ref, a_own_ref, onehot_ref), rest = rest[:4], rest[4:]
        (dx_ref, kept_ref, sent_ref, dq_kept_ref, dq_sent_ref), rest = rest[:5], rest[5:]
        dq_ref, w_ref, near_out, marks_ref, strip_ref, gen_ref, do_ref, near_ref, ds_ref, grads_ref, sems = rest
    else:
        dx_ref, dq_ref, w_ref, near_out, marks_ref, do_ref, near_ref, ds_ref, grads_ref, sems = rest
    quad, core, side_chunk = sc_ref[0, QUAD], sc_ref[0, CORE], sc_ref[slot, CHUNK]
    chunk = q_ref.shape[0]
    block = kv0_ref.shape[0]
    mine = 2 * block
    tiles = mine // TILE
    steps = mine // (2 * TILE)
    number = rows_of(WIDTH2, 1)
    lane = lanes_of(1, WIDTH2)
    start_fetch(sc_ref, 0, [source_ref], do_ref, None, sems)
    build_near(near_ref, vec_ref, 1, range(HEADS))
    ext_turned = jnp.concatenate([e0_ref[...].T, e1_ref[...].T], axis=1).astype(WIDE)
    if own:
        build_strip(strip_ref, near_ref, table_ref, True, chunk, range(HEADS))
        visible_mask(
            gen_ref, extq_ref[...].astype(WIDE)[:, SEG : SEG + 1], rowq_ref[0:1, :], rowq_ref[3:4, :], core, False
        )
        ds_ref[:, :TILE, :] = jnp.zeros((2, TILE, mine), LOW)
        ds_ref[:, chunk + TILE :, :] = jnp.zeros((2, TILE, mine), LOW)
    wait_fetch(sc_ref, [source_ref], do_ref, None, sems)
    low, high = near_flags(quad, side_chunk, core)
    keys_before = side_chunk < quad
    gap = side_chunk - quad
    spread = jnp.where(jnp.abs(gap) <= 1, 1, 0)
    first_mark = jnp.where(spread == 1, 16 + 8 * gap, jnp.where(gap < 0, 0, 1))
    mark_of_key = first_mark + spread * (rows_of(mine, 1) // TILE)
    ext = do_ref[:, INNER:]
    made = {}

    def both(pair, base):
        return jnp.concatenate([kv0_ref[:, pair_slice(pair, base)], kv1_ref[:, pair_slice(pair, base)]], axis=0)

    def operands(pair):
        if pair in made:
            return made[pair]
        q_pair, do_pair = q_ref[:, pair_slice(pair)], do_ref[:, pair_slice(pair)]
        k_pair = both(pair, 0)
        k_turned, v_turned = k_pair.T, both(pair, INNER).T
        zero = jnp.zeros_like(k_turned)
        k_sides, v_sides, k_marked = [], [], []
        for hh in range(2):
            head = 2 * pair + hh
            rows = (number == head) | (number == head + HEADS) | (number == head + 2 * HEADS)
            rows = jnp.broadcast_to(jnp.where(rows, 1.0, 0.0), (WIDTH2, mine))
            if not own:
                far = jnp.where(
                    keys_before, far_bias(table_ref, False, head), far_bias(table_ref, True, head)
                )
                wide = jnp.full((1, mine), far, WIDE)
                for at, piece in zip((ONE_A, ONE_B, ONE_C), three_pieces(wide)):
                    rows = jnp.where(number == at, piece, rows)
                rows = jnp.where(number == OFF, 1.0, rows)
                rows = jnp.where(number == ONE_D, ext_turned[MASK : MASK + 1, :], rows)
            k_sides.append(
                jnp.concatenate([row_half(k_turned, hh, zero), rows.astype(LOW)], axis=0)
            )
            first = 3 * HEADS + head
            rows = (number == first) | (number == first + HEADS) | (number == first + 2 * HEADS)
            rows = jnp.broadcast_to(jnp.where(rows, 1.0, 0.0), (WIDTH2, mine)).astype(LOW)
            v_sides.append(jnp.concatenate([row_half(v_turned, hh, zero), rows], axis=0))
            marks = jnp.where(lane - HD * (1 - hh) == mark_of_key, 1.0, 0.0).astype(LOW)
            k_marked.append(lane_half(k_pair, hh, marks))
        made[pair] = (
            jnp.concatenate([q_pair, ext], axis=1), jnp.concatenate([do_pair, ext], axis=1),
            q_pair.T, do_pair.T, k_sides, v_sides, k_marked,
        )
        return made[pair]

    def first(item):
        pair, step, hh = item
        head, lanes = 2 * pair + hh, step_lanes(step)
        q_ext, do_ext, _, _, k_sides, v_sides, _ = operands(pair)
        s = dot_nn(q_ext, k_sides[hh][:, lanes])
        if own:
            s = s + strip_rows(strip_ref, head, 2 * step, 2, core, chunk) + gen_ref[:, lanes]
        else:
            s = fix_near(
                s, step, steps, near_fixes(near_ref, table_ref, (low, high), head, head, True)
            )
        return s, dot_nn(do_ext, v_sides[hh][:, lanes])

    products = {}

    def second(item, found):
        pair, step, hh = item
        head, lanes = 2 * pair + hh, step_lanes(step)
        s, dp = found
        p = jnp.exp(s)
        ds = (p * dp).astype(LOW)
        _, _, q_turned, do_turned, _, _, k_marked = operands(pair)
        half = slice(hh * HD, (hh + 1) * HD)
        grads_ref[head_rows(head), lanes] = dot_nn(q_turned, ds)[half, :].astype(LOW)
        rows = slice(INNER + head * HD, INNER + (head + 1) * HD)
        grads_ref[rows, lanes] = dot_nn(do_turned, p.astype(LOW))[half, :].astype(LOW)
        ds_ref[hh, TILE : chunk + TILE, lanes] = ds
        if not own:
            base = near_in[head] if slot > 0 else jnp.zeros((NEAR, TILE), WIDE)
            if step == 0:
                near_out[head, :TILE, :] = base[:TILE] + low * ds[chunk - TILE :, :TILE].astype(WIDE)
                near_out[head, TILE : 2 * TILE, :] = base[TILE : 2 * TILE]
            if step == steps - 1:
                near_out[head, 2 * TILE :, :] = base[2 * TILE :] + high * ds[:TILE, TILE:].astype(WIDE)
        if step == steps - 1:
            product = dot_nn(ds_ref[hh, TILE : chunk + TILE, :], k_marked[hh])
            for tile in range(chunk // TILE):
                total = jnp.sum(product[tile * TILE : (tile + 1) * TILE, :], axis=0, keepdims=True)
                if slot > 0:
                    total = total + marks_in[head, tile : tile + 1, :]
                marks_ref[head, tile : tile + 1, :] = total
            if own:
                total = near_in[head]
                for tile in range(tiles):
                    at = pl.ds(pl.multiple_of(tile_place(tile, core) * TILE, TILE), NEAR)
                    part = ds_ref[hh, at, tile * TILE : (tile + 1) * TILE]
                    total = total + part.astype(WIDE)
                near_out[head] = total
            products[hh] = product
            if hh == 1:
                total = jnp.where(lane < HD, products[0], products[1])
                if slot > 0:
                    total = total + dq_in[:, pair_slice(pair)]
                dq_ref[:, pair_slice(pair)] = total

    pipelined(forward_items(mine), first, second, 1)
    a = jnp.concatenate([a0_ref[...], a1_ref[...]], axis=0)
    grads = grads_ref[...]
    weights = dot_nn(grads, a)
    if slot > 0:
        weights = weights + w_in[...]
    dx = dot_nt(grads[:INNER, :].T, wk_ref[...]) + dot_nt(grads[INNER:, :].T, wv_ref[...])
    dx_ref[...] = dx.astype(dx_ref.dtype)
    if not own:
        w_ref[...] = weights
        return

    put = functools.partial(put_rows, core, kept_ref, sent_ref)
    dq = dq_ref[...].astype(LOW)
    put(0, dot_tn(dq, a_own_ref[...]))
    put(INNER, weights)
    for part in range(2):
        rows = slice(part * block, (part + 1) * block)
        at = pl.ds(pl.multiple_of(part * mine + core * block, block), block)
        dq_kept_ref[rows, :] = dq_ref[at, :]
        at = pl.ds(pl.multiple_of(part * mine + (1 - core) * block, block), block)
        dq_sent_ref[rows, :] = dq_ref[at, :].astype(LOW)

    flip = (rows_of(TILE, TILE) + lanes_of(TILE, TILE) == TILE - 1).astype(WIDE)
    exact = functools.partial(
        jnp.dot, precision=lax.Precision.HIGHEST, preferred_element_type=WIDE
    )
    head_row = rows_of(8, 1)
    table = jnp.zeros((8, WIDTH2), WIDE)
    for part in range(3):
        sums = jnp.zeros((8, 2 * TILE), WIDE)
        for head in range(HEADS):
            turned = exact(flip, near_out[head, part * TILE : (part + 1) * TILE, :])
            padded = jnp.concatenate([turned, jnp.zeros((TILE, TILE), WIDE)], axis=1)
            skewed = pltpu.roll(padded, 0, 1, stride=1, stride_axis=0)
            sums = jnp.where(head_row == head, jnp.sum(skewed, axis=0, keepdims=True), sums)
        table = table + exact(sums, onehot_ref[part * 2 * TILE : (part + 1) * 2 * TILE, :])
    query_tile = rows_of(chunk // TILE, 1)
    for head in range(HEADS):
        mark = lane - HD * (1 - head % 2)
        inside = (mark >= 8) & (mark < 32)
        kind, tile = mark // 8, mark % 8
        at = (kind - 2) * (chunk // TILE) + tile_place(tile, core)
        relative = at - query_tile
        found = marks_ref[head]
        before = (mark == 0) | (inside & (relative < -1))
        after = (mark == 1) | (inside & (relative > 1))
        for chosen, bucket in ((before, FAR_BEFORE), (after, FAR_AFTER)):
            total = jnp.sum(jnp.where(chosen, found, 0.0))
            table = table + jnp.where((head_row == head) & (lane == bucket), total, 0.0)
    rest_rows = 2 * kept_ref.shape[0] - 3 * INNER
    columns = kept_ref.shape[1]
    small = jnp.concatenate([table, jnp.zeros((8, columns - WIDTH2), WIDE)], axis=1)
    small = jnp.concatenate([small, jnp.zeros((rest_rows - 8, columns), WIDE)], axis=0)
    put(3 * INNER, small)


def chain_kernel(slot, quads, sc_ref, *refs):
    mine, refs = refs[: slot + 1], refs[slot + 1 :]
    up_ref, down_ref = refs[-2:]
    for column, came, out_ref in ((UP, 0, up_ref), (DOWN, 1, down_ref)):
        for index, dx_ref in enumerate(mine):

            @pl.when(sc_ref[slot, column] == index)
            def _():
                value = dx_ref[...]
                if slot > 0:
                    edge = 0 if column == UP else quads - 1
                    came_before = refs[came][...].astype(WIDE)
                    total = value.astype(WIDE) + jnp.where(
                        sc_ref[0, QUAD] != edge, came_before, 0.0
                    )
                    value = total.astype(LOW)
                out_ref[...] = value


def join_kernel(sc_ref, kept_ref, got_ref, out_ref):
    side = sc_ref[0, SIDE]
    out_ref[side] = kept_ref[...]
    out_ref[1 - side] = got_ref[...]


def total_kernel(quads, sc_ref, dx_ref, up_ref, down_ref, out_ref):
    quad = sc_ref[0, QUAD]
    total = dx_ref[...] + jnp.where(quad > 0, up_ref[...].astype(WIDE), 0.0)
    out_ref[...] = total + jnp.where(quad < quads - 1, down_ref[...].astype(WIDE), 0.0)


def input_kernel(
    sc_ref, dx_ref, dq_ref, dq_got_ref, x_ref, grad_res_ref, wq_ref, gain_ref, keep_ref, send_ref
):
    side = sc_ref[0, SIDE]
    block = x_ref.shape[0] // 2
    gain = gain_ref[...]
    for part in range(2):
        rows = slice(part * block, (part + 1) * block)
        queries = (dq_ref[rows, :] + dq_got_ref[rows, :].astype(WIDE)).astype(LOW)
        grad_in = dot_nt(queries, wq_ref[...]) + dx_ref[rows, :]
        x = x_ref[rows, :].astype(WIDE)
        scale = rms_scale(x)
        z = x * scale
        u = grad_in * gain
        result = grad_res_ref[rows, :] + scale * (u - z * jnp.mean(u * z, axis=-1, keepdims=True))
        result = result.astype(LOW)

        @pl.when(side == part)
        def _():
            keep_ref[...] = result

        @pl.when(side != part)
        def _():
            send_ref[...] = result


def tie_kernel(sc_ref, *refs):
    pass


def add_kernel(sc_ref, order_ref, *refs):
    outs = refs[-order_ref.shape[0] :]
    ins = refs[: len(refs) - len(outs)]
    for index, out_ref in enumerate(outs):
        which = order_ref[index]
        total = ins[0][which].astype(WIDE)
        for in_ref in ins[1:]:
            total = total + in_ref[which].astype(WIDE)
        out_ref[...] = total.astype(LOW)


def place_kernel(sc_ref, owner_ref, *refs):
    out_ref = refs[-1]
    for index, part_ref in enumerate(refs[:-1]):
        out_ref[owner_ref[index]] = part_ref[...]


def whole_rows(core, kept_ref, got_ref, first, count):
    half = kept_ref.shape[0]
    parts = []
    for number in range(2):
        low, high = max(first, number * half), min(first + count, (number + 1) * half)
        if low < high:
            rows = slice(low - number * half, high - number * half)
            part = jnp.where(core == number, kept_ref[rows, :], got_ref[rows, :])
            parts.append(part.astype(WIDE))
    return parts[0] if len(parts) == 1 else jnp.concatenate(parts, axis=0)


def unpack_feed_kernel(sc_ref, kept_ref, got_ref, out_ref, gate_ref, up_ref, down_ref, gain_ref):
    take = functools.partial(whole_rows, sc_ref[0, CORE], kept_ref, got_ref)
    width, hidden = gate_ref.shape
    row = 0
    for grads in (gate_ref, up_ref):
        for start in range(0, hidden, width):
            grads[:, start : start + width] = take(row, width)
            row += width
    down_ref[...] = take(row, hidden)
    row += hidden
    out_ref[...] = take(row, INNER)
    row += INNER
    gain_ref[...] = take(row, 16)[0:1, :]


def unpack_last_kernel(
    sc_ref, kept_ref, got_ref, wq_ref, wk_ref, wv_ref, gain_ref, query_ref, key_ref, value_ref, table_ref, gain_grad_ref,
):
    take = functools.partial(whole_rows, sc_ref[0, CORE], kept_ref, got_ref)
    total = jnp.zeros(gain_ref.shape, WIDE)
    for kind, (w_ref, out_ref) in enumerate(
        ((wq_ref, query_ref), (wk_ref, key_ref), (wv_ref, value_ref))
    ):
        grads = take(kind * INNER, INNER)
        out_ref[...] = grads.T
        total = total + jnp.sum(grads * w_ref[...].T.astype(WIDE), axis=0, keepdims=True)
    gain_grad_ref[...] = total / gain_ref[...]
    table_ref[...] = take(3 * INNER, 16)[:HEADS, :BUCKETS]


def staged_sum(kept, sent, between, plan, plan_out, add, place):
    came = [kept, lax.ppermute(sent, "blk", between)]
    after = yield sent
    for axes, size, index, peer, pairs in plan:
        order = jnp.stack([index] + [peer(index, shift) for shift in range(1, size)])
        own, *sends = add(order.astype(jnp.int32), came, after)
        came = [own] + [
            lax.ppermute(part, axes, pairs(shift)) for shift, part in enumerate(sends, 1)
        ]
        after = yield own
    (value,) = add(jnp.zeros((1,), jnp.int32), came, after)
    for axes, size, index, peer, pairs in plan_out:
        came = [lax.ppermute(value, axes, pairs(shift)) for shift in range(1, size)]
        after = yield value
        owners = jnp.stack([index] + [peer(index, -shift) for shift in range(1, size)])
        value = place(owners.astype(jnp.int32), [value] + came, after)
    got = lax.ppermute(value, "blk", between)
    after = yield value
    yield (value, got)


def advance(stages, count, after):
    for _ in range(count):
        tie = stages.send((after,))
    return tie


def finish(stages):
    for now in iter(lambda: stages.send(()), None):
        if isinstance(now, tuple):
            return now


def nearest_order(quads):
    return [
        sorted(range(quads), key=lambda k: (abs(k - place), k)) for place in range(quads)
    ]


def chunk_plan(quads):
    plans = []
    for place in range(quads):
        due = [(quads - 1 + place - d, d) for d in range(place + 1, quads)]
        due += [(quads - 1 - place + d, d) for d in range(place)]
        order = [d for _, d in sorted(due)] + [place]
        rows = []
        for slot in range(quads):
            up, down = quads - 1 + place - slot, place - (quads - 1) + slot
            rows.append(
                (
                    order[slot],
                    order.index(up) if place < up < quads else -1,
                    order.index(down) if 0 <= down < place else -1,
                )
            )
        plans.append(rows)
    return plans


def onehot_tables():
    thresholds = bucket_edges()

    def bucket(offset):
        half_count, exact_count, edges = thresholds
        distance = abs(offset)
        beyond = sum(distance >= edge for edge in edges)
        return (half_count if offset > 0 else 0) + (
            distance if distance < exact_count else exact_count + beyond
        )

    rows = np.zeros((BUCKETS, 2 * TURN), np.float32)
    for turn in range(TURN):
        back = turn if turn < TILE else turn - TURN
        rows[bucket(-TILE - back), turn] = 1.0
        rows[bucket(TILE + back), TURN + turn] = 1.0
    diagonals = np.zeros((6 * TILE, WIDTH2), np.float32)
    for part in range(3):
        for at in range(2 * TILE - 1):
            diagonals[part * 2 * TILE + at, bucket(1 + at - TILE * part)] = 1.0
    return rows, diagonals


def body(
    hidden_in,
    item_lengths,
    live_mask,
    cotangent,
    query_weight,
    key_weight,
    value_weight,
    output_weight,
    bucket_bias_table,
    norm_attention,
    norm_feed,
    gate_weight,
    up_weight,
    down_weight,
):
    streams, block, width = hidden_in.shape
    hidden = gate_weight.shape[1]
    blocks = lax.axis_size("blk")
    parts = lax.axis_size("dp")
    quads = blocks // 4
    here = lax.axis_index("blk")
    replica = lax.axis_index("dp")
    core, side, quad = here % 2, (here // 2) % 2, here // 4
    mine, chunk = 2 * block, 4 * block

    across = [(k, k ^ 2) for k in range(blocks)]
    between = [(k, k ^ 1) for k in range(blocks)]
    onward = []
    for k in range(blocks):
        if k % 2 == 0:
            onward.append((k, k + 4 if k + 4 < blocks else k + 1))
        else:
            onward.append((k, k - 4 if k >= 4 else k - 1))

    order = nearest_order(quads)
    distances = [
        sorted({abs(order[place][step] - place) for place in range(quads)}) for step in range(quads)
    ]
    spots = jnp.asarray(np.array(order, np.int32).T)
    nearest = jnp.asarray(np.array([found[0] for found in distances], np.int32))[:, None]
    is_here = jnp.arange(quads, dtype=jnp.int32)[None, :] == quad
    place = jnp.sum(jnp.where(is_here, spots, 0), axis=1, keepdims=True)
    swapped = ((place > quad) != (core == 1)) & (place != quad)
    source = 2 * (jnp.abs(place - quad) - nearest) + swapped.astype(jnp.int32)
    first_end = jnp.where(side == 0, item_lengths[0, 0], item_lengths[1, 0])
    col = jnp.arange(16, dtype=jnp.int32)[None, :]
    plans = np.array(chunk_plan(quads), np.int32)
    mine_of = [
        jnp.sum(jnp.where(is_here, jnp.asarray(plans[:, :, n].T), 0), axis=1, keepdims=True)
        for n in range(3)
    ]
    sc = jnp.where(col == QUAD, quad, 0)
    sc = jnp.where(col == CORE, core, sc)
    sc = jnp.where(col == SIDE, side, sc)
    sc = jnp.where(col == PLACE, place, sc)
    sc = jnp.where(col == SOURCE, source, sc)
    for at, values in zip((CHUNK, UP, DOWN), mine_of):
        sc = jnp.where(col == at, values, sc)
    sc = jnp.where(col == FIRST_END, first_end, sc).astype(jnp.int32)

    turned_onehot, diagonal_onehot = (jnp.asarray(t) for t in onehot_tables())

    smem = pl.BlockSpec(memory_space=pltpu.SMEM)
    vmem = pl.BlockSpec(memory_space=pltpu.VMEM)
    anywhere = pl.BlockSpec(memory_space=pl.ANY)
    shape = jax.ShapeDtypeStruct
    strip_rows_count = 2 * chunk - TILE
    near_shape = pltpu.VMEM((HEADS, NEAR, TILE), WIDE)
    strip_shape = pltpu.VMEM((HEADS, strip_rows_count, TILE), WIDE)
    gen_shape = pltpu.VMEM((chunk, mine), WIDE)
    dma = pltpu.SemaphoreType.DMA
    pairs_in_chunk = mine * chunk * HEADS

    def call(kernel, name, in_specs, out_specs, out_shape, scratch, operands, grid=(1,), aliases=None, us=5.0, after=(), limit=24):
        count = 1 + len(operands)

        def without_ties(*refs):
            kernel(*refs[:count], *refs[count + len(after) :])

        return pl.pallas_call(
            without_ties if after else kernel,
            grid_spec=pltpu.PrefetchScalarGridSpec(
                num_scalar_prefetch=1,
                grid=grid,
                in_specs=list(in_specs) + [anywhere] * len(after),
                out_specs=out_specs,
                scratch_shapes=scratch,
            ),
            out_shape=out_shape,
            input_output_aliases=aliases or {},
            compiler_params=pltpu.CompilerParams(vmem_limit_bytes=limit * 1024 * 1024),
            cost_estimate=pl.CostEstimate(
                flops=int(us * (1e9 if us >= 4 else 1e7)), bytes_accessed=1 << 12, transcendentals=0
            ),
            name=name,
        )(sc, *operands, *after)

    def far_away(array):
        return pltpu.with_memory_space_constraint(array, pltpu.HBM)

    def tied(arrays, after):
        count = len(arrays)
        return call(
            tie_kernel, "tie", [anywhere] * count, (anywhere,) * count,
            tuple(shape(a.shape, a.dtype) for a in arrays), [], arrays,
            aliases={1 + n: n for n in range(count)}, us=0.3, after=after, limit=16,
        )

    def pick(both, index):
        return lax.dynamic_index_in_dim(both, index, 0, False)

    live_rows = jnp.pad(live_mask.astype(LOW)[:, None, :], ((0, 0), (0, 15), (0, width - block)))
    payload = jnp.concatenate([pick(hidden_in, 1 - side), pick(live_rows, 1 - side)], axis=0)
    got = lax.ppermute(payload, "blk", across)
    packed, x_low, rowk, rowq, vec = call(
        norm_kernel, "norm_rows", [smem] + [vmem] * 6, (vmem,) * 5,
        (
            shape((mine + 16, width), LOW), pltpu.HBM((mine, width), LOW), shape((8, chunk), WIDE),
            shape((8, mine), WIDE), shape((8, 2 * TURN), WIDE),
        ), [],
        (item_lengths, hidden_in, live_mask, got, norm_attention[None, :], bucket_bias_table, turned_onehot),
        us=2.0, limit=56,
    )
    own_chunk = jnp.concatenate([packed, lax.ppermute(packed, "blk", between)], axis=0)
    cot_got = lax.ppermute(pick(cotangent, 1 - side), "blk", across)

    qkv_shape = pltpu.HBM((quads * chunk, 3 * INNER), LOW)
    ext_shape = pltpu.HBM((quads * chunk, WIDTH2), LOW)
    state_shapes = (shape((INNER, mine), WIDE), shape((16, mine), WIDE))

    def chunk_out(step, columns):
        return pl.BlockSpec((chunk, columns), lambda i, sc: (sc[step, PLACE], 0))

    a_shape = pltpu.HBM((quads * chunk, width), LOW)
    chunk_scratch = [pltpu.VMEM((2, 16, width), LOW)]
    held = lax.ppermute(own_chunk, "blk", onward)
    qkv, ext, normed, qx, acc, ml = call(
        forward_own_kernel, "attend_own", [smem, anywhere] + [vmem] * 6,
        (chunk_out(0, 3 * INNER), chunk_out(0, WIDTH2), chunk_out(0, width), vmem, vmem, vmem),
        (qkv_shape, ext_shape, a_shape, shape((HEADS, 2 * WIDTH2, mine), LOW)) + state_shapes,
        chunk_scratch + [strip_shape, near_shape, gen_shape, dma((6,))],
        (bucket_bias_table, own_chunk, key_weight, value_weight, query_weight, vec, rowq, rowk),
        us=12.0,
    )

    came = []
    for step in range(1, quads):
        held, acc = lax.optimization_barrier((held, acc))
        came.append((held, lax.ppermute(held, "blk", between)))
        if step + 1 < quads:
            held = lax.ppermute(held, "blk", onward)
        arrays = [array for distance in distances[step] for array in came[distance - 1]]
        qkv, ext, normed, acc, ml = call(
            functools.partial(forward_kernel, step, len(arrays)), "attend_other",
            [smem] + [vmem] * 7 + [anywhere] * (3 + len(arrays)),
            (chunk_out(step, 3 * INNER), chunk_out(step, WIDTH2), chunk_out(step, width), vmem, vmem),
            (qkv_shape, ext_shape, a_shape) + state_shapes,
            chunk_scratch + [near_shape, dma((6,))],
            (bucket_bias_table, key_weight, value_weight, query_weight, vec, qx, acc, ml, qkv, ext, normed, *arrays),
            aliases={7: 3, 8: 4, 9: 0, 10: 1, 11: 2}, us=10.0,
        )

    (do_mine, out_kept, out_sent, grad_res, act, feed, grad_gate, grad_up,
     context, branch, gain_grad, cot) = call(
        middle_kernel, "feed_both_ways", [vmem] * 11, (vmem,) * 12,
        (
            shape((mine, INNER + WIDTH2), LOW),
            shape((block, width), LOW), shape((block, width), LOW), pltpu.HBM((mine, width), WIDE),
            shape((mine, hidden), LOW), shape((mine, width), LOW), shape((mine, hidden), LOW),
            shape((mine, hidden), LOW), shape((mine, INNER), LOW), shape((mine, width), LOW),
            shape((8, width), WIDE), shape((mine, width), LOW),
        ), [],
        (
            acc, ml, x_low, cotangent, cot_got, rowq, output_weight, gate_weight, up_weight, down_weight,
            norm_feed[None, :],
        ),
        us=12.0,
    )
    do_other = lax.ppermute(do_mine, "blk", between)
    do_chunk = jnp.concatenate([do_mine, do_other], axis=0)

    def joined(kept, got, after):
        return call(
            join_kernel, "join", [vmem] * 2, vmem, shape((2, block, width), LOW), [], (kept, got),
            us=1.0, after=after, limit=16,
        )

    def over_blocks(shift):
        return [(k, (k + 4 * shift) % blocks) for k in range(blocks)]

    over_side = ("blk", 2, side, lambda i, s: i ^ 1, lambda s: across)
    over_parts = (
        "dp", parts, replica, lambda i, s: (i + s) % parts,
        lambda s: [(k, (k + s) % parts) for k in range(parts)],
    )
    over_quads = ("blk", quads, quad, lambda i, s: (i + s) % quads, over_blocks)
    if parts == 2:

        def square_pairs(shift):
            pairs = []
            for k in range(blocks):
                for r in range(parts):
                    k2, r2 = k ^ (2 * (shift >> 1)), r ^ (shift & 1)
                    pairs.append((k * parts + r, k2 * parts + r2))
            return pairs

        over_square = (("blk", "dp"), 4, side * 2 + replica, lambda i, s: i ^ abs(s), square_pairs)
        plan = [over_square, over_quads]
    else:
        plan = [over_side, over_parts, over_quads]
    plan_out = plan[::-1]
    groups = len(plan) - 1
    pieces_in_all = 8 * 2 * 2 * parts * quads

    def padded(rows):
        return -(-rows // pieces_in_all) * pieces_in_all

    feed_rows = padded(3 * hidden + INNER + 8) // 2
    feed_kept, feed_sent = call(
        feed_grads_kernel, "feed_weight_grads", [vmem] * 8, (vmem, vmem),
        (shape((feed_rows, width), LOW),) * 2, [],
        (act, feed, grad_gate, grad_up, context, branch, cot, gain_grad), us=7.0, after=(do_chunk,),
    )
    def add_parts(order, arrays, after):
        size = order.shape[0]
        split = [a.reshape((size, a.shape[0] // size, a.shape[1])) for a in arrays]
        return call(
            add_kernel, "add_parts", [smem] + [vmem] * len(split), (vmem,) * size,
            (shape(split[0].shape[1:], LOW),) * size, [], (order, *split), us=2.0, after=after, limit=16,
        )

    def place_parts(owners, arrays, after):
        one = arrays[0].shape
        whole = call(
            place_kernel, "place_parts", [smem] + [vmem] * len(arrays), vmem,
            shape((len(arrays),) + one, LOW), [], (owners, *arrays), us=1.0, after=after, limit=16,
        )
        return whole.reshape((-1,) + one[1:])

    feed_stages = staged_sum(feed_kept, feed_sent, between, plan, plan_out, add_parts, place_parts)
    next(feed_stages)
    out_got = lax.ppermute(out_sent, "blk", across)
    ties = [do_chunk, feed_stages.send((do_chunk,))]

    qkv, ext, normed = far_away(qkv), far_away(ext), far_away(normed)
    upward = [(k, k + 4) for k in range(blocks - 4)]
    downward = [(k + 4, k) for k in range(blocks - 4)]
    last_rows = padded(3 * INNER + 8) // 2
    state_shape = (
        shape((chunk, INNER), WIDE), shape((2 * INNER, width), WIDE), shape((HEADS, NEAR, TILE), WIDE),
        shape((HEADS, chunk // TILE, WIDTH2), WIDE),
    )

    def chunk_rows(slot, n, columns):
        return pl.BlockSpec(
            (block, columns), lambda i, sc: (4 * sc[slot, CHUNK] + sc[0, CORE] + 2 * n, 0)
        )

    state, gradients, came = (), [], ()
    for slot in range(quads):
        own = slot == quads - 1
        operands = (
            bucket_bias_table, do_chunk, qkv, qkv, qkv, normed, normed, ext, ext, key_weight, value_weight, vec,
        ) + tuple(state)
        in_specs = [
            smem, anywhere, pl.BlockSpec((chunk, INNER), lambda i, sc: (sc[0, QUAD], 2)),
            chunk_rows(slot, 0, 2 * INNER), chunk_rows(slot, 1, 2 * INNER),
            chunk_rows(slot, 0, width), chunk_rows(slot, 1, width),
            chunk_rows(slot, 0, WIDTH2), chunk_rows(slot, 1, WIDTH2), vmem, vmem, vmem,
        ] + [vmem] * len(state)
        scratch = [
            pltpu.VMEM((chunk, INNER + WIDTH2), LOW), near_shape, pltpu.VMEM((2, chunk + 2 * TILE, mine), LOW),
            pltpu.VMEM((2 * INNER, mine), LOW), dma((4,)),
        ]
        outs = (shape((mine, width), WIDE if own else LOW),)
        if own:
            operands += (ext, rowq, normed, diagonal_onehot)
            in_specs += [
                pl.BlockSpec((chunk, WIDTH2), lambda i, sc: (sc[0, QUAD], 0)), vmem,
                pl.BlockSpec((chunk, width), lambda i, sc: (sc[0, QUAD], 0)), vmem,
            ]
            outs += (shape((last_rows, width), LOW),) * 2
            outs += (shape((mine, INNER), WIDE), shape((mine, INNER), LOW))
            scratch = [
                pltpu.VMEM(s.shape, s.dtype) for s in state_shape
            ] + [strip_shape, gen_shape] + scratch
        else:
            outs += state_shape
        found = call(
            functools.partial(chunk_kernel, slot, own), "grad_chunk", in_specs, (vmem,) * len(outs), outs, scratch,
            operands, us=10.0, after=ties, limit=32 if own else 28,
            aliases={13 + n: 1 + n for n in range(4)} if slot and not own else None,
        )
        gradients.append(found[0])
        if own:
            kept, sent, dq_kept, dq_sent = found[1:]
            break
        state = found[1:]
        up, down = call(
            functools.partial(chain_kernel, slot, quads), "chain", [vmem] * (len(gradients) + len(came)), (vmem,) * 2,
            (shape((mine, width), LOW),) * 2, [], tuple(gradients) + tuple(came), us=1.0, limit=16,
        )
        came = (lax.ppermute(up, "blk", upward), lax.ppermute(down, "blk", downward))
        ties = [up]
        if slot < 3:
            ties.append(advance(feed_stages, 1 if slot == 1 else groups, up))
        if slot == 0:
            ties.append(out_got)
    total = call(
        functools.partial(total_kernel, quads), "total", [vmem] * 3, vmem, shape((mine, width), WIDE), [],
        (gradients[-1], *came), us=1.0, after=(kept,), limit=16,
    )
    tie = advance(feed_stages, 1, total)
    sent, dq_sent = tied((sent, dq_sent), (tie,))
    last_stages = staged_sum(kept, sent, between, plan, plan_out, add_parts, place_parts)
    next(last_stages)
    dq_got = lax.ppermute(dq_sent, "blk", between)
    feed_kept, feed_got = feed_stages.send(())
    tie = advance(last_stages, 1, tie)
    in_kept, in_sent = call(
        input_kernel, "grad_input", [vmem] * 7, (vmem,) * 2,
        (shape((block, width), LOW), shape((block, width), LOW)), [],
        (total, dq_kept, dq_got, x_low, grad_res, query_weight, norm_attention[None, :]),
        us=2.0, after=(tie,),
    )
    grad_out, grad_gate, grad_up, grad_down, grad_norm_feed = call(
        unpack_feed_kernel, "unpack_feed", [vmem] * 2, (vmem,) * 5,
        (
            shape((INNER, width), WIDE), shape((width, hidden), WIDE), shape((width, hidden), WIDE),
            shape((hidden, width), WIDE), shape((1, width), WIDE),
        ), [],
        (feed_kept, feed_got), us=3.9, after=(in_kept,),
    )
    output = joined(out_kept, out_got, (grad_norm_feed,))
    for _ in range(groups):
        tie = last_stages.send((output,))
    (in_sent,) = tied((in_sent,), (tie,))
    in_got = lax.ppermute(in_sent, "blk", across)
    tie = last_stages.send(())
    input_gradient = joined(in_kept, in_got, (tie,))
    for _ in range(groups):
        tie = last_stages.send((input_gradient,))
    last_stages.send(())
    last_kept, last_got = finish(last_stages)
    grad_query, grad_key, grad_value, grad_table, grad_norm_attention = call(
        unpack_last_kernel, "unpack_attention", [vmem] * 6, (vmem,) * 5,
        (shape((width, INNER), WIDE),) * 3 + (shape((HEADS, BUCKETS), WIDE), shape((1, width), WIDE)), [],
        (last_kept, last_got, query_weight, key_weight, value_weight, norm_attention[None, :]), us=2.0,
    )
    return (
        output,
        input_gradient,
        grad_query,
        grad_key,
        grad_value,
        grad_out,
        grad_table.T,
        grad_norm_attention[0],
        grad_norm_feed[0],
        grad_gate,
        grad_up,
        grad_down,
    )


def solution(mesh):
    return jax.shard_map(
        body,
        mesh=mesh,
        in_specs=(
            P("dp", "blk", None),
            P("dp", None),
            P("dp", "blk"),
            P("dp", "blk", None),
            P(),
            P(),
            P(),
            P(),
            P(),
            P(),
            P(),
            P(),
            P(),
            P(),
        ),
        out_specs=(
            P("dp", "blk", None),
            P("dp", "blk", None),
            P(),
            P(),
            P(),
            P(),
            P(),
            P(),
            P(),
            P(),
            P(),
            P(),
        ),
        check_vma=False,
    )
```

```python
import functools

import jax
import jax.numpy as jnp
import numpy as np
from jax import lax
from jax.experimental import pallas as pl
from jax.experimental.pallas import tpu as pltpu
from jax.sharding import PartitionSpec as P

HEADS = 6
HD = 64
WIDTH2 = 2 * HD
PAIRS = HEADS // 2
INNER = HEADS * HD
BUCKETS = 32
MAXDIST = 128
EPSILON = 1e-06
BIG = 1e30
TILE = 128
NEAR = 3 * TILE
TURN = 4 * TILE
FAR_BEFORE = BUCKETS // 2 - 1
FAR_AFTER = BUCKETS - 1
LOW = jnp.bfloat16
WIDE = jnp.float32
GELU_A = 0.7978845608028654
GELU_B = 0.044715

QUAD, CORE, SIDE, PLACE, SOURCE, FIRST_END, CHUNK, UP, DOWN = range(9)
MASK, BEFORE, AFTER, PEN, STAT, LIVE, SEG = 0, 1, 2, 7, 8, 11, 12
ONE_A, OFF, ONE_B, ONE_C, ONE_D = 36, 37, 38, 39, 40


def bucket_edges():
    half_count = BUCKETS // 2
    exact_count = half_count // 2
    log_levels = half_count - exact_count
    thresholds = []
    for level_index in range(1, log_levels):
        candidate = exact_count
        while (
            candidate**log_levels * exact_count**level_index
            < MAXDIST**level_index * exact_count**log_levels
        ):
            candidate = candidate + 1
        thresholds.append(candidate)
    return (half_count, exact_count, thresholds)


def dot_nt(left, right):
    return lax.dot_general(
        left, right, (((1,), (1,)), ((), ())), preferred_element_type=WIDE
    )


def dot_nn(left, right):
    return jnp.dot(left, right, preferred_element_type=WIDE)


def dot_tn(left, right):
    return lax.dot_general(
        left, right, (((0,), (0,)), ((), ())), preferred_element_type=WIDE
    )


def rows_of(count, width):
    return lax.broadcasted_iota(jnp.int32, (count, width), 0)


def lanes_of(count, width):
    return lax.broadcasted_iota(jnp.int32, (count, width), 1)


def lane_half(array, half, other):
    return jnp.where(lanes_of(1, WIDTH2) // HD == half, array, other)


def row_half(array, half, other):
    return jnp.where(rows_of(WIDTH2, 1) // HD == half, array, other)


def pair_slice(pair, base=0):
    return slice(base + pair * WIDTH2, base + (pair + 1) * WIDTH2)


def tile_place(tile, core):
    return (tile // 2) * 4 + core * 2 + tile % 2


def rms_scale(values):
    return lax.rsqrt(jnp.mean(values * values, axis=-1, keepdims=True) + EPSILON)


def three_pieces(values):
    high = values.astype(LOW).astype(WIDE)
    mid = (values - high).astype(LOW).astype(WIDE)
    low = (values - high - mid).astype(LOW).astype(WIDE)
    return high, mid, low


def pipelined(items, first, second, depth):
    ahead = []
    for item in items:
        ahead.append((item, first(item)))
        if len(ahead) > depth:
            second(*ahead.pop(0))
    for waiting in ahead:
        second(*waiting)


def far_bias(table_ref, after, head):
    return table_ref[FAR_AFTER if after else FAR_BEFORE, head]


def build_near(near_ref, vec_ref, back, heads):
    for index, head in enumerate(heads):
        row = vec_ref[head : head + 1, back * TURN : (back + 1) * TURN]
        row = jnp.broadcast_to(row, (NEAR, TURN))
        near_ref[index] = pltpu.roll(row, 0, 1, stride=1, stride_axis=0)[:, :TILE]


def build_strip(strip_ref, near_ref, table_ref, back, chunk, heads):
    edge = chunk - TILE
    rest = strip_ref.shape[1] - edge - 2 * TILE
    for index, head in enumerate(heads):
        far_before = far_bias(table_ref, back, head)
        far_after = far_bias(table_ref, not back, head)
        strip_ref[index, : edge - TILE, :] = jnp.full((edge - TILE, TILE), far_before, WIDE)
        strip_ref[index, edge - TILE : edge + 2 * TILE, :] = near_ref[index]
        strip_ref[index, edge + 2 * TILE :, :] = jnp.full((rest, TILE), far_after, WIDE)


def strip_rows(strip_ref, index, first_tile, tiles, core, chunk):
    parts = []
    for tile in range(first_tile, first_tile + tiles):
        start = (chunk - TILE) - tile_place(tile, core) * TILE
        parts.append(strip_ref[index, pl.ds(pl.multiple_of(start, TILE), chunk), :])
    return jnp.concatenate(parts, axis=1)


def near_fixes(near_ref, table_ref, flags, index, head, back):
    low, high = flags
    return (
        low * (near_ref[index, :TILE, :] - far_bias(table_ref, back, head)),
        high * (near_ref[index, 2 * TILE :, :] - far_bias(table_ref, not back, head)),
    )


def fix_near(scores, step, steps, fixes):
    low, high = fixes
    chunk, width = scores.shape
    if step == 0:
        last = jnp.concatenate(
            [scores[chunk - TILE :, :TILE] + low, scores[chunk - TILE :, TILE:]], axis=1
        )
        scores = jnp.concatenate([scores[: chunk - TILE], last], axis=0)
    if step == steps - 1:
        first = jnp.concatenate(
            [scores[:TILE, : width - TILE], scores[:TILE, width - TILE :] + high], axis=1
        )
        scores = jnp.concatenate([first, scores[TILE:]], axis=0)
    return scores


def near_flags(place, quad, core):
    low = jnp.where((place == quad - 1) & (core == 0), 1.0, 0.0)
    high = jnp.where((place == quad + 1) & (core == 1), 1.0, 0.0)
    return low, high


def natural_row(even, odd):
    block = even.shape[1] // 2
    return jnp.concatenate(
        [even[:, :block], odd[:, :block], even[:, block:], odd[:, block:]], axis=1
    )


def key_columns(rows, lanes):
    places = rows[0].shape[1]
    stack = jnp.zeros((16, places), WIDE)
    spread = jnp.zeros((16, WIDTH2), WIDE)
    number, lane = rows_of(16, 1), lanes_of(16, WIDTH2)
    for index, row in enumerate(rows):
        stack = jnp.where(number == index, row, stack)
    for index, at, scale in lanes:
        spread = jnp.where((number == index) & (lane == at), scale, spread)
    return dot_tn(stack.astype(LOW), spread.astype(LOW))


def visible_mask(gen_ref, segment_column, segment_row, live, core, keys_down):
    chunk, mine = gen_ref.shape
    down = rows_of(chunk, 1)
    for tile in range(mine // TILE):
        lanes = slice(tile * TILE, (tile + 1) * TILE)
        across = tile_place(tile, core) * TILE + lanes_of(1, TILE)
        alive = live if keys_down else live[:, lanes]
        visible = (segment_column == segment_row[:, lanes]) & ((alive > 0.5) | (down == across))
        gen_ref[:, lanes] = jnp.where(visible, 0.0, -BIG)


def project(a, weight_refs, qkv_ref):
    for part, w_ref in enumerate(weight_refs):
        cols = slice(part * INNER, (part + 1) * INNER)
        qkv_ref[:, cols] = dot_nn(a, w_ref[...]).astype(LOW)


def halves_copies(source, swapped, core, rows_ref, live_ref, sems):
    first_core = 1 - core if swapped else core
    block = rows_ref.shape[0] // 4
    half = source.shape[0] // 2
    copies = []
    for index in range(2):
        owner = first_core if index == 0 else 1 - first_core
        for part in range(2):
            at = pl.multiple_of(part * 2 * block + owner * block, block)
            copies.append((source.at[pl.ds(index * half + part * block, block), :], rows_ref.at[pl.ds(at, block), :]))
        if live_ref is not None:
            copies.append((source.at[pl.ds(index * half + 2 * block, 16), :], live_ref.at[owner]))
    return [
        pltpu.make_async_copy(start, end, sems.at[index]) for index, (start, end) in enumerate(copies)
    ]


def start_fetch(sc_ref, step, sources, rows_ref, live_ref, sems):
    core = sc_ref[0, CORE]
    for index, source in enumerate(sources):

        @pl.when(sc_ref[step, SOURCE] == index)
        def _():
            for copy in halves_copies(source, index % 2 == 1, core, rows_ref, live_ref, sems):
                copy.start()


def wait_fetch(sc_ref, sources, rows_ref, live_ref, sems):
    for copy in halves_copies(sources[0], False, sc_ref[0, CORE], rows_ref, live_ref, sems):
        copy.wait()


def norm_kernel(
    sc_ref, lengths_ref, hidden_ref, live_ref, got_ref, gain_ref, table_ref, onehot_ref,
    packed_ref, x_ref, rowk_ref, rowq_ref, vec_ref,
):
    side, core, quad = sc_ref[0, SIDE], sc_ref[0, CORE], sc_ref[0, QUAD]
    block = hidden_ref.shape[1]
    mine, chunk = 2 * block, 4 * block
    kept, got = hidden_ref[side], got_ref[:block, :]
    live_kept = live_ref[pl.ds(side, 1), :].astype(WIDE)
    live_got = got_ref[block : block + 16, :block].astype(WIDE)[0:1, :]
    for part in range(2):
        rows = jnp.where(side == part, kept, got)
        x_ref[part * block : (part + 1) * block, :] = rows
        wide = rows.astype(WIDE)
        normed = wide * rms_scale(wide) * gain_ref[...]
        packed_ref[part * block : (part + 1) * block, :] = normed.astype(LOW)
    live = jnp.concatenate(
        [jnp.where(side == 0, live_kept, live_got), jnp.where(side == 0, live_got, live_kept)],
        axis=1,
    )
    packed_ref[mine:, :] = jnp.broadcast_to(live, (16, mine)).astype(LOW)

    places = quad * chunk + lanes_of(1, chunk)

    def one_item(item, carry):
        end, segment = carry
        end = end + lengths_ref[side, item]
        return end, segment + jnp.where(places >= end, 1.0, 0.0)

    zero = jnp.zeros((1, chunk), WIDE)
    end, segment = lax.fori_loop(0, lengths_ref.shape[1], one_item, (jnp.int32(0), zero))
    rowk_ref[...] = jnp.broadcast_to(segment, (8, chunk))
    own = jnp.concatenate(
        [
            rowk_ref[0:1, pl.ds(pl.multiple_of(part * mine + core * block, block), block)]
            for part in range(2)
        ],
        axis=1,
    )
    number = rows_of(8, 1)
    rowq = jnp.where(number == 0, own, 0.0)
    rowq = jnp.where(number == 2, jnp.where(own > 0.5, BIG, 0.0), rowq)
    rowq = jnp.where(number == 3, live, rowq)
    off = jnp.where((live > 0.5) & (own < 0.5), 0.0, -BIG)
    rowq_ref[...] = jnp.where(number == 4, off, rowq)
    found = lax.dot_general(
        table_ref[...], onehot_ref[...], (((0,), (0,)), ((), ())),
        precision=lax.Precision.HIGHEST, preferred_element_type=WIDE,
    )
    vec_ref[...] = jnp.concatenate([found, jnp.zeros((8 - HEADS, found.shape[1]), WIDE)], axis=0)


def forward_items(mine):
    steps = mine // (2 * TILE)
    return [(pair, step, hh) for pair in range(PAIRS) for step in range(steps) for hh in range(2)]


def forward_operands(qkv_ref, ext):
    made = {}

    def operands(pair):
        if pair not in made:
            k_ext = jnp.concatenate([qkv_ref[:, pair_slice(pair)], ext], axis=1)
            v_turned = qkv_ref[:, pair_slice(pair, INNER)].T
            made[pair] = (
                k_ext, [row_half(v_turned, hh, jnp.ones_like(v_turned)) for hh in range(2)]
            )
        return made[pair]

    return operands


def step_lanes(step):
    return slice(step * 2 * TILE, (step + 1) * 2 * TILE)


def head_rows(head):
    return slice(head * HD, (head + 1) * HD)


def forward_own_kernel(
    sc_ref, table_ref, source_ref, wk_ref, wv_ref, wq_ref, vec_ref, rowq_ref, rowk_ref,
    qkv_ref, ext_ref, a_ref, qx_ref, acc_ref, ml_ref, q_own_ref,
    live_ref, strip_ref, near_ref, gen_ref, sems,
):
    core = sc_ref[0, CORE]
    chunk = qkv_ref.shape[0]
    mine = acc_ref.shape[1]
    block = mine // 2
    start_fetch(sc_ref, 0, [source_ref], a_ref, live_ref, sems)
    build_near(near_ref, vec_ref, 0, range(HEADS))
    build_strip(strip_ref, near_ref, table_ref, False, chunk, range(HEADS))
    number = rows_of(WIDTH2, 1)
    for head in range(HEADS):
        rows = jnp.where(number == MASK, 1.0, 0.0)
        for which, after in ((BEFORE, False), (AFTER, True)):
            far = jnp.full((1, mine), far_bias(table_ref, after, head), WIDE)
            for piece, value in enumerate(three_pieces(far)):
                rows = jnp.where(number == which + 2 * piece, value, rows)
        rows = jnp.where(number == PEN, -rowq_ref[2:3, :], rows)
        qx_ref[head, WIDTH2:, :] = rows.astype(LOW)
    wait_fetch(sc_ref, [source_ref], a_ref, live_ref, sems)
    project(a_ref[...], (wk_ref, wv_ref, wq_ref), qkv_ref)
    q_own_ref[...] = qkv_ref[:, 2 * INNER :]
    live = natural_row(live_ref[0].astype(WIDE)[0:1, :], live_ref[1].astype(WIDE)[0:1, :])
    columns = key_columns(
        [jnp.ones_like(live), live, rowk_ref[0:1, :]],
        [(0, STAT, 1.0), (0, STAT + 1, 1.0), (0, STAT + 2, 1.0), (1, LIVE, 1.0), (2, SEG, 1.0)],
    )
    ext_ref[...] = columns.astype(LOW)
    visible_mask(
        gen_ref, columns[:, SEG : SEG + 1], rowq_ref[0:1, :], columns[:, LIVE : LIVE + 1], core, True
    )
    for part in range(2):
        at = pl.ds(pl.multiple_of(part * mine + core * block, block), block)
        lanes = slice(part * block, (part + 1) * block)
        for pair in range(PAIRS):
            turned = qkv_ref[at, pair_slice(pair, 2 * INNER)].T
            for hh in range(2):
                qx_ref[2 * pair + hh, :WIDTH2, lanes] = row_half(
                    turned, hh, jnp.zeros_like(turned)
                )
    ml_ref[...] = jnp.zeros_like(ml_ref)
    operands = forward_operands(qkv_ref, ext_ref[...])

    def first(item):
        pair, step, hh = item
        s = dot_nn(operands(pair)[0], qx_ref[2 * pair + hh, :, step_lanes(step)])
        s = s + strip_rows(strip_ref, 2 * pair + hh, 2 * step, 2, core, chunk)
        return s + gen_ref[:, step_lanes(step)]

    def second(item, s):
        pair, step, hh = item
        head, lanes = 2 * pair + hh, step_lanes(step)
        top = jnp.max(s, axis=0, keepdims=True)
        p = jnp.exp(s - top).astype(LOW)
        pv = dot_nn(operands(pair)[1][hh], p)
        ml_ref[head : head + 1, lanes] = top
        ml_ref[8 + head : 9 + head, lanes] = pv[HD * (1 - hh) : HD * (1 - hh) + 1, :]
        acc_ref[head_rows(head), lanes] = pv[hh * HD : (hh + 1) * HD, :]

    pipelined(forward_items(mine), first, second, 2)


def forward_kernel(
    step_number, sources, sc_ref, table_ref, wk_ref, wv_ref, wq_ref, vec_ref, qx_ref, acc_in, ml_in,
    qkv_in, ext_in, a_in, *rest,
):
    source_refs, rest = rest[:sources], rest[sources:]
    qkv_ref, ext_ref, a_ref, acc_ref, ml_ref, live_ref, near_ref, sems = rest
    quad, core, place = (sc_ref[step_number, i] for i in (QUAD, CORE, PLACE))
    chunk = qkv_ref.shape[0]
    mine = acc_ref.shape[1]
    start_fetch(sc_ref, step_number, source_refs, a_ref, live_ref, sems)
    build_near(near_ref, vec_ref, 0, range(HEADS))
    wait_fetch(sc_ref, source_refs, a_ref, live_ref, sems)
    project(a_ref[...], (wk_ref, wv_ref, wq_ref), qkv_ref)
    live = natural_row(live_ref[0].astype(WIDE)[0:1, :], live_ref[1].astype(WIDE)[0:1, :])
    places = place * chunk + lanes_of(1, chunk)
    seen = (live > 0.5) & (places < sc_ref[step_number, FIRST_END])
    is_before = jnp.where(place < quad, 1.0, 0.0)
    is_after = 1.0 - is_before
    marks = [(0, MASK, 1.0), (1, PEN, 1.0)]
    marks += [(1, STAT + n, 1.0) for n in range(3)]
    marks += [(1, BEFORE + 2 * n, is_before) for n in range(3)]
    marks += [(1, AFTER + 2 * n, is_after) for n in range(3)]
    ext = key_columns([jnp.where(seen, 0.0, -BIG), jnp.ones_like(live)], marks).astype(LOW)
    ext_ref[...] = ext
    flags = near_flags(place, quad, core)
    steps = mine // (2 * TILE)
    operands = forward_operands(qkv_ref, ext)

    def first(item):
        pair, step, hh = item
        head = 2 * pair + hh
        s = dot_nn(operands(pair)[0], qx_ref[head, :, step_lanes(step)])
        return fix_near(s, step, steps, near_fixes(near_ref, table_ref, flags, head, head, False))

    def second(item, s):
        pair, step, hh = item
        head, lanes = 2 * pair + hh, step_lanes(step)
        old = ml_in[head : head + 1, lanes]
        top = jnp.maximum(old, jnp.max(s, axis=0, keepdims=True))
        keep = jnp.exp(old - top)
        p = jnp.exp(s - top).astype(LOW)
        pv = dot_nn(operands(pair)[1][hh], p)
        ml_ref[head : head + 1, lanes] = top
        total = ml_in[8 + head : 9 + head, lanes] * keep
        ml_ref[8 + head : 9 + head, lanes] = total + pv[HD * (1 - hh) : HD * (1 - hh) + 1, :]
        rows = head_rows(head)
        acc_ref[rows, lanes] = acc_in[rows, lanes] * keep + pv[hh * HD : (hh + 1) * HD, :]

    pipelined(forward_items(mine), first, second, 2)


def middle_kernel(
    sc_ref, acc_ref, ml_ref, x_ref, cot_in, cot_got, rowq_ref, wo_ref, gate_ref, up_ref, down_ref, gain_ref,
    do_ref, keep_ref, send_ref, grad_res_ref, act_ref, feed_ref, gg_ref, gu_ref,
    ctx_ref, branch_ref, gain_grad_ref, cot_ref,
):
    side = sc_ref[0, SIDE]
    mine = x_ref.shape[0]
    block = mine // 2
    gain = gain_ref[...]
    context = []
    for head in range(HEADS):
        context.append(acc_ref[head_rows(head), :] / ml_ref[8 + head : 9 + head, :])
    for pair in range(PAIRS):
        both = jnp.concatenate(context[2 * pair : 2 * pair + 2], axis=0).astype(LOW)
        ctx_ref[:, pair_slice(pair)] = both.T
    gain_grad = jnp.zeros_like(gain)
    cot_kept = cot_in[side]
    for part in range(2):
        rows = slice(part * block, (part + 1) * block)
        cot_ref[rows, :] = jnp.where(side == part, cot_kept, cot_got[...])

    def first(part):
        rows = slice(part * block, (part + 1) * block)
        residual = x_ref[rows, :].astype(WIDE) + dot_nn(ctx_ref[rows, :], wo_ref[...])
        scale = rms_scale(residual)
        z = residual * scale
        feed = (z * gain).astype(LOW)
        feed_ref[rows, :] = feed
        v = dot_nn(feed, gate_ref[...])
        up = dot_nn(feed, up_ref[...])
        return residual, scale, z, v, up, dot_nt(cot_ref[rows, :], down_ref[...])

    def second(part, made):
        nonlocal gain_grad
        residual, scale, z, v, up, grad_hidden = made
        rows = slice(part * block, (part + 1) * block)
        square = v * v
        t = jnp.tanh(GELU_A * v * (1.0 + GELU_B * square))
        half = 0.5 * (1.0 + t)
        g = v * half
        slope = half + 0.5 * v * (1.0 - t * t) * (GELU_A * (1.0 + 3.0 * GELU_B * square))
        act = (g * up).astype(LOW)
        act_ref[rows, :] = act
        grad_gate = (grad_hidden * up * slope).astype(LOW)
        grad_up = (grad_hidden * g).astype(LOW)
        gg_ref[rows, :] = grad_gate
        gu_ref[rows, :] = grad_up
        grad_feed = dot_nt(grad_gate, gate_ref[...]) + dot_nt(grad_up, up_ref[...])
        u = grad_feed * gain
        gain_grad = gain_grad + jnp.sum(grad_feed * z, axis=0, keepdims=True)
        cot = cot_ref[rows, :].astype(WIDE)
        grad_res = cot + scale * (u - z * jnp.mean(u * z, axis=-1, keepdims=True))
        grad_res_ref[rows, :] = grad_res
        branch = grad_res.astype(LOW)
        branch_ref[rows, :] = branch
        do_ref[rows, :INNER] = dot_nt(branch, wo_ref[...]).astype(LOW)
        output = (residual + dot_nn(act, down_ref[...])).astype(LOW)

        @pl.when(side == part)
        def _():
            keep_ref[...] = output

        @pl.when(side != part)
        def _():
            send_ref[...] = output

    pipelined(range(2), first, second, 1)
    gain_grad_ref[...] = jnp.broadcast_to(gain_grad, gain_grad_ref.shape)
    number = rows_of(WIDTH2, 1)
    stat = jnp.where((number == ONE_A) | ((number >= ONE_B) & (number <= ONE_D)), 1.0, 0.0)
    stat = jnp.where(number == OFF, -rowq_ref[2:3, :], stat)
    for pair in range(PAIRS):
        turned = do_ref[:, pair_slice(pair)].T
        for hh in range(2):
            head = 2 * pair + hh
            grads = turned[hh * HD : (hh + 1) * HD, :].astype(WIDE)
            delta = jnp.sum(grads * context[head], axis=0, keepdims=True)
            lse = ml_ref[head : head + 1, :] + jnp.log(ml_ref[8 + head : 9 + head, :])
            for base, value in ((0, lse), (3 * HEADS, delta)):
                for index, piece in enumerate(three_pieces(-value)):
                    stat = jnp.where(number == base + HEADS * index + head, piece, stat)
    do_ref[:, INNER:] = stat.astype(LOW).T


def put_half(core, keep_ref, send_ref, row, value):
    rows = keep_ref.shape[0]
    half, start = row // rows, row % rows

    @pl.when(core == half)
    def _():
        keep_ref[start : start + value.shape[0], : value.shape[1]] = value

    @pl.when(core != half)
    def _():
        send_ref[start : start + value.shape[0], : value.shape[1]] = value


def put_rows(core, keep_ref, send_ref, row, value):
    rows = keep_ref.shape[0]
    value = value.astype(LOW)
    first = min(value.shape[0], rows - row % rows)
    put_half(core, keep_ref, send_ref, row, value[:first])
    if first < value.shape[0]:
        put_half(core, keep_ref, send_ref, row + first, value[first:])


def feed_grads_kernel(
    sc_ref, act_ref, feed_ref, gg_ref, gu_ref, ctx_ref, branch_ref, cot_ref, gain_grad_ref,
    keep_ref, send_ref,
):
    core = sc_ref[0, CORE]
    put = functools.partial(put_rows, core, keep_ref, send_ref)
    width = keep_ref.shape[1]
    hidden = act_ref.shape[1]
    feed = feed_ref[...].T
    row = 0
    for grads in (gg_ref, gu_ref):
        for start in range(0, hidden, width):
            put(row, dot_nn(feed, grads[:, start : start + width]))
            row += width
    act = act_ref[...].T
    put(row, dot_nn(act, cot_ref[...]))
    row += hidden
    put(row, dot_nn(ctx_ref[...].T, branch_ref[...]))
    row += INNER
    rest = 2 * keep_ref.shape[0] - row
    put(row, jnp.where(rows_of(rest, 1) == 0, gain_grad_ref[0:1, :], 0.0))


def order_kernel(sc_ref, mine_ref, other_ref, out_ref):
    core = sc_ref[0, CORE]
    block = mine_ref.shape[0] // 2
    for owner, ref in ((core, mine_ref), (1 - core, other_ref)):
        for part in range(2):
            at = pl.ds(pl.multiple_of(part * 2 * block + owner * block, block), block)
            out_ref[at, :] = ref[part * block : (part + 1) * block, :]


def chunk_kernel(slot, own, sc_ref, table_ref, do_ref, q_ref, kv0_ref, kv1_ref, a0_ref, a1_ref, e0_ref, e1_ref,
                 wk_ref, wv_ref, vec_ref, *rest):
    if slot > 0:
        (dq_in, w_in, near_in, marks_in), rest = rest[:4], rest[4:]
    if own:
        (extq_ref, rowq_ref, a_own_ref, onehot_ref), rest = rest[:4], rest[4:]
        (dx_ref, kept_ref, sent_ref, dq_kept_ref, dq_sent_ref), rest = rest[:5], rest[5:]
        dq_ref, w_ref, near_out, marks_ref, strip_ref, gen_ref, near_ref, ds_ref, grads_ref = rest
    else:
        dx_ref, dq_ref, w_ref, near_out, marks_ref, near_ref, ds_ref, grads_ref = rest
    quad, core, side_chunk = sc_ref[0, QUAD], sc_ref[0, CORE], sc_ref[slot, CHUNK]
    chunk = q_ref.shape[0]
    block = kv0_ref.shape[0]
    mine = 2 * block
    tiles = mine // TILE
    steps = mine // (2 * TILE)
    number = rows_of(WIDTH2, 1)
    lane = lanes_of(1, WIDTH2)
    build_near(near_ref, vec_ref, 1, range(HEADS))
    ext_turned = jnp.concatenate([e0_ref[...].T, e1_ref[...].T], axis=1).astype(WIDE)
    if own:
        build_strip(strip_ref, near_ref, table_ref, True, chunk, range(HEADS))
        visible_mask(
            gen_ref, extq_ref[...].astype(WIDE)[:, SEG : SEG + 1], rowq_ref[0:1, :], rowq_ref[3:4, :], core, False
        )
        ds_ref[:, :TILE, :] = jnp.zeros((2, TILE, mine), LOW)
        ds_ref[:, chunk + TILE :, :] = jnp.zeros((2, TILE, mine), LOW)
    low, high = near_flags(quad, side_chunk, core)
    keys_before = side_chunk < quad
    gap = side_chunk - quad
    spread = jnp.where(jnp.abs(gap) <= 1, 1, 0)
    first_mark = jnp.where(spread == 1, 16 + 8 * gap, jnp.where(gap < 0, 0, 1))
    mark_of_key = first_mark + spread * (rows_of(mine, 1) // TILE)
    ext = do_ref[:, INNER:]
    made = {}

    def both(pair, base):
        return jnp.concatenate([kv0_ref[:, pair_slice(pair, base)], kv1_ref[:, pair_slice(pair, base)]], axis=0)

    def operands(pair):
        if pair in made:
            return made[pair]
        q_pair, do_pair = q_ref[:, pair_slice(pair)], do_ref[:, pair_slice(pair)]
        k_pair = both(pair, 0)
        k_turned, v_turned = k_pair.T, both(pair, INNER).T
        zero = jnp.zeros_like(k_turned)
        k_sides, v_sides, k_marked = [], [], []
        for hh in range(2):
            head = 2 * pair + hh
            rows = (number == head) | (number == head + HEADS) | (number == head + 2 * HEADS)
            rows = jnp.broadcast_to(jnp.where(rows, 1.0, 0.0), (WIDTH2, mine))
            if not own:
                far = jnp.where(
                    keys_before, far_bias(table_ref, False, head), far_bias(table_ref, True, head)
                )
                wide = jnp.full((1, mine), far, WIDE)
                for at, piece in zip((ONE_A, ONE_B, ONE_C), three_pieces(wide)):
                    rows = jnp.where(number == at, piece, rows)
                rows = jnp.where(number == OFF, 1.0, rows)
                rows = jnp.where(number == ONE_D, ext_turned[MASK : MASK + 1, :], rows)
            k_sides.append(
                jnp.concatenate([row_half(k_turned, hh, zero), rows.astype(LOW)], axis=0)
            )
            first = 3 * HEADS + head
            rows = (number == first) | (number == first + HEADS) | (number == first + 2 * HEADS)
            rows = jnp.broadcast_to(jnp.where(rows, 1.0, 0.0), (WIDTH2, mine)).astype(LOW)
            v_sides.append(jnp.concatenate([row_half(v_turned, hh, zero), rows], axis=0))
            marks = jnp.where(lane - HD * (1 - hh) == mark_of_key, 1.0, 0.0).astype(LOW)
            k_marked.append(lane_half(k_pair, hh, marks))
        made[pair] = (
            jnp.concatenate([q_pair, ext], axis=1), jnp.concatenate([do_pair, ext], axis=1),
            q_pair.T, do_pair.T, k_sides, v_sides, k_marked,
        )
        return made[pair]

    def first(item):
        pair, step, hh = item
        head, lanes = 2 * pair + hh, step_lanes(step)
        q_ext, do_ext, _, _, k_sides, v_sides, _ = operands(pair)
        s = dot_nn(q_ext, k_sides[hh][:, lanes])
        if own:
            s = s + strip_rows(strip_ref, head, 2 * step, 2, core, chunk) + gen_ref[:, lanes]
        else:
            s = fix_near(
                s, step, steps, near_fixes(near_ref, table_ref, (low, high), head, head, True)
            )
        return s, dot_nn(do_ext, v_sides[hh][:, lanes])

    products = {}

    def second(item, found):
        pair, step, hh = item
        head, lanes = 2 * pair + hh, step_lanes(step)
        s, dp = found
        p = jnp.exp(s)
        ds = (p * dp).astype(LOW)
        _, _, q_turned, do_turned, _, _, k_marked = operands(pair)
        half = slice(hh * HD, (hh + 1) * HD)
        grads_ref[head_rows(head), lanes] = dot_nn(q_turned, ds)[half, :].astype(LOW)
        rows = slice(INNER + head * HD, INNER + (head + 1) * HD)
        grads_ref[rows, lanes] = dot_nn(do_turned, p.astype(LOW))[half, :].astype(LOW)
        ds_ref[hh, TILE : chunk + TILE, lanes] = ds
        if not own:
            base = near_in[head] if slot > 0 else jnp.zeros((NEAR, TILE), WIDE)
            if step == 0:
                near_out[head, :TILE, :] = base[:TILE] + low * ds[chunk - TILE :, :TILE].astype(WIDE)
                near_out[head, TILE : 2 * TILE, :] = base[TILE : 2 * TILE]
            if step == steps - 1:
                near_out[head, 2 * TILE :, :] = base[2 * TILE :] + high * ds[:TILE, TILE:].astype(WIDE)
        if step == steps - 1:
            product = dot_nn(ds_ref[hh, TILE : chunk + TILE, :], k_marked[hh])
            for tile in range(chunk // TILE):
                total = jnp.sum(product[tile * TILE : (tile + 1) * TILE, :], axis=0, keepdims=True)
                if slot > 0:
                    total = total + marks_in[head, tile : tile + 1, :]
                marks_ref[head, tile : tile + 1, :] = total
            if own:
                total = near_in[head]
                for tile in range(tiles):
                    at = pl.ds(pl.multiple_of(tile_place(tile, core) * TILE, TILE), NEAR)
                    part = ds_ref[hh, at, tile * TILE : (tile + 1) * TILE]
                    total = total + part.astype(WIDE)
                near_out[head] = total
            products[hh] = product
            if hh == 1:
                total = jnp.where(lane < HD, products[0], products[1])
                if slot > 0:
                    total = total + dq_in[:, pair_slice(pair)]
                dq_ref[:, pair_slice(pair)] = total

    pipelined(forward_items(mine), first, second, 1)
    a = jnp.concatenate([a0_ref[...], a1_ref[...]], axis=0)
    grads = grads_ref[...]
    weights = dot_nn(grads, a)
    if slot > 0:
        weights = weights + w_in[...]
    dx = dot_nt(grads[:INNER, :].T, wk_ref[...]) + dot_nt(grads[INNER:, :].T, wv_ref[...])
    dx_ref[...] = dx.astype(dx_ref.dtype)
    if not own:
        w_ref[...] = weights
        return

    put = functools.partial(put_rows, core, kept_ref, sent_ref)
    dq = dq_ref[...].astype(LOW)
    put(0, dot_tn(dq, a_own_ref[...]))
    put(INNER, weights)
    for part in range(2):
        rows = slice(part * block, (part + 1) * block)
        at = pl.ds(pl.multiple_of(part * mine + core * block, block), block)
        dq_kept_ref[rows, :] = dq_ref[at, :]
        at = pl.ds(pl.multiple_of(part * mine + (1 - core) * block, block), block)
        dq_sent_ref[rows, :] = dq_ref[at, :].astype(LOW)

    flip = (rows_of(TILE, TILE) + lanes_of(TILE, TILE) == TILE - 1).astype(WIDE)
    exact = functools.partial(
        jnp.dot, precision=lax.Precision.HIGHEST, preferred_element_type=WIDE
    )
    head_row = rows_of(8, 1)
    table = jnp.zeros((8, WIDTH2), WIDE)
    for part in range(3):
        sums = jnp.zeros((8, 2 * TILE), WIDE)
        for head in range(HEADS):
            turned = exact(flip, near_out[head, part * TILE : (part + 1) * TILE, :])
            padded = jnp.concatenate([turned, jnp.zeros((TILE, TILE), WIDE)], axis=1)
            skewed = pltpu.roll(padded, 0, 1, stride=1, stride_axis=0)
            sums = jnp.where(head_row == head, jnp.sum(skewed, axis=0, keepdims=True), sums)
        table = table + exact(sums, onehot_ref[part * 2 * TILE : (part + 1) * 2 * TILE, :])
    query_tile = rows_of(chunk // TILE, 1)
    for head in range(HEADS):
        mark = lane - HD * (1 - head % 2)
        inside = (mark >= 8) & (mark < 32)
        kind, tile = mark // 8, mark % 8
        at = (kind - 2) * (chunk // TILE) + tile_place(tile, core)
        relative = at - query_tile
        found = marks_ref[head]
        before = (mark == 0) | (inside & (relative < -1))
        after = (mark == 1) | (inside & (relative > 1))
        for chosen, bucket in ((before, FAR_BEFORE), (after, FAR_AFTER)):
            total = jnp.sum(jnp.where(chosen, found, 0.0))
            table = table + jnp.where((head_row == head) & (lane == bucket), total, 0.0)
    rest_rows = 2 * kept_ref.shape[0] - 3 * INNER
    columns = kept_ref.shape[1]
    small = jnp.concatenate([table, jnp.zeros((8, columns - WIDTH2), WIDE)], axis=1)
    small = jnp.concatenate([small, jnp.zeros((rest_rows - 8, columns), WIDE)], axis=0)
    put(3 * INNER, small)


def chain_kernel(slot, quads, sc_ref, *refs):
    mine, refs = refs[: slot + 1], refs[slot + 1 :]
    up_ref, down_ref = refs[-2:]
    core = sc_ref[0, CORE]
    for column, came, out_ref in ((UP, 0, up_ref), (DOWN, 1, down_ref)):
        edge = jnp.where(core == came, 0, quads - 1)
        for index, dx_ref in enumerate(mine):

            @pl.when(sc_ref[slot, column] == index)
            def _():
                value = dx_ref[...]
                if slot > 0:
                    came_before = refs[came][...].astype(WIDE)
                    total = value.astype(WIDE) + jnp.where(
                        sc_ref[0, QUAD] != edge, came_before, 0.0
                    )
                    value = total.astype(LOW)
                out_ref[...] = value


def join_kernel(sc_ref, kept_ref, got_ref, out_ref):
    side = sc_ref[0, SIDE]
    out_ref[side] = kept_ref[...]
    out_ref[1 - side] = got_ref[...]


def total_kernel(quads, sc_ref, dx_ref, first_ref, second_ref, out_ref):
    quad, core = sc_ref[0, QUAD], sc_ref[0, CORE]
    total = dx_ref[...]
    for came, came_ref in enumerate((first_ref, second_ref)):
        edge = jnp.where(core == came, 0, quads - 1)
        total = total + jnp.where(quad != edge, came_ref[...].astype(WIDE), 0.0)
    out_ref[...] = total


def input_kernel(
    sc_ref, dx_ref, dq_ref, dq_got_ref, x_ref, grad_res_ref, wq_ref, gain_ref, keep_ref, send_ref
):
    side = sc_ref[0, SIDE]
    block = x_ref.shape[0] // 2
    gain = gain_ref[...]
    for part in range(2):
        rows = slice(part * block, (part + 1) * block)
        queries = (dq_ref[rows, :] + dq_got_ref[rows, :].astype(WIDE)).astype(LOW)
        grad_in = dot_nt(queries, wq_ref[...]) + dx_ref[rows, :]
        x = x_ref[rows, :].astype(WIDE)
        scale = rms_scale(x)
        z = x * scale
        u = grad_in * gain
        result = grad_res_ref[rows, :] + scale * (u - z * jnp.mean(u * z, axis=-1, keepdims=True))
        result = result.astype(LOW)

        @pl.when(side == part)
        def _():
            keep_ref[...] = result

        @pl.when(side != part)
        def _():
            send_ref[...] = result


def tie_kernel(sc_ref, *refs):
    pass


def add_kernel(sc_ref, order_ref, *refs):
    outs = refs[-order_ref.shape[0] :]
    ins = refs[: len(refs) - len(outs)]
    for index, out_ref in enumerate(outs):
        which = order_ref[index]
        total = ins[0][which].astype(WIDE)
        for in_ref in ins[1:]:
            total = total + in_ref[which].astype(WIDE)
        out_ref[...] = total.astype(LOW)


def place_kernel(sc_ref, owner_ref, *refs):
    out_ref = refs[-1]
    for index, part_ref in enumerate(refs[:-1]):
        out_ref[owner_ref[index]] = part_ref[...]


def whole_rows(core, kept_ref, got_ref, first, count):
    half = kept_ref.shape[0]
    parts = []
    for number in range(2):
        low, high = max(first, number * half), min(first + count, (number + 1) * half)
        if low < high:
            rows = slice(low - number * half, high - number * half)
            part = jnp.where(core == number, kept_ref[rows, :], got_ref[rows, :])
            parts.append(part.astype(WIDE))
    return parts[0] if len(parts) == 1 else jnp.concatenate(parts, axis=0)


def unpack_feed_kernel(sc_ref, kept_ref, got_ref, out_ref, gate_ref, up_ref, down_ref, gain_ref):
    take = functools.partial(whole_rows, sc_ref[0, CORE], kept_ref, got_ref)
    width, hidden = gate_ref.shape
    row = 0
    for grads in (gate_ref, up_ref):
        for start in range(0, hidden, width):
            grads[:, start : start + width] = take(row, width)
            row += width
    down_ref[...] = take(row, hidden)
    row += hidden
    out_ref[...] = take(row, INNER)
    row += INNER
    gain_ref[...] = take(row, 16)[0:1, :]


def unpack_last_kernel(
    sc_ref, kept_ref, got_ref, wq_ref, wk_ref, wv_ref, gain_ref, query_ref, key_ref, value_ref, table_ref, gain_grad_ref,
):
    take = functools.partial(whole_rows, sc_ref[0, CORE], kept_ref, got_ref)
    total = jnp.zeros(gain_ref.shape, WIDE)
    for kind, (w_ref, out_ref) in enumerate(
        ((wq_ref, query_ref), (wk_ref, key_ref), (wv_ref, value_ref))
    ):
        grads = take(kind * INNER, INNER)
        out_ref[...] = grads.T
        total = total + jnp.sum(grads * w_ref[...].T.astype(WIDE), axis=0, keepdims=True)
    gain_grad_ref[...] = total / gain_ref[...]
    table_ref[...] = take(3 * INNER, 16)[:HEADS, :BUCKETS]


def staged_sum(kept, sent, between, plan, plan_out, add, place):
    came = [kept, lax.ppermute(sent, "blk", between)]
    after = yield sent
    for axes, size, index, peer, pairs in plan:
        order = jnp.stack([index] + [peer(index, shift) for shift in range(1, size)])
        own, *sends = add(order.astype(jnp.int32), came, after)
        came = [own] + [
            lax.ppermute(part, axes, pairs(shift)) for shift, part in enumerate(sends, 1)
        ]
        after = yield own
    (value,) = add(jnp.zeros((1,), jnp.int32), came, after)
    for axes, size, index, peer, pairs in plan_out:
        came = [lax.ppermute(value, axes, pairs(shift)) for shift in range(1, size)]
        after = yield value
        owners = jnp.stack([index] + [peer(index, -shift) for shift in range(1, size)])
        value = place(owners.astype(jnp.int32), [value] + came, after)
    got = lax.ppermute(value, "blk", between)
    after = yield value
    yield (value, got)


def advance(stages, count, after):
    for _ in range(count):
        tie = stages.send((after,))
    return tie


def finish(stages):
    for now in iter(lambda: stages.send(()), None):
        if isinstance(now, tuple):
            return now


def nearest_order(quads):
    return [
        sorted(range(quads), key=lambda k: (abs(k - place), k)) for place in range(quads)
    ]


def chunk_plan(quads):
    plans = []
    for place in range(quads):
        due = [(quads - 1 + place - d, d) for d in range(place + 1, quads)]
        due += [(quads - 1 - place + d, d) for d in range(place)]
        order = [d for _, d in sorted(due)] + [place]
        rows = []
        for slot in range(quads):
            up, down = quads - 1 + place - slot, place - (quads - 1) + slot
            rows.append(
                (
                    order[slot],
                    order.index(up) if place < up < quads else -1,
                    order.index(down) if 0 <= down < place else -1,
                )
            )
        plans.append(rows)
    return plans


def onehot_tables():
    thresholds = bucket_edges()

    def bucket(offset):
        half_count, exact_count, edges = thresholds
        distance = abs(offset)
        beyond = sum(distance >= edge for edge in edges)
        return (half_count if offset > 0 else 0) + (
            distance if distance < exact_count else exact_count + beyond
        )

    rows = np.zeros((BUCKETS, 2 * TURN), np.float32)
    for turn in range(TURN):
        back = turn if turn < TILE else turn - TURN
        rows[bucket(-TILE - back), turn] = 1.0
        rows[bucket(TILE + back), TURN + turn] = 1.0
    diagonals = np.zeros((6 * TILE, WIDTH2), np.float32)
    for part in range(3):
        for at in range(2 * TILE - 1):
            diagonals[part * 2 * TILE + at, bucket(1 + at - TILE * part)] = 1.0
    return rows, diagonals


def body(
    hidden_in,
    item_lengths,
    live_mask,
    cotangent,
    query_weight,
    key_weight,
    value_weight,
    output_weight,
    bucket_bias_table,
    norm_attention,
    norm_feed,
    gate_weight,
    up_weight,
    down_weight,
):
    streams, block, width = hidden_in.shape
    hidden = gate_weight.shape[1]
    blocks = lax.axis_size("blk")
    parts = lax.axis_size("dp")
    quads = blocks // 4
    here = lax.axis_index("blk")
    replica = lax.axis_index("dp")
    core, side, quad = here % 2, (here // 2) % 2, here // 4
    mine, chunk = 2 * block, 4 * block

    across = [(k, k ^ 2) for k in range(blocks)]
    between = [(k, k ^ 1) for k in range(blocks)]
    onward = []
    for k in range(blocks):
        if k % 2 == 0:
            onward.append((k, k + 4 if k + 4 < blocks else k + 1))
        else:
            onward.append((k, k - 4 if k >= 4 else k - 1))

    order = nearest_order(quads)
    distances = [
        sorted({abs(order[place][step] - place) for place in range(quads)}) for step in range(quads)
    ]
    spots = jnp.asarray(np.array(order, np.int32).T)
    nearest = jnp.asarray(np.array([found[0] for found in distances], np.int32))[:, None]
    is_here = jnp.arange(quads, dtype=jnp.int32)[None, :] == quad
    place = jnp.sum(jnp.where(is_here, spots, 0), axis=1, keepdims=True)
    swapped = ((place > quad) != (core == 1)) & (place != quad)
    source = 2 * (jnp.abs(place - quad) - nearest) + swapped.astype(jnp.int32)
    first_end = jnp.where(side == 0, item_lengths[0, 0], item_lengths[1, 0])
    col = jnp.arange(16, dtype=jnp.int32)[None, :]
    plans = np.array(chunk_plan(quads), np.int32)
    mine_of = [
        jnp.sum(jnp.where(is_here, jnp.asarray(plans[:, :, n].T), 0), axis=1, keepdims=True)
        for n in range(3)
    ]
    sc = jnp.where(col == QUAD, quad, 0)
    sc = jnp.where(col == CORE, core, sc)
    sc = jnp.where(col == SIDE, side, sc)
    sc = jnp.where(col == PLACE, place, sc)
    sc = jnp.where(col == SOURCE, source, sc)
    is_first = core == 0
    up_down = [jnp.where(is_first, mine_of[1], mine_of[2]), jnp.where(is_first, mine_of[2], mine_of[1])]
    for at, values in zip((CHUNK, UP, DOWN), (mine_of[0], *up_down)):
        sc = jnp.where(col == at, values, sc)
    sc = jnp.where(col == FIRST_END, first_end, sc).astype(jnp.int32)

    turned_onehot, diagonal_onehot = (jnp.asarray(t) for t in onehot_tables())

    smem = pl.BlockSpec(memory_space=pltpu.SMEM)
    vmem = pl.BlockSpec(memory_space=pltpu.VMEM)
    anywhere = pl.BlockSpec(memory_space=pl.ANY)
    shape = jax.ShapeDtypeStruct
    strip_rows_count = 2 * chunk - TILE
    near_shape = pltpu.VMEM((HEADS, NEAR, TILE), WIDE)
    strip_shape = pltpu.VMEM((HEADS, strip_rows_count, TILE), WIDE)
    gen_shape = pltpu.VMEM((chunk, mine), WIDE)
    dma = pltpu.SemaphoreType.DMA
    pairs_in_chunk = mine * chunk * HEADS

    def call(kernel, name, in_specs, out_specs, out_shape, scratch, operands, grid=(1,), aliases=None, us=5.0, after=(), limit=24,
             mark=False):
        count = 1 + len(operands)
        if mark:
            out_specs, out_shape = tuple(out_specs) + (vmem,), tuple(out_shape) + (shape((8, 128), WIDE),)
        last = count + len(after) + (len(out_shape) - 1 if mark else 0)

        def without_ties(*refs):
            if mark:
                refs[last][...] = jnp.zeros((8, 128), WIDE)
                refs = refs[:last] + refs[last + 1 :]
            kernel(*refs[:count], *refs[count + len(after) :])

        return pl.pallas_call(
            without_ties if after or mark else kernel,
            grid_spec=pltpu.PrefetchScalarGridSpec(
                num_scalar_prefetch=1,
                grid=grid,
                in_specs=list(in_specs) + [anywhere] * len(after),
                out_specs=out_specs,
                scratch_shapes=scratch,
            ),
            out_shape=out_shape,
            input_output_aliases=aliases or {},
            compiler_params=pltpu.CompilerParams(vmem_limit_bytes=limit * 1024 * 1024),
            cost_estimate=pl.CostEstimate(
                flops=int(us * (1e9 if us >= 4 else 1e7)), bytes_accessed=1 << 12, transcendentals=0
            ),
            name=name,
        )(sc, *operands, *after)

    def far_away(array):
        return pltpu.with_memory_space_constraint(array, pltpu.HBM)

    def tied(arrays, after):
        count = len(arrays)
        return call(
            tie_kernel, "tie", [anywhere] * count, (anywhere,) * count,
            tuple(shape(a.shape, a.dtype) for a in arrays), [], arrays,
            aliases={1 + n: n for n in range(count)}, us=0.3, after=after, limit=16,
        )

    def pick(both, index):
        return lax.dynamic_index_in_dim(both, index, 0, False)

    live_rows = jnp.pad(live_mask.astype(LOW)[:, None, :], ((0, 0), (0, 15), (0, width - block)))
    payload = jnp.concatenate([pick(hidden_in, 1 - side), pick(live_rows, 1 - side)], axis=0)
    got = lax.ppermute(payload, "blk", across)
    packed, x_low, rowk, rowq, vec = call(
        norm_kernel, "norm_rows", [smem] + [vmem] * 6, (vmem,) * 5,
        (
            shape((mine + 16, width), LOW), pltpu.HBM((mine, width), LOW), shape((8, chunk), WIDE),
            shape((8, mine), WIDE), shape((8, 2 * TURN), WIDE),
        ), [],
        (item_lengths, hidden_in, live_mask, got, norm_attention[None, :], bucket_bias_table, turned_onehot),
        us=2.0, limit=56,
    )
    own_chunk = jnp.concatenate([packed, lax.ppermute(packed, "blk", between)], axis=0)
    cot_got = lax.ppermute(pick(cotangent, 1 - side), "blk", across)

    qkv_shape = pltpu.HBM((quads * chunk, 3 * INNER), LOW)
    ext_shape = pltpu.HBM((quads * chunk, WIDTH2), LOW)
    state_shapes = (shape((INNER, mine), WIDE), shape((16, mine), WIDE))

    def chunk_out(step, columns):
        return pl.BlockSpec((chunk, columns), lambda i, sc: (sc[step, PLACE], 0))

    a_shape = pltpu.HBM((quads * chunk, width), LOW)
    chunk_scratch = [pltpu.VMEM((2, 16, width), LOW)]
    held = lax.ppermute(own_chunk, "blk", onward)
    qkv, ext, normed, qx, acc, ml, q_own = call(
        forward_own_kernel, "attend_own", [smem, anywhere] + [vmem] * 6,
        (chunk_out(0, 3 * INNER), chunk_out(0, WIDTH2), chunk_out(0, width), vmem, vmem, vmem, vmem),
        (qkv_shape, ext_shape, a_shape, shape((HEADS, 2 * WIDTH2, mine), LOW)) + state_shapes
        + (shape((chunk, INNER), LOW),),
        chunk_scratch + [strip_shape, near_shape, gen_shape, dma((6,))],
        (bucket_bias_table, own_chunk, key_weight, value_weight, query_weight, vec, rowq, rowk),
        us=12.0,
    )

    came = []
    for step in range(1, quads):
        held, acc = lax.optimization_barrier((held, acc))
        came.append((held, lax.ppermute(held, "blk", between)))
        if step + 1 < quads:
            held = lax.ppermute(held, "blk", onward)
        arrays = [array for distance in distances[step] for array in came[distance - 1]]
        qkv, ext, normed, acc, ml = call(
            functools.partial(forward_kernel, step, len(arrays)), "attend_other",
            [smem] + [vmem] * 7 + [anywhere] * (3 + len(arrays)),
            (chunk_out(step, 3 * INNER), chunk_out(step, WIDTH2), chunk_out(step, width), vmem, vmem),
            (qkv_shape, ext_shape, a_shape) + state_shapes,
            chunk_scratch + [near_shape, dma((6,))],
            (bucket_bias_table, key_weight, value_weight, query_weight, vec, qx, acc, ml, qkv, ext, normed, *arrays),
            aliases={7: 3, 8: 4, 9: 0, 10: 1, 11: 2}, us=10.0,
        )

    (do_mine, out_kept, out_sent, grad_res, act, feed, grad_gate, grad_up,
     context, branch, gain_grad, cot) = call(
        middle_kernel, "feed_both_ways", [vmem] * 11, (vmem,) * 12,
        (
            shape((mine, INNER + WIDTH2), LOW),
            shape((block, width), LOW), shape((block, width), LOW), pltpu.HBM((mine, width), WIDE),
            shape((mine, hidden), LOW), shape((mine, width), LOW), shape((mine, hidden), LOW),
            shape((mine, hidden), LOW), shape((mine, INNER), LOW), shape((mine, width), LOW),
            shape((8, width), WIDE), shape((mine, width), LOW),
        ), [],
        (
            acc, ml, x_low, cotangent, cot_got, rowq, output_weight, gate_weight, up_weight, down_weight,
            norm_feed[None, :],
        ),
        us=12.0,
    )
    do_other = lax.ppermute(do_mine, "blk", between)
    def joined(kept, got, after):
        return call(
            join_kernel, "join", [vmem] * 2, (vmem,), (pltpu.HBM((2, block, width), LOW),), [], (kept, got),
            us=1.0, after=after, limit=16, mark=True,
        )

    def over_blocks(shift):
        return [(k, k ^ (4 * shift)) for k in range(blocks)]

    over_side = ("blk", 2, side, lambda i, s: i ^ 1, lambda s: across)
    over_parts = (
        "dp", parts, replica, lambda i, s: (i + s) % parts,
        lambda s: [(k, (k + s) % parts) for k in range(parts)],
    )
    over_quads = ("blk", quads, quad, lambda i, s: i ^ abs(s), over_blocks)
    if parts == 2:

        def square_pairs(shift):
            pairs = []
            for k in range(blocks):
                for r in range(parts):
                    k2, r2 = k ^ (2 * (shift >> 1)), r ^ (shift & 1)
                    pairs.append((k * parts + r, k2 * parts + r2))
            return pairs

        over_square = (("blk", "dp"), 4, side * 2 + replica, lambda i, s: i ^ abs(s), square_pairs)
        plan = [over_square, over_quads]
    else:
        plan = [over_side, over_parts, over_quads]
    plan_out = plan[::-1]
    groups = len(plan) - 1
    pieces_in_all = 8 * 2 * 2 * parts * quads

    def padded(rows):
        return -(-rows // pieces_in_all) * pieces_in_all

    feed_rows = padded(3 * hidden + INNER + 8) // 2
    feed_kept, feed_sent = call(
        feed_grads_kernel, "feed_weight_grads", [vmem] * 8, (vmem, vmem),
        (shape((feed_rows, width), LOW),) * 2, [],
        (act, feed, grad_gate, grad_up, context, branch, cot, gain_grad), us=7.0,
    )
    def add_parts(order, arrays, after):
        size = order.shape[0]
        split = [a.reshape((size, a.shape[0] // size, a.shape[1])) for a in arrays]
        return call(
            add_kernel, "add_parts", [smem] + [vmem] * len(split), (vmem,) * size,
            (shape(split[0].shape[1:], LOW),) * size, [], (order, *split), us=2.0, after=after, limit=16,
        )

    def place_parts(owners, arrays, after):
        one = arrays[0].shape
        whole = call(
            place_kernel, "place_parts", [smem] + [vmem] * len(arrays), vmem,
            shape((len(arrays),) + one, LOW), [], (owners, *arrays), us=1.0, after=after, limit=16,
        )
        return whole.reshape((-1,) + one[1:])

    feed_stages = staged_sum(feed_kept, feed_sent, between, plan, plan_out, add_parts, place_parts)
    next(feed_stages)
    out_got = lax.ppermute(out_sent, "blk", across)
    tie = feed_stages.send(())
    do_chunk = call(
        order_kernel, "order", [vmem] * 2, vmem, shape((chunk, INNER + WIDTH2), LOW), [], (do_mine, do_other),
        us=1.0, after=(tie,), limit=16,
    )

    ties = [tie]

    qkv, ext, normed = far_away(qkv), far_away(ext), far_away(normed)
    backward = [(end, start) for start, end in onward]
    last_rows = padded(3 * INNER + 8) // 2
    state_shape = (
        shape((chunk, INNER), WIDE), shape((2 * INNER, width), WIDE), shape((HEADS, NEAR, TILE), WIDE),
        shape((HEADS, chunk // TILE, WIDTH2), WIDE),
    )

    def chunk_rows(slot, n, columns):
        return pl.BlockSpec(
            (block, columns), lambda i, sc: (4 * sc[slot, CHUNK] + sc[0, CORE] + 2 * n, 0)
        )

    state, gradients, came = (), [], ()
    for slot in range(quads):
        own = slot == quads - 1
        operands = (
            bucket_bias_table, do_chunk, q_own, qkv, qkv, normed, normed, ext, ext, key_weight, value_weight, vec,
        ) + tuple(state)
        in_specs = [
            smem, vmem, vmem,
            chunk_rows(slot, 0, 2 * INNER), chunk_rows(slot, 1, 2 * INNER),
            chunk_rows(slot, 0, width), chunk_rows(slot, 1, width),
            chunk_rows(slot, 0, WIDTH2), chunk_rows(slot, 1, WIDTH2), vmem, vmem, vmem,
        ] + [vmem] * len(state)
        scratch = [
            near_shape, pltpu.VMEM((2, chunk + 2 * TILE, mine), LOW), pltpu.VMEM((2 * INNER, mine), LOW),
        ]
        outs = (shape((mine, width), WIDE if own else LOW),)
        if own:
            operands += (ext, rowq, normed, diagonal_onehot)
            in_specs += [
                pl.BlockSpec((chunk, WIDTH2), lambda i, sc: (sc[0, QUAD], 0)), vmem,
                pl.BlockSpec((chunk, width), lambda i, sc: (sc[0, QUAD], 0)), vmem,
            ]
            outs += (shape((last_rows, width), LOW),) * 2
            outs += (shape((mine, INNER), WIDE), shape((mine, INNER), LOW))
            scratch = [
                pltpu.VMEM(s.shape, s.dtype) for s in state_shape
            ] + [strip_shape, gen_shape] + scratch
        else:
            outs += state_shape
        found = call(
            functools.partial(chunk_kernel, slot, own), "grad_chunk", in_specs, (vmem,) * len(outs), outs, scratch,
            operands, us=10.0, after=ties, limit=32 if own else 28,
            aliases={13 + n: 1 + n for n in range(4)} if slot and not own else None,
        )
        gradients.append(found[0])
        if own:
            kept, sent, dq_kept, dq_sent = found[1:]
            break
        state = found[1:]
        up, down = call(
            functools.partial(chain_kernel, slot, quads), "chain", [vmem] * (len(gradients) + len(came)), (vmem,) * 2,
            (shape((mine, width), LOW),) * 2, [], tuple(gradients) + tuple(came), us=1.0, limit=16,
        )
        came = (lax.ppermute(up, "blk", onward), lax.ppermute(down, "blk", backward))
        ties = [up]
        if slot < 3:
            ties.append(advance(feed_stages, 1 if slot == 1 else groups, up))
        if slot == 0:
            ties.append(out_got)
    total = call(
        functools.partial(total_kernel, quads), "total", [vmem] * 3, vmem, shape((mine, width), WIDE), [],
        (gradients[-1], *came), us=1.0, after=(kept,), limit=16,
    )
    tie = advance(feed_stages, 1, total)
    sent, dq_sent = tied((sent, dq_sent), (tie,))
    last_stages = staged_sum(kept, sent, between, plan, plan_out, add_parts, place_parts)
    next(last_stages)
    dq_got = lax.ppermute(dq_sent, "blk", between)
    feed_kept, feed_got = feed_stages.send(())
    output, tie = joined(out_kept, out_got, (tie,))
    tie = advance(last_stages, 1, tie)
    in_kept, in_sent = call(
        input_kernel, "grad_input", [vmem] * 7, (vmem,) * 2,
        (shape((block, width), LOW), shape((block, width), LOW)), [],
        (total, dq_kept, dq_got, x_low, grad_res, query_weight, norm_attention[None, :]),
        us=2.0, after=(tie,),
    )
    grad_out, grad_gate, grad_up, grad_down, grad_norm_feed, mark = call(
        unpack_feed_kernel, "unpack_feed", [vmem] * 2, (vmem,) * 5,
        (
            pltpu.HBM((INNER, width), WIDE), pltpu.HBM((width, hidden), WIDE), pltpu.HBM((width, hidden), WIDE),
            pltpu.HBM((hidden, width), WIDE), pltpu.HBM((1, width), WIDE),
        ), [],
        (feed_kept, feed_got), us=3.9, after=(in_kept,), mark=True,
    )
    for _ in range(groups):
        tie = last_stages.send((mark,))
    tie = last_stages.send((tie,))
    (in_sent,) = tied((in_sent,), (tie,))
    in_got = lax.ppermute(in_sent, "blk", across)
    for _ in range(groups):
        tie = last_stages.send(())
    input_gradient, mark = joined(in_kept, in_got, (tie,))
    last_stages.send((mark,))
    last_kept, last_got = finish(last_stages)
    grad_query, grad_key, grad_value, grad_table, grad_norm_attention = call(
        unpack_last_kernel, "unpack_attention", [vmem] * 6, (vmem,) * 5,
        (pltpu.HBM((width, INNER), WIDE),) * 3 + (shape((HEADS, BUCKETS), WIDE), shape((1, width), WIDE)), [],
        (last_kept, last_got, query_weight, key_weight, value_weight, norm_attention[None, :]), us=2.0,
    )
    return (
        output,
        input_gradient,
        grad_query,
        grad_key,
        grad_value,
        grad_out,
        grad_table.T,
        grad_norm_attention[0],
        grad_norm_feed[0],
        grad_gate,
        grad_up,
        grad_down,
    )


def solution(mesh):
    return jax.shard_map(
        body,
        mesh=mesh,
        in_specs=(
            P("dp", "blk", None),
            P("dp", None),
            P("dp", "blk"),
            P("dp", "blk", None),
            P(),
            P(),
            P(),
            P(),
            P(),
            P(),
            P(),
            P(),
            P(),
            P(),
        ),
        out_specs=(
            P("dp", "blk", None),
            P("dp", "blk", None),
            P(),
            P(),
            P(),
            P(),
            P(),
            P(),
            P(),
            P(),
            P(),
            P(),
        ),
        check_vma=False,
    )
```

```python
import functools

import jax
import jax.numpy as jnp
import numpy as np
from jax import lax
from jax.experimental import pallas as pl
from jax.experimental.pallas import tpu as pltpu
from jax.sharding import PartitionSpec as P

HEADS = 6
HD = 64
WIDTH2 = 2 * HD
PAIRS = HEADS // 2
INNER = HEADS * HD
BUCKETS = 32
MAXDIST = 128
EPSILON = 1e-06
BIG = 1e30
TILE = 128
NEAR = 3 * TILE
TURN = 4 * TILE
FAR_BEFORE = BUCKETS // 2 - 1
FAR_AFTER = BUCKETS - 1
LOW = jnp.bfloat16
WIDE = jnp.float32
GELU_A = 0.7978845608028654
GELU_B = 0.044715

QUAD, CORE, SIDE, PLACE, SOURCE, FIRST_END, CHUNK, UP, DOWN = range(9)
MASK, BEFORE, AFTER, PEN, STAT, LIVE, SEG = 0, 1, 2, 7, 8, 11, 12
ONE_A, OFF, ONE_B, ONE_C, ONE_D = 36, 37, 38, 39, 40


def bucket_edges():
    half_count = BUCKETS // 2
    exact_count = half_count // 2
    log_levels = half_count - exact_count
    thresholds = []
    for level_index in range(1, log_levels):
        candidate = exact_count
        while (
            candidate**log_levels * exact_count**level_index
            < MAXDIST**level_index * exact_count**log_levels
        ):
            candidate = candidate + 1
        thresholds.append(candidate)
    return (half_count, exact_count, thresholds)


def dot_nt(left, right):
    return lax.dot_general(
        left, right, (((1,), (1,)), ((), ())), preferred_element_type=WIDE
    )


def dot_nn(left, right):
    return jnp.dot(left, right, preferred_element_type=WIDE)


def dot_tn(left, right):
    return lax.dot_general(
        left, right, (((0,), (0,)), ((), ())), preferred_element_type=WIDE
    )


def rows_of(count, width):
    return lax.broadcasted_iota(jnp.int32, (count, width), 0)


def lanes_of(count, width):
    return lax.broadcasted_iota(jnp.int32, (count, width), 1)


def lane_half(array, half, other):
    return jnp.where(lanes_of(1, WIDTH2) // HD == half, array, other)


def row_half(array, half, other):
    return jnp.where(rows_of(WIDTH2, 1) // HD == half, array, other)


def pair_slice(pair, base=0):
    return slice(base + pair * WIDTH2, base + (pair + 1) * WIDTH2)


def tile_place(tile, core):
    return (tile // 2) * 4 + core * 2 + tile % 2


def rms_scale(values):
    return lax.rsqrt(jnp.mean(values * values, axis=-1, keepdims=True) + EPSILON)


def three_pieces(values):
    high = values.astype(LOW).astype(WIDE)
    mid = (values - high).astype(LOW).astype(WIDE)
    low = (values - high - mid).astype(LOW).astype(WIDE)
    return high, mid, low


def pipelined(items, first, second, depth):
    ahead = []
    for item in items:
        ahead.append((item, first(item)))
        if len(ahead) > depth:
            second(*ahead.pop(0))
    for waiting in ahead:
        second(*waiting)


def far_bias(table_ref, after, head):
    return table_ref[FAR_AFTER if after else FAR_BEFORE, head]


def build_near(near_ref, vec_ref, back, heads):
    for index, head in enumerate(heads):
        row = vec_ref[head : head + 1, back * TURN : (back + 1) * TURN]
        row = jnp.broadcast_to(row, (NEAR, TURN))
        near_ref[index] = pltpu.roll(row, 0, 1, stride=1, stride_axis=0)[:, :TILE]


def build_strip(strip_ref, near_ref, table_ref, back, chunk, heads):
    edge = chunk - TILE
    rest = strip_ref.shape[1] - edge - 2 * TILE
    for index, head in enumerate(heads):
        far_before = far_bias(table_ref, back, head)
        far_after = far_bias(table_ref, not back, head)
        strip_ref[index, : edge - TILE, :] = jnp.full((edge - TILE, TILE), far_before, WIDE)
        strip_ref[index, edge - TILE : edge + 2 * TILE, :] = near_ref[index]
        strip_ref[index, edge + 2 * TILE :, :] = jnp.full((rest, TILE), far_after, WIDE)


def strip_rows(strip_ref, index, first_tile, tiles, core, chunk):
    parts = []
    for tile in range(first_tile, first_tile + tiles):
        start = (chunk - TILE) - tile_place(tile, core) * TILE
        parts.append(strip_ref[index, pl.ds(pl.multiple_of(start, TILE), chunk), :])
    return jnp.concatenate(parts, axis=1)


def near_fixes(near_ref, table_ref, flags, index, head, back):
    low, high = flags
    return (
        low * (near_ref[index, :TILE, :] - far_bias(table_ref, back, head)),
        high * (near_ref[index, 2 * TILE :, :] - far_bias(table_ref, not back, head)),
    )


def fix_near(scores, step, steps, fixes):
    low, high = fixes
    chunk, width = scores.shape
    if step == 0:
        last = jnp.concatenate(
            [scores[chunk - TILE :, :TILE] + low, scores[chunk - TILE :, TILE:]], axis=1
        )
        scores = jnp.concatenate([scores[: chunk - TILE], last], axis=0)
    if step == steps - 1:
        first = jnp.concatenate(
            [scores[:TILE, : width - TILE], scores[:TILE, width - TILE :] + high], axis=1
        )
        scores = jnp.concatenate([first, scores[TILE:]], axis=0)
    return scores


def near_flags(place, quad, core):
    low = jnp.where((place == quad - 1) & (core == 0), 1.0, 0.0)
    high = jnp.where((place == quad + 1) & (core == 1), 1.0, 0.0)
    return low, high


def natural_row(even, odd):
    block = even.shape[1] // 2
    return jnp.concatenate(
        [even[:, :block], odd[:, :block], even[:, block:], odd[:, block:]], axis=1
    )


def key_columns(rows, lanes):
    places = rows[0].shape[1]
    stack = jnp.zeros((16, places), WIDE)
    spread = jnp.zeros((16, WIDTH2), WIDE)
    number, lane = rows_of(16, 1), lanes_of(16, WIDTH2)
    for index, row in enumerate(rows):
        stack = jnp.where(number == index, row, stack)
    for index, at, scale in lanes:
        spread = jnp.where((number == index) & (lane == at), scale, spread)
    return dot_tn(stack.astype(LOW), spread.astype(LOW))


def visible_mask(gen_ref, segment_column, segment_row, live, core, keys_down):
    chunk, mine = gen_ref.shape
    down = rows_of(chunk, 1)
    for tile in range(mine // TILE):
        lanes = slice(tile * TILE, (tile + 1) * TILE)
        across = tile_place(tile, core) * TILE + lanes_of(1, TILE)
        alive = live if keys_down else live[:, lanes]
        visible = (segment_column == segment_row[:, lanes]) & ((alive > 0.5) | (down == across))
        gen_ref[:, lanes] = jnp.where(visible, 0.0, -BIG)


def project(a, weight_refs, qkv_ref):
    for part, w_ref in enumerate(weight_refs):
        cols = slice(part * INNER, (part + 1) * INNER)
        qkv_ref[:, cols] = dot_nn(a, w_ref[...]).astype(LOW)


def halves_copies(source, swapped, core, rows_ref, live_ref, sems):
    first_core = 1 - core if swapped else core
    block = rows_ref.shape[0] // 4
    half = source.shape[0] // 2
    copies = []
    for index in range(2):
        owner = first_core if index == 0 else 1 - first_core
        for part in range(2):
            at = pl.multiple_of(part * 2 * block + owner * block, block)
            copies.append((source.at[pl.ds(index * half + part * block, block), :], rows_ref.at[pl.ds(at, block), :]))
        if live_ref is not None:
            copies.append((source.at[pl.ds(index * half + 2 * block, 16), :], live_ref.at[owner]))
    return [
        pltpu.make_async_copy(start, end, sems.at[index]) for index, (start, end) in enumerate(copies)
    ]


def start_fetch(sc_ref, step, sources, rows_ref, live_ref, sems):
    core = sc_ref[0, CORE]
    for index, source in enumerate(sources):

        @pl.when(sc_ref[step, SOURCE] == index)
        def _():
            for copy in halves_copies(source, index % 2 == 1, core, rows_ref, live_ref, sems):
                copy.start()


def wait_fetch(sc_ref, sources, rows_ref, live_ref, sems):
    for copy in halves_copies(sources[0], False, sc_ref[0, CORE], rows_ref, live_ref, sems):
        copy.wait()


def norm_kernel(sc_ref, hidden_ref, live_ref, got_ref, gain_ref, packed_ref, x_ref):
    side = sc_ref[0, SIDE]
    block = hidden_ref.shape[1]
    mine = 2 * block
    kept, got = hidden_ref[side], got_ref[:block, :]
    live_kept = live_ref[pl.ds(side, 1), :].astype(WIDE)
    live_got = got_ref[block : block + 16, :block].astype(WIDE)[0:1, :]
    for part in range(2):
        rows = jnp.where(side == part, kept, got)
        x_ref[part * block : (part + 1) * block, :] = rows
        wide = rows.astype(WIDE)
        normed = wide * rms_scale(wide) * gain_ref[...]
        packed_ref[part * block : (part + 1) * block, :] = normed.astype(LOW)
    live = jnp.concatenate(
        [jnp.where(side == 0, live_kept, live_got), jnp.where(side == 0, live_got, live_kept)],
        axis=1,
    )
    packed_ref[mine:, :] = jnp.broadcast_to(live, (16, mine)).astype(LOW)


def places_kernel(sc_ref, lengths_ref, packed_ref, table_ref, onehot_ref, rowk_ref, rowq_ref, vec_ref):
    side, core, quad = sc_ref[0, SIDE], sc_ref[0, CORE], sc_ref[0, QUAD]
    mine, chunk = rowq_ref.shape[1], rowk_ref.shape[1]
    block = mine // 2
    live = packed_ref[mine : mine + 16, :].astype(WIDE)[0:1, :]
    places = quad * chunk + lanes_of(1, chunk)

    def one_item(item, carry):
        end, segment = carry
        end = end + lengths_ref[side, item]
        return end, segment + jnp.where(places >= end, 1.0, 0.0)

    zero = jnp.zeros((1, chunk), WIDE)
    end, segment = lax.fori_loop(0, lengths_ref.shape[1], one_item, (jnp.int32(0), zero))
    rowk_ref[...] = jnp.broadcast_to(segment, (8, chunk))
    own = jnp.concatenate(
        [
            rowk_ref[0:1, pl.ds(pl.multiple_of(part * mine + core * block, block), block)]
            for part in range(2)
        ],
        axis=1,
    )
    number = rows_of(8, 1)
    rowq = jnp.where(number == 0, own, 0.0)
    rowq = jnp.where(number == 2, jnp.where(own > 0.5, BIG, 0.0), rowq)
    rowq = jnp.where(number == 3, live, rowq)
    rowq_ref[...] = rowq
    found = lax.dot_general(
        table_ref[...], onehot_ref[...], (((0,), (0,)), ((), ())),
        precision=lax.Precision.HIGHEST, preferred_element_type=WIDE,
    )
    vec_ref[...] = jnp.concatenate([found, jnp.zeros((8 - HEADS, found.shape[1]), WIDE)], axis=0)


def forward_items(mine):
    steps = mine // (2 * TILE)
    return [(pair, step, hh) for pair in range(PAIRS) for step in range(steps) for hh in range(2)]


def forward_operands(qkv_ref, ext):
    made = {}

    def operands(pair):
        if pair not in made:
            k_ext = jnp.concatenate([qkv_ref[:, pair_slice(pair)], ext], axis=1)
            v_turned = qkv_ref[:, pair_slice(pair, INNER)].T
            made[pair] = (
                k_ext, [row_half(v_turned, hh, jnp.ones_like(v_turned)) for hh in range(2)]
            )
        return made[pair]

    return operands


def step_lanes(step):
    return slice(step * 2 * TILE, (step + 1) * 2 * TILE)


def head_rows(head):
    return slice(head * HD, (head + 1) * HD)


def forward_own_kernel(
    sc_ref, table_ref, source_ref, wk_ref, wv_ref, wq_ref, vec_ref, rowq_ref, rowk_ref,
    qkv_ref, ext_ref, a_ref, qx_ref, acc_ref, ml_ref, q_own_ref,
    live_ref, strip_ref, near_ref, gen_ref, sems,
):
    core = sc_ref[0, CORE]
    chunk = qkv_ref.shape[0]
    mine = acc_ref.shape[1]
    block = mine // 2
    start_fetch(sc_ref, 0, [source_ref], a_ref, live_ref, sems)
    build_near(near_ref, vec_ref, 0, range(HEADS))
    build_strip(strip_ref, near_ref, table_ref, False, chunk, range(HEADS))
    number = rows_of(WIDTH2, 1)
    for head in range(HEADS):
        rows = jnp.where(number == MASK, 1.0, 0.0)
        for which, after in ((BEFORE, False), (AFTER, True)):
            far = jnp.full((1, mine), far_bias(table_ref, after, head), WIDE)
            for piece, value in enumerate(three_pieces(far)):
                rows = jnp.where(number == which + 2 * piece, value, rows)
        rows = jnp.where(number == PEN, -rowq_ref[2:3, :], rows)
        qx_ref[head, WIDTH2:, :] = rows.astype(LOW)
    wait_fetch(sc_ref, [source_ref], a_ref, live_ref, sems)
    project(a_ref[...], (wk_ref, wv_ref, wq_ref), qkv_ref)
    q_own_ref[...] = qkv_ref[:, 2 * INNER :]
    live = natural_row(live_ref[0].astype(WIDE)[0:1, :], live_ref[1].astype(WIDE)[0:1, :])
    columns = key_columns(
        [jnp.ones_like(live), live, rowk_ref[0:1, :]],
        [(0, STAT, 1.0), (0, STAT + 1, 1.0), (0, STAT + 2, 1.0), (1, LIVE, 1.0), (2, SEG, 1.0)],
    )
    ext_ref[...] = columns.astype(LOW)
    visible_mask(
        gen_ref, columns[:, SEG : SEG + 1], rowq_ref[0:1, :], columns[:, LIVE : LIVE + 1], core, True
    )
    for part in range(2):
        at = pl.ds(pl.multiple_of(part * mine + core * block, block), block)
        lanes = slice(part * block, (part + 1) * block)
        for pair in range(PAIRS):
            turned = qkv_ref[at, pair_slice(pair, 2 * INNER)].T
            for hh in range(2):
                qx_ref[2 * pair + hh, :WIDTH2, lanes] = row_half(
                    turned, hh, jnp.zeros_like(turned)
                )
    ml_ref[...] = jnp.zeros_like(ml_ref)
    operands = forward_operands(qkv_ref, ext_ref[...])

    def first(item):
        pair, step, hh = item
        s = dot_nn(operands(pair)[0], qx_ref[2 * pair + hh, :, step_lanes(step)])
        s = s + strip_rows(strip_ref, 2 * pair + hh, 2 * step, 2, core, chunk)
        return s + gen_ref[:, step_lanes(step)]

    def second(item, s):
        pair, step, hh = item
        head, lanes = 2 * pair + hh, step_lanes(step)
        top = jnp.max(s, axis=0, keepdims=True)
        p = jnp.exp(s - top).astype(LOW)
        pv = dot_nn(operands(pair)[1][hh], p)
        ml_ref[head : head + 1, lanes] = top
        ml_ref[8 + head : 9 + head, lanes] = pv[HD * (1 - hh) : HD * (1 - hh) + 1, :]
        acc_ref[head_rows(head), lanes] = pv[hh * HD : (hh + 1) * HD, :]

    pipelined(forward_items(mine), first, second, 2)


def forward_kernel(
    step_number, sources, sc_ref, table_ref, wk_ref, wv_ref, wq_ref, vec_ref, qx_ref, acc_in, ml_in,
    qkv_in, ext_in, a_in, *rest,
):
    source_refs, rest = rest[:sources], rest[sources:]
    qkv_ref, ext_ref, a_ref, acc_ref, ml_ref, live_ref, near_ref, sems = rest
    quad, core, place = (sc_ref[step_number, i] for i in (QUAD, CORE, PLACE))
    chunk = qkv_ref.shape[0]
    mine = acc_ref.shape[1]
    start_fetch(sc_ref, step_number, source_refs, a_ref, live_ref, sems)
    build_near(near_ref, vec_ref, 0, range(HEADS))
    wait_fetch(sc_ref, source_refs, a_ref, live_ref, sems)
    project(a_ref[...], (wk_ref, wv_ref, wq_ref), qkv_ref)
    live = natural_row(live_ref[0].astype(WIDE)[0:1, :], live_ref[1].astype(WIDE)[0:1, :])
    places = place * chunk + lanes_of(1, chunk)
    seen = (live > 0.5) & (places < sc_ref[step_number, FIRST_END])
    is_before = jnp.where(place < quad, 1.0, 0.0)
    is_after = 1.0 - is_before
    marks = [(0, MASK, 1.0), (1, PEN, 1.0)]
    marks += [(1, STAT + n, 1.0) for n in range(3)]
    marks += [(1, BEFORE + 2 * n, is_before) for n in range(3)]
    marks += [(1, AFTER + 2 * n, is_after) for n in range(3)]
    ext = key_columns([jnp.where(seen, 0.0, -BIG), jnp.ones_like(live)], marks).astype(LOW)
    ext_ref[...] = ext
    flags = near_flags(place, quad, core)
    steps = mine // (2 * TILE)
    operands = forward_operands(qkv_ref, ext)

    def first(item):
        pair, step, hh = item
        head = 2 * pair + hh
        s = dot_nn(operands(pair)[0], qx_ref[head, :, step_lanes(step)])
        return fix_near(s, step, steps, near_fixes(near_ref, table_ref, flags, head, head, False))

    def second(item, s):
        pair, step, hh = item
        head, lanes = 2 * pair + hh, step_lanes(step)
        old = ml_in[head : head + 1, lanes]
        top = jnp.maximum(old, jnp.max(s, axis=0, keepdims=True))
        keep = jnp.exp(old - top)
        p = jnp.exp(s - top).astype(LOW)
        pv = dot_nn(operands(pair)[1][hh], p)
        ml_ref[head : head + 1, lanes] = top
        total = ml_in[8 + head : 9 + head, lanes] * keep
        ml_ref[8 + head : 9 + head, lanes] = total + pv[HD * (1 - hh) : HD * (1 - hh) + 1, :]
        rows = head_rows(head)
        acc_ref[rows, lanes] = acc_in[rows, lanes] * keep + pv[hh * HD : (hh + 1) * HD, :]

    pipelined(forward_items(mine), first, second, 2)


def middle_kernel(
    sc_ref, acc_ref, ml_ref, x_ref, cot_in, cot_got, rowq_ref, wo_ref, gate_ref, up_ref, down_ref, gain_ref,
    do_ref, keep_ref, send_ref, grad_res_ref, act_ref, feed_ref, gg_ref, gu_ref,
    ctx_ref, branch_ref, gain_grad_ref, cot_ref,
):
    side = sc_ref[0, SIDE]
    mine = x_ref.shape[0]
    block = mine // 2
    gain = gain_ref[...]
    context = []
    for head in range(HEADS):
        context.append(acc_ref[head_rows(head), :] / ml_ref[8 + head : 9 + head, :])
    for pair in range(PAIRS):
        both = jnp.concatenate(context[2 * pair : 2 * pair + 2], axis=0).astype(LOW)
        ctx_ref[:, pair_slice(pair)] = both.T
    gain_grad = jnp.zeros_like(gain)
    cot_kept = cot_in[side]
    for part in range(2):
        rows = slice(part * block, (part + 1) * block)
        cot_ref[rows, :] = jnp.where(side == part, cot_kept, cot_got[...])

    def first(part):
        rows = slice(part * block, (part + 1) * block)
        residual = x_ref[rows, :].astype(WIDE) + dot_nn(ctx_ref[rows, :], wo_ref[...])
        scale = rms_scale(residual)
        z = residual * scale
        feed = (z * gain).astype(LOW)
        feed_ref[rows, :] = feed
        v = dot_nn(feed, gate_ref[...])
        up = dot_nn(feed, up_ref[...])
        return residual, scale, z, v, up, dot_nt(cot_ref[rows, :], down_ref[...])

    def second(part, made):
        nonlocal gain_grad
        residual, scale, z, v, up, grad_hidden = made
        rows = slice(part * block, (part + 1) * block)
        square = v * v
        t = jnp.tanh(GELU_A * v * (1.0 + GELU_B * square))
        half = 0.5 * (1.0 + t)
        g = v * half
        slope = half + 0.5 * v * (1.0 - t * t) * (GELU_A * (1.0 + 3.0 * GELU_B * square))
        act = (g * up).astype(LOW)
        act_ref[rows, :] = act
        grad_gate = (grad_hidden * up * slope).astype(LOW)
        grad_up = (grad_hidden * g).astype(LOW)
        gg_ref[rows, :] = grad_gate
        gu_ref[rows, :] = grad_up
        grad_feed = dot_nt(grad_gate, gate_ref[...]) + dot_nt(grad_up, up_ref[...])
        u = grad_feed * gain
        gain_grad = gain_grad + jnp.sum(grad_feed * z, axis=0, keepdims=True)
        cot = cot_ref[rows, :].astype(WIDE)
        grad_res = cot + scale * (u - z * jnp.mean(u * z, axis=-1, keepdims=True))
        grad_res_ref[rows, :] = grad_res
        branch = grad_res.astype(LOW)
        branch_ref[rows, :] = branch
        do_ref[rows, :INNER] = dot_nt(branch, wo_ref[...]).astype(LOW)
        output = (residual + dot_nn(act, down_ref[...])).astype(LOW)

        @pl.when(side == part)
        def _():
            keep_ref[...] = output

        @pl.when(side != part)
        def _():
            send_ref[...] = output

    pipelined(range(2), first, second, 1)
    gain_grad_ref[...] = jnp.broadcast_to(gain_grad, gain_grad_ref.shape)
    number = rows_of(WIDTH2, 1)
    stat = jnp.where((number == ONE_A) | ((number >= ONE_B) & (number <= ONE_D)), 1.0, 0.0)
    stat = jnp.where(number == OFF, -rowq_ref[2:3, :], stat)
    for pair in range(PAIRS):
        turned = do_ref[:, pair_slice(pair)].T
        for hh in range(2):
            head = 2 * pair + hh
            grads = turned[hh * HD : (hh + 1) * HD, :].astype(WIDE)
            delta = jnp.sum(grads * context[head], axis=0, keepdims=True)
            lse = ml_ref[head : head + 1, :] + jnp.log(ml_ref[8 + head : 9 + head, :])
            for base, value in ((0, lse), (3 * HEADS, delta)):
                for index, piece in enumerate(three_pieces(-value)):
                    stat = jnp.where(number == base + HEADS * index + head, piece, stat)
    do_ref[:, INNER:] = stat.astype(LOW).T


def put_half(core, keep_ref, send_ref, row, value):
    rows = keep_ref.shape[0]
    half, start = row // rows, row % rows

    @pl.when(core == half)
    def _():
        keep_ref[start : start + value.shape[0], : value.shape[1]] = value

    @pl.when(core != half)
    def _():
        send_ref[start : start + value.shape[0], : value.shape[1]] = value


def put_rows(core, keep_ref, send_ref, row, value):
    rows = keep_ref.shape[0]
    value = value.astype(LOW)
    first = min(value.shape[0], rows - row % rows)
    put_half(core, keep_ref, send_ref, row, value[:first])
    if first < value.shape[0]:
        put_half(core, keep_ref, send_ref, row + first, value[first:])


def feed_grads_kernel(
    sc_ref, act_ref, feed_ref, gg_ref, gu_ref, ctx_ref, branch_ref, cot_ref, gain_grad_ref,
    keep_ref, send_ref,
):
    core = sc_ref[0, CORE]
    put = functools.partial(put_rows, core, keep_ref, send_ref)
    width = keep_ref.shape[1]
    hidden = act_ref.shape[1]
    feed = feed_ref[...].T
    row = 0
    for grads in (gg_ref, gu_ref):
        for start in range(0, hidden, width):
            put(row, dot_nn(feed, grads[:, start : start + width]))
            row += width
    act = act_ref[...].T
    put(row, dot_nn(act, cot_ref[...]))
    row += hidden
    put(row, dot_nn(ctx_ref[...].T, branch_ref[...]))
    row += INNER
    rest = 2 * keep_ref.shape[0] - row
    put(row, jnp.where(rows_of(rest, 1) == 0, gain_grad_ref[0:1, :], 0.0))


def order_kernel(sc_ref, mine_ref, other_ref, out_ref):
    core = sc_ref[0, CORE]
    block = mine_ref.shape[0] // 2
    for owner, ref in ((core, mine_ref), (1 - core, other_ref)):
        for part in range(2):
            at = pl.ds(pl.multiple_of(part * 2 * block + owner * block, block), block)
            out_ref[at, :] = ref[part * block : (part + 1) * block, :]


def chunk_kernel(slot, own, sc_ref, table_ref, do_ref, q_ref, kv0_ref, kv1_ref, a0_ref, a1_ref, e0_ref, e1_ref,
                 wk_ref, wv_ref, vec_ref, *rest):
    if slot > 0:
        (dq_in, w_in, near_in, marks_in), rest = rest[:4], rest[4:]
    if own:
        (extq_ref, rowq_ref, a_own_ref), rest = rest[:3], rest[3:]
        (dx_ref, kept_ref, sent_ref, dq_kept_ref, dq_sent_ref, near_out, marks_ref), rest = rest[:7], rest[7:]
        dq_ref, strip_ref, gen_ref, near_ref, ds_ref, grads_ref = rest
    else:
        dx_ref, dq_ref, w_ref, near_out, marks_ref, near_ref, ds_ref, grads_ref = rest
    quad, core, side_chunk = sc_ref[0, QUAD], sc_ref[0, CORE], sc_ref[slot, CHUNK]
    chunk = q_ref.shape[0]
    block = kv0_ref.shape[0]
    mine = 2 * block
    tiles = mine // TILE
    steps = mine // (2 * TILE)
    number = rows_of(WIDTH2, 1)
    lane = lanes_of(1, WIDTH2)
    build_near(near_ref, vec_ref, 1, range(HEADS))
    ext_turned = jnp.concatenate([e0_ref[...].T, e1_ref[...].T], axis=1).astype(WIDE)
    if own:
        build_strip(strip_ref, near_ref, table_ref, True, chunk, range(HEADS))
        visible_mask(
            gen_ref, extq_ref[...].astype(WIDE)[:, SEG : SEG + 1], rowq_ref[0:1, :], rowq_ref[3:4, :], core, False
        )
        ds_ref[:, :TILE, :] = jnp.zeros((2, TILE, mine), LOW)
        ds_ref[:, chunk + TILE :, :] = jnp.zeros((2, TILE, mine), LOW)
    low, high = near_flags(quad, side_chunk, core)
    keys_before = side_chunk < quad
    gap = side_chunk - quad
    spread = jnp.where(jnp.abs(gap) <= 1, 1, 0)
    first_mark = jnp.where(spread == 1, 16 + 8 * gap, jnp.where(gap < 0, 0, 1))
    mark_of_key = first_mark + spread * (rows_of(mine, 1) // TILE)
    ext = do_ref[:, INNER:]
    made = {}

    def both(pair, base):
        return jnp.concatenate([kv0_ref[:, pair_slice(pair, base)], kv1_ref[:, pair_slice(pair, base)]], axis=0)

    def operands(pair):
        if pair in made:
            return made[pair]
        q_pair, do_pair = q_ref[:, pair_slice(pair)], do_ref[:, pair_slice(pair)]
        k_pair = both(pair, 0)
        k_turned, v_turned = k_pair.T, both(pair, INNER).T
        zero = jnp.zeros_like(k_turned)
        k_sides, v_sides, k_marked = [], [], []
        for hh in range(2):
            head = 2 * pair + hh
            rows = (number == head) | (number == head + HEADS) | (number == head + 2 * HEADS)
            rows = jnp.broadcast_to(jnp.where(rows, 1.0, 0.0), (WIDTH2, mine))
            if not own:
                far = jnp.where(
                    keys_before, far_bias(table_ref, False, head), far_bias(table_ref, True, head)
                )
                wide = jnp.full((1, mine), far, WIDE)
                for at, piece in zip((ONE_A, ONE_B, ONE_C), three_pieces(wide)):
                    rows = jnp.where(number == at, piece, rows)
                rows = jnp.where(number == OFF, 1.0, rows)
                rows = jnp.where(number == ONE_D, ext_turned[MASK : MASK + 1, :], rows)
            k_sides.append(
                jnp.concatenate([row_half(k_turned, hh, zero), rows.astype(LOW)], axis=0)
            )
            first = 3 * HEADS + head
            rows = (number == first) | (number == first + HEADS) | (number == first + 2 * HEADS)
            rows = jnp.broadcast_to(jnp.where(rows, 1.0, 0.0), (WIDTH2, mine)).astype(LOW)
            v_sides.append(jnp.concatenate([row_half(v_turned, hh, zero), rows], axis=0))
            marks = jnp.where(lane - HD * (1 - hh) == mark_of_key, 1.0, 0.0).astype(LOW)
            k_marked.append(lane_half(k_pair, hh, marks))
        made[pair] = (
            jnp.concatenate([q_pair, ext], axis=1), jnp.concatenate([do_pair, ext], axis=1),
            q_pair.T, do_pair.T, k_sides, v_sides, k_marked,
        )
        return made[pair]

    def first(item):
        pair, step, hh = item
        head, lanes = 2 * pair + hh, step_lanes(step)
        q_ext, do_ext, _, _, k_sides, v_sides, _ = operands(pair)
        s = dot_nn(q_ext, k_sides[hh][:, lanes])
        if own:
            s = s + strip_rows(strip_ref, head, 2 * step, 2, core, chunk) + gen_ref[:, lanes]
        else:
            s = fix_near(
                s, step, steps, near_fixes(near_ref, table_ref, (low, high), head, head, True)
            )
        return s, dot_nn(do_ext, v_sides[hh][:, lanes])

    products = {}

    def second(item, found):
        pair, step, hh = item
        head, lanes = 2 * pair + hh, step_lanes(step)
        s, dp = found
        p = jnp.exp(s)
        ds = (p * dp).astype(LOW)
        _, _, q_turned, do_turned, _, _, k_marked = operands(pair)
        half = slice(hh * HD, (hh + 1) * HD)
        grads_ref[head_rows(head), lanes] = dot_nn(q_turned, ds)[half, :].astype(LOW)
        rows = slice(INNER + head * HD, INNER + (head + 1) * HD)
        grads_ref[rows, lanes] = dot_nn(do_turned, p.astype(LOW))[half, :].astype(LOW)
        ds_ref[hh, TILE : chunk + TILE, lanes] = ds
        if not own:
            base = near_in[head] if slot > 0 else jnp.zeros((NEAR, TILE), WIDE)
            if step == 0:
                near_out[head, :TILE, :] = base[:TILE] + low * ds[chunk - TILE :, :TILE].astype(WIDE)
                near_out[head, TILE : 2 * TILE, :] = base[TILE : 2 * TILE]
            if step == steps - 1:
                near_out[head, 2 * TILE :, :] = base[2 * TILE :] + high * ds[:TILE, TILE:].astype(WIDE)
        if step == steps - 1:
            product = dot_nn(ds_ref[hh, TILE : chunk + TILE, :], k_marked[hh])
            for tile in range(chunk // TILE):
                total = jnp.sum(product[tile * TILE : (tile + 1) * TILE, :], axis=0, keepdims=True)
                if slot > 0:
                    total = total + marks_in[head, tile : tile + 1, :]
                marks_ref[head, tile : tile + 1, :] = total
            if own:
                total = near_in[head]
                for tile in range(tiles):
                    at = pl.ds(pl.multiple_of(tile_place(tile, core) * TILE, TILE), NEAR)
                    part = ds_ref[hh, at, tile * TILE : (tile + 1) * TILE]
                    total = total + part.astype(WIDE)
                near_out[head] = total
            products[hh] = product
            if hh == 1:
                total = jnp.where(lane < HD, products[0], products[1])
                if slot > 0:
                    total = total + dq_in[:, pair_slice(pair)]
                dq_ref[:, pair_slice(pair)] = total

    pipelined(forward_items(mine), first, second, 1)
    a = jnp.concatenate([a0_ref[...], a1_ref[...]], axis=0)
    grads = grads_ref[...]
    weights = dot_nn(grads, a)
    if slot > 0:
        weights = weights + w_in[...]
    dx = dot_nt(grads[:INNER, :].T, wk_ref[...]) + dot_nt(grads[INNER:, :].T, wv_ref[...])
    dx_ref[...] = dx.astype(dx_ref.dtype)
    if not own:
        w_ref[...] = weights
        return

    half = kept_ref.shape[0]
    filled = 3 * INNER // 2
    dq = dq_ref[...].astype(LOW)
    rows = jnp.concatenate([dot_tn(dq, a_own_ref[...]), weights], axis=0).astype(LOW)
    empty = jnp.zeros((half - filled, width_of(kept_ref)), LOW)
    for part in range(2):
        put_half(core, kept_ref, sent_ref, part * half, rows[part * filled : (part + 1) * filled])
        put_half(core, kept_ref, sent_ref, part * half + filled, empty)
    for part in range(2):
        rows = slice(part * block, (part + 1) * block)
        at = pl.ds(pl.multiple_of(part * mine + core * block, block), block)
        dq_kept_ref[rows, :] = dq_ref[at, :]
        at = pl.ds(pl.multiple_of(part * mine + (1 - core) * block, block), block)
        dq_sent_ref[rows, :] = dq_ref[at, :].astype(LOW)


def width_of(ref):
    return ref.shape[1]


def table_kernel(sc_ref, near_out, marks_ref, onehot_ref, kept_in, kept_ref, small_ref, sem):
    core = sc_ref[0, CORE]
    lane = lanes_of(1, WIDTH2)
    tiles_in_chunk = marks_ref.shape[1]
    flip = (rows_of(TILE, TILE) + lanes_of(TILE, TILE) == TILE - 1).astype(LOW)
    head_row = rows_of(8, 1)
    table = jnp.zeros((8, WIDTH2), WIDE)
    for part in range(3):
        blocks = jnp.concatenate(
            [near_out[head, part * TILE : (part + 1) * TILE, :] for head in range(HEADS)], axis=1
        )
        turned = sum(dot_nn(flip, piece.astype(LOW)) for piece in three_pieces(blocks))
        sums = jnp.zeros((8, 2 * TILE), WIDE)
        for head in range(HEADS):
            padded = jnp.concatenate(
                [turned[:, head * TILE : (head + 1) * TILE], jnp.zeros((TILE, TILE), WIDE)], axis=1
            )
            skewed = pltpu.roll(padded, 0, 1, stride=1, stride_axis=0)
            sums = jnp.where(head_row == head, jnp.sum(skewed, axis=0, keepdims=True), sums)
        onehot = onehot_ref[part * 2 * TILE : (part + 1) * 2 * TILE, :].astype(LOW)
        table = table + sum(dot_nn(piece.astype(LOW), onehot) for piece in three_pieces(sums))
    query_tile = rows_of(tiles_in_chunk, 1)
    for head in range(HEADS):
        mark = lane - HD * (1 - head % 2)
        inside = (mark >= 8) & (mark < 32)
        kind, tile = mark // 8, mark % 8
        at = (kind - 2) * (tiles_in_chunk) + tile_place(tile, core)
        relative = at - query_tile
        found = marks_ref[head]
        before = (mark == 0) | (inside & (relative < -1))
        after = (mark == 1) | (inside & (relative > 1))
        for chosen, bucket in ((before, FAR_BEFORE), (after, FAR_AFTER)):
            total = jnp.sum(jnp.where(chosen, found, 0.0))
            table = table + jnp.where((head_row == head) & (lane == bucket), total, 0.0)
    small_ref[...] = jnp.zeros_like(small_ref)
    small_ref[:8, :WIDTH2] = table.astype(LOW)
    at = pl.ds(3 * INNER // 2, small_ref.shape[0])
    copy = pltpu.make_async_copy(small_ref, kept_ref.at[at, :], sem)
    copy.start()
    copy.wait()


def chain_kernel(slot, quads, sc_ref, *refs):
    mine, refs = refs[: slot + 1], refs[slot + 1 :]
    up_ref, down_ref = refs[-2:]
    core = sc_ref[0, CORE]
    for column, came, out_ref in ((UP, 0, up_ref), (DOWN, 1, down_ref)):
        edge = jnp.where(core == came, 0, quads - 1)
        for index, dx_ref in enumerate(mine):

            @pl.when(sc_ref[slot, column] == index)
            def _():
                value = dx_ref[...]
                if slot > 0:
                    came_before = refs[came][...].astype(WIDE)
                    total = value.astype(WIDE) + jnp.where(
                        sc_ref[0, QUAD] != edge, came_before, 0.0
                    )
                    value = total.astype(LOW)
                out_ref[...] = value


def join_kernel(sc_ref, kept_ref, got_ref, out_ref):
    side = sc_ref[0, SIDE]
    out_ref[side] = kept_ref[...]
    out_ref[1 - side] = got_ref[...]


def total_kernel(quads, sc_ref, dx_ref, first_ref, second_ref, out_ref):
    quad, core = sc_ref[0, QUAD], sc_ref[0, CORE]
    total = dx_ref[...]
    for came, came_ref in enumerate((first_ref, second_ref)):
        edge = jnp.where(core == came, 0, quads - 1)
        total = total + jnp.where(quad != edge, came_ref[...].astype(WIDE), 0.0)
    out_ref[...] = total


def input_kernel(
    sc_ref, dx_ref, dq_ref, dq_got_ref, x_ref, grad_res_ref, wq_ref, gain_ref, keep_ref, send_ref
):
    side = sc_ref[0, SIDE]
    block = x_ref.shape[0] // 2
    gain = gain_ref[...]
    for part in range(2):
        rows = slice(part * block, (part + 1) * block)
        queries = (dq_ref[rows, :] + dq_got_ref[rows, :].astype(WIDE)).astype(LOW)
        grad_in = dot_nt(queries, wq_ref[...]) + dx_ref[rows, :]
        x = x_ref[rows, :].astype(WIDE)
        scale = rms_scale(x)
        z = x * scale
        u = grad_in * gain
        result = grad_res_ref[rows, :] + scale * (u - z * jnp.mean(u * z, axis=-1, keepdims=True))
        result = result.astype(LOW)

        @pl.when(side == part)
        def _():
            keep_ref[...] = result

        @pl.when(side != part)
        def _():
            send_ref[...] = result


def tie_kernel(sc_ref, *refs):
    pass


def add_kernel(sc_ref, order_ref, *refs):
    outs = refs[-order_ref.shape[0] :]
    ins = refs[: len(refs) - len(outs)]
    for index, out_ref in enumerate(outs):
        which = order_ref[index]
        total = ins[0][which].astype(WIDE)
        for in_ref in ins[1:]:
            total = total + in_ref[which].astype(WIDE)
        out_ref[...] = total.astype(LOW)


def tree_kernel(sc_ref, *refs):
    values = [ref[...].astype(WIDE) for ref in refs[:-1]]
    while len(values) > 1:
        values = [values[n] + values[n + 1] for n in range(0, len(values), 2)]
    refs[-1][...] = values[0].astype(LOW)


def place_kernel(sc_ref, owner_ref, *refs):
    out_ref = refs[-1]
    for index, part_ref in enumerate(refs[:-1]):
        out_ref[owner_ref[index]] = part_ref[...]


def whole_rows(core, kept_ref, got_ref, first, count):
    half = kept_ref.shape[0]
    parts = []
    for number in range(2):
        low, high = max(first, number * half), min(first + count, (number + 1) * half)
        if low < high:
            rows = slice(low - number * half, high - number * half)
            part = jnp.where(core == number, kept_ref[rows, :], got_ref[rows, :])
            parts.append(part.astype(WIDE))
    return parts[0] if len(parts) == 1 else jnp.concatenate(parts, axis=0)


def unpack_feed_kernel(sc_ref, kept_ref, got_ref, out_ref, gate_ref, up_ref, down_ref, gain_ref):
    take = functools.partial(whole_rows, sc_ref[0, CORE], kept_ref, got_ref)
    width, hidden = gate_ref.shape
    row = 0
    for grads in (gate_ref, up_ref):
        for start in range(0, hidden, width):
            grads[:, start : start + width] = take(row, width)
            row += width
    down_ref[...] = take(row, hidden)
    row += hidden
    out_ref[...] = take(row, INNER)
    row += INNER
    gain_ref[...] = take(row, 16)[0:1, :]


def unpack_last_kernel(
    sc_ref, kept_ref, got_ref, wq_ref, wk_ref, wv_ref, gain_ref, query_ref, key_ref, value_ref, table_ref, gain_grad_ref,
):
    core = sc_ref[0, CORE]
    filled = 3 * INNER // 2
    first = jnp.where(core == 0, kept_ref[...], got_ref[...]).astype(WIDE)
    second = jnp.where(core == 0, got_ref[...], kept_ref[...]).astype(WIDE)
    grads = jnp.concatenate([first[:filled], second[:filled]], axis=0)
    total = jnp.zeros(gain_ref.shape, WIDE)
    for kind, (w_ref, out_ref) in enumerate(
        ((wq_ref, query_ref), (wk_ref, key_ref), (wv_ref, value_ref))
    ):
        part = grads[kind * INNER : (kind + 1) * INNER]
        out_ref[...] = part.T
        total = total + jnp.sum(part * w_ref[...].T.astype(WIDE), axis=0, keepdims=True)
    gain_grad_ref[...] = total / gain_ref[...]
    small = first[filled : filled + 8] + second[filled : filled + 8]
    table_ref[...] = small[:HEADS, :BUCKETS]


def staged_sum(kept, sent, between, plan, plan_out, add, place, whole=None, tree=None):
    came = [kept, lax.ppermute(sent, "blk", between)]
    after = yield sent
    for axes, size, index, peer, pairs in plan:
        order = jnp.stack([index] + [peer(index, shift) for shift in range(1, size)])
        own, *sends = add(order.astype(jnp.int32), came, after)
        came = [own] + [
            lax.ppermute(part, axes, pairs(shift)) for shift, part in enumerate(sends, 1)
        ]
        after = yield own
    (value,) = add(jnp.zeros((1,), jnp.int32), came, after)
    if whole is not None:
        axes, size, _, _, pairs = whole
        came = [value] + [lax.ppermute(value, axes, pairs(shift)) for shift in range(1, size)]
        after = yield value
        value = tree(came, after)
    for axes, size, index, peer, pairs in plan_out:
        came = [lax.ppermute(value, axes, pairs(shift)) for shift in range(1, size)]
        after = yield value
        owners = jnp.stack([index] + [peer(index, -shift) for shift in range(1, size)])
        value = place(owners.astype(jnp.int32), [value] + came, after)
    got = lax.ppermute(value, "blk", between)
    after = yield value
    yield (value, got)


def advance(stages, count, after):
    for _ in range(count):
        tie = stages.send((after,))
    return tie


def finish(stages):
    for now in iter(lambda: stages.send(()), None):
        if isinstance(now, tuple):
            return now


def nearest_order(quads):
    return [
        sorted(range(quads), key=lambda k: (abs(k - place), k)) for place in range(quads)
    ]


def chunk_plan(quads):
    plans = []
    for place in range(quads):
        due = [(quads - 1 + place - d, d) for d in range(place + 1, quads)]
        due += [(quads - 1 - place + d, d) for d in range(place)]
        order = [d for _, d in sorted(due)] + [place]
        rows = []
        for slot in range(quads):
            up, down = quads - 1 + place - slot, place - (quads - 1) + slot
            rows.append(
                (
                    order[slot],
                    order.index(up) if place < up < quads else -1,
                    order.index(down) if 0 <= down < place else -1,
                )
            )
        plans.append(rows)
    return plans


def onehot_tables():
    thresholds = bucket_edges()

    def bucket(offset):
        half_count, exact_count, edges = thresholds
        distance = abs(offset)
        beyond = sum(distance >= edge for edge in edges)
        return (half_count if offset > 0 else 0) + (
            distance if distance < exact_count else exact_count + beyond
        )

    rows = np.zeros((BUCKETS, 2 * TURN), np.float32)
    for turn in range(TURN):
        back = turn if turn < TILE else turn - TURN
        rows[bucket(-TILE - back), turn] = 1.0
        rows[bucket(TILE + back), TURN + turn] = 1.0
    diagonals = np.zeros((6 * TILE, WIDTH2), np.float32)
    for part in range(3):
        for at in range(2 * TILE - 1):
            diagonals[part * 2 * TILE + at, bucket(1 + at - TILE * part)] = 1.0
    return rows, diagonals


def body(
    hidden_in,
    item_lengths,
    live_mask,
    cotangent,
    query_weight,
    key_weight,
    value_weight,
    output_weight,
    bucket_bias_table,
    norm_attention,
    norm_feed,
    gate_weight,
    up_weight,
    down_weight,
):
    streams, block, width = hidden_in.shape
    hidden = gate_weight.shape[1]
    blocks = lax.axis_size("blk")
    parts = lax.axis_size("dp")
    quads = blocks // 4
    here = lax.axis_index("blk")
    replica = lax.axis_index("dp")
    core, side, quad = here % 2, (here // 2) % 2, here // 4
    mine, chunk = 2 * block, 4 * block

    across = [(k, k ^ 2) for k in range(blocks)]
    between = [(k, k ^ 1) for k in range(blocks)]
    onward = []
    for k in range(blocks):
        if k % 2 == 0:
            onward.append((k, k + 4 if k + 4 < blocks else k + 1))
        else:
            onward.append((k, k - 4 if k >= 4 else k - 1))

    order = nearest_order(quads)
    distances = [
        sorted({abs(order[place][step] - place) for place in range(quads)}) for step in range(quads)
    ]
    spots = jnp.asarray(np.array(order, np.int32).T)
    nearest = jnp.asarray(np.array([found[0] for found in distances], np.int32))[:, None]
    is_here = jnp.arange(quads, dtype=jnp.int32)[None, :] == quad
    place = jnp.sum(jnp.where(is_here, spots, 0), axis=1, keepdims=True)
    swapped = ((place > quad) != (core == 1)) & (place != quad)
    source = 2 * (jnp.abs(place - quad) - nearest) + swapped.astype(jnp.int32)
    first_end = jnp.where(side == 0, item_lengths[0, 0], item_lengths[1, 0])
    col = jnp.arange(16, dtype=jnp.int32)[None, :]
    plans = np.array(chunk_plan(quads), np.int32)
    mine_of = [
        jnp.sum(jnp.where(is_here, jnp.asarray(plans[:, :, n].T), 0), axis=1, keepdims=True)
        for n in range(3)
    ]
    sc = jnp.where(col == QUAD, quad, 0)
    sc = jnp.where(col == CORE, core, sc)
    sc = jnp.where(col == SIDE, side, sc)
    sc = jnp.where(col == PLACE, place, sc)
    sc = jnp.where(col == SOURCE, source, sc)
    is_first = core == 0
    up_down = [jnp.where(is_first, mine_of[1], mine_of[2]), jnp.where(is_first, mine_of[2], mine_of[1])]
    for at, values in zip((CHUNK, UP, DOWN), (mine_of[0], *up_down)):
        sc = jnp.where(col == at, values, sc)
    sc = jnp.where(col == FIRST_END, first_end, sc).astype(jnp.int32)

    turned_onehot, diagonal_onehot = (jnp.asarray(t) for t in onehot_tables())

    smem = pl.BlockSpec(memory_space=pltpu.SMEM)
    vmem = pl.BlockSpec(memory_space=pltpu.VMEM)
    anywhere = pl.BlockSpec(memory_space=pl.ANY)
    shape = jax.ShapeDtypeStruct
    strip_rows_count = 2 * chunk - TILE
    near_shape = pltpu.VMEM((HEADS, NEAR, TILE), WIDE)
    strip_shape = pltpu.VMEM((HEADS, strip_rows_count, TILE), WIDE)
    gen_shape = pltpu.VMEM((chunk, mine), WIDE)
    dma = pltpu.SemaphoreType.DMA
    pairs_in_chunk = mine * chunk * HEADS

    def call(kernel, name, in_specs, out_specs, out_shape, scratch, operands, grid=(1,), aliases=None, us=5.0, after=(), limit=24,
             mark=False):
        count = 1 + len(operands)
        if mark:
            out_specs, out_shape = tuple(out_specs) + (vmem,), tuple(out_shape) + (shape((8, 128), WIDE),)
        last = count + len(after) + (len(out_shape) - 1 if mark else 0)

        def without_ties(*refs):
            if mark:
                refs[last][...] = jnp.zeros((8, 128), WIDE)
                refs = refs[:last] + refs[last + 1 :]
            kernel(*refs[:count], *refs[count + len(after) :])

        return pl.pallas_call(
            without_ties if after or mark else kernel,
            grid_spec=pltpu.PrefetchScalarGridSpec(
                num_scalar_prefetch=1,
                grid=grid,
                in_specs=list(in_specs) + [anywhere] * len(after),
                out_specs=out_specs,
                scratch_shapes=scratch,
            ),
            out_shape=out_shape,
            input_output_aliases=aliases or {},
            compiler_params=pltpu.CompilerParams(vmem_limit_bytes=limit * 1024 * 1024),
            cost_estimate=pl.CostEstimate(
                flops=int(us * (1e9 if us >= 4 else 1e7)), bytes_accessed=1 << 12, transcendentals=0
            ),
            name=name,
        )(sc, *operands, *after)

    def far_away(array):
        return pltpu.with_memory_space_constraint(array, pltpu.HBM)

    def tied(arrays, after):
        count = len(arrays)
        return call(
            tie_kernel, "tie", [anywhere] * count, (anywhere,) * count,
            tuple(shape(a.shape, a.dtype) for a in arrays), [], arrays,
            aliases={1 + n: n for n in range(count)}, us=0.3, after=after, limit=16,
        )

    def pick(both, index):
        return lax.dynamic_index_in_dim(both, index, 0, False)

    live_rows = jnp.pad(live_mask.astype(LOW)[:, None, :], ((0, 0), (0, 15), (0, width - block)))
    payload = jnp.concatenate([pick(hidden_in, 1 - side), pick(live_rows, 1 - side)], axis=0)
    got = lax.ppermute(payload, "blk", across)
    packed, x_low = call(
        norm_kernel, "norm_rows", [vmem] * 4, (vmem,) * 2,
        (shape((mine + 16, width), LOW), pltpu.HBM((mine, width), LOW)), [],
        (hidden_in, live_mask, got, norm_attention[None, :]), us=2.0, limit=56,
    )
    own_chunk = jnp.concatenate([packed, lax.ppermute(packed, "blk", between)], axis=0)
    cot_got = lax.ppermute(pick(cotangent, 1 - side), "blk", across)

    qkv_shape = pltpu.HBM((quads * chunk, 3 * INNER), LOW)
    ext_shape = pltpu.HBM((quads * chunk, WIDTH2), LOW)
    state_shapes = (shape((INNER, mine), WIDE), shape((16, mine), WIDE))

    def chunk_out(step, columns):
        return pl.BlockSpec((chunk, columns), lambda i, sc: (sc[step, PLACE], 0))

    a_shape = pltpu.HBM((quads * chunk, width), LOW)
    chunk_scratch = [pltpu.VMEM((2, 16, width), LOW)]
    held = lax.ppermute(own_chunk, "blk", onward)
    rowk, rowq, vec = call(
        places_kernel, "places", [smem] + [vmem] * 3, (vmem,) * 3,
        (shape((8, chunk), WIDE), shape((8, mine), WIDE), shape((8, 2 * TURN), WIDE)), [],
        (item_lengths, packed, bucket_bias_table, turned_onehot), us=2.0, after=(own_chunk,), limit=16,
    )
    qkv, ext, normed, qx, acc, ml, q_own = call(
        forward_own_kernel, "attend_own", [smem, anywhere] + [vmem] * 6,
        (chunk_out(0, 3 * INNER), chunk_out(0, WIDTH2), chunk_out(0, width), vmem, vmem, vmem, vmem),
        (qkv_shape, ext_shape, a_shape, shape((HEADS, 2 * WIDTH2, mine), LOW)) + state_shapes
        + (shape((chunk, INNER), LOW),),
        chunk_scratch + [strip_shape, near_shape, gen_shape, dma((6,))],
        (bucket_bias_table, own_chunk, key_weight, value_weight, query_weight, vec, rowq, rowk),
        us=12.0,
    )

    came = []
    for step in range(1, quads):
        held, acc = lax.optimization_barrier((held, acc))
        came.append((held, lax.ppermute(held, "blk", between)))
        if step + 1 < quads:
            held = lax.ppermute(held, "blk", onward)
        arrays = [array for distance in distances[step] for array in came[distance - 1]]
        qkv, ext, normed, acc, ml = call(
            functools.partial(forward_kernel, step, len(arrays)), "attend_other",
            [smem] + [vmem] * 7 + [anywhere] * (3 + len(arrays)),
            (chunk_out(step, 3 * INNER), chunk_out(step, WIDTH2), chunk_out(step, width), vmem, vmem),
            (qkv_shape, ext_shape, a_shape) + state_shapes,
            chunk_scratch + [near_shape, dma((6,))],
            (bucket_bias_table, key_weight, value_weight, query_weight, vec, qx, acc, ml, qkv, ext, normed, *arrays),
            aliases={7: 3, 8: 4, 9: 0, 10: 1, 11: 2}, us=10.0,
        )

    (do_mine, out_kept, out_sent, grad_res, act, feed, grad_gate, grad_up,
     context, branch, gain_grad, cot) = call(
        middle_kernel, "feed_both_ways", [vmem] * 11, (vmem,) * 12,
        (
            shape((mine, INNER + WIDTH2), LOW),
            shape((block, width), LOW), shape((block, width), LOW), pltpu.HBM((mine, width), WIDE),
            shape((mine, hidden), LOW), shape((mine, width), LOW), shape((mine, hidden), LOW),
            shape((mine, hidden), LOW), shape((mine, INNER), LOW), shape((mine, width), LOW),
            shape((8, width), WIDE), shape((mine, width), LOW),
        ), [],
        (
            acc, ml, x_low, cotangent, cot_got, rowq, output_weight, gate_weight, up_weight, down_weight,
            norm_feed[None, :],
        ),
        us=12.0,
    )
    do_other = lax.ppermute(do_mine, "blk", between)
    def joined(kept, got, after):
        return call(
            join_kernel, "join", [vmem] * 2, (vmem,), (pltpu.HBM((2, block, width), LOW),), [], (kept, got),
            us=1.0, after=after, limit=16, mark=True,
        )

    def over_blocks(shift):
        return [(k, k ^ (4 * shift)) for k in range(blocks)]

    over_side = ("blk", 2, side, lambda i, s: i ^ 1, lambda s: across)
    over_parts = (
        "dp", parts, replica, lambda i, s: (i + s) % parts,
        lambda s: [(k, (k + s) % parts) for k in range(parts)],
    )
    over_quads = ("blk", quads, quad, lambda i, s: i ^ abs(s), over_blocks)
    if parts == 2:

        def square_pairs(shift):
            pairs = []
            for k in range(blocks):
                for r in range(parts):
                    k2, r2 = k ^ (2 * (shift >> 1)), r ^ (shift & 1)
                    pairs.append((k * parts + r, k2 * parts + r2))
            return pairs

        over_square = (("blk", "dp"), 4, side * 2 + replica, lambda i, s: i ^ abs(s), square_pairs)
        plan = [over_square, over_quads]
    else:
        plan = [over_side, over_parts, over_quads]
    plan_out = plan[::-1]
    groups = len(plan) - 1
    pieces_in_all = 8 * 2 * 2 * parts * quads

    def padded(rows):
        return -(-rows // pieces_in_all) * pieces_in_all

    feed_rows = padded(3 * hidden + INNER + 8) // 2
    feed_kept, feed_sent = call(
        feed_grads_kernel, "feed_weight_grads", [vmem] * 8, (vmem, vmem),
        (shape((feed_rows, width), LOW),) * 2, [],
        (act, feed, grad_gate, grad_up, context, branch, cot, gain_grad), us=7.0,
    )
    def add_parts(order, arrays, after):
        size = order.shape[0]
        split = [a.reshape((size, a.shape[0] // size, a.shape[1])) for a in arrays]
        return call(
            add_kernel, "add_parts", [smem] + [vmem] * len(split), (vmem,) * size,
            (shape(split[0].shape[1:], LOW),) * size, [], (order, *split), us=2.0, after=after, limit=16,
        )

    def place_parts(owners, arrays, after):
        one = arrays[0].shape
        whole = call(
            place_kernel, "place_parts", [smem] + [vmem] * len(arrays), vmem,
            shape((len(arrays),) + one, LOW), [], (owners, *arrays), us=1.0, after=after, limit=16,
        )
        return whole.reshape((-1,) + one[1:])

    def tree_parts(arrays, after):
        return call(
            tree_kernel, "tree_parts", [vmem] * len(arrays), vmem, shape(arrays[0].shape, LOW), [], tuple(arrays),
            us=1.0, after=after, limit=16,
        )

    feed_stages = staged_sum(feed_kept, feed_sent, between, plan, plan_out, add_parts, place_parts)
    next(feed_stages)
    out_got = lax.ppermute(out_sent, "blk", across)
    tie = feed_stages.send(())
    do_chunk = call(
        order_kernel, "order", [vmem] * 2, vmem, shape((chunk, INNER + WIDTH2), LOW), [], (do_mine, do_other),
        us=1.0, after=(tie,), limit=16,
    )

    ties = [tie]

    qkv, ext, normed = far_away(qkv), far_away(ext), far_away(normed)
    backward = [(end, start) for start, end in onward]
    last_rows = padded(3 * INNER + 32) // 2
    state_shape = (
        shape((chunk, INNER), WIDE), shape((2 * INNER, width), WIDE), shape((HEADS, NEAR, TILE), WIDE),
        shape((HEADS, chunk // TILE, WIDTH2), WIDE),
    )

    def chunk_rows(slot, n, columns):
        return pl.BlockSpec(
            (block, columns), lambda i, sc: (4 * sc[slot, CHUNK] + sc[0, CORE] + 2 * n, 0)
        )

    state, gradients, came = (), [], ()
    for slot in range(quads):
        own = slot == quads - 1
        operands = (
            bucket_bias_table, do_chunk, q_own, qkv, qkv, normed, normed, ext, ext, key_weight, value_weight, vec,
        ) + tuple(state)
        in_specs = [
            smem, vmem, vmem,
            chunk_rows(slot, 0, 2 * INNER), chunk_rows(slot, 1, 2 * INNER),
            chunk_rows(slot, 0, width), chunk_rows(slot, 1, width),
            chunk_rows(slot, 0, WIDTH2), chunk_rows(slot, 1, WIDTH2), vmem, vmem, vmem,
        ] + [vmem] * len(state)
        scratch = [
            near_shape, pltpu.VMEM((2, chunk + 2 * TILE, mine), LOW), pltpu.VMEM((2 * INNER, mine), LOW),
        ]
        outs = (shape((mine, width), WIDE if own else LOW),)
        if own:
            operands += (ext, rowq, normed)
            in_specs += [
                pl.BlockSpec((chunk, WIDTH2), lambda i, sc: (sc[0, QUAD], 0)), vmem,
                pl.BlockSpec((chunk, width), lambda i, sc: (sc[0, QUAD], 0)),
            ]
            outs += (shape((last_rows, width), LOW),) * 2
            outs += (shape((mine, INNER), WIDE), shape((mine, INNER), LOW)) + state_shape[2:]
            scratch = [pltpu.VMEM((chunk, INNER), WIDE), strip_shape, gen_shape] + scratch
        else:
            outs += state_shape
        found = call(
            functools.partial(chunk_kernel, slot, own), "grad_chunk", in_specs, (vmem,) * len(outs), outs, scratch,
            operands, us=10.0, after=ties, limit=32 if own else 28,
            aliases={13 + n: 1 + n for n in range(4)} if slot and not own else None,
        )
        gradients.append(found[0])
        if own:
            kept, sent, dq_kept, dq_sent, near_grad, marks = found[1:]
            break
        state = found[1:]
        ties = []
        if 0 < slot < 3:
            ties.append(advance(feed_stages, 1 if slot == 1 else groups, found[0]))
        up, down = call(
            functools.partial(chain_kernel, slot, quads), "chain", [vmem] * (len(gradients) + len(came)), (vmem,) * 2,
            (shape((mine, width), LOW),) * 2, [], tuple(gradients) + tuple(came), us=1.0, after=ties, limit=16,
        )
        came = (lax.ppermute(up, "blk", onward), lax.ppermute(down, "blk", backward))
        ties = ties + [up]
        if slot == 0:
            ties.append(advance(feed_stages, groups, up))
            ties.append(out_got)
    total = call(
        functools.partial(total_kernel, quads), "total", [vmem] * 3, vmem, shape((mine, width), WIDE), [],
        (gradients[-1], *came), us=1.0, after=(kept,), limit=16,
    )
    tie = advance(feed_stages, 1, total)
    sent, dq_sent = tied((sent, dq_sent), (tie,))
    kept = call(
        table_kernel, "bias_table", [vmem] * 3 + [anywhere], anywhere, shape(kept.shape, LOW),
        [pltpu.VMEM((16, width), LOW), dma], (near_grad, marks, diagonal_onehot, kept),
        aliases={4: 0}, us=2.0, after=(sent,), limit=16,
    )
    last_stages = staged_sum(
        kept, sent, between, plan[:-1], plan_out[1:], add_parts, place_parts, over_quads, tree_parts
    )
    next(last_stages)
    dq_got = lax.ppermute(dq_sent, "blk", between)
    feed_kept, feed_got = feed_stages.send(())
    output, tie = joined(out_kept, out_got, (tie,))
    tie = advance(last_stages, 1, tie)
    in_kept, in_sent = call(
        input_kernel, "grad_input", [vmem] * 7, (vmem,) * 2,
        (shape((block, width), LOW), shape((block, width), LOW)), [],
        (total, dq_kept, dq_got, x_low, grad_res, query_weight, norm_attention[None, :]),
        us=2.0, after=(tie,),
    )
    grad_out, grad_gate, grad_up, grad_down, grad_norm_feed, mark = call(
        unpack_feed_kernel, "unpack_feed", [vmem] * 2, (vmem,) * 5,
        (
            pltpu.HBM((INNER, width), WIDE), pltpu.HBM((width, hidden), WIDE), pltpu.HBM((width, hidden), WIDE),
            pltpu.HBM((hidden, width), WIDE), pltpu.HBM((1, width), WIDE),
        ), [],
        (feed_kept, feed_got), us=3.9, after=(in_kept,), mark=True,
    )
    (in_sent,) = tied((in_sent,), (mark,))
    for _ in range(groups):
        tie = last_stages.send((mark,))
    in_got = lax.ppermute(in_sent, "blk", across)
    input_gradient, mark = joined(in_kept, in_got, (tie,))
    last_stages.send((mark,))
    for _ in range(groups):
        last_stages.send(())
    last_kept, last_got = finish(last_stages)
    grad_query, grad_key, grad_value, grad_table, grad_norm_attention = call(
        unpack_last_kernel, "unpack_attention", [vmem] * 6, (vmem,) * 5,
        (pltpu.HBM((width, INNER), WIDE),) * 3 + (shape((HEADS, BUCKETS), WIDE), shape((1, width), WIDE)), [],
        (last_kept, last_got, query_weight, key_weight, value_weight, norm_attention[None, :]), us=2.0,
    )
    return (
        output,
        input_gradient,
        grad_query,
        grad_key,
        grad_value,
        grad_out,
        grad_table.T,
        grad_norm_attention[0],
        grad_norm_feed[0],
        grad_gate,
        grad_up,
        grad_down,
    )


def solution(mesh):
    return jax.shard_map(
        body,
        mesh=mesh,
        in_specs=(
            P("dp", "blk", None),
            P("dp", None),
            P("dp", "blk"),
            P("dp", "blk", None),
            P(),
            P(),
            P(),
            P(),
            P(),
            P(),
            P(),
            P(),
            P(),
            P(),
        ),
        out_specs=(
            P("dp", "blk", None),
            P("dp", "blk", None),
            P(),
            P(),
            P(),
            P(),
            P(),
            P(),
            P(),
            P(),
            P(),
            P(),
        ),
        check_vma=False,
    )
```

```python
import functools

import jax
import jax.numpy as jnp
import numpy as np
from jax import lax
from jax.experimental import pallas as pl
from jax.experimental.pallas import tpu as pltpu
from jax.sharding import PartitionSpec as P

HEADS = 6
HD = 64
WIDTH2 = 2 * HD
PAIRS = HEADS // 2
INNER = HEADS * HD
BUCKETS = 32
MAXDIST = 128
EPSILON = 1e-06
BIG = 1e30
TILE = 128
NEAR = 3 * TILE
TURN = 4 * TILE
FAR_BEFORE = BUCKETS // 2 - 1
FAR_AFTER = BUCKETS - 1
LOW = jnp.bfloat16
WIDE = jnp.float32
GELU_A = 0.7978845608028654
GELU_B = 0.044715

QUAD, CORE, SIDE, PLACE, SOURCE, FIRST_END, CHUNK, UP, DOWN = range(9)
MASK, BEFORE, AFTER, PEN, STAT, LIVE, SEG = 0, 1, 2, 7, 8, 11, 12
ONE_A, OFF, ONE_B, ONE_C, ONE_D = 36, 37, 38, 39, 40


def bucket_edges():
    half_count = BUCKETS // 2
    exact_count = half_count // 2
    log_levels = half_count - exact_count
    thresholds = []
    for level_index in range(1, log_levels):
        candidate = exact_count
        while (
            candidate**log_levels * exact_count**level_index
            < MAXDIST**level_index * exact_count**log_levels
        ):
            candidate = candidate + 1
        thresholds.append(candidate)
    return (half_count, exact_count, thresholds)


def dot_nt(left, right):
    return lax.dot_general(
        left, right, (((1,), (1,)), ((), ())), preferred_element_type=WIDE
    )


def dot_nn(left, right):
    return jnp.dot(left, right, preferred_element_type=WIDE)


def dot_tn(left, right):
    return lax.dot_general(
        left, right, (((0,), (0,)), ((), ())), preferred_element_type=WIDE
    )


def rows_of(count, width):
    return lax.broadcasted_iota(jnp.int32, (count, width), 0)


def lanes_of(count, width):
    return lax.broadcasted_iota(jnp.int32, (count, width), 1)


def lane_half(array, half, other):
    return jnp.where(lanes_of(1, WIDTH2) // HD == half, array, other)


def row_half(array, half, other):
    return jnp.where(rows_of(WIDTH2, 1) // HD == half, array, other)


def pair_slice(pair, base=0):
    return slice(base + pair * WIDTH2, base + (pair + 1) * WIDTH2)


def tile_place(tile, core):
    return (tile // 2) * 4 + core * 2 + tile % 2


def rms_scale(values):
    return lax.rsqrt(jnp.mean(values * values, axis=-1, keepdims=True) + EPSILON)


def three_pieces(values):
    high = values.astype(LOW).astype(WIDE)
    mid = (values - high).astype(LOW).astype(WIDE)
    low = (values - high - mid).astype(LOW).astype(WIDE)
    return high, mid, low


def pipelined(items, first, second, depth):
    ahead = []
    for item in items:
        ahead.append((item, first(item)))
        if len(ahead) > depth:
            second(*ahead.pop(0))
    for waiting in ahead:
        second(*waiting)


def far_bias(table_ref, after, head):
    return table_ref[FAR_AFTER if after else FAR_BEFORE, head]


def build_near(near_ref, vec_ref, back, heads):
    for index, head in enumerate(heads):
        row = vec_ref[head : head + 1, back * TURN : (back + 1) * TURN]
        row = jnp.broadcast_to(row, (NEAR, TURN))
        near_ref[index] = pltpu.roll(row, 0, 1, stride=1, stride_axis=0)[:, :TILE]


def build_strip(strip_ref, near_ref, table_ref, back, chunk, heads):
    edge = chunk - TILE
    rest = strip_ref.shape[1] - edge - 2 * TILE
    for index, head in enumerate(heads):
        far_before = far_bias(table_ref, back, head)
        far_after = far_bias(table_ref, not back, head)
        strip_ref[index, : edge - TILE, :] = jnp.full((edge - TILE, TILE), far_before, WIDE)
        strip_ref[index, edge - TILE : edge + 2 * TILE, :] = near_ref[index]
        strip_ref[index, edge + 2 * TILE :, :] = jnp.full((rest, TILE), far_after, WIDE)


def strip_rows(strip_ref, index, first_tile, tiles, core, chunk):
    parts = []
    for tile in range(first_tile, first_tile + tiles):
        start = (chunk - TILE) - tile_place(tile, core) * TILE
        parts.append(strip_ref[index, pl.ds(pl.multiple_of(start, TILE), chunk), :])
    return jnp.concatenate(parts, axis=1)


def near_fixes(near_ref, table_ref, flags, index, head, back):
    low, high = flags
    return (
        low * (near_ref[index, :TILE, :] - far_bias(table_ref, back, head)),
        high * (near_ref[index, 2 * TILE :, :] - far_bias(table_ref, not back, head)),
    )


def fix_near(scores, step, steps, fixes):
    low, high = fixes
    chunk, width = scores.shape
    if step == 0:
        last = jnp.concatenate(
            [scores[chunk - TILE :, :TILE] + low, scores[chunk - TILE :, TILE:]], axis=1
        )
        scores = jnp.concatenate([scores[: chunk - TILE], last], axis=0)
    if step == steps - 1:
        first = jnp.concatenate(
            [scores[:TILE, : width - TILE], scores[:TILE, width - TILE :] + high], axis=1
        )
        scores = jnp.concatenate([first, scores[TILE:]], axis=0)
    return scores


def near_flags(place, quad, core):
    low = jnp.where((place == quad - 1) & (core == 0), 1.0, 0.0)
    high = jnp.where((place == quad + 1) & (core == 1), 1.0, 0.0)
    return low, high


def natural_row(even, odd):
    block = even.shape[1] // 2
    return jnp.concatenate(
        [even[:, :block], odd[:, :block], even[:, block:], odd[:, block:]], axis=1
    )


def key_columns(rows, lanes):
    places = rows[0].shape[1]
    stack = jnp.zeros((16, places), WIDE)
    spread = jnp.zeros((16, WIDTH2), WIDE)
    number, lane = rows_of(16, 1), lanes_of(16, WIDTH2)
    for index, row in enumerate(rows):
        stack = jnp.where(number == index, row, stack)
    for index, at, scale in lanes:
        spread = jnp.where((number == index) & (lane == at), scale, spread)
    return dot_tn(stack.astype(LOW), spread.astype(LOW))


def visible_mask(gen_ref, segment_column, segment_row, live, core, keys_down):
    chunk, mine = gen_ref.shape
    down = rows_of(chunk, 1)
    for tile in range(mine // TILE):
        lanes = slice(tile * TILE, (tile + 1) * TILE)
        across = tile_place(tile, core) * TILE + lanes_of(1, TILE)
        alive = live if keys_down else live[:, lanes]
        visible = (segment_column == segment_row[:, lanes]) & ((alive > 0.5) | (down == across))
        gen_ref[:, lanes] = jnp.where(visible, 0.0, -BIG)


def project(a, weight_refs, qkv_ref):
    for part, w_ref in enumerate(weight_refs):
        cols = slice(part * INNER, (part + 1) * INNER)
        qkv_ref[:, cols] = dot_nn(a, w_ref[...]).astype(LOW)


def halves_copies(source, swapped, core, rows_ref, live_ref, sems):
    first_core = 1 - core if swapped else core
    block = rows_ref.shape[0] // 4
    half = source.shape[0] // 2
    copies = []
    for index in range(2):
        owner = first_core if index == 0 else 1 - first_core
        for part in range(2):
            at = pl.multiple_of(part * 2 * block + owner * block, block)
            copies.append((source.at[pl.ds(index * half + part * block, block), :], rows_ref.at[pl.ds(at, block), :]))
        if live_ref is not None:
            copies.append((source.at[pl.ds(index * half + 2 * block, 16), :], live_ref.at[owner]))
    return [
        pltpu.make_async_copy(start, end, sems.at[index]) for index, (start, end) in enumerate(copies)
    ]


def start_fetch(sc_ref, step, sources, rows_ref, live_ref, sems):
    core = sc_ref[0, CORE]
    for index, source in enumerate(sources):

        @pl.when(sc_ref[step, SOURCE] == index)
        def _():
            for copy in halves_copies(source, index % 2 == 1, core, rows_ref, live_ref, sems):
                copy.start()


def wait_fetch(sc_ref, sources, rows_ref, live_ref, sems):
    for copy in halves_copies(sources[0], False, sc_ref[0, CORE], rows_ref, live_ref, sems):
        copy.wait()


def norm_kernel(sc_ref, hidden_ref, live_ref, got_ref, gain_ref, packed_ref, x_ref):
    side = sc_ref[0, SIDE]
    block = hidden_ref.shape[1]
    mine = 2 * block
    kept, got = hidden_ref[side], got_ref[:block, :]
    live_kept = live_ref[pl.ds(side, 1), :].astype(WIDE)
    live_got = got_ref[block : block + 16, :block].astype(WIDE)[0:1, :]
    for part in range(2):
        rows = jnp.where(side == part, kept, got)
        x_ref[part * block : (part + 1) * block, :] = rows
        wide = rows.astype(WIDE)
        normed = wide * rms_scale(wide) * gain_ref[...]
        packed_ref[part * block : (part + 1) * block, :] = normed.astype(LOW)
    live = jnp.concatenate(
        [jnp.where(side == 0, live_kept, live_got), jnp.where(side == 0, live_got, live_kept)],
        axis=1,
    )
    packed_ref[mine:, :] = jnp.broadcast_to(live, (16, mine)).astype(LOW)


def places_kernel(sc_ref, lengths_ref, packed_ref, table_ref, onehot_ref, rowk_ref, rowq_ref, vec_ref):
    side, core, quad = sc_ref[0, SIDE], sc_ref[0, CORE], sc_ref[0, QUAD]
    mine, chunk = rowq_ref.shape[1], rowk_ref.shape[1]
    block = mine // 2
    live = packed_ref[mine : mine + 16, :].astype(WIDE)[0:1, :]
    places = quad * chunk + lanes_of(1, chunk)

    def one_item(item, carry):
        end, segment = carry
        end = end + lengths_ref[side, item]
        return end, segment + jnp.where(places >= end, 1.0, 0.0)

    zero = jnp.zeros((1, chunk), WIDE)
    end, segment = lax.fori_loop(0, lengths_ref.shape[1], one_item, (jnp.int32(0), zero))
    rowk_ref[...] = jnp.broadcast_to(segment, (8, chunk))
    own = jnp.concatenate(
        [
            rowk_ref[0:1, pl.ds(pl.multiple_of(part * mine + core * block, block), block)]
            for part in range(2)
        ],
        axis=1,
    )
    number = rows_of(8, 1)
    rowq = jnp.where(number == 0, own, 0.0)
    rowq = jnp.where(number == 2, jnp.where(own > 0.5, BIG, 0.0), rowq)
    rowq = jnp.where(number == 3, live, rowq)
    rowq_ref[...] = rowq
    found = lax.dot_general(
        table_ref[...], onehot_ref[...], (((0,), (0,)), ((), ())),
        precision=lax.Precision.HIGHEST, preferred_element_type=WIDE,
    )
    vec_ref[...] = jnp.concatenate([found, jnp.zeros((8 - HEADS, found.shape[1]), WIDE)], axis=0)


def forward_items(mine):
    steps = mine // (2 * TILE)
    return [(pair, step, hh) for pair in range(PAIRS) for step in range(steps) for hh in range(2)]


def forward_operands(qkv_ref, ext):
    made = {}

    def operands(pair):
        if pair not in made:
            k_ext = jnp.concatenate([qkv_ref[:, pair_slice(pair)], ext], axis=1)
            v_turned = qkv_ref[:, pair_slice(pair, INNER)].T
            made[pair] = (
                k_ext, [row_half(v_turned, hh, jnp.ones_like(v_turned)) for hh in range(2)]
            )
        return made[pair]

    return operands


def step_lanes(step):
    return slice(step * 2 * TILE, (step + 1) * 2 * TILE)


def head_rows(head):
    return slice(head * HD, (head + 1) * HD)


def forward_own_kernel(
    sc_ref, table_ref, source_ref, wk_ref, wv_ref, wq_ref, vec_ref, rowq_ref, rowk_ref,
    qkv_ref, ext_ref, a_ref, qx_ref, acc_ref, ml_ref, q_own_ref,
    live_ref, strip_ref, near_ref, gen_ref, sems,
):
    core = sc_ref[0, CORE]
    chunk = qkv_ref.shape[0]
    mine = acc_ref.shape[1]
    block = mine // 2
    start_fetch(sc_ref, 0, [source_ref], a_ref, live_ref, sems)
    build_near(near_ref, vec_ref, 0, range(HEADS))
    build_strip(strip_ref, near_ref, table_ref, False, chunk, range(HEADS))
    number = rows_of(WIDTH2, 1)
    for head in range(HEADS):
        rows = jnp.where(number == MASK, 1.0, 0.0)
        for which, after in ((BEFORE, False), (AFTER, True)):
            far = jnp.full((1, mine), far_bias(table_ref, after, head), WIDE)
            for piece, value in enumerate(three_pieces(far)):
                rows = jnp.where(number == which + 2 * piece, value, rows)
        rows = jnp.where(number == PEN, -rowq_ref[2:3, :], rows)
        qx_ref[head, WIDTH2:, :] = rows.astype(LOW)
    wait_fetch(sc_ref, [source_ref], a_ref, live_ref, sems)
    project(a_ref[...], (wk_ref, wv_ref, wq_ref), qkv_ref)
    q_own_ref[...] = qkv_ref[:, 2 * INNER :]
    live = natural_row(live_ref[0].astype(WIDE)[0:1, :], live_ref[1].astype(WIDE)[0:1, :])
    columns = key_columns(
        [jnp.ones_like(live), live, rowk_ref[0:1, :]],
        [(0, STAT, 1.0), (0, STAT + 1, 1.0), (0, STAT + 2, 1.0), (1, LIVE, 1.0), (2, SEG, 1.0)],
    )
    ext_ref[...] = columns.astype(LOW)
    visible_mask(
        gen_ref, columns[:, SEG : SEG + 1], rowq_ref[0:1, :], columns[:, LIVE : LIVE + 1], core, True
    )
    for part in range(2):
        at = pl.ds(pl.multiple_of(part * mine + core * block, block), block)
        lanes = slice(part * block, (part + 1) * block)
        for pair in range(PAIRS):
            turned = qkv_ref[at, pair_slice(pair, 2 * INNER)].T
            for hh in range(2):
                qx_ref[2 * pair + hh, :WIDTH2, lanes] = row_half(
                    turned, hh, jnp.zeros_like(turned)
                )
    ml_ref[...] = jnp.zeros_like(ml_ref)
    operands = forward_operands(qkv_ref, ext_ref[...])

    def first(item):
        pair, step, hh = item
        s = dot_nn(operands(pair)[0], qx_ref[2 * pair + hh, :, step_lanes(step)])
        s = s + strip_rows(strip_ref, 2 * pair + hh, 2 * step, 2, core, chunk)
        return s + gen_ref[:, step_lanes(step)]

    def second(item, s):
        pair, step, hh = item
        head, lanes = 2 * pair + hh, step_lanes(step)
        top = jnp.max(s, axis=0, keepdims=True)
        p = jnp.exp(s - top).astype(LOW)
        pv = dot_nn(operands(pair)[1][hh], p)
        ml_ref[head : head + 1, lanes] = top
        ml_ref[8 + head : 9 + head, lanes] = pv[HD * (1 - hh) : HD * (1 - hh) + 1, :]
        acc_ref[head_rows(head), lanes] = pv[hh * HD : (hh + 1) * HD, :]

    pipelined(forward_items(mine), first, second, 2)


def forward_kernel(
    step_number, sources, sc_ref, table_ref, wk_ref, wv_ref, wq_ref, vec_ref, qx_ref, acc_in, ml_in,
    qkv_in, ext_in, a_in, *rest,
):
    source_refs, rest = rest[:sources], rest[sources:]
    qkv_ref, ext_ref, a_ref, acc_ref, ml_ref, live_ref, near_ref, sems = rest
    quad, core, place = (sc_ref[step_number, i] for i in (QUAD, CORE, PLACE))
    chunk = qkv_ref.shape[0]
    mine = acc_ref.shape[1]
    start_fetch(sc_ref, step_number, source_refs, a_ref, live_ref, sems)
    build_near(near_ref, vec_ref, 0, range(HEADS))
    wait_fetch(sc_ref, source_refs, a_ref, live_ref, sems)
    project(a_ref[...], (wk_ref, wv_ref, wq_ref), qkv_ref)
    live = natural_row(live_ref[0].astype(WIDE)[0:1, :], live_ref[1].astype(WIDE)[0:1, :])
    places = place * chunk + lanes_of(1, chunk)
    seen = (live > 0.5) & (places < sc_ref[step_number, FIRST_END])
    is_before = jnp.where(place < quad, 1.0, 0.0)
    is_after = 1.0 - is_before
    marks = [(0, MASK, 1.0), (1, PEN, 1.0)]
    marks += [(1, STAT + n, 1.0) for n in range(3)]
    marks += [(1, BEFORE + 2 * n, is_before) for n in range(3)]
    marks += [(1, AFTER + 2 * n, is_after) for n in range(3)]
    ext = key_columns([jnp.where(seen, 0.0, -BIG), jnp.ones_like(live)], marks).astype(LOW)
    ext_ref[...] = ext
    flags = near_flags(place, quad, core)
    steps = mine // (2 * TILE)
    operands = forward_operands(qkv_ref, ext)

    def first(item):
        pair, step, hh = item
        head = 2 * pair + hh
        s = dot_nn(operands(pair)[0], qx_ref[head, :, step_lanes(step)])
        return fix_near(s, step, steps, near_fixes(near_ref, table_ref, flags, head, head, False))

    def second(item, s):
        pair, step, hh = item
        head, lanes = 2 * pair + hh, step_lanes(step)
        old = ml_in[head : head + 1, lanes]
        top = jnp.maximum(old, jnp.max(s, axis=0, keepdims=True))
        keep = jnp.exp(old - top)
        p = jnp.exp(s - top).astype(LOW)
        pv = dot_nn(operands(pair)[1][hh], p)
        ml_ref[head : head + 1, lanes] = top
        total = ml_in[8 + head : 9 + head, lanes] * keep
        ml_ref[8 + head : 9 + head, lanes] = total + pv[HD * (1 - hh) : HD * (1 - hh) + 1, :]
        rows = head_rows(head)
        acc_ref[rows, lanes] = acc_in[rows, lanes] * keep + pv[hh * HD : (hh + 1) * HD, :]

    pipelined(forward_items(mine), first, second, 2)


def middle_kernel(
    sc_ref, acc_ref, ml_ref, x_ref, cot_in, cot_got, rowq_ref, wo_ref, gate_ref, up_ref, down_ref, gain_ref,
    do_ref, keep_ref, send_ref, grad_res_ref, act_ref, feed_ref, gg_ref, gu_ref,
    ctx_ref, branch_ref, gain_grad_ref, cot_ref,
):
    side = sc_ref[0, SIDE]
    mine = x_ref.shape[0]
    block = mine // 2
    gain = gain_ref[...]
    context = []
    for head in range(HEADS):
        context.append(acc_ref[head_rows(head), :] / ml_ref[8 + head : 9 + head, :])
    for pair in range(PAIRS):
        both = jnp.concatenate(context[2 * pair : 2 * pair + 2], axis=0).astype(LOW)
        ctx_ref[:, pair_slice(pair)] = both.T
    gain_grad = jnp.zeros_like(gain)
    cot_kept = cot_in[side]
    for part in range(2):
        rows = slice(part * block, (part + 1) * block)
        cot_ref[rows, :] = jnp.where(side == part, cot_kept, cot_got[...])

    def first(part):
        rows = slice(part * block, (part + 1) * block)
        residual = x_ref[rows, :].astype(WIDE) + dot_nn(ctx_ref[rows, :], wo_ref[...])
        scale = rms_scale(residual)
        z = residual * scale
        feed = (z * gain).astype(LOW)
        feed_ref[rows, :] = feed
        v = dot_nn(feed, gate_ref[...])
        up = dot_nn(feed, up_ref[...])
        return residual, scale, z, v, up, dot_nt(cot_ref[rows, :], down_ref[...])

    def second(part, made):
        nonlocal gain_grad
        residual, scale, z, v, up, grad_hidden = made
        rows = slice(part * block, (part + 1) * block)
        square = v * v
        t = jnp.tanh(GELU_A * v * (1.0 + GELU_B * square))
        half = 0.5 * (1.0 + t)
        g = v * half
        slope = half + 0.5 * v * (1.0 - t * t) * (GELU_A * (1.0 + 3.0 * GELU_B * square))
        act = (g * up).astype(LOW)
        act_ref[rows, :] = act
        grad_gate = (grad_hidden * up * slope).astype(LOW)
        grad_up = (grad_hidden * g).astype(LOW)
        gg_ref[rows, :] = grad_gate
        gu_ref[rows, :] = grad_up
        grad_feed = dot_nt(grad_gate, gate_ref[...]) + dot_nt(grad_up, up_ref[...])
        u = grad_feed * gain
        gain_grad = gain_grad + jnp.sum(grad_feed * z, axis=0, keepdims=True)
        cot = cot_ref[rows, :].astype(WIDE)
        grad_res = cot + scale * (u - z * jnp.mean(u * z, axis=-1, keepdims=True))
        grad_res_ref[rows, :] = grad_res
        branch = grad_res.astype(LOW)
        branch_ref[rows, :] = branch
        do_ref[rows, :INNER] = dot_nt(branch, wo_ref[...]).astype(LOW)
        output = (residual + dot_nn(act, down_ref[...])).astype(LOW)

        @pl.when(side == part)
        def _():
            keep_ref[...] = output

        @pl.when(side != part)
        def _():
            send_ref[...] = output

    pipelined(range(2), first, second, 1)
    gain_grad_ref[...] = jnp.broadcast_to(gain_grad, gain_grad_ref.shape)
    number = rows_of(WIDTH2, 1)
    stat = jnp.where((number == ONE_A) | ((number >= ONE_B) & (number <= ONE_D)), 1.0, 0.0)
    stat = jnp.where(number == OFF, -rowq_ref[2:3, :], stat)
    for pair in range(PAIRS):
        turned = do_ref[:, pair_slice(pair)].T
        for hh in range(2):
            head = 2 * pair + hh
            grads = turned[hh * HD : (hh + 1) * HD, :].astype(WIDE)
            delta = jnp.sum(grads * context[head], axis=0, keepdims=True)
            lse = ml_ref[head : head + 1, :] + jnp.log(ml_ref[8 + head : 9 + head, :])
            for base, value in ((0, lse), (3 * HEADS, delta)):
                for index, piece in enumerate(three_pieces(-value)):
                    stat = jnp.where(number == base + HEADS * index + head, piece, stat)
    do_ref[:, INNER:] = stat.astype(LOW).T


def put_half(core, keep_ref, send_ref, row, value):
    rows = keep_ref.shape[0]
    half, start = row // rows, row % rows

    @pl.when(core == half)
    def _():
        keep_ref[start : start + value.shape[0], : value.shape[1]] = value

    @pl.when(core != half)
    def _():
        send_ref[start : start + value.shape[0], : value.shape[1]] = value


def put_rows(core, keep_ref, send_ref, row, value):
    rows = keep_ref.shape[0]
    value = value.astype(LOW)
    first = min(value.shape[0], rows - row % rows)
    put_half(core, keep_ref, send_ref, row, value[:first])
    if first < value.shape[0]:
        put_half(core, keep_ref, send_ref, row + first, value[first:])


def feed_grads_kernel(
    sc_ref, act_ref, feed_ref, gg_ref, gu_ref, ctx_ref, branch_ref, cot_ref, gain_grad_ref,
    keep_ref, send_ref,
):
    core = sc_ref[0, CORE]
    put = functools.partial(put_rows, core, keep_ref, send_ref)
    width = keep_ref.shape[1]
    hidden = act_ref.shape[1]
    feed = feed_ref[...].T
    row = 0
    for grads in (gg_ref, gu_ref):
        for start in range(0, hidden, width):
            put(row, dot_nn(feed, grads[:, start : start + width]))
            row += width
    act = act_ref[...].T
    put(row, dot_nn(act, cot_ref[...]))
    row += hidden
    put(row, dot_nn(ctx_ref[...].T, branch_ref[...]))
    row += INNER
    rest = 2 * keep_ref.shape[0] - row
    put(row, jnp.where(rows_of(rest, 1) == 0, gain_grad_ref[0:1, :], 0.0))


def order_kernel(sc_ref, mine_ref, other_ref, out_ref):
    core = sc_ref[0, CORE]
    block = mine_ref.shape[0] // 2
    for owner, ref in ((core, mine_ref), (1 - core, other_ref)):
        for part in range(2):
            at = pl.ds(pl.multiple_of(part * 2 * block + owner * block, block), block)
            out_ref[at, :] = ref[part * block : (part + 1) * block, :]


def chunk_kernel(slot, own, sc_ref, table_ref, do_ref, q_ref, kv0_ref, kv1_ref, a0_ref, a1_ref, e0_ref, e1_ref,
                 wk_ref, wv_ref, vec_ref, *rest):
    if slot > 0:
        (dq_in, w_in, near_in, marks_in), rest = rest[:4], rest[4:]
    if own:
        (extq_ref, rowq_ref, a_own_ref), rest = rest[:3], rest[3:]
        (dx_ref, kept_ref, sent_ref, dq_kept_ref, dq_sent_ref, near_out, marks_ref), rest = rest[:7], rest[7:]
        dq_ref, strip_ref, gen_ref, near_ref, ds_ref, grads_ref = rest
    else:
        dx_ref, dq_ref, w_ref, near_out, marks_ref, near_ref, ds_ref, grads_ref = rest
    quad, core, side_chunk = sc_ref[0, QUAD], sc_ref[0, CORE], sc_ref[slot, CHUNK]
    chunk = q_ref.shape[0]
    block = kv0_ref.shape[0]
    mine = 2 * block
    tiles = mine // TILE
    steps = mine // (2 * TILE)
    number = rows_of(WIDTH2, 1)
    lane = lanes_of(1, WIDTH2)
    build_near(near_ref, vec_ref, 1, range(HEADS))
    ext_turned = jnp.concatenate([e0_ref[...].T, e1_ref[...].T], axis=1).astype(WIDE)
    if own:
        build_strip(strip_ref, near_ref, table_ref, True, chunk, range(HEADS))
        visible_mask(
            gen_ref, extq_ref[...].astype(WIDE)[:, SEG : SEG + 1], rowq_ref[0:1, :], rowq_ref[3:4, :], core, False
        )
        ds_ref[:, :TILE, :] = jnp.zeros((2, TILE, mine), LOW)
        ds_ref[:, chunk + TILE :, :] = jnp.zeros((2, TILE, mine), LOW)
    low, high = near_flags(quad, side_chunk, core)
    keys_before = side_chunk < quad
    gap = side_chunk - quad
    spread = jnp.where(jnp.abs(gap) <= 1, 1, 0)
    first_mark = jnp.where(spread == 1, 16 + 8 * gap, jnp.where(gap < 0, 0, 1))
    mark_of_key = first_mark + spread * (rows_of(mine, 1) // TILE)
    ext = do_ref[:, INNER:]
    made = {}

    def both(pair, base):
        return jnp.concatenate([kv0_ref[:, pair_slice(pair, base)], kv1_ref[:, pair_slice(pair, base)]], axis=0)

    def operands(pair):
        if pair in made:
            return made[pair]
        q_pair, do_pair = q_ref[:, pair_slice(pair)], do_ref[:, pair_slice(pair)]
        k_pair = both(pair, 0)
        k_turned, v_turned = k_pair.T, both(pair, INNER).T
        zero = jnp.zeros_like(k_turned)
        k_sides, v_sides, k_marked = [], [], []
        for hh in range(2):
            head = 2 * pair + hh
            rows = (number == head) | (number == head + HEADS) | (number == head + 2 * HEADS)
            rows = jnp.broadcast_to(jnp.where(rows, 1.0, 0.0), (WIDTH2, mine))
            if not own:
                far = jnp.where(
                    keys_before, far_bias(table_ref, False, head), far_bias(table_ref, True, head)
                )
                wide = jnp.full((1, mine), far, WIDE)
                for at, piece in zip((ONE_A, ONE_B, ONE_C), three_pieces(wide)):
                    rows = jnp.where(number == at, piece, rows)
                rows = jnp.where(number == OFF, 1.0, rows)
                rows = jnp.where(number == ONE_D, ext_turned[MASK : MASK + 1, :], rows)
            k_sides.append(
                jnp.concatenate([row_half(k_turned, hh, zero), rows.astype(LOW)], axis=0)
            )
            first = 3 * HEADS + head
            rows = (number == first) | (number == first + HEADS) | (number == first + 2 * HEADS)
            rows = jnp.broadcast_to(jnp.where(rows, 1.0, 0.0), (WIDTH2, mine)).astype(LOW)
            v_sides.append(jnp.concatenate([row_half(v_turned, hh, zero), rows], axis=0))
            marks = jnp.where(lane - HD * (1 - hh) == mark_of_key, 1.0, 0.0).astype(LOW)
            k_marked.append(lane_half(k_pair, hh, marks))
        made[pair] = (
            jnp.concatenate([q_pair, ext], axis=1), jnp.concatenate([do_pair, ext], axis=1),
            q_pair.T, do_pair.T, k_sides, v_sides, k_marked,
        )
        return made[pair]

    def first(item):
        pair, step, hh = item
        head, lanes = 2 * pair + hh, step_lanes(step)
        q_ext, do_ext, _, _, k_sides, v_sides, _ = operands(pair)
        s = dot_nn(q_ext, k_sides[hh][:, lanes])
        if own:
            s = s + strip_rows(strip_ref, head, 2 * step, 2, core, chunk) + gen_ref[:, lanes]
        else:
            s = fix_near(
                s, step, steps, near_fixes(near_ref, table_ref, (low, high), head, head, True)
            )
        return s, dot_nn(do_ext, v_sides[hh][:, lanes])

    products = {}

    def second(item, found):
        pair, step, hh = item
        head, lanes = 2 * pair + hh, step_lanes(step)
        s, dp = found
        p = jnp.exp(s)
        ds = (p * dp).astype(LOW)
        _, _, q_turned, do_turned, _, _, k_marked = operands(pair)
        half = slice(hh * HD, (hh + 1) * HD)
        grads_ref[head_rows(head), lanes] = dot_nn(q_turned, ds)[half, :].astype(LOW)
        rows = slice(INNER + head * HD, INNER + (head + 1) * HD)
        grads_ref[rows, lanes] = dot_nn(do_turned, p.astype(LOW))[half, :].astype(LOW)
        ds_ref[hh, TILE : chunk + TILE, lanes] = ds
        if not own:
            base = near_in[head] if slot > 0 else jnp.zeros((NEAR, TILE), WIDE)
            if step == 0:
                near_out[head, :TILE, :] = base[:TILE] + low * ds[chunk - TILE :, :TILE].astype(WIDE)
                near_out[head, TILE : 2 * TILE, :] = base[TILE : 2 * TILE]
            if step == steps - 1:
                near_out[head, 2 * TILE :, :] = base[2 * TILE :] + high * ds[:TILE, TILE:].astype(WIDE)
        if step == steps - 1:
            product = dot_nn(ds_ref[hh, TILE : chunk + TILE, :], k_marked[hh])
            for tile in range(chunk // TILE):
                total = jnp.sum(product[tile * TILE : (tile + 1) * TILE, :], axis=0, keepdims=True)
                if slot > 0:
                    total = total + marks_in[head, tile : tile + 1, :]
                marks_ref[head, tile : tile + 1, :] = total
            if own:
                total = near_in[head]
                for tile in range(tiles):
                    at = pl.ds(pl.multiple_of(tile_place(tile, core) * TILE, TILE), NEAR)
                    part = ds_ref[hh, at, tile * TILE : (tile + 1) * TILE]
                    total = total + part.astype(WIDE)
                near_out[head] = total
            products[hh] = product
            if hh == 1:
                total = jnp.where(lane < HD, products[0], products[1])
                if slot > 0:
                    total = total + dq_in[:, pair_slice(pair)]
                dq_ref[:, pair_slice(pair)] = total

    pipelined(forward_items(mine), first, second, 1)
    a = jnp.concatenate([a0_ref[...], a1_ref[...]], axis=0)
    grads = grads_ref[...]
    weights = dot_nn(grads, a)
    if slot > 0:
        weights = weights + w_in[...]
    dx = dot_nt(grads[:INNER, :].T, wk_ref[...]) + dot_nt(grads[INNER:, :].T, wv_ref[...])
    dx_ref[...] = dx.astype(dx_ref.dtype)
    if not own:
        w_ref[...] = weights
        return

    half = kept_ref.shape[0]
    filled = 3 * INNER // 2
    dq = dq_ref[...].astype(LOW)
    rows = jnp.concatenate([dot_tn(dq, a_own_ref[...]), weights], axis=0).astype(LOW)
    empty = jnp.zeros((half - filled, width_of(kept_ref)), LOW)
    for part in range(2):
        put_half(core, kept_ref, sent_ref, part * half, rows[part * filled : (part + 1) * filled])
        put_half(core, kept_ref, sent_ref, part * half + filled, empty)
    for part in range(2):
        rows = slice(part * block, (part + 1) * block)
        at = pl.ds(pl.multiple_of(part * mine + core * block, block), block)
        dq_kept_ref[rows, :] = dq_ref[at, :]
        at = pl.ds(pl.multiple_of(part * mine + (1 - core) * block, block), block)
        dq_sent_ref[rows, :] = dq_ref[at, :].astype(LOW)


def width_of(ref):
    return ref.shape[1]


def table_kernel(sc_ref, near_out, marks_ref, onehot_ref, kept_in, kept_ref, small_ref, sem):
    core = sc_ref[0, CORE]
    lane = lanes_of(1, WIDTH2)
    tiles_in_chunk = marks_ref.shape[1]
    flip = (rows_of(TILE, TILE) + lanes_of(TILE, TILE) == TILE - 1).astype(LOW)
    head_row = rows_of(8, 1)
    table = jnp.zeros((8, WIDTH2), WIDE)
    for part in range(3):
        blocks = jnp.concatenate(
            [near_out[head, part * TILE : (part + 1) * TILE, :] for head in range(HEADS)], axis=1
        )
        turned = sum(dot_nn(flip, piece.astype(LOW)) for piece in three_pieces(blocks))
        sums = jnp.zeros((8, 2 * TILE), WIDE)
        for head in range(HEADS):
            padded = jnp.concatenate(
                [turned[:, head * TILE : (head + 1) * TILE], jnp.zeros((TILE, TILE), WIDE)], axis=1
            )
            skewed = pltpu.roll(padded, 0, 1, stride=1, stride_axis=0)
            sums = jnp.where(head_row == head, jnp.sum(skewed, axis=0, keepdims=True), sums)
        onehot = onehot_ref[part * 2 * TILE : (part + 1) * 2 * TILE, :].astype(LOW)
        table = table + sum(dot_nn(piece.astype(LOW), onehot) for piece in three_pieces(sums))
    query_tile = rows_of(tiles_in_chunk, 1)
    for head in range(HEADS):
        mark = lane - HD * (1 - head % 2)
        inside = (mark >= 8) & (mark < 32)
        kind, tile = mark // 8, mark % 8
        at = (kind - 2) * (tiles_in_chunk) + tile_place(tile, core)
        relative = at - query_tile
        found = marks_ref[head]
        before = (mark == 0) | (inside & (relative < -1))
        after = (mark == 1) | (inside & (relative > 1))
        for chosen, bucket in ((before, FAR_BEFORE), (after, FAR_AFTER)):
            total = jnp.sum(jnp.where(chosen, found, 0.0))
            table = table + jnp.where((head_row == head) & (lane == bucket), total, 0.0)
    small_ref[...] = jnp.zeros_like(small_ref)
    small_ref[:8, :WIDTH2] = table.astype(LOW)
    at = pl.ds(3 * INNER // 2, small_ref.shape[0])
    copy = pltpu.make_async_copy(small_ref, kept_ref.at[at, :], sem)
    copy.start()
    copy.wait()


def chain_kernel(slot, quads, sc_ref, *refs):
    mine, refs = refs[: slot + 1], refs[slot + 1 :]
    up_ref, down_ref = refs[-2:]
    core = sc_ref[0, CORE]
    for column, came, out_ref in ((UP, 0, up_ref), (DOWN, 1, down_ref)):
        edge = jnp.where(core == came, 0, quads - 1)
        for index, dx_ref in enumerate(mine):

            @pl.when(sc_ref[slot, column] == index)
            def _():
                value = dx_ref[...]
                if slot > 0:
                    came_before = refs[came][...].astype(WIDE)
                    total = value.astype(WIDE) + jnp.where(
                        sc_ref[0, QUAD] != edge, came_before, 0.0
                    )
                    value = total.astype(LOW)
                out_ref[...] = value


def join_kernel(sc_ref, kept_ref, got_ref, out_ref):
    side = sc_ref[0, SIDE]
    out_ref[side] = kept_ref[...]
    out_ref[1 - side] = got_ref[...]


def total_kernel(quads, sc_ref, dx_ref, first_ref, second_ref, out_ref):
    quad, core = sc_ref[0, QUAD], sc_ref[0, CORE]
    total = dx_ref[...]
    for came, came_ref in enumerate((first_ref, second_ref)):
        edge = jnp.where(core == came, 0, quads - 1)
        total = total + jnp.where(quad != edge, came_ref[...].astype(WIDE), 0.0)
    out_ref[...] = total


def input_kernel(
    sc_ref, dx_ref, dq_ref, dq_got_ref, x_ref, grad_res_ref, wq_ref, gain_ref, keep_ref, send_ref
):
    side = sc_ref[0, SIDE]
    block = x_ref.shape[0] // 2
    gain = gain_ref[...]
    for part in range(2):
        rows = slice(part * block, (part + 1) * block)
        queries = (dq_ref[rows, :] + dq_got_ref[rows, :].astype(WIDE)).astype(LOW)
        grad_in = dot_nt(queries, wq_ref[...]) + dx_ref[rows, :]
        x = x_ref[rows, :].astype(WIDE)
        scale = rms_scale(x)
        z = x * scale
        u = grad_in * gain
        result = grad_res_ref[rows, :] + scale * (u - z * jnp.mean(u * z, axis=-1, keepdims=True))
        result = result.astype(LOW)

        @pl.when(side == part)
        def _():
            keep_ref[...] = result

        @pl.when(side != part)
        def _():
            send_ref[...] = result


def tie_kernel(sc_ref, *refs):
    pass


def add_kernel(sc_ref, order_ref, *refs):
    outs = refs[-order_ref.shape[0] :]
    ins = refs[: len(refs) - len(outs)]
    for index, out_ref in enumerate(outs):
        which = order_ref[index]
        total = ins[0][which].astype(WIDE)
        for in_ref in ins[1:]:
            total = total + in_ref[which].astype(WIDE)
        out_ref[...] = total.astype(LOW)


def tree_kernel(sc_ref, *refs):
    values = [ref[...].astype(WIDE) for ref in refs[:-1]]
    while len(values) > 1:
        values = [values[n] + values[n + 1] for n in range(0, len(values), 2)]
    refs[-1][...] = values[0].astype(LOW)


def place_kernel(sc_ref, owner_ref, *refs):
    out_ref = refs[-1]
    for index, part_ref in enumerate(refs[:-1]):
        out_ref[owner_ref[index]] = part_ref[...]


def whole_rows(core, kept_ref, got_ref, first, count):
    half = kept_ref.shape[0]
    parts = []
    for number in range(2):
        low, high = max(first, number * half), min(first + count, (number + 1) * half)
        if low < high:
            rows = slice(low - number * half, high - number * half)
            part = jnp.where(core == number, kept_ref[rows, :], got_ref[rows, :])
            parts.append(part.astype(WIDE))
    return parts[0] if len(parts) == 1 else jnp.concatenate(parts, axis=0)


def unpack_feed_kernel(sc_ref, kept_ref, got_ref, out_ref, gate_ref, up_ref, down_ref, gain_ref):
    take = functools.partial(whole_rows, sc_ref[0, CORE], kept_ref, got_ref)
    width, hidden = gate_ref.shape
    row = 0
    for grads in (gate_ref, up_ref):
        for start in range(0, hidden, width):
            grads[:, start : start + width] = take(row, width)
            row += width
    down_ref[...] = take(row, hidden)
    row += hidden
    out_ref[...] = take(row, INNER)
    row += INNER
    gain_ref[...] = take(row, 16)[0:1, :]


def unpack_last_kernel(
    sc_ref, kept_ref, got_ref, wq_ref, wk_ref, wv_ref, gain_ref, query_ref, key_ref, value_ref, table_ref, gain_grad_ref,
):
    core = sc_ref[0, CORE]
    filled = 3 * INNER // 2
    first = jnp.where(core == 0, kept_ref[...], got_ref[...])
    second = jnp.where(core == 0, got_ref[...], kept_ref[...])
    grads = jnp.concatenate([first[:filled], second[:filled]], axis=0)
    total = jnp.zeros(gain_ref.shape, WIDE)
    for kind, (w_ref, out_ref) in enumerate(
        ((wq_ref, query_ref), (wk_ref, key_ref), (wv_ref, value_ref))
    ):
        part = grads[kind * INNER : (kind + 1) * INNER]
        out_ref[...] = part.T.astype(WIDE)
        products = part.astype(WIDE) * w_ref[...].T.astype(WIDE)
        total = total + jnp.sum(products, axis=0, keepdims=True)
    gain_grad_ref[...] = total / gain_ref[...]
    small = first[filled : filled + 16].astype(WIDE) + second[filled : filled + 16].astype(WIDE)
    table_ref[...] = small[:HEADS, :BUCKETS]


def staged_sum(kept, sent, between, plan, plan_out, add, place, whole=None, tree=None):
    came = [kept, lax.ppermute(sent, "blk", between)]
    after = yield sent
    for axes, size, index, peer, pairs in plan:
        order = jnp.stack([index] + [peer(index, shift) for shift in range(1, size)])
        own, *sends = add(order.astype(jnp.int32), came, after)
        came = [own] + [
            lax.ppermute(part, axes, pairs(shift)) for shift, part in enumerate(sends, 1)
        ]
        after = yield own
    (value,) = add(jnp.zeros((1,), jnp.int32), came, after)
    if whole is not None:
        axes, size, _, _, pairs = whole
        for number in range(size.bit_length() - 1):
            came = [value, lax.ppermute(value, axes, pairs(1 << number))]
            after = yield value
            value = tree(came, after)
    for axes, size, index, peer, pairs in plan_out:
        came = [lax.ppermute(value, axes, pairs(shift)) for shift in range(1, size)]
        after = yield value
        owners = jnp.stack([index] + [peer(index, -shift) for shift in range(1, size)])
        value = place(owners.astype(jnp.int32), [value] + came, after)
    got = lax.ppermute(value, "blk", between)
    after = yield value
    yield (value, got)


def advance(stages, count, after):
    for _ in range(count):
        tie = stages.send((after,))
    return tie


def finish(stages):
    for now in iter(lambda: stages.send(()), None):
        if isinstance(now, tuple):
            return now


def nearest_order(quads):
    return [
        sorted(range(quads), key=lambda k: (abs(k - place), k)) for place in range(quads)
    ]


def chunk_plan(quads):
    plans = []
    for place in range(quads):
        due = [(quads - 1 + place - d, d) for d in range(place + 1, quads)]
        due += [(quads - 1 - place + d, d) for d in range(place)]
        order = [d for _, d in sorted(due)] + [place]
        rows = []
        for slot in range(quads):
            up, down = quads - 1 + place - slot, place - (quads - 1) + slot
            rows.append(
                (
                    order[slot],
                    order.index(up) if place < up < quads else -1,
                    order.index(down) if 0 <= down < place else -1,
                )
            )
        plans.append(rows)
    return plans


def onehot_tables():
    thresholds = bucket_edges()

    def bucket(offset):
        half_count, exact_count, edges = thresholds
        distance = abs(offset)
        beyond = sum(distance >= edge for edge in edges)
        return (half_count if offset > 0 else 0) + (
            distance if distance < exact_count else exact_count + beyond
        )

    rows = np.zeros((BUCKETS, 2 * TURN), np.float32)
    for turn in range(TURN):
        back = turn if turn < TILE else turn - TURN
        rows[bucket(-TILE - back), turn] = 1.0
        rows[bucket(TILE + back), TURN + turn] = 1.0
    diagonals = np.zeros((6 * TILE, WIDTH2), np.float32)
    for part in range(3):
        for at in range(2 * TILE - 1):
            diagonals[part * 2 * TILE + at, bucket(1 + at - TILE * part)] = 1.0
    return rows, diagonals


def body(
    hidden_in,
    item_lengths,
    live_mask,
    cotangent,
    query_weight,
    key_weight,
    value_weight,
    output_weight,
    bucket_bias_table,
    norm_attention,
    norm_feed,
    gate_weight,
    up_weight,
    down_weight,
):
    streams, block, width = hidden_in.shape
    hidden = gate_weight.shape[1]
    blocks = lax.axis_size("blk")
    parts = lax.axis_size("dp")
    quads = blocks // 4
    here = lax.axis_index("blk")
    replica = lax.axis_index("dp")
    core, side, quad = here % 2, (here // 2) % 2, here // 4
    mine, chunk = 2 * block, 4 * block

    across = [(k, k ^ 2) for k in range(blocks)]
    between = [(k, k ^ 1) for k in range(blocks)]
    onward = []
    for k in range(blocks):
        if k % 2 == 0:
            onward.append((k, k + 4 if k + 4 < blocks else k + 1))
        else:
            onward.append((k, k - 4 if k >= 4 else k - 1))

    order = nearest_order(quads)
    distances = [
        sorted({abs(order[place][step] - place) for place in range(quads)}) for step in range(quads)
    ]
    spots = jnp.asarray(np.array(order, np.int32).T)
    nearest = jnp.asarray(np.array([found[0] for found in distances], np.int32))[:, None]
    is_here = jnp.arange(quads, dtype=jnp.int32)[None, :] == quad
    place = jnp.sum(jnp.where(is_here, spots, 0), axis=1, keepdims=True)
    swapped = ((place > quad) != (core == 1)) & (place != quad)
    source = 2 * (jnp.abs(place - quad) - nearest) + swapped.astype(jnp.int32)
    first_end = jnp.where(side == 0, item_lengths[0, 0], item_lengths[1, 0])
    col = jnp.arange(16, dtype=jnp.int32)[None, :]
    plans = np.array(chunk_plan(quads), np.int32)
    mine_of = [
        jnp.sum(jnp.where(is_here, jnp.asarray(plans[:, :, n].T), 0), axis=1, keepdims=True)
        for n in range(3)
    ]
    sc = jnp.where(col == QUAD, quad, 0)
    sc = jnp.where(col == CORE, core, sc)
    sc = jnp.where(col == SIDE, side, sc)
    sc = jnp.where(col == PLACE, place, sc)
    sc = jnp.where(col == SOURCE, source, sc)
    is_first = core == 0
    up_down = [jnp.where(is_first, mine_of[1], mine_of[2]), jnp.where(is_first, mine_of[2], mine_of[1])]
    for at, values in zip((CHUNK, UP, DOWN), (mine_of[0], *up_down)):
        sc = jnp.where(col == at, values, sc)
    sc = jnp.where(col == FIRST_END, first_end, sc).astype(jnp.int32)

    turned_onehot, diagonal_onehot = (jnp.asarray(t) for t in onehot_tables())

    smem = pl.BlockSpec(memory_space=pltpu.SMEM)
    vmem = pl.BlockSpec(memory_space=pltpu.VMEM)
    anywhere = pl.BlockSpec(memory_space=pl.ANY)
    shape = jax.ShapeDtypeStruct
    strip_rows_count = 2 * chunk - TILE
    near_shape = pltpu.VMEM((HEADS, NEAR, TILE), WIDE)
    strip_shape = pltpu.VMEM((HEADS, strip_rows_count, TILE), WIDE)
    gen_shape = pltpu.VMEM((chunk, mine), WIDE)
    dma = pltpu.SemaphoreType.DMA
    pairs_in_chunk = mine * chunk * HEADS

    def call(kernel, name, in_specs, out_specs, out_shape, scratch, operands, grid=(1,), aliases=None, us=5.0, after=(), limit=24,
             mark=False):
        count = 1 + len(operands)
        if mark:
            out_specs, out_shape = tuple(out_specs) + (vmem,), tuple(out_shape) + (shape((8, 128), WIDE),)
        last = count + len(after) + (len(out_shape) - 1 if mark else 0)

        def without_ties(*refs):
            if mark:
                refs[last][...] = jnp.zeros((8, 128), WIDE)
                refs = refs[:last] + refs[last + 1 :]
            kernel(*refs[:count], *refs[count + len(after) :])

        return pl.pallas_call(
            without_ties if after or mark else kernel,
            grid_spec=pltpu.PrefetchScalarGridSpec(
                num_scalar_prefetch=1,
                grid=grid,
                in_specs=list(in_specs) + [anywhere] * len(after),
                out_specs=out_specs,
                scratch_shapes=scratch,
            ),
            out_shape=out_shape,
            input_output_aliases=aliases or {},
            compiler_params=pltpu.CompilerParams(vmem_limit_bytes=limit * 1024 * 1024),
            cost_estimate=pl.CostEstimate(
                flops=int(us * (1e9 if us >= 4 else 1e7)), bytes_accessed=1 << 12, transcendentals=0
            ),
            name=name,
        )(sc, *operands, *after)

    def far_away(array):
        return pltpu.with_memory_space_constraint(array, pltpu.HBM)

    def tied(arrays, after):
        count = len(arrays)
        return call(
            tie_kernel, "tie", [anywhere] * count, (anywhere,) * count,
            tuple(shape(a.shape, a.dtype) for a in arrays), [], arrays,
            aliases={1 + n: n for n in range(count)}, us=0.3, after=after, limit=16,
        )

    def pick(both, index):
        return lax.dynamic_index_in_dim(both, index, 0, False)

    live_rows = jnp.pad(live_mask.astype(LOW)[:, None, :], ((0, 0), (0, 15), (0, width - block)))
    payload = jnp.concatenate([pick(hidden_in, 1 - side), pick(live_rows, 1 - side)], axis=0)
    got = lax.ppermute(payload, "blk", across)
    packed, x_low = call(
        norm_kernel, "norm_rows", [vmem] * 4, (vmem,) * 2,
        (shape((mine + 16, width), LOW), pltpu.HBM((mine, width), LOW)), [],
        (far_away(hidden_in), far_away(live_mask), got, far_away(norm_attention[None, :])), us=2.0,
    )
    own_chunk = jnp.concatenate([packed, lax.ppermute(packed, "blk", between)], axis=0)
    cot_got = lax.ppermute(pick(cotangent, 1 - side), "blk", across)

    qkv_shape = pltpu.HBM((quads * chunk, 3 * INNER), LOW)
    ext_shape = pltpu.HBM((quads * chunk, WIDTH2), LOW)
    state_shapes = (shape((INNER, mine), WIDE), shape((16, mine), WIDE))

    def chunk_out(step, columns):
        return pl.BlockSpec((chunk, columns), lambda i, sc: (sc[step, PLACE], 0))

    a_shape = pltpu.HBM((quads * chunk, width), LOW)
    chunk_scratch = [pltpu.VMEM((2, 16, width), LOW)]
    held = lax.ppermute(own_chunk, "blk", onward)
    rowk, rowq, vec = call(
        places_kernel, "places", [smem] + [vmem] * 3, (vmem,) * 3,
        (shape((8, chunk), WIDE), shape((8, mine), WIDE), shape((8, 2 * TURN), WIDE)), [],
        (item_lengths, packed, bucket_bias_table, turned_onehot), us=2.0, after=(own_chunk,), limit=16,
    )
    qkv, ext, normed, qx, acc, ml, q_own = call(
        forward_own_kernel, "attend_own", [smem, anywhere] + [vmem] * 6,
        (chunk_out(0, 3 * INNER), chunk_out(0, WIDTH2), chunk_out(0, width), vmem, vmem, vmem, vmem),
        (qkv_shape, ext_shape, a_shape, shape((HEADS, 2 * WIDTH2, mine), LOW)) + state_shapes
        + (shape((chunk, INNER), LOW),),
        chunk_scratch + [strip_shape, near_shape, gen_shape, dma((6,))],
        (bucket_bias_table, own_chunk, key_weight, value_weight, query_weight, vec, rowq, rowk),
        us=12.0,
    )

    came = []
    for step in range(1, quads):
        held, acc = lax.optimization_barrier((held, acc))
        came.append((held, lax.ppermute(held, "blk", between)))
        if step + 1 < quads:
            held = lax.ppermute(held, "blk", onward)
        arrays = [array for distance in distances[step] for array in came[distance - 1]]
        qkv, ext, normed, acc, ml = call(
            functools.partial(forward_kernel, step, len(arrays)), "attend_other",
            [smem] + [vmem] * 7 + [anywhere] * (3 + len(arrays)),
            (chunk_out(step, 3 * INNER), chunk_out(step, WIDTH2), chunk_out(step, width), vmem, vmem),
            (qkv_shape, ext_shape, a_shape) + state_shapes,
            chunk_scratch + [near_shape, dma((6,))],
            (bucket_bias_table, key_weight, value_weight, query_weight, vec, qx, acc, ml, qkv, ext, normed, *arrays),
            aliases={7: 3, 8: 4, 9: 0, 10: 1, 11: 2}, us=10.0,
        )

    (do_mine, out_kept, out_sent, grad_res, act, feed, grad_gate, grad_up,
     context, branch, gain_grad, cot) = call(
        middle_kernel, "feed_both_ways", [vmem] * 11, (vmem,) * 12,
        (
            shape((mine, INNER + WIDTH2), LOW),
            shape((block, width), LOW), shape((block, width), LOW), pltpu.HBM((mine, width), WIDE),
            shape((mine, hidden), LOW), shape((mine, width), LOW), shape((mine, hidden), LOW),
            shape((mine, hidden), LOW), shape((mine, INNER), LOW), shape((mine, width), LOW),
            shape((8, width), WIDE), shape((mine, width), LOW),
        ), [],
        (
            acc, ml, x_low, cotangent, cot_got, rowq, output_weight, gate_weight, up_weight, down_weight,
            norm_feed[None, :],
        ),
        us=12.0,
    )
    do_other = lax.ppermute(do_mine, "blk", between)
    def joined(kept, got, after):
        return call(
            join_kernel, "join", [vmem] * 2, (vmem,), (pltpu.HBM((2, block, width), LOW),), [], (kept, got),
            us=1.0, after=after, limit=16, mark=True,
        )

    def over_blocks(shift):
        return [(k, k ^ (4 * shift)) for k in range(blocks)]

    over_side = ("blk", 2, side, lambda i, s: i ^ 1, lambda s: across)
    over_parts = (
        "dp", parts, replica, lambda i, s: (i + s) % parts,
        lambda s: [(k, (k + s) % parts) for k in range(parts)],
    )
    over_quads = ("blk", quads, quad, lambda i, s: i ^ abs(s), over_blocks)
    if parts == 2:

        def square_pairs(shift):
            pairs = []
            for k in range(blocks):
                for r in range(parts):
                    k2, r2 = k ^ (2 * (shift >> 1)), r ^ (shift & 1)
                    pairs.append((k * parts + r, k2 * parts + r2))
            return pairs

        over_square = (("blk", "dp"), 4, side * 2 + replica, lambda i, s: i ^ abs(s), square_pairs)
        plan = [over_square, over_quads]
    else:
        plan = [over_side, over_parts, over_quads]
    plan_out = plan[::-1]
    groups = len(plan) - 1
    pieces_in_all = 8 * 2 * 2 * parts * quads

    def padded(rows):
        return -(-rows // pieces_in_all) * pieces_in_all

    feed_rows = padded(3 * hidden + INNER + 8) // 2
    feed_kept, feed_sent = call(
        feed_grads_kernel, "feed_weight_grads", [vmem] * 8, (vmem, vmem),
        (shape((feed_rows, width), LOW),) * 2, [],
        (act, feed, grad_gate, grad_up, context, branch, cot, gain_grad), us=7.0,
    )
    def add_parts(order, arrays, after):
        size = order.shape[0]
        split = [a.reshape((size, a.shape[0] // size, a.shape[1])) for a in arrays]
        return call(
            add_kernel, "add_parts", [smem] + [vmem] * len(split), (vmem,) * size,
            (shape(split[0].shape[1:], LOW),) * size, [], (order, *split), us=2.0, after=after, limit=16,
        )

    def place_parts(owners, arrays, after):
        one = arrays[0].shape
        whole = call(
            place_kernel, "place_parts", [smem] + [vmem] * len(arrays), vmem,
            shape((len(arrays),) + one, LOW), [], (owners, *arrays), us=1.0, after=after, limit=16,
        )
        return whole.reshape((-1,) + one[1:])

    def tree_parts(arrays, after):
        return call(
            tree_kernel, "tree_parts", [vmem] * len(arrays), vmem, shape(arrays[0].shape, LOW), [], tuple(arrays),
            us=1.0, after=after, limit=16,
        )

    feed_stages = staged_sum(feed_kept, feed_sent, between, plan, plan_out, add_parts, place_parts)
    next(feed_stages)
    out_got = lax.ppermute(out_sent, "blk", across)
    tie = feed_stages.send(())
    do_chunk = call(
        order_kernel, "order", [vmem] * 2, vmem, shape((chunk, INNER + WIDTH2), LOW), [], (do_mine, do_other),
        us=1.0, after=(tie,), limit=16,
    )

    ties = [tie]

    qkv, ext, normed = far_away(qkv), far_away(ext), far_away(normed)
    backward = [(end, start) for start, end in onward]
    last_rows = padded(3 * INNER + 32) // 2
    state_shape = (
        shape((chunk, INNER), WIDE), shape((2 * INNER, width), WIDE), shape((HEADS, NEAR, TILE), WIDE),
        shape((HEADS, chunk // TILE, WIDTH2), WIDE),
    )

    def chunk_rows(slot, n, columns):
        return pl.BlockSpec(
            (block, columns), lambda i, sc: (4 * sc[slot, CHUNK] + sc[0, CORE] + 2 * n, 0)
        )

    state, gradients, came = (), [], ()
    for slot in range(quads):
        own = slot == quads - 1
        operands = (
            bucket_bias_table, do_chunk, q_own, qkv, qkv, normed, normed, ext, ext, key_weight, value_weight, vec,
        ) + tuple(state)
        in_specs = [
            smem, vmem, vmem,
            chunk_rows(slot, 0, 2 * INNER), chunk_rows(slot, 1, 2 * INNER),
            chunk_rows(slot, 0, width), chunk_rows(slot, 1, width),
            chunk_rows(slot, 0, WIDTH2), chunk_rows(slot, 1, WIDTH2), vmem, vmem, vmem,
        ] + [vmem] * len(state)
        scratch = [
            near_shape, pltpu.VMEM((2, chunk + 2 * TILE, mine), LOW), pltpu.VMEM((2 * INNER, mine), LOW),
        ]
        outs = (shape((mine, width), WIDE if own else LOW),)
        if own:
            operands += (ext, rowq, normed)
            in_specs += [
                pl.BlockSpec((chunk, WIDTH2), lambda i, sc: (sc[0, QUAD], 0)), vmem,
                pl.BlockSpec((chunk, width), lambda i, sc: (sc[0, QUAD], 0)),
            ]
            outs += (shape((last_rows, width), LOW),) * 2
            outs += (shape((mine, INNER), WIDE), shape((mine, INNER), LOW)) + state_shape[2:]
            scratch = [pltpu.VMEM((chunk, INNER), WIDE), strip_shape, gen_shape] + scratch
        else:
            outs += state_shape
        found = call(
            functools.partial(chunk_kernel, slot, own), "grad_chunk", in_specs, (vmem,) * len(outs), outs, scratch,
            operands, us=10.0, after=ties, limit=32 if own else 28,
            aliases={13 + n: 1 + n for n in range(4)} if slot and not own else None,
        )
        gradients.append(found[0])
        if own:
            kept, sent, dq_kept, dq_sent, near_grad, marks = found[1:]
            break
        state = found[1:]
        ties = []
        if 0 < slot < 3:
            ties.append(advance(feed_stages, 1 if slot == 1 else groups, found[0]))
        up, down = call(
            functools.partial(chain_kernel, slot, quads), "chain", [vmem] * (len(gradients) + len(came)), (vmem,) * 2,
            (shape((mine, width), LOW),) * 2, [], tuple(gradients) + tuple(came), us=1.0, after=ties, limit=16,
        )
        came = (lax.ppermute(up, "blk", onward), lax.ppermute(down, "blk", backward))
        ties = ties + [up]
        if slot == 0:
            output, mark = joined(out_kept, out_got, (up,))
            ties.append(advance(feed_stages, groups, mark))
    total = call(
        functools.partial(total_kernel, quads), "total", [vmem] * 3, vmem, shape((mine, width), WIDE), [],
        (gradients[-1], *came), us=1.0, after=(kept,), limit=16,
    )
    tie = advance(feed_stages, 1, total)
    sent, dq_sent = tied((sent, dq_sent), (tie,))
    kept = call(
        table_kernel, "bias_table", [vmem] * 3 + [anywhere], anywhere, shape(kept.shape, LOW),
        [pltpu.VMEM((16, width), LOW), dma], (near_grad, marks, diagonal_onehot, kept),
        aliases={4: 0}, us=2.0, after=(sent,), limit=16,
    )
    last_stages = staged_sum(
        kept, sent, between, plan[:-1], plan_out[1:], add_parts, place_parts, over_quads, tree_parts
    )
    next(last_stages)
    dq_got = lax.ppermute(dq_sent, "blk", between)
    feed_kept, feed_got = feed_stages.send(())
    tie = advance(last_stages, 1, kept)
    in_kept, in_sent = call(
        input_kernel, "grad_input", [vmem] * 7, (vmem,) * 2,
        (shape((block, width), LOW), shape((block, width), LOW)), [],
        (total, dq_kept, dq_got, x_low, grad_res, query_weight, norm_attention[None, :]),
        us=2.0, after=(tie,),
    )
    grad_out, grad_gate, grad_up, grad_down, grad_norm_feed, mark = call(
        unpack_feed_kernel, "unpack_feed", [vmem] * 2, (vmem,) * 5,
        (
            pltpu.HBM((INNER, width), WIDE), pltpu.HBM((width, hidden), WIDE), pltpu.HBM((width, hidden), WIDE),
            pltpu.HBM((hidden, width), WIDE), pltpu.HBM((1, width), WIDE),
        ), [],
        (feed_kept, feed_got), us=3.9, after=(in_kept,), mark=True,
    )
    (in_sent,) = tied((in_sent,), (mark,))
    for _ in range(groups):
        tie = last_stages.send((mark,))
    in_got = lax.ppermute(in_sent, "blk", across)
    doublings = quads.bit_length() - 1
    for _ in range(doublings - 1):
        tie = last_stages.send(())
    input_gradient, mark = joined(in_kept, in_got, (tie,))
    last_stages.send((mark,))
    for _ in range(groups):
        last_stages.send(())
    last_kept, last_got = finish(last_stages)
    grad_query, grad_key, grad_value, grad_table, grad_norm_attention = call(
        unpack_last_kernel, "unpack_attention", [vmem] * 6, (vmem,) * 5,
        (pltpu.HBM((width, INNER), WIDE),) * 3 + (shape((HEADS, BUCKETS), WIDE), shape((1, width), WIDE)), [],
        (last_kept, last_got, query_weight, key_weight, value_weight, norm_attention[None, :]), us=2.0,
    )
    return (
        output,
        input_gradient,
        grad_query,
        grad_key,
        grad_value,
        grad_out,
        grad_table.T,
        grad_norm_attention[0],
        grad_norm_feed[0],
        grad_gate,
        grad_up,
        grad_down,
    )


def solution(mesh):
    return jax.shard_map(
        body,
        mesh=mesh,
        in_specs=(
            P("dp", "blk", None),
            P("dp", None),
            P("dp", "blk"),
            P("dp", "blk", None),
            P(),
            P(),
            P(),
            P(),
            P(),
            P(),
            P(),
            P(),
            P(),
            P(),
        ),
        out_specs=(
            P("dp", "blk", None),
            P("dp", "blk", None),
            P(),
            P(),
            P(),
            P(),
            P(),
            P(),
            P(),
            P(),
            P(),
            P(),
        ),
        check_vma=False,
    )
```

```python
import functools

import jax
import jax.numpy as jnp
import numpy as np
from jax import lax
from jax.experimental import pallas as pl
from jax.experimental.pallas import tpu as pltpu
from jax.sharding import PartitionSpec as P

HEADS = 6
HD = 64
WIDTH2 = 2 * HD
PAIRS = HEADS // 2
INNER = HEADS * HD
BUCKETS = 32
MAXDIST = 128
EPSILON = 1e-06
BIG = 1e30
TILE = 128
NEAR = 3 * TILE
TURN = 4 * TILE
FAR_BEFORE = BUCKETS // 2 - 1
FAR_AFTER = BUCKETS - 1
LOW = jnp.bfloat16
WIDE = jnp.float32
GELU_A = 0.7978845608028654
GELU_B = 0.044715

QUAD, CORE, SIDE, PLACE, SOURCE, FIRST_END, CHUNK, UP, DOWN = range(9)
MASK, BEFORE, AFTER, PEN, STAT, LIVE, SEG = 0, 1, 2, 7, 8, 11, 12
ONE_A, OFF, ONE_B, ONE_C, ONE_D = 36, 37, 38, 39, 40


def bucket_edges():
    half_count = BUCKETS // 2
    exact_count = half_count // 2
    log_levels = half_count - exact_count
    thresholds = []
    for level_index in range(1, log_levels):
        candidate = exact_count
        while (
            candidate**log_levels * exact_count**level_index
            < MAXDIST**level_index * exact_count**log_levels
        ):
            candidate = candidate + 1
        thresholds.append(candidate)
    return (half_count, exact_count, thresholds)


def dot_nt(left, right):
    return lax.dot_general(
        left, right, (((1,), (1,)), ((), ())), preferred_element_type=WIDE
    )


def dot_nn(left, right):
    return jnp.dot(left, right, preferred_element_type=WIDE)


def dot_tn(left, right):
    return lax.dot_general(
        left, right, (((0,), (0,)), ((), ())), preferred_element_type=WIDE
    )


def rows_of(count, width):
    return lax.broadcasted_iota(jnp.int32, (count, width), 0)


def lanes_of(count, width):
    return lax.broadcasted_iota(jnp.int32, (count, width), 1)


def lane_half(array, half, other):
    return jnp.where(lanes_of(1, WIDTH2) // HD == half, array, other)


def row_half(array, half, other):
    return jnp.where(rows_of(WIDTH2, 1) // HD == half, array, other)


def pair_slice(pair, base=0):
    return slice(base + pair * WIDTH2, base + (pair + 1) * WIDTH2)


def tile_place(tile, core):
    return (tile // 2) * 4 + core * 2 + tile % 2


def rms_scale(values):
    return lax.rsqrt(jnp.mean(values * values, axis=-1, keepdims=True) + EPSILON)


def three_pieces(values):
    high = values.astype(LOW).astype(WIDE)
    mid = (values - high).astype(LOW).astype(WIDE)
    low = (values - high - mid).astype(LOW).astype(WIDE)
    return high, mid, low


def pipelined(items, first, second, depth):
    ahead = []
    for item in items:
        ahead.append((item, first(item)))
        if len(ahead) > depth:
            second(*ahead.pop(0))
    for waiting in ahead:
        second(*waiting)


def far_bias(table_ref, after, head):
    return table_ref[FAR_AFTER if after else FAR_BEFORE, head]


def build_near(near_ref, vec_ref, back, heads):
    for index, head in enumerate(heads):
        row = vec_ref[head : head + 1, back * TURN : (back + 1) * TURN]
        row = jnp.broadcast_to(row, (NEAR, TURN))
        near_ref[index] = pltpu.roll(row, 0, 1, stride=1, stride_axis=0)[:, :TILE]


def build_strip(strip_ref, near_ref, table_ref, back, chunk, heads):
    edge = chunk - TILE
    rest = strip_ref.shape[1] - edge - 2 * TILE
    for index, head in enumerate(heads):
        far_before = far_bias(table_ref, back, head)
        far_after = far_bias(table_ref, not back, head)
        strip_ref[index, : edge - TILE, :] = jnp.full((edge - TILE, TILE), far_before, WIDE)
        strip_ref[index, edge - TILE : edge + 2 * TILE, :] = near_ref[index]
        strip_ref[index, edge + 2 * TILE :, :] = jnp.full((rest, TILE), far_after, WIDE)


def strip_rows(strip_ref, index, first_tile, tiles, core, chunk):
    parts = []
    for tile in range(first_tile, first_tile + tiles):
        start = (chunk - TILE) - tile_place(tile, core) * TILE
        parts.append(strip_ref[index, pl.ds(pl.multiple_of(start, TILE), chunk), :])
    return jnp.concatenate(parts, axis=1)


def near_fixes(near_ref, table_ref, flags, index, head, back):
    low, high = flags
    return (
        low * (near_ref[index, :TILE, :] - far_bias(table_ref, back, head)),
        high * (near_ref[index, 2 * TILE :, :] - far_bias(table_ref, not back, head)),
    )


def fix_near(scores, step, steps, fixes):
    low, high = fixes
    chunk, width = scores.shape
    if step == 0:
        last = jnp.concatenate(
            [scores[chunk - TILE :, :TILE] + low, scores[chunk - TILE :, TILE:]], axis=1
        )
        scores = jnp.concatenate([scores[: chunk - TILE], last], axis=0)
    if step == steps - 1:
        first = jnp.concatenate(
            [scores[:TILE, : width - TILE], scores[:TILE, width - TILE :] + high], axis=1
        )
        scores = jnp.concatenate([first, scores[TILE:]], axis=0)
    return scores


def near_flags(place, quad, core):
    low = jnp.where((place == quad - 1) & (core == 0), 1.0, 0.0)
    high = jnp.where((place == quad + 1) & (core == 1), 1.0, 0.0)
    return low, high


def natural_row(even, odd):
    block = even.shape[1] // 2
    return jnp.concatenate(
        [even[:, :block], odd[:, :block], even[:, block:], odd[:, block:]], axis=1
    )


def key_columns(rows, lanes):
    places = rows[0].shape[1]
    stack = jnp.zeros((16, places), WIDE)
    spread = jnp.zeros((16, WIDTH2), WIDE)
    number, lane = rows_of(16, 1), lanes_of(16, WIDTH2)
    for index, row in enumerate(rows):
        stack = jnp.where(number == index, row, stack)
    for index, at, scale in lanes:
        spread = jnp.where((number == index) & (lane == at), scale, spread)
    return dot_tn(stack.astype(LOW), spread.astype(LOW))


def visible_mask(gen_ref, segment_column, segment_row, live, core, keys_down):
    chunk, mine = gen_ref.shape
    down = rows_of(chunk, 1)
    for tile in range(mine // TILE):
        lanes = slice(tile * TILE, (tile + 1) * TILE)
        across = tile_place(tile, core) * TILE + lanes_of(1, TILE)
        alive = live if keys_down else live[:, lanes]
        visible = (segment_column == segment_row[:, lanes]) & ((alive > 0.5) | (down == across))
        gen_ref[:, lanes] = jnp.where(visible, 0.0, -BIG)


def project(a, weight_refs, qkv_ref):
    for part, w_ref in enumerate(weight_refs):
        cols = slice(part * INNER, (part + 1) * INNER)
        qkv_ref[:, cols] = dot_nn(a, w_ref[...]).astype(LOW)


def halves_copies(source, swapped, core, rows_ref, live_ref, sems):
    first_core = 1 - core if swapped else core
    block = rows_ref.shape[0] // 4
    half = source.shape[0] // 2
    copies = []
    for index in range(2):
        owner = first_core if index == 0 else 1 - first_core
        for part in range(2):
            at = pl.multiple_of(part * 2 * block + owner * block, block)
            copies.append((source.at[pl.ds(index * half + part * block, block), :], rows_ref.at[pl.ds(at, block), :]))
        if live_ref is not None:
            copies.append((source.at[pl.ds(index * half + 2 * block, 16), :], live_ref.at[owner]))
    return [
        pltpu.make_async_copy(start, end, sems.at[index]) for index, (start, end) in enumerate(copies)
    ]


def start_fetch(sc_ref, step, sources, rows_ref, live_ref, sems):
    core = sc_ref[0, CORE]
    for index, source in enumerate(sources):

        @pl.when(sc_ref[step, SOURCE] == index)
        def _():
            for copy in halves_copies(source, index % 2 == 1, core, rows_ref, live_ref, sems):
                copy.start()


def wait_fetch(sc_ref, sources, rows_ref, live_ref, sems):
    for copy in halves_copies(sources[0], False, sc_ref[0, CORE], rows_ref, live_ref, sems):
        copy.wait()


def norm_kernel(sc_ref, hidden_ref, live_ref, got_ref, gain_ref, packed_ref, x_ref):
    side = sc_ref[0, SIDE]
    block = hidden_ref.shape[1]
    mine = 2 * block
    kept, got = hidden_ref[side], got_ref[:block, :]
    live_kept = live_ref[pl.ds(side, 1), :].astype(WIDE)
    live_got = got_ref[block : block + 16, :block].astype(WIDE)[0:1, :]
    for part in range(2):
        rows = jnp.where(side == part, kept, got)
        x_ref[part * block : (part + 1) * block, :] = rows
        wide = rows.astype(WIDE)
        normed = wide * rms_scale(wide) * gain_ref[...]
        packed_ref[part * block : (part + 1) * block, :] = normed.astype(LOW)
    live = jnp.concatenate(
        [jnp.where(side == 0, live_kept, live_got), jnp.where(side == 0, live_got, live_kept)],
        axis=1,
    )
    packed_ref[mine:, :] = jnp.broadcast_to(live, (16, mine)).astype(LOW)


def places_kernel(sc_ref, lengths_ref, packed_ref, table_ref, onehot_ref, rowk_ref, rowq_ref, vec_ref):
    side, core, quad = sc_ref[0, SIDE], sc_ref[0, CORE], sc_ref[0, QUAD]
    mine, chunk = rowq_ref.shape[1], rowk_ref.shape[1]
    block = mine // 2
    live = packed_ref[mine : mine + 16, :].astype(WIDE)[0:1, :]
    places = quad * chunk + lanes_of(1, chunk)

    def one_item(item, carry):
        end, segment = carry
        end = end + lengths_ref[side, item]
        return end, segment + jnp.where(places >= end, 1.0, 0.0)

    zero = jnp.zeros((1, chunk), WIDE)
    end, segment = lax.fori_loop(0, lengths_ref.shape[1], one_item, (jnp.int32(0), zero), unroll=8)
    rowk_ref[...] = jnp.broadcast_to(segment, (8, chunk))
    own = jnp.concatenate(
        [
            rowk_ref[0:1, pl.ds(pl.multiple_of(part * mine + core * block, block), block)]
            for part in range(2)
        ],
        axis=1,
    )
    number = rows_of(8, 1)
    rowq = jnp.where(number == 0, own, 0.0)
    rowq = jnp.where(number == 2, jnp.where(own > 0.5, BIG, 0.0), rowq)
    rowq = jnp.where(number == 3, live, rowq)
    rowq_ref[...] = rowq
    found = lax.dot_general(
        table_ref[...], onehot_ref[...], (((0,), (0,)), ((), ())),
        precision=lax.Precision.HIGHEST, preferred_element_type=WIDE,
    )
    vec_ref[...] = jnp.concatenate([found, jnp.zeros((8 - HEADS, found.shape[1]), WIDE)], axis=0)


def forward_items(mine):
    steps = mine // (2 * TILE)
    return [(pair, step, hh) for pair in range(PAIRS) for step in range(steps) for hh in range(2)]


def forward_operands(qkv_ref, ext):
    made = {}

    def operands(pair):
        if pair not in made:
            k_ext = jnp.concatenate([qkv_ref[:, pair_slice(pair)], ext], axis=1)
            v_turned = qkv_ref[:, pair_slice(pair, INNER)].T
            made[pair] = (
                k_ext, [row_half(v_turned, hh, jnp.ones_like(v_turned)) for hh in range(2)]
            )
        return made[pair]

    return operands


def step_lanes(step):
    return slice(step * 2 * TILE, (step + 1) * 2 * TILE)


def head_rows(head):
    return slice(head * HD, (head + 1) * HD)


def forward_own_kernel(
    sc_ref, table_ref, source_ref, wk_ref, wv_ref, wq_ref, vec_ref, rowq_ref, rowk_ref,
    qkv_ref, ext_ref, a_ref, qx_ref, acc_ref, ml_ref, q_own_ref,
    live_ref, strip_ref, near_ref, gen_ref, sems,
):
    core = sc_ref[0, CORE]
    chunk = qkv_ref.shape[0]
    mine = acc_ref.shape[1]
    block = mine // 2
    start_fetch(sc_ref, 0, [source_ref], a_ref, live_ref, sems)
    build_near(near_ref, vec_ref, 0, range(HEADS))
    build_strip(strip_ref, near_ref, table_ref, False, chunk, range(HEADS))
    number = rows_of(WIDTH2, 1)
    for head in range(HEADS):
        rows = jnp.where(number == MASK, 1.0, 0.0)
        for which, after in ((BEFORE, False), (AFTER, True)):
            far = jnp.full((1, mine), far_bias(table_ref, after, head), WIDE)
            for piece, value in enumerate(three_pieces(far)):
                rows = jnp.where(number == which + 2 * piece, value, rows)
        rows = jnp.where(number == PEN, -rowq_ref[2:3, :], rows)
        qx_ref[head, WIDTH2:, :] = rows.astype(LOW)
    wait_fetch(sc_ref, [source_ref], a_ref, live_ref, sems)
    project(a_ref[...], (wk_ref, wv_ref, wq_ref), qkv_ref)
    q_own_ref[...] = qkv_ref[:, 2 * INNER :]
    live = natural_row(live_ref[0].astype(WIDE)[0:1, :], live_ref[1].astype(WIDE)[0:1, :])
    columns = key_columns(
        [jnp.ones_like(live), live, rowk_ref[0:1, :]],
        [(0, STAT, 1.0), (0, STAT + 1, 1.0), (0, STAT + 2, 1.0), (1, LIVE, 1.0), (2, SEG, 1.0)],
    )
    ext_ref[...] = columns.astype(LOW)
    visible_mask(
        gen_ref, columns[:, SEG : SEG + 1], rowq_ref[0:1, :], columns[:, LIVE : LIVE + 1], core, True
    )
    for part in range(2):
        at = pl.ds(pl.multiple_of(part * mine + core * block, block), block)
        lanes = slice(part * block, (part + 1) * block)
        for pair in range(PAIRS):
            turned = qkv_ref[at, pair_slice(pair, 2 * INNER)].T
            for hh in range(2):
                qx_ref[2 * pair + hh, :WIDTH2, lanes] = row_half(
                    turned, hh, jnp.zeros_like(turned)
                )
    ml_ref[...] = jnp.zeros_like(ml_ref)
    operands = forward_operands(qkv_ref, ext_ref[...])

    def first(item):
        pair, step, hh = item
        s = dot_nn(operands(pair)[0], qx_ref[2 * pair + hh, :, step_lanes(step)])
        s = s + strip_rows(strip_ref, 2 * pair + hh, 2 * step, 2, core, chunk)
        return s + gen_ref[:, step_lanes(step)]

    def second(item, s):
        pair, step, hh = item
        head, lanes = 2 * pair + hh, step_lanes(step)
        top = jnp.max(s, axis=0, keepdims=True)
        p = jnp.exp(s - top).astype(LOW)
        pv = dot_nn(operands(pair)[1][hh], p)
        ml_ref[head : head + 1, lanes] = top
        ml_ref[8 + head : 9 + head, lanes] = pv[HD * (1 - hh) : HD * (1 - hh) + 1, :]
        acc_ref[head_rows(head), lanes] = pv[hh * HD : (hh + 1) * HD, :]

    pipelined(forward_items(mine), first, second, 2)


def forward_kernel(
    step_number, sources, sc_ref, table_ref, wk_ref, wv_ref, wq_ref, vec_ref, qx_ref, acc_in, ml_in,
    qkv_in, ext_in, a_in, *rest,
):
    source_refs, rest = rest[:sources], rest[sources:]
    qkv_ref, ext_ref, a_ref, acc_ref, ml_ref, live_ref, near_ref, sems = rest
    quad, core, place = (sc_ref[step_number, i] for i in (QUAD, CORE, PLACE))
    chunk = qkv_ref.shape[0]
    mine = acc_ref.shape[1]
    start_fetch(sc_ref, step_number, source_refs, a_ref, live_ref, sems)
    build_near(near_ref, vec_ref, 0, range(HEADS))
    wait_fetch(sc_ref, source_refs, a_ref, live_ref, sems)
    project(a_ref[...], (wk_ref, wv_ref, wq_ref), qkv_ref)
    live = natural_row(live_ref[0].astype(WIDE)[0:1, :], live_ref[1].astype(WIDE)[0:1, :])
    places = place * chunk + lanes_of(1, chunk)
    seen = (live > 0.5) & (places < sc_ref[step_number, FIRST_END])
    is_before = jnp.where(place < quad, 1.0, 0.0)
    is_after = 1.0 - is_before
    marks = [(0, MASK, 1.0), (1, PEN, 1.0)]
    marks += [(1, STAT + n, 1.0) for n in range(3)]
    marks += [(1, BEFORE + 2 * n, is_before) for n in range(3)]
    marks += [(1, AFTER + 2 * n, is_after) for n in range(3)]
    ext = key_columns([jnp.where(seen, 0.0, -BIG), jnp.ones_like(live)], marks).astype(LOW)
    ext_ref[...] = ext
    flags = near_flags(place, quad, core)
    steps = mine // (2 * TILE)
    operands = forward_operands(qkv_ref, ext)

    def first(item):
        pair, step, hh = item
        head = 2 * pair + hh
        s = dot_nn(operands(pair)[0], qx_ref[head, :, step_lanes(step)])
        return fix_near(s, step, steps, near_fixes(near_ref, table_ref, flags, head, head, False))

    def second(item, s):
        pair, step, hh = item
        head, lanes = 2 * pair + hh, step_lanes(step)
        old = ml_in[head : head + 1, lanes]
        top = jnp.maximum(old, jnp.max(s, axis=0, keepdims=True))
        keep = jnp.exp(old - top)
        p = jnp.exp(s - top).astype(LOW)
        pv = dot_nn(operands(pair)[1][hh], p)
        ml_ref[head : head + 1, lanes] = top
        total = ml_in[8 + head : 9 + head, lanes] * keep
        ml_ref[8 + head : 9 + head, lanes] = total + pv[HD * (1 - hh) : HD * (1 - hh) + 1, :]
        rows = head_rows(head)
        acc_ref[rows, lanes] = acc_in[rows, lanes] * keep + pv[hh * HD : (hh + 1) * HD, :]

    pipelined(forward_items(mine), first, second, 2)


def middle_kernel(
    sc_ref, acc_ref, ml_ref, x_ref, cot_in, cot_got, rowq_ref, wo_ref, gate_ref, up_ref, down_ref, gain_ref,
    do_ref, keep_ref, send_ref, grad_res_ref, act_ref, feed_ref, gg_ref, gu_ref,
    ctx_ref, branch_ref, gain_grad_ref, cot_ref,
):
    side = sc_ref[0, SIDE]
    mine = x_ref.shape[0]
    block = mine // 2
    gain = gain_ref[...]
    context = []
    for head in range(HEADS):
        context.append(acc_ref[head_rows(head), :] / ml_ref[8 + head : 9 + head, :])
    for pair in range(PAIRS):
        both = jnp.concatenate(context[2 * pair : 2 * pair + 2], axis=0).astype(LOW)
        ctx_ref[:, pair_slice(pair)] = both.T
    gain_grad = jnp.zeros_like(gain)
    cot_kept = cot_in[side]
    for part in range(2):
        rows = slice(part * block, (part + 1) * block)
        cot_ref[rows, :] = jnp.where(side == part, cot_kept, cot_got[...])

    def first(part):
        rows = slice(part * block, (part + 1) * block)
        residual = x_ref[rows, :].astype(WIDE) + dot_nn(ctx_ref[rows, :], wo_ref[...])
        scale = rms_scale(residual)
        z = residual * scale
        feed = (z * gain).astype(LOW)
        feed_ref[rows, :] = feed
        v = dot_nn(feed, gate_ref[...])
        up = dot_nn(feed, up_ref[...])
        return residual, scale, z, v, up, dot_nt(cot_ref[rows, :], down_ref[...])

    def second(part, made):
        nonlocal gain_grad
        residual, scale, z, v, up, grad_hidden = made
        rows = slice(part * block, (part + 1) * block)
        square = v * v
        t = jnp.tanh(GELU_A * v * (1.0 + GELU_B * square))
        half = 0.5 * (1.0 + t)
        g = v * half
        slope = half + 0.5 * v * (1.0 - t * t) * (GELU_A * (1.0 + 3.0 * GELU_B * square))
        act = (g * up).astype(LOW)
        act_ref[rows, :] = act
        grad_gate = (grad_hidden * up * slope).astype(LOW)
        grad_up = (grad_hidden * g).astype(LOW)
        gg_ref[rows, :] = grad_gate
        gu_ref[rows, :] = grad_up
        grad_feed = dot_nt(grad_gate, gate_ref[...]) + dot_nt(grad_up, up_ref[...])
        u = grad_feed * gain
        gain_grad = gain_grad + jnp.sum(grad_feed * z, axis=0, keepdims=True)
        cot = cot_ref[rows, :].astype(WIDE)
        grad_res = cot + scale * (u - z * jnp.mean(u * z, axis=-1, keepdims=True))
        grad_res_ref[rows, :] = grad_res
        branch = grad_res.astype(LOW)
        branch_ref[rows, :] = branch
        do_ref[rows, :INNER] = dot_nt(branch, wo_ref[...]).astype(LOW)
        output = (residual + dot_nn(act, down_ref[...])).astype(LOW)

        @pl.when(side == part)
        def _():
            keep_ref[...] = output

        @pl.when(side != part)
        def _():
            send_ref[...] = output

    pipelined(range(2), first, second, 1)
    gain_grad_ref[...] = jnp.broadcast_to(gain_grad, gain_grad_ref.shape)
    number = rows_of(WIDTH2, 1)
    stat = jnp.where((number == ONE_A) | ((number >= ONE_B) & (number <= ONE_D)), 1.0, 0.0)
    stat = jnp.where(number == OFF, -rowq_ref[2:3, :], stat)
    for pair in range(PAIRS):
        turned = do_ref[:, pair_slice(pair)].T
        for hh in range(2):
            head = 2 * pair + hh
            grads = turned[hh * HD : (hh + 1) * HD, :].astype(WIDE)
            delta = jnp.sum(grads * context[head], axis=0, keepdims=True)
            lse = ml_ref[head : head + 1, :] + jnp.log(ml_ref[8 + head : 9 + head, :])
            for base, value in ((0, lse), (3 * HEADS, delta)):
                for index, piece in enumerate(three_pieces(-value)):
                    stat = jnp.where(number == base + HEADS * index + head, piece, stat)
    do_ref[:, INNER:] = stat.astype(LOW).T


def put_half(core, keep_ref, send_ref, row, value):
    rows = keep_ref.shape[0]
    half, start = row // rows, row % rows

    @pl.when(core == half)
    def _():
        keep_ref[start : start + value.shape[0], : value.shape[1]] = value

    @pl.when(core != half)
    def _():
        send_ref[start : start + value.shape[0], : value.shape[1]] = value


def put_rows(core, keep_ref, send_ref, row, value):
    rows = keep_ref.shape[0]
    value = value.astype(LOW)
    first = min(value.shape[0], rows - row % rows)
    put_half(core, keep_ref, send_ref, row, value[:first])
    if first < value.shape[0]:
        put_half(core, keep_ref, send_ref, row + first, value[first:])


def feed_grads_kernel(
    sc_ref, act_ref, feed_ref, gg_ref, gu_ref, ctx_ref, branch_ref, cot_ref, gain_grad_ref,
    keep_ref, send_ref,
):
    core = sc_ref[0, CORE]
    put = functools.partial(put_rows, core, keep_ref, send_ref)
    width = keep_ref.shape[1]
    hidden = act_ref.shape[1]
    feed = feed_ref[...].T
    row = 0
    for grads in (gg_ref, gu_ref):
        for start in range(0, hidden, width):
            put(row, dot_nn(feed, grads[:, start : start + width]))
            row += width
    act = act_ref[...].T
    put(row, dot_nn(act, cot_ref[...]))
    row += hidden
    put(row, dot_nn(ctx_ref[...].T, branch_ref[...]))
    row += INNER
    rest = 2 * keep_ref.shape[0] - row
    put(row, jnp.where(rows_of(rest, 1) == 0, gain_grad_ref[0:1, :], 0.0))


def order_kernel(sc_ref, mine_ref, other_ref, out_ref):
    core = sc_ref[0, CORE]
    block = mine_ref.shape[0] // 2
    for owner, ref in ((core, mine_ref), (1 - core, other_ref)):
        for part in range(2):
            at = pl.ds(pl.multiple_of(part * 2 * block + owner * block, block), block)
            out_ref[at, :] = ref[part * block : (part + 1) * block, :]


def chunk_kernel(slot, own, sc_ref, table_ref, do_ref, q_ref, kv0_ref, kv1_ref, a0_ref, a1_ref, e0_ref, e1_ref,
                 wk_ref, wv_ref, vec_ref, *rest):
    if slot > 0:
        (dq_in, w_in, near_in, marks_in), rest = rest[:4], rest[4:]
    if own:
        (extq_ref, rowq_ref, a_own_ref), rest = rest[:3], rest[3:]
        (dx_ref, kept_ref, sent_ref, dq_kept_ref, dq_sent_ref, near_out, marks_ref), rest = rest[:7], rest[7:]
        dq_ref, strip_ref, gen_ref, near_ref, ds_ref, grads_ref = rest
    else:
        dx_ref, dq_ref, w_ref, near_out, marks_ref, near_ref, ds_ref, grads_ref = rest
    quad, core, side_chunk = sc_ref[0, QUAD], sc_ref[0, CORE], sc_ref[slot, CHUNK]
    chunk = q_ref.shape[0]
    block = kv0_ref.shape[0]
    mine = 2 * block
    tiles = mine // TILE
    steps = mine // (2 * TILE)
    number = rows_of(WIDTH2, 1)
    lane = lanes_of(1, WIDTH2)
    build_near(near_ref, vec_ref, 1, range(HEADS))
    ext_turned = jnp.concatenate([e0_ref[...].T, e1_ref[...].T], axis=1).astype(WIDE)
    if own:
        build_strip(strip_ref, near_ref, table_ref, True, chunk, range(HEADS))
        visible_mask(
            gen_ref, extq_ref[...].astype(WIDE)[:, SEG : SEG + 1], rowq_ref[0:1, :], rowq_ref[3:4, :], core, False
        )
        ds_ref[:, :TILE, :] = jnp.zeros((2, TILE, mine), LOW)
        ds_ref[:, chunk + TILE :, :] = jnp.zeros((2, TILE, mine), LOW)
    low, high = near_flags(quad, side_chunk, core)
    keys_before = side_chunk < quad
    gap = side_chunk - quad
    spread = jnp.where(jnp.abs(gap) <= 1, 1, 0)
    first_mark = jnp.where(spread == 1, 16 + 8 * gap, jnp.where(gap < 0, 0, 1))
    mark_of_key = first_mark + spread * (rows_of(mine, 1) // TILE)
    ext = do_ref[:, INNER:]
    made = {}

    def both(pair, base):
        return jnp.concatenate([kv0_ref[:, pair_slice(pair, base)], kv1_ref[:, pair_slice(pair, base)]], axis=0)

    def operands(pair):
        if pair in made:
            return made[pair]
        q_pair, do_pair = q_ref[:, pair_slice(pair)], do_ref[:, pair_slice(pair)]
        k_pair = both(pair, 0)
        k_turned, v_turned = k_pair.T, both(pair, INNER).T
        zero = jnp.zeros_like(k_turned)
        k_sides, v_sides, k_marked = [], [], []
        for hh in range(2):
            head = 2 * pair + hh
            rows = (number == head) | (number == head + HEADS) | (number == head + 2 * HEADS)
            rows = jnp.broadcast_to(jnp.where(rows, 1.0, 0.0), (WIDTH2, mine))
            if not own:
                far = jnp.where(
                    keys_before, far_bias(table_ref, False, head), far_bias(table_ref, True, head)
                )
                wide = jnp.full((1, mine), far, WIDE)
                for at, piece in zip((ONE_A, ONE_B, ONE_C), three_pieces(wide)):
                    rows = jnp.where(number == at, piece, rows)
                rows = jnp.where(number == OFF, 1.0, rows)
                rows = jnp.where(number == ONE_D, ext_turned[MASK : MASK + 1, :], rows)
            k_sides.append(
                jnp.concatenate([row_half(k_turned, hh, zero), rows.astype(LOW)], axis=0)
            )
            first = 3 * HEADS + head
            rows = (number == first) | (number == first + HEADS) | (number == first + 2 * HEADS)
            rows = jnp.broadcast_to(jnp.where(rows, 1.0, 0.0), (WIDTH2, mine)).astype(LOW)
            v_sides.append(jnp.concatenate([row_half(v_turned, hh, zero), rows], axis=0))
            marks = jnp.where(lane - HD * (1 - hh) == mark_of_key, 1.0, 0.0).astype(LOW)
            k_marked.append(lane_half(k_pair, hh, marks))
        made[pair] = (
            jnp.concatenate([q_pair, ext], axis=1), jnp.concatenate([do_pair, ext], axis=1),
            q_pair.T, do_pair.T, k_sides, v_sides, k_marked,
        )
        return made[pair]

    def first(item):
        pair, step, hh = item
        head, lanes = 2 * pair + hh, step_lanes(step)
        q_ext, do_ext, _, _, k_sides, v_sides, _ = operands(pair)
        s = dot_nn(q_ext, k_sides[hh][:, lanes])
        if own:
            s = s + strip_rows(strip_ref, head, 2 * step, 2, core, chunk) + gen_ref[:, lanes]
        else:
            s = fix_near(
                s, step, steps, near_fixes(near_ref, table_ref, (low, high), head, head, True)
            )
        return s, dot_nn(do_ext, v_sides[hh][:, lanes])

    products = {}

    def second(item, found):
        pair, step, hh = item
        head, lanes = 2 * pair + hh, step_lanes(step)
        s, dp = found
        p = jnp.exp(s)
        ds = (p * dp).astype(LOW)
        _, _, q_turned, do_turned, _, _, k_marked = operands(pair)
        half = slice(hh * HD, (hh + 1) * HD)
        grads_ref[head_rows(head), lanes] = dot_nn(q_turned, ds)[half, :].astype(LOW)
        rows = slice(INNER + head * HD, INNER + (head + 1) * HD)
        grads_ref[rows, lanes] = dot_nn(do_turned, p.astype(LOW))[half, :].astype(LOW)
        ds_ref[hh, TILE : chunk + TILE, lanes] = ds
        if not own:
            base = near_in[head] if slot > 0 else jnp.zeros((NEAR, TILE), WIDE)
            if step == 0:
                near_out[head, :TILE, :] = base[:TILE] + low * ds[chunk - TILE :, :TILE].astype(WIDE)
                near_out[head, TILE : 2 * TILE, :] = base[TILE : 2 * TILE]
            if step == steps - 1:
                near_out[head, 2 * TILE :, :] = base[2 * TILE :] + high * ds[:TILE, TILE:].astype(WIDE)
        if step == steps - 1:
            product = dot_nn(ds_ref[hh, TILE : chunk + TILE, :], k_marked[hh])
            for tile in range(chunk // TILE):
                total = jnp.sum(product[tile * TILE : (tile + 1) * TILE, :], axis=0, keepdims=True)
                if slot > 0:
                    total = total + marks_in[head, tile : tile + 1, :]
                marks_ref[head, tile : tile + 1, :] = total
            if own:
                total = near_in[head]
                for tile in range(tiles):
                    at = pl.ds(pl.multiple_of(tile_place(tile, core) * TILE, TILE), NEAR)
                    part = ds_ref[hh, at, tile * TILE : (tile + 1) * TILE]
                    total = total + part.astype(WIDE)
                near_out[head] = total
            products[hh] = product
            if hh == 1:
                total = jnp.where(lane < HD, products[0], products[1])
                if slot > 0:
                    total = total + dq_in[:, pair_slice(pair)]
                dq_ref[:, pair_slice(pair)] = total

    pipelined(forward_items(mine), first, second, 1)
    a = jnp.concatenate([a0_ref[...], a1_ref[...]], axis=0)
    grads = grads_ref[...]
    weights = dot_nn(grads, a)
    if slot > 0:
        weights = weights + w_in[...]
    dx = dot_nt(grads[:INNER, :].T, wk_ref[...]) + dot_nt(grads[INNER:, :].T, wv_ref[...])
    dx_ref[...] = dx.astype(dx_ref.dtype)
    if not own:
        w_ref[...] = weights
        return

    half = kept_ref.shape[0]
    filled = 3 * INNER // 2
    dq = dq_ref[...].astype(LOW)
    rows = jnp.concatenate([dot_tn(dq, a_own_ref[...]), weights], axis=0).astype(LOW)
    empty = jnp.zeros((half - filled, width_of(kept_ref)), LOW)
    for part in range(2):
        put_half(core, kept_ref, sent_ref, part * half, rows[part * filled : (part + 1) * filled])
        put_half(core, kept_ref, sent_ref, part * half + filled, empty)
    for part in range(2):
        rows = slice(part * block, (part + 1) * block)
        at = pl.ds(pl.multiple_of(part * mine + core * block, block), block)
        dq_kept_ref[rows, :] = dq_ref[at, :]
        at = pl.ds(pl.multiple_of(part * mine + (1 - core) * block, block), block)
        dq_sent_ref[rows, :] = dq_ref[at, :].astype(LOW)


def width_of(ref):
    return ref.shape[1]


def table_kernel(sc_ref, near_out, marks_ref, onehot_ref, kept_in, kept_ref, small_ref, sem):
    core = sc_ref[0, CORE]
    lane = lanes_of(1, WIDTH2)
    tiles_in_chunk = marks_ref.shape[1]
    flip = (rows_of(TILE, TILE) + lanes_of(TILE, TILE) == TILE - 1).astype(LOW)
    head_row = rows_of(8, 1)
    table = jnp.zeros((8, WIDTH2), WIDE)
    for part in range(3):
        blocks = jnp.concatenate(
            [near_out[head, part * TILE : (part + 1) * TILE, :] for head in range(HEADS)], axis=1
        )
        turned = sum(dot_nn(flip, piece.astype(LOW)) for piece in three_pieces(blocks))
        sums = jnp.zeros((8, 2 * TILE), WIDE)
        for head in range(HEADS):
            padded = jnp.concatenate(
                [turned[:, head * TILE : (head + 1) * TILE], jnp.zeros((TILE, TILE), WIDE)], axis=1
            )
            skewed = pltpu.roll(padded, 0, 1, stride=1, stride_axis=0)
            sums = jnp.where(head_row == head, jnp.sum(skewed, axis=0, keepdims=True), sums)
        onehot = onehot_ref[part * 2 * TILE : (part + 1) * 2 * TILE, :].astype(LOW)
        table = table + sum(dot_nn(piece.astype(LOW), onehot) for piece in three_pieces(sums))
    query_tile = rows_of(tiles_in_chunk, 1)
    for head in range(HEADS):
        mark = lane - HD * (1 - head % 2)
        inside = (mark >= 8) & (mark < 32)
        kind, tile = mark // 8, mark % 8
        at = (kind - 2) * (tiles_in_chunk) + tile_place(tile, core)
        relative = at - query_tile
        found = marks_ref[head]
        before = (mark == 0) | (inside & (relative < -1))
        after = (mark == 1) | (inside & (relative > 1))
        for chosen, bucket in ((before, FAR_BEFORE), (after, FAR_AFTER)):
            total = jnp.sum(jnp.where(chosen, found, 0.0))
            table = table + jnp.where((head_row == head) & (lane == bucket), total, 0.0)
    small_ref[...] = jnp.zeros_like(small_ref)
    small_ref[:8, :WIDTH2] = table.astype(LOW)
    at = pl.ds(3 * INNER // 2, small_ref.shape[0])
    copy = pltpu.make_async_copy(small_ref, kept_ref.at[at, :], sem)
    copy.start()
    copy.wait()


def chain_kernel(slot, quads, sc_ref, *refs):
    mine, refs = refs[: slot + 1], refs[slot + 1 :]
    up_ref, down_ref = refs[-2:]
    core = sc_ref[0, CORE]
    for column, came, out_ref in ((UP, 0, up_ref), (DOWN, 1, down_ref)):
        edge = jnp.where(core == came, 0, quads - 1)
        for index, dx_ref in enumerate(mine):

            @pl.when(sc_ref[slot, column] == index)
            def _():
                value = dx_ref[...]
                if slot > 0:
                    came_before = refs[came][...].astype(WIDE)
                    total = value.astype(WIDE) + jnp.where(
                        sc_ref[0, QUAD] != edge, came_before, 0.0
                    )
                    value = total.astype(LOW)
                out_ref[...] = value


def join_kernel(sc_ref, kept_ref, got_ref, out_ref):
    side = sc_ref[0, SIDE]
    out_ref[side] = kept_ref[...]
    out_ref[1 - side] = got_ref[...]


def total_kernel(quads, sc_ref, dx_ref, first_ref, second_ref, out_ref):
    quad, core = sc_ref[0, QUAD], sc_ref[0, CORE]
    total = dx_ref[...]
    for came, came_ref in enumerate((first_ref, second_ref)):
        edge = jnp.where(core == came, 0, quads - 1)
        total = total + jnp.where(quad != edge, came_ref[...].astype(WIDE), 0.0)
    out_ref[...] = total


def behind_kernel(quads, parts, sc_ref, owner_ref, *refs):
    ins, outs = refs[: parts + 5], refs[parts + 5 :]
    place_kernel(sc_ref, owner_ref, *ins[:parts], outs[0])
    total_kernel(quads, sc_ref, *ins[parts : parts + 3], outs[1])


def input_kernel(
    sc_ref, dx_ref, dq_ref, dq_got_ref, x_ref, grad_res_ref, wq_ref, gain_ref, keep_ref, send_ref
):
    side = sc_ref[0, SIDE]
    block = x_ref.shape[0] // 2
    gain = gain_ref[...]
    for part in range(2):
        rows = slice(part * block, (part + 1) * block)
        queries = (dq_ref[rows, :] + dq_got_ref[rows, :].astype(WIDE)).astype(LOW)
        grad_in = dot_nt(queries, wq_ref[...]) + dx_ref[rows, :]
        x = x_ref[rows, :].astype(WIDE)
        scale = rms_scale(x)
        z = x * scale
        u = grad_in * gain
        result = grad_res_ref[rows, :] + scale * (u - z * jnp.mean(u * z, axis=-1, keepdims=True))
        result = result.astype(LOW)

        @pl.when(side == part)
        def _():
            keep_ref[...] = result

        @pl.when(side != part)
        def _():
            send_ref[...] = result


def tie_kernel(sc_ref, *refs):
    pass


def add_kernel(sc_ref, order_ref, *refs):
    outs = refs[-order_ref.shape[0] :]
    ins = refs[: len(refs) - len(outs)]
    for index, out_ref in enumerate(outs):
        which = order_ref[index]
        total = ins[0][which].astype(WIDE)
        for in_ref in ins[1:]:
            total = total + in_ref[which].astype(WIDE)
        out_ref[...] = total.astype(LOW)


def tree_kernel(sc_ref, *refs):
    values = [ref[...].astype(WIDE) for ref in refs[:-1]]
    while len(values) > 1:
        values = [values[n] + values[n + 1] for n in range(0, len(values), 2)]
    refs[-1][...] = values[0].astype(LOW)


def place_kernel(sc_ref, owner_ref, *refs):
    out_ref = refs[-1]
    for index, part_ref in enumerate(refs[:-1]):
        out_ref[owner_ref[index]] = part_ref[...]


def whole_rows(core, kept_ref, got_ref, first, count):
    half = kept_ref.shape[0]
    parts = []
    for number in range(2):
        low, high = max(first, number * half), min(first + count, (number + 1) * half)
        if low < high:
            rows = slice(low - number * half, high - number * half)
            part = jnp.where(core == number, kept_ref[rows, :], got_ref[rows, :])
            parts.append(part.astype(WIDE))
    return parts[0] if len(parts) == 1 else jnp.concatenate(parts, axis=0)


def unpack_feed_kernel(sc_ref, kept_ref, got_ref, out_ref, gate_ref, up_ref, down_ref, gain_ref):
    take = functools.partial(whole_rows, sc_ref[0, CORE], kept_ref, got_ref)
    width, hidden = gate_ref.shape
    row = 0
    for grads in (gate_ref, up_ref):
        for start in range(0, hidden, width):
            grads[:, start : start + width] = take(row, width)
            row += width
    down_ref[...] = take(row, hidden)
    row += hidden
    out_ref[...] = take(row, INNER)
    row += INNER
    gain_ref[...] = take(row, 16)[0:1, :]


def unpack_last_kernel(
    sc_ref, kept_ref, got_ref, wq_ref, wk_ref, wv_ref, gain_ref, query_ref, key_ref, value_ref, table_ref, gain_grad_ref,
):
    core = sc_ref[0, CORE]
    filled = 3 * INNER // 2
    first = jnp.where(core == 0, kept_ref[...], got_ref[...])
    second = jnp.where(core == 0, got_ref[...], kept_ref[...])
    grads = jnp.concatenate([first[:filled], second[:filled]], axis=0)
    total = jnp.zeros(gain_ref.shape, WIDE)
    for kind, (w_ref, out_ref) in enumerate(
        ((wq_ref, query_ref), (wk_ref, key_ref), (wv_ref, value_ref))
    ):
        part = grads[kind * INNER : (kind + 1) * INNER]
        out_ref[...] = part.T.astype(WIDE)
        products = part.astype(WIDE) * w_ref[...].T.astype(WIDE)
        total = total + jnp.sum(products, axis=0, keepdims=True)
    gain_grad_ref[...] = total / gain_ref[...]
    small = first[filled : filled + 16].astype(WIDE) + second[filled : filled + 16].astype(WIDE)
    table_ref[...] = small[:HEADS, :BUCKETS]


def staged_sum(kept, sent, between, plan, plan_out, add, place, whole=None, tree=None):
    came = [kept, lax.ppermute(sent, "blk", between)]
    after = yield sent
    for axes, size, index, peer, pairs in plan:
        order = jnp.stack([index] + [peer(index, shift) for shift in range(1, size)])
        own, *sends = add(order.astype(jnp.int32), came, after)
        came = [own] + [
            lax.ppermute(part, axes, pairs(shift)) for shift, part in enumerate(sends, 1)
        ]
        after = yield own
    (value,) = add(jnp.zeros((1,), jnp.int32), came, after)
    if whole is not None:
        axes, size, _, _, pairs = whole
        for number in range(size.bit_length() - 1):
            came = [value, lax.ppermute(value, axes, pairs(1 << number))]
            after = yield value
            value = tree(came, after)
    for axes, size, index, peer, pairs in plan_out:
        came = [lax.ppermute(value, axes, pairs(shift)) for shift in range(1, size)]
        after = yield value
        owners = jnp.stack([index] + [peer(index, -shift) for shift in range(1, size)])
        value = place(owners.astype(jnp.int32), [value] + came, after)
    got = lax.ppermute(value, "blk", between)
    after = yield value
    yield (value, got)


def advance(stages, count, after):
    for _ in range(count):
        tie = stages.send((after,))
    return tie


def finish(stages):
    for now in iter(lambda: stages.send(()), None):
        if isinstance(now, tuple):
            return now


def nearest_order(quads):
    return [
        sorted(range(quads), key=lambda k: (abs(k - place), k)) for place in range(quads)
    ]


def chunk_plan(quads):
    plans = []
    for place in range(quads):
        due = [(quads - 1 + place - d, d) for d in range(place + 1, quads)]
        due += [(quads - 1 - place + d, d) for d in range(place)]
        order = [d for _, d in sorted(due)] + [place]
        rows = []
        for slot in range(quads):
            up, down = quads - 1 + place - slot, place - (quads - 1) + slot
            rows.append(
                (
                    order[slot],
                    order.index(up) if place < up < quads else -1,
                    order.index(down) if 0 <= down < place else -1,
                )
            )
        plans.append(rows)
    return plans


def onehot_tables():
    thresholds = bucket_edges()

    def bucket(offset):
        half_count, exact_count, edges = thresholds
        distance = abs(offset)
        beyond = sum(distance >= edge for edge in edges)
        return (half_count if offset > 0 else 0) + (
            distance if distance < exact_count else exact_count + beyond
        )

    rows = np.zeros((BUCKETS, 2 * TURN), np.float32)
    for turn in range(TURN):
        back = turn if turn < TILE else turn - TURN
        rows[bucket(-TILE - back), turn] = 1.0
        rows[bucket(TILE + back), TURN + turn] = 1.0
    diagonals = np.zeros((6 * TILE, WIDTH2), np.float32)
    for part in range(3):
        for at in range(2 * TILE - 1):
            diagonals[part * 2 * TILE + at, bucket(1 + at - TILE * part)] = 1.0
    return rows, diagonals


def body(
    hidden_in,
    item_lengths,
    live_mask,
    cotangent,
    query_weight,
    key_weight,
    value_weight,
    output_weight,
    bucket_bias_table,
    norm_attention,
    norm_feed,
    gate_weight,
    up_weight,
    down_weight,
):
    streams, block, width = hidden_in.shape
    hidden = gate_weight.shape[1]
    blocks = lax.axis_size("blk")
    parts = lax.axis_size("dp")
    quads = blocks // 4
    here = lax.axis_index("blk")
    replica = lax.axis_index("dp")
    core, side, quad = here % 2, (here // 2) % 2, here // 4
    mine, chunk = 2 * block, 4 * block

    across = [(k, k ^ 2) for k in range(blocks)]
    between = [(k, k ^ 1) for k in range(blocks)]
    onward = []
    for k in range(blocks):
        if k % 2 == 0:
            onward.append((k, k + 4 if k + 4 < blocks else k + 1))
        else:
            onward.append((k, k - 4 if k >= 4 else k - 1))

    order = nearest_order(quads)
    distances = [
        sorted({abs(order[place][step] - place) for place in range(quads)}) for step in range(quads)
    ]
    spots = jnp.asarray(np.array(order, np.int32).T)
    nearest = jnp.asarray(np.array([found[0] for found in distances], np.int32))[:, None]
    is_here = jnp.arange(quads, dtype=jnp.int32)[None, :] == quad
    place = jnp.sum(jnp.where(is_here, spots, 0), axis=1, keepdims=True)
    swapped = ((place > quad) != (core == 1)) & (place != quad)
    source = 2 * (jnp.abs(place - quad) - nearest) + swapped.astype(jnp.int32)
    first_end = jnp.where(side == 0, item_lengths[0, 0], item_lengths[1, 0])
    col = jnp.arange(16, dtype=jnp.int32)[None, :]
    plans = np.array(chunk_plan(quads), np.int32)
    mine_of = [
        jnp.sum(jnp.where(is_here, jnp.asarray(plans[:, :, n].T), 0), axis=1, keepdims=True)
        for n in range(3)
    ]
    sc = jnp.where(col == QUAD, quad, 0)
    sc = jnp.where(col == CORE, core, sc)
    sc = jnp.where(col == SIDE, side, sc)
    sc = jnp.where(col == PLACE, place, sc)
    sc = jnp.where(col == SOURCE, source, sc)
    is_first = core == 0
    up_down = [jnp.where(is_first, mine_of[1], mine_of[2]), jnp.where(is_first, mine_of[2], mine_of[1])]
    for at, values in zip((CHUNK, UP, DOWN), (mine_of[0], *up_down)):
        sc = jnp.where(col == at, values, sc)
    sc = jnp.where(col == FIRST_END, first_end, sc).astype(jnp.int32)

    turned_onehot, diagonal_onehot = (jnp.asarray(t) for t in onehot_tables())

    smem = pl.BlockSpec(memory_space=pltpu.SMEM)
    vmem = pl.BlockSpec(memory_space=pltpu.VMEM)
    anywhere = pl.BlockSpec(memory_space=pl.ANY)
    shape = jax.ShapeDtypeStruct
    strip_rows_count = 2 * chunk - TILE
    near_shape = pltpu.VMEM((HEADS, NEAR, TILE), WIDE)
    strip_shape = pltpu.VMEM((HEADS, strip_rows_count, TILE), WIDE)
    gen_shape = pltpu.VMEM((chunk, mine), WIDE)
    dma = pltpu.SemaphoreType.DMA
    pairs_in_chunk = mine * chunk * HEADS

    def call(kernel, name, in_specs, out_specs, out_shape, scratch, operands, grid=(1,), aliases=None, us=5.0, after=(), limit=24,
             mark=False):
        count = 1 + len(operands)
        if mark:
            out_specs, out_shape = tuple(out_specs) + (vmem,), tuple(out_shape) + (shape((8, 128), WIDE),)
        last = count + len(after) + (len(out_shape) - 1 if mark else 0)

        def without_ties(*refs):
            if mark:
                refs[last][...] = jnp.zeros((8, 128), WIDE)
                refs = refs[:last] + refs[last + 1 :]
            kernel(*refs[:count], *refs[count + len(after) :])

        return pl.pallas_call(
            without_ties if after or mark else kernel,
            grid_spec=pltpu.PrefetchScalarGridSpec(
                num_scalar_prefetch=1,
                grid=grid,
                in_specs=list(in_specs) + [anywhere] * len(after),
                out_specs=out_specs,
                scratch_shapes=scratch,
            ),
            out_shape=out_shape,
            input_output_aliases=aliases or {},
            compiler_params=pltpu.CompilerParams(vmem_limit_bytes=limit * 1024 * 1024),
            cost_estimate=pl.CostEstimate(
                flops=int(us * (1e9 if us >= 4 else 1e7)), bytes_accessed=1 << 12, transcendentals=0
            ),
            name=name,
        )(sc, *operands, *after)

    def far_away(array):
        return pltpu.with_memory_space_constraint(array, pltpu.HBM)

    def tied(arrays, after):
        count = len(arrays)
        return call(
            tie_kernel, "tie", [anywhere] * count, (anywhere,) * count,
            tuple(shape(a.shape, a.dtype) for a in arrays), [], arrays,
            aliases={1 + n: n for n in range(count)}, us=0.3, after=after, limit=16,
        )

    def pick(both, index):
        return lax.dynamic_index_in_dim(both, index, 0, False)

    live_rows = jnp.pad(live_mask.astype(LOW)[:, None, :], ((0, 0), (0, 15), (0, width - block)))
    payload = jnp.concatenate([pick(hidden_in, 1 - side), pick(live_rows, 1 - side)], axis=0)
    got = lax.ppermute(payload, "blk", across)
    packed, x_low = call(
        norm_kernel, "norm_rows", [vmem] * 4, (vmem,) * 2,
        (shape((mine + 16, width), LOW), pltpu.HBM((mine, width), LOW)), [],
        (far_away(hidden_in), far_away(live_mask), got, far_away(norm_attention[None, :])), us=2.0,
    )
    own_chunk = jnp.concatenate([packed, lax.ppermute(packed, "blk", between)], axis=0)
    cot_got = lax.ppermute(pick(cotangent, 1 - side), "blk", across)

    qkv_shape = pltpu.HBM((quads * chunk, 3 * INNER), LOW)
    ext_shape = pltpu.HBM((quads * chunk, WIDTH2), LOW)
    state_shapes = (shape((INNER, mine), WIDE), shape((16, mine), WIDE))

    def chunk_out(step, columns):
        return pl.BlockSpec((chunk, columns), lambda i, sc: (sc[step, PLACE], 0))

    a_shape = pltpu.HBM((quads * chunk, width), LOW)
    chunk_scratch = [pltpu.VMEM((2, 16, width), LOW)]
    held = lax.ppermute(own_chunk, "blk", onward)
    rowk, rowq, vec = call(
        places_kernel, "places", [smem] + [vmem] * 3, (vmem,) * 3,
        (shape((8, chunk), WIDE), shape((8, mine), WIDE), shape((8, 2 * TURN), WIDE)), [],
        (item_lengths, packed, bucket_bias_table, turned_onehot), us=2.0, after=(own_chunk,), limit=16,
    )
    qkv, ext, normed, qx, acc, ml, q_own = call(
        forward_own_kernel, "attend_own", [smem, anywhere] + [vmem] * 6,
        (chunk_out(0, 3 * INNER), chunk_out(0, WIDTH2), chunk_out(0, width), vmem, vmem, vmem, vmem),
        (qkv_shape, ext_shape, a_shape, shape((HEADS, 2 * WIDTH2, mine), LOW)) + state_shapes
        + (shape((chunk, INNER), LOW),),
        chunk_scratch + [strip_shape, near_shape, gen_shape, dma((6,))],
        (bucket_bias_table, own_chunk, key_weight, value_weight, query_weight, vec, rowq, rowk),
        us=12.0,
    )

    came = []
    for step in range(1, quads):
        held, acc = lax.optimization_barrier((held, acc))
        came.append((held, lax.ppermute(held, "blk", between)))
        if step + 1 < quads:
            held = lax.ppermute(held, "blk", onward)
        arrays = [array for distance in distances[step] for array in came[distance - 1]]
        qkv, ext, normed, acc, ml = call(
            functools.partial(forward_kernel, step, len(arrays)), "attend_other",
            [smem] + [vmem] * 7 + [anywhere] * (3 + len(arrays)),
            (chunk_out(step, 3 * INNER), chunk_out(step, WIDTH2), chunk_out(step, width), vmem, vmem),
            (qkv_shape, ext_shape, a_shape) + state_shapes,
            chunk_scratch + [near_shape, dma((6,))],
            (bucket_bias_table, key_weight, value_weight, query_weight, vec, qx, acc, ml, qkv, ext, normed, *arrays),
            aliases={7: 3, 8: 4, 9: 0, 10: 1, 11: 2}, us=10.0,
        )

    (do_mine, out_kept, out_sent, grad_res, act, feed, grad_gate, grad_up,
     context, branch, gain_grad, cot) = call(
        middle_kernel, "feed_both_ways", [vmem] * 11, (vmem,) * 12,
        (
            shape((mine, INNER + WIDTH2), LOW),
            shape((block, width), LOW), shape((block, width), LOW), pltpu.HBM((mine, width), WIDE),
            shape((mine, hidden), LOW), shape((mine, width), LOW), shape((mine, hidden), LOW),
            shape((mine, hidden), LOW), shape((mine, INNER), LOW), shape((mine, width), LOW),
            shape((8, width), WIDE), shape((mine, width), LOW),
        ), [],
        (
            acc, ml, x_low, cotangent, cot_got, rowq, output_weight, gate_weight, up_weight, down_weight,
            norm_feed[None, :],
        ),
        us=12.0,
    )
    do_other = lax.ppermute(do_mine, "blk", between)
    def joined(kept, got, after):
        return call(
            join_kernel, "join", [vmem] * 2, (vmem,), (pltpu.HBM((2, block, width), LOW),), [], (kept, got),
            us=1.0, after=after, limit=16, mark=True,
        )

    def over_blocks(shift):
        return [(k, k ^ (4 * shift)) for k in range(blocks)]

    over_side = ("blk", 2, side, lambda i, s: i ^ 1, lambda s: across)
    over_parts = (
        "dp", parts, replica, lambda i, s: (i + s) % parts,
        lambda s: [(k, (k + s) % parts) for k in range(parts)],
    )
    over_quads = ("blk", quads, quad, lambda i, s: i ^ abs(s), over_blocks)
    if parts == 2:

        def square_pairs(shift):
            pairs = []
            for k in range(blocks):
                for r in range(parts):
                    k2, r2 = k ^ (2 * (shift >> 1)), r ^ (shift & 1)
                    pairs.append((k * parts + r, k2 * parts + r2))
            return pairs

        over_square = (("blk", "dp"), 4, side * 2 + replica, lambda i, s: i ^ abs(s), square_pairs)
        plan = [over_square, over_quads]
    else:
        plan = [over_side, over_parts, over_quads]
    plan_out = plan[::-1]
    groups = len(plan) - 1
    pieces_in_all = 8 * 2 * 2 * parts * quads

    def padded(rows):
        return -(-rows // pieces_in_all) * pieces_in_all

    feed_rows = padded(3 * hidden + INNER + 8) // 2
    feed_kept, feed_sent = call(
        feed_grads_kernel, "feed_weight_grads", [vmem] * 8, (vmem, vmem),
        (shape((feed_rows, width), LOW),) * 2, [],
        (act, feed, grad_gate, grad_up, context, branch, cot, gain_grad), us=7.0,
    )
    def add_parts(order, arrays, after):
        size = order.shape[0]
        split = [a.reshape((size, a.shape[0] // size, a.shape[1])) for a in arrays]
        return call(
            add_kernel, "add_parts", [smem] + [vmem] * len(split), (vmem,) * size,
            (shape(split[0].shape[1:], LOW),) * size, [], (order, *split), us=2.0, after=after, limit=16,
        )

    behind, passed = [], []

    def place_parts(owners, arrays, after):
        one = arrays[0].shape
        if behind:
            count = len(arrays)
            *wide, sent, dq_sent = behind.pop()
            whole, *found = call(
                functools.partial(behind_kernel, quads, count), "behind_last_chunk",
                [smem] + [vmem] * (count + 3) + [anywhere] * 2, (vmem, vmem, anywhere, anywhere),
                (
                    shape((count,) + one, LOW), shape((mine, width), WIDE), shape(sent.shape, LOW),
                    shape(dq_sent.shape, LOW),
                ), [],
                (owners, *arrays, *wide, sent, dq_sent), us=2.0, after=after, limit=16,
                aliases={count + 5: 2, count + 6: 3},
            )
            passed.extend(found)
            return whole.reshape((-1,) + one[1:])
        whole = call(
            place_kernel, "place_parts", [smem] + [vmem] * len(arrays), vmem,
            shape((len(arrays),) + one, LOW), [], (owners, *arrays), us=1.0, after=after, limit=16,
        )
        return whole.reshape((-1,) + one[1:])

    def tree_parts(arrays, after):
        return call(
            tree_kernel, "tree_parts", [vmem] * len(arrays), vmem, shape(arrays[0].shape, LOW), [], tuple(arrays),
            us=1.0, after=after, limit=16,
        )

    feed_stages = staged_sum(feed_kept, feed_sent, between, plan, plan_out, add_parts, place_parts)
    next(feed_stages)
    out_got = lax.ppermute(out_sent, "blk", across)
    tie = feed_stages.send(())
    do_chunk = call(
        order_kernel, "order", [vmem] * 2, vmem, shape((chunk, INNER + WIDTH2), LOW), [], (do_mine, do_other),
        us=1.0, after=(tie,), limit=16,
    )

    ties = [tie]

    qkv, ext, normed = far_away(qkv), far_away(ext), far_away(normed)
    backward = [(end, start) for start, end in onward]
    last_pieces = 8 * 2 * 2 * parts
    last_rows = -(-(3 * INNER + 32) // last_pieces) * last_pieces // 2
    state_shape = (
        shape((chunk, INNER), WIDE), shape((2 * INNER, width), WIDE), shape((HEADS, NEAR, TILE), WIDE),
        shape((HEADS, chunk // TILE, WIDTH2), WIDE),
    )

    def chunk_rows(slot, n, columns):
        return pl.BlockSpec(
            (block, columns), lambda i, sc: (4 * sc[slot, CHUNK] + sc[0, CORE] + 2 * n, 0)
        )

    state, gradients, came = (), [], ()
    for slot in range(quads):
        own = slot == quads - 1
        operands = (
            bucket_bias_table, do_chunk, q_own, qkv, qkv, normed, normed, ext, ext, key_weight, value_weight, vec,
        ) + tuple(state)
        in_specs = [
            smem, vmem, vmem,
            chunk_rows(slot, 0, 2 * INNER), chunk_rows(slot, 1, 2 * INNER),
            chunk_rows(slot, 0, width), chunk_rows(slot, 1, width),
            chunk_rows(slot, 0, WIDTH2), chunk_rows(slot, 1, WIDTH2), vmem, vmem, vmem,
        ] + [vmem] * len(state)
        scratch = [
            near_shape, pltpu.VMEM((2, chunk + 2 * TILE, mine), LOW), pltpu.VMEM((2 * INNER, mine), LOW),
        ]
        outs = (shape((mine, width), WIDE if own else LOW),)
        if own:
            operands += (ext, rowq, normed)
            in_specs += [
                pl.BlockSpec((chunk, WIDTH2), lambda i, sc: (sc[0, QUAD], 0)), vmem,
                pl.BlockSpec((chunk, width), lambda i, sc: (sc[0, QUAD], 0)),
            ]
            outs += (shape((last_rows, width), LOW),) * 2
            outs += (shape((mine, INNER), WIDE), shape((mine, INNER), LOW)) + state_shape[2:]
            scratch = [pltpu.VMEM((chunk, INNER), WIDE), strip_shape, gen_shape] + scratch
        else:
            outs += state_shape
        found = call(
            functools.partial(chunk_kernel, slot, own), "grad_chunk", in_specs, (vmem,) * len(outs), outs, scratch,
            operands, us=10.0, after=ties, limit=32 if own else 28,
            aliases={13 + n: 1 + n for n in range(4)} if slot and not own else None,
        )
        gradients.append(found[0])
        if own:
            kept, sent, dq_kept, dq_sent, near_grad, marks = found[1:]
            break
        state = found[1:]
        ties = []
        if 0 < slot < 3:
            ties.append(advance(feed_stages, 1 if slot == 1 else groups, found[0]))
        up, down = call(
            functools.partial(chain_kernel, slot, quads), "chain", [vmem] * (len(gradients) + len(came)), (vmem,) * 2,
            (shape((mine, width), LOW),) * 2, [], tuple(gradients) + tuple(came), us=1.0, after=ties, limit=16,
        )
        came = (lax.ppermute(up, "blk", onward), lax.ppermute(down, "blk", backward))
        ties = ties + [up]
        if slot == 0:
            output, mark = joined(out_kept, out_got, (up,))
            ties.append(advance(feed_stages, groups, mark))
    behind.append((gradients[-1], *came, sent, dq_sent))
    tie = advance(feed_stages, 1, kept)
    total, sent, dq_sent = passed
    kept = call(
        table_kernel, "bias_table", [vmem] * 3 + [anywhere], anywhere, shape(kept.shape, LOW),
        [pltpu.VMEM((16, width), LOW), dma], (near_grad, marks, diagonal_onehot, kept),
        aliases={4: 0}, us=2.0, after=(sent,), limit=16,
    )
    last_stages = staged_sum(
        kept, sent, between, plan[:-1], plan_out[1:], add_parts, place_parts, over_quads, tree_parts
    )
    next(last_stages)
    dq_got = lax.ppermute(dq_sent, "blk", between)
    feed_kept, feed_got = feed_stages.send(())
    tie = advance(last_stages, 1, kept)
    in_kept, in_sent = call(
        input_kernel, "grad_input", [vmem] * 7, (vmem,) * 2,
        (shape((block, width), LOW), shape((block, width), LOW)), [],
        (total, dq_kept, dq_got, x_low, grad_res, query_weight, norm_attention[None, :]),
        us=2.0, after=(tie,),
    )
    grad_out, grad_gate, grad_up, grad_down, grad_norm_feed, mark = call(
        unpack_feed_kernel, "unpack_feed", [vmem] * 2, (vmem,) * 5,
        (
            pltpu.HBM((INNER, width), WIDE), pltpu.HBM((width, hidden), WIDE), pltpu.HBM((width, hidden), WIDE),
            pltpu.HBM((hidden, width), WIDE), pltpu.HBM((1, width), WIDE),
        ), [],
        (feed_kept, feed_got), us=3.9, after=(in_kept,), mark=True,
    )
    (in_sent,) = tied((in_sent,), (mark,))
    for _ in range(groups):
        tie = last_stages.send((mark,))
    in_got = lax.ppermute(in_sent, "blk", across)
    doublings = quads.bit_length() - 1
    for _ in range(doublings - 1):
        tie = last_stages.send(())
    input_gradient, mark = joined(in_kept, in_got, (tie,))
    last_stages.send((mark,))
    for _ in range(groups):
        last_stages.send(())
    last_kept, last_got = finish(last_stages)
    grad_query, grad_key, grad_value, grad_table, grad_norm_attention = call(
        unpack_last_kernel, "unpack_attention", [vmem] * 6, (vmem,) * 5,
        (pltpu.HBM((width, INNER), WIDE),) * 3 + (shape((HEADS, BUCKETS), WIDE), shape((1, width), WIDE)), [],
        (last_kept, last_got, query_weight, key_weight, value_weight, norm_attention[None, :]), us=2.0,
    )
    return (
        output,
        input_gradient,
        grad_query,
        grad_key,
        grad_value,
        grad_out,
        grad_table.T,
        grad_norm_attention[0],
        grad_norm_feed[0],
        grad_gate,
        grad_up,
        grad_down,
    )


def solution(mesh):
    return jax.shard_map(
        body,
        mesh=mesh,
        in_specs=(
            P("dp", "blk", None),
            P("dp", None),
            P("dp", "blk"),
            P("dp", "blk", None),
            P(),
            P(),
            P(),
            P(),
            P(),
            P(),
            P(),
            P(),
            P(),
            P(),
        ),
        out_specs=(
            P("dp", "blk", None),
            P("dp", "blk", None),
            P(),
            P(),
            P(),
            P(),
            P(),
            P(),
            P(),
            P(),
            P(),
            P(),
        ),
        check_vma=False,
    )
```
